128 devices in a mesh: bucket: 8 (over z, core), shard: 16 (over x, y).
Axes of the slice: x: 4, y: 4, z: 4, core: 2. Of those that a mesh axis runs over, the one named last changes fastest.
Arguments:
- head_rows: bfloat16 [65536, 400], P(('bucket', 'shard'))
- tail_rows: bfloat16 [65536, 400], P(('bucket', 'shard')), may hold values from -2.5 to 2.5
- rel_ids: int32 [65536], P(('bucket', 'shard')), may hold values from 0 to 511
- relations: float32 [512, 400], replicated, as said below
- edge_weights: float32 [65536], P(('bucket', 'shard')), may hold values from 0.5 to 2
- neg_rows: bfloat16 [8192, 400], P('bucket')
- send_slots: int32 [16384, 16], P(('bucket', 'shard')), may hold values from -1 to 1023, as said below
- dest_rows: int32 [16384, 16], P(('bucket', 'shard')), may hold values from 0 to 1024, as said below
Outputs:
- ent_grad: float32 [131072, 400], P(('bucket', 'shard'))
- neg_grad: float32 [8192, 400], P(('bucket', 'shard'))
- rel_grad: float32 [512, 400], replicated
The draws below stay inside these ranges and needn't reach their ends.
Inputs may be any that keep to these rules, and one draw needn't show every extreme that they name: `send_slots`: each of a device's 2 * 512 edge ends stands in exactly one of its slots; -1 marks an empty slot. `dest_rows`: A row below 1024 in every used slot; exactly 1024 in every empty slot. `relations`: the magnitude of every relation's real part is at least 0.5.
All inputs are finite; a program needn't handle non-finite values.
Results may differ from the reference program's by a relative error of at most 0.0035.
Values may be sent and summed in bfloat16 or wider, within the bound.
A program may use at most 128 MiB of HBM per device.

```python
import math
import jax
import jax.numpy as jnp
from jax import lax

D = 400
E_DEV = 512
ENT_DEV = 1024
REL = 512
EDGES = 65536
NEGS = 8192
SLOT = 16
ENTITIES = 131072
N_BUCKET = 8
N_SHARD = 16


def relation_kinds(key):
    return jax.random.randint(jax.random.fold_in(key, 101), (EDGES,), 0, REL)


def relation_table(key):
    half_width = D // 2
    base_key = jax.random.fold_in(key, 301)
    magnitude = jax.random.uniform(jax.random.fold_in(base_key, 1), (REL, half_width), jnp.float32, 0.5, 1.5)
    signs = (jax.random.randint(jax.random.fold_in(base_key, 2), (REL, half_width), 0, 2) * 2 - 1).astype(jnp.float32)
    imag_part = jnp.clip(0.5 * jax.random.normal(jax.random.fold_in(base_key, 3), (REL, half_width), jnp.float32), -1.5, 1.5)
    return jnp.concatenate([magnitude * signs, imag_part], axis=1)


def negative_normal(key):
    return jnp.clip(0.3 * jax.random.normal(jax.random.fold_in(key, 401), (NEGS, D), jnp.float32), -1.8, 1.8)


def owner_layout(key):
    devices = N_BUCKET * N_SHARD
    hot_owner = jax.random.randint(jax.random.fold_in(key, 201), (), 0, devices)
    peer_rows = jnp.arange(devices, dtype=jnp.int32)

    def one_sender(sender):
        sender_key = jax.random.fold_in(jax.random.fold_in(key, 202), sender)
        endpoint_order = jax.random.permutation(jax.random.fold_in(sender_key, 1), 2 * E_DEV).astype(jnp.int32)
        slot_ranks = jax.random.permutation(jax.random.fold_in(sender_key, 2), (devices - 1) * SLOT).reshape(devices - 1, SLOT)
        occupied = slot_ranks < 2 * E_DEV - SLOT
        other_row = jnp.clip(peer_rows - (peer_rows > hot_owner).astype(jnp.int32), 0, devices - 2)
        used_mask = jnp.where((peer_rows == hot_owner)[:, None], True, occupied[other_row])
        flat_mask = used_mask.reshape(-1)
        position = jnp.cumsum(flat_mask.astype(jnp.int32)) - 1
        slot_list = jnp.where(flat_mask, endpoint_order[jnp.clip(position, 0, 2 * E_DEV - 1)], -1).reshape(devices, SLOT)
        row_draw = jax.random.randint(jax.random.fold_in(sender_key, 3), (devices, SLOT), 0, ENT_DEV)
        row_list = jnp.where(used_mask, row_draw, ENT_DEV)
        return (slot_list.astype(jnp.int32), row_list.astype(jnp.int32))
    slot_list, row_list = jax.vmap(one_sender)(jnp.arange(devices, dtype=jnp.int32))
    return (slot_list.reshape(devices * devices, SLOT), row_list.reshape(devices * devices, SLOT))


def draw_rel_ids(key, part):
    return relation_kinds(key).astype(jnp.int32)


def draw_relations(key, part):
    return relation_table(key).astype(jnp.float32)


def draw_neg_rows(key, part):
    values = negative_normal(key)
    return values.astype(jnp.bfloat16)


def draw_send_slots(key, part):
    return owner_layout(key)[0]


def draw_dest_rows(key, part):
    return owner_layout(key)[1]


def draw_head_rows(key, part):
    own_key = jax.random.fold_in(key, 11)
    values = jnp.clip(0.3 * jax.random.normal(own_key, (EDGES, D), jnp.float32), -1.8, 1.8)
    return values.astype(jnp.bfloat16)


def level_of(stream_key, extent, split, smallest, high):
    def one(dim, shards_of):
        steps = jax.random.uniform(jax.random.fold_in(jax.random.fold_in(stream_key, 6), dim), (shards_of,), jnp.float32, smallest / len(split), high / len(split))
        return jnp.repeat(jnp.exp(steps), extent[dim] // shards_of).reshape((-1,) + (1,) * (len(extent) - dim - 1))

    level = one(*split[0])
    for cut in split[1:]:
        level = level * one(*cut)
    return level


def scatter_about(stream_key, dims, deviation, most, cuts=(), kind=jnp.bfloat16):
    values = deviation * jax.random.normal(stream_key, dims, jnp.float32)
    if cuts:
        values = values * level_of(stream_key, dims, cuts, -0.22, 0.18)
    return jnp.clip(values, -most, most).astype(kind)


def setup_inputs(seed: int = 0) -> dict:
    keys = jax.random.split(jax.random.key(seed), 9)
    head_rows = draw_head_rows(jax.random.fold_in(keys[8], 71), 0)
    tail_rows = scatter_about(keys[1], (EDGES, D), 0.3, 2.5, ((0, 128),))
    rel_ids = draw_rel_ids(jax.random.fold_in(keys[8], 71), 0)
    relations = draw_relations(jax.random.fold_in(keys[8], 71), 0)
    edge_weights = jnp.clip(jnp.exp(math.log(2.0) - 1.3862944 * jax.random.uniform(keys[4], (EDGES,), jnp.float32) ** level_of(keys[4], (EDGES,), ((0, 128),), -0.2, 0.2)), 0.5, 2.0)
    neg_rows = draw_neg_rows(jax.random.fold_in(keys[8], 71), 0)
    send_slots = draw_send_slots(jax.random.fold_in(keys[8], 71), 0)
    dest_rows = draw_dest_rows(jax.random.fold_in(keys[8], 71), 0)
    return dict(head_rows=head_rows, tail_rows=tail_rows, rel_ids=rel_ids, relations=relations, edge_weights=edge_weights, neg_rows=neg_rows, send_slots=send_slots, dest_rows=dest_rows)


def split_halves(values, half_width):
    return values[:, :half_width], values[:, half_width:]


def edge_gradients(heads, tails, relation_rows, weights, negatives):
    half_width = heads.shape[1] // 2
    head_real, head_imag = split_halves(heads.astype(jnp.float32), half_width)
    rel_real, rel_imag = split_halves(relation_rows, half_width)
    queries = jnp.concatenate([head_real * rel_real - head_imag * rel_imag, head_real * rel_imag + head_imag * rel_real], axis=1).astype(jnp.bfloat16)
    query_wide = queries.astype(jnp.float32)
    tail_wide = tails.astype(jnp.float32)
    positive = jnp.sum(query_wide * tail_wide, axis=1)
    scores = jnp.dot(queries, negatives.T, preferred_element_type=jnp.float32)
    log_total = jax.nn.logsumexp(jnp.concatenate([positive[:, None], scores], axis=1), axis=1)
    pos_coef = weights * (jnp.exp(positive - log_total) - 1.0)
    neg_coef = (jnp.exp(scores - log_total[:, None]) * weights[:, None]).astype(jnp.bfloat16)
    query_grad = pos_coef[:, None] * tail_wide + jnp.dot(neg_coef, negatives, preferred_element_type=jnp.float32)
    neg_term = jnp.dot(neg_coef.T, queries, preferred_element_type=jnp.float32)
    tail_grad = pos_coef[:, None] * query_wide
    grad_real, grad_imag = split_halves(query_grad, half_width)
    head_grad = jnp.concatenate([grad_real * rel_real + grad_imag * rel_imag, grad_imag * rel_real - grad_real * rel_imag], axis=1)
    rel_term = jnp.concatenate([grad_real * head_real + grad_imag * head_imag, grad_imag * head_real - grad_real * head_imag], axis=1)
    return head_grad, tail_grad, neg_term, rel_term


def reference(head_rows, tail_rows, rel_ids, relations, edge_weights, neg_rows, send_slots, dest_rows):
    devices = N_BUCKET * N_SHARD
    model_width = head_rows.shape[1]

    def sender_step(running, sender):
        entity_sum, negative_sum, relation_sum = running
        first_edge = (sender * E_DEV).astype(jnp.int32)
        heads = lax.dynamic_slice_in_dim(head_rows, first_edge, E_DEV, 0)
        tails = lax.dynamic_slice_in_dim(tail_rows, first_edge, E_DEV, 0)
        kinds = lax.dynamic_slice_in_dim(rel_ids, first_edge, E_DEV, 0)
        weights = lax.dynamic_slice_in_dim(edge_weights, first_edge, E_DEV, 0)
        relation_rows = jnp.take(relations, kinds, axis=0)
        head_grad, tail_grad, neg_term, rel_term = edge_gradients(heads, tails, relation_rows, weights, neg_rows)
        relation_sum = relation_sum + jax.ops.segment_sum(rel_term, kinds, num_segments=REL)
        endpoints = jnp.concatenate([head_grad, tail_grad], axis=0)
        first_slot = (sender * devices).astype(jnp.int32)
        slot_list = lax.dynamic_slice_in_dim(send_slots, first_slot, devices, 0)
        row_list = lax.dynamic_slice_in_dim(dest_rows, first_slot, devices, 0)
        is_valid = slot_list >= 0
        packed = jnp.where(is_valid[:, :, None], endpoints[jnp.maximum(slot_list, 0)], 0.0)
        owners = jnp.arange(devices, dtype=jnp.int32)[:, None]
        target_rows = jnp.where(is_valid, owners * ENT_DEV + row_list, devices * ENT_DEV)
        entity_sum = entity_sum.at[target_rows.reshape(-1)].add(packed.reshape(-1, model_width), mode="drop")
        return (entity_sum, negative_sum + neg_term, relation_sum), None

    start_state = (jnp.zeros((ENTITIES, model_width), jnp.float32), jnp.zeros((NEGS, model_width), jnp.float32), jnp.zeros((REL, model_width), jnp.float32))
    final_state, _ = lax.scan(sender_step, start_state, jnp.arange(devices, dtype=jnp.int32))
    entity_sum, negative_sum, relation_sum = final_state
    return entity_sum, negative_sum, relation_sum
```

```python
import functools

import jax
import jax.numpy as jnp
from jax import lax
from jax.experimental import pallas as pl
from jax.experimental.pallas import tpu as pltpu
from jax.sharding import PartitionSpec as P

D = 400
HALF = 200
DP = 512
E_DEV = 512
ENT_DEV = 1024
REL = 512
NEG_DEV = 1024
SLOT = 16
NB = 8
NS = 16
NZ = 4
EC = 256
NEG_OWN = 64

MESH = pl.DeviceIdType.MESH
F32 = jnp.float32
BF16 = jnp.bfloat16

Q_S, ST_S, O_S, SL_S, RC_S, R2_S, R3_S, R4_S, R5_S, A1_S, B1_S, A2_S, B2_S, ENT_S, Z_S, X_S, Y_S = range(17)


def nt(a, b):
    return lax.dot_general(a, b, (((1,), (1,)), ((), ())), preferred_element_type=F32)


def nn(a, b):
    return jnp.dot(a, b, preferred_element_type=F32)


def iota(shape, dim):
    return lax.broadcasted_iota(jnp.int32, shape, dim)


def transpose_rows(x):
    n = x.shape[0]
    wide = jnp.concatenate([x, jnp.zeros((n, DP - D), x.dtype)], axis=1)
    return wide.T[:D]


def wait_bytes(ref, sem):
    pltpu.make_async_copy(ref, ref, sem).wait()


def kernel(
    head, tail, ids, rel, wts, neg, slots, drows,
    ent_out, neg_out, rel_out,
    nb, nbt, prob, qt, sq, hts, tts, rts, mb, st, ot, ot_in, lt, qs, ends, rt_hi, rt_lo,
    packed, arrived, slot_col, dest_col, ga, gb, ra1, rb1, a2, ra2, b2, rb2,
    rp, rp_in, r1b, r2in, r2all, rfin,
    send, recv, zrecv, xrecv, yrecv,
):
    bucket, shard = lax.axis_index("bucket"), lax.axis_index("shard")
    z, c = bucket // 2, bucket % 2
    x, y = shard // 4, shard % 4
    oc = 1 - c
    me = bucket * NS + shard
    partner = (z * 2 + oc, shard)

    def rcopy(src, dst, s_sem, r_sem, device):
        copy = pltpu.make_async_remote_copy(
            src_ref=src, dst_ref=dst, send_sem=s_sem, recv_sem=r_sem,
            device_id=device, device_id_type=MESH,
        )
        copy.start()

    barrier = pltpu.get_barrier_semaphore()

    def greet(i, carry):
        d = lax.rem(me + i, NB * NS)
        pl.semaphore_signal(barrier, inc=1, device_id=(d // NS, d % NS), device_id_type=MESH)
        return carry

    lax.fori_loop(1, NB * NS, greet, 0)

    nb[z, :, 0:384] = neg[:, 0:384]
    nb[z, :, 384:512] = jnp.concatenate(
        [neg[:, 384:400], jnp.zeros((NEG_DEV, 112), BF16)], axis=1
    )

    rel_t = transpose_rows(rel[...])
    rel_1 = rel_t.astype(BF16)
    rest = rel_t - rel_1.astype(F32)
    rel_2 = rest.astype(BF16)
    rel_3 = (rest - rel_2.astype(F32)).astype(BF16)
    for j in range(2):
        rows = slice(j * EC, (j + 1) * EC)
        h_t = transpose_rows(head[rows, :].astype(F32))
        t_t = transpose_rows(tail[rows, :].astype(F32))
        hot = (iota((REL, EC), 0) == ids[0:1, rows]).astype(F32).astype(BF16)
        r_t = (nn(rel_1, hot) + nn(rel_2, hot)) + nn(rel_3, hot)
        hre, him = h_t[:HALF], h_t[HALF:]
        rre, rim = r_t[:HALF], r_t[HALF:]
        q = jnp.concatenate([hre * rre - him * rim, hre * rim + him * rre], axis=0).astype(BF16)
        qt[2 * c + j, 0:D, :] = q
        qt[2 * c + j, D:DP, :] = jnp.zeros((DP - D, EC), BF16)
        sq[2 * c + j, 0:1, :] = jnp.sum(q.astype(F32) * t_t, axis=0, keepdims=True)
        sq[2 * c + j, 1:2, :] = wts[0:1, rows]
        hts[j] = h_t
        tts[j] = t_t
        rts[j] = r_t
        rows8 = jnp.zeros((6, EC), F32)
        sq[2 * c + j, 2:8, :] = rows8

    pl.semaphore_wait(barrier, NB * NS - 1)

    for k in (1, 3, 2):
        zz = lax.rem(z + k, NZ)
        for off in (x * 128, 512 + y * 128):
            part = nb.at[z, pl.ds(pl.multiple_of(off, 128), 128)]
            rcopy(part, part, send.at[Z_S], zrecv.at[k], (zz * 2 + c, shard))
    mine = pl.ds(2 * c, 2)
    rcopy(qt.at[mine], qt.at[mine], send.at[Q_S], recv.at[Q_S], partner)
    rcopy(sq.at[mine], sq.at[mine], send.at[SL_S], recv.at[SL_S], partner)

    for b in range(NB):
        slot_col[b] = jnp.broadcast_to(slots[b : b + 1, :].astype(F32), (128, 256)).T
        dest_col[b] = jnp.broadcast_to(drows[b : b + 1, :].astype(F32), (128, 256)).T

    wait_bytes(qt.at[mine], recv.at[Q_S])
    wait_bytes(sq.at[mine], recv.at[SL_S])

    def forward(k):
        src = lax.rem(z + NZ - k, NZ)
        wait_bytes(nb.at[src, pl.ds(0, 256)], zrecv.at[k])
        part_x = nb.at[src, pl.ds(pl.multiple_of(x * 128, 128), 128)]
        part_y = nb.at[src, pl.ds(pl.multiple_of(512 + y * 128, 128), 128)]
        for i in (1, 3, 2):
            xx, yy = lax.rem(x + i, 4), lax.rem(y + i, 4)
            rcopy(part_x, part_x, send.at[X_S], xrecv.at[k], (bucket, xx * 4 + y))
            rcopy(part_y, part_y, send.at[Y_S], yrecv.at[k], (bucket, x * 4 + yy))

    def block(zb, first):
        for r in range(4):
            rr = slice(r * 256, (r + 1) * 256)
            nbt[:, rr] = nb[zb, rr, :].astype(F32).T.astype(BF16)

        def chunk(g, carry):
            s = nn(nb[zb], qt[g])
            m = jnp.max(s, axis=0, keepdims=True)
            p = jnp.exp(s - m)
            l = jnp.sum(p, axis=0, keepdims=True)
            pb = p.astype(BF16)
            prob[zb, g] = pb
            o = nn(nbt[0:D, :], pb)
            mb[zb, g, 0:1, :] = m
            if first:
                st[c, g, 0:1, :] = m
                st[c, g, 1:2, :] = l
                st[c, g, 2:8, :] = jnp.zeros((6, EC), F32)
                ot[g] = o
            else:
                m_old = st[c, g, 0:1, :]
                m_new = jnp.maximum(m_old, m)
                f_old = jnp.exp(m_old - m_new)
                f_new = jnp.exp(m - m_new)
                st[c, g, 0:1, :] = m_new
                st[c, g, 1:2, :] = st[c, g, 1:2, :] * f_old + l * f_new
                ot[g] = ot[g] * f_old + o * f_new
            return carry

        lax.fori_loop(0, 4, chunk, 0)

    block(z, True)
    for k in (1, 3, 2):
        forward(k)
    for k in (1, 3, 2):
        src = lax.rem(z + NZ - k, NZ)
        wait_bytes(nb.at[src, pl.ds(0, 384)], xrecv.at[k])
        wait_bytes(nb.at[src, pl.ds(0, 384)], yrecv.at[k])
        block(src, False)

    rcopy(st.at[c], st.at[c], send.at[ST_S], recv.at[ST_S], partner)
    rcopy(ot.at[pl.ds(2 * oc, 2)], ot_in, send.at[O_S], recv.at[O_S], partner)
    wait_bytes(st.at[c], recv.at[ST_S])
    for g in range(4):
        pos = sq[g, 0:1, :]
        m0, m1 = st[0, g, 0:1, :], st[1, g, 0:1, :]
        top = jnp.maximum(pos, jnp.maximum(m0, m1))
        total = (
            jnp.exp(pos - top)
            + st[0, g, 1:2, :] * jnp.exp(m0 - top)
            + st[1, g, 1:2, :] * jnp.exp(m1 - top)
        )
        lt[g, 0:1, :] = top + jnp.log(total)
    wait_bytes(ot_in, recv.at[O_S])

    ends[D:DP, :] = jnp.zeros((DP - D, 2 * E_DEV), BF16)
    for j in range(2):
        cols = slice(j * EC, (j + 1) * EC)
        tail_cols = slice(E_DEV + j * EC, E_DEV + (j + 1) * EC)
        g = 2 * c + j
        pos, w, ltot = sq[g, 0:1, :], sq[g, 1:2, :], lt[g, 0:1, :]
        pos_coef = w * (jnp.exp(pos - ltot) - 1.0)
        own = w * jnp.exp(st[c, g, 0:1, :] - ltot)
        other = w * jnp.exp(st[oc, g, 0:1, :] - ltot)
        grad = pos_coef * tts[j] + ot[g] * own + ot_in[j] * other
        gre, gim = grad[:HALF], grad[HALF:]
        rre, rim = rts[j, :HALF, :], rts[j, HALF:, :]
        hre, him = hts[j, :HALF, :], hts[j, HALF:, :]
        ends[0:D, cols] = jnp.concatenate(
            [gre * rre + gim * rim, gim * rre - gre * rim], axis=0
        ).astype(BF16)
        ends[0:D, tail_cols] = (pos_coef * qt[g, 0:D, :].astype(F32)).astype(BF16)
        term = jnp.concatenate([gre * hre + gim * him, gim * hre - gre * him], axis=0)
        hi = term.astype(BF16)
        rt_hi[:, cols] = hi
        rt_lo[:, cols] = (term - hi.astype(F32)).astype(BF16)

    def pack(k, carry):
        bb = lax.rem(bucket + k, NB)
        sc = slot_col[bb]
        sel = jnp.concatenate(
            [(sc == (iota((256, 128), 1) + 128 * t).astype(F32)).astype(F32).astype(BF16) for t in range(8)],
            axis=1,
        )
        rows = nt(sel, ends[...])
        dc = dest_col[bb]
        high = jnp.floor(dc * (1.0 / 32.0))
        lane = iota((256, 128), 1)
        code = jnp.where(lane == 16, high, jnp.where(lane == 17, dc - 32.0 * high, 0.0))
        packed[bb, :, 0:384] = rows[:, 0:384].astype(BF16)
        packed[bb, :, 384:512] = (rows[:, 384:512] + code).astype(BF16)

        def to_owner(j, carry2):
            ss = lax.rem(shard + j, NS)
            src = packed.at[bb, pl.ds(pl.multiple_of(ss * SLOT, SLOT), SLOT)]
            dst = arrived.at[pl.ds(pl.multiple_of(me * SLOT, SLOT), SLOT)]
            own_block = jnp.logical_and(k == 0, j == 0)

            @pl.when(own_block)
            def _():
                pltpu.make_async_copy(src, dst, recv.at[ENT_S]).start()

            @pl.when(jnp.logical_not(own_block))
            def _():
                rcopy(src, dst, send.at[ENT_S], recv.at[ENT_S], (bb, ss))

            return carry2

        lax.fori_loop(0, NS, to_owner, 0)
        return carry

    lax.fori_loop(0, NB, pack, 0)

    def rel_chunk(r, carry):
        hot = (iota((128, E_DEV), 0) + r * 128 == ids[...]).astype(F32).astype(BF16)
        rp[pl.ds(pl.multiple_of(r * 128, 128), 128), :] = nt(hot, rt_hi[...]) + nt(hot, rt_lo[...])
        return carry

    lax.fori_loop(0, 4, rel_chunk, 0)
    rcopy(
        rp.at[pl.ds(pl.multiple_of(oc * 256, 256), 256)], rp_in, send.at[RC_S], recv.at[RC_S], partner
    )

    def neg_block(zb):
        for g in range(4):
            scale = sq[g, 1:2, :] * jnp.exp(mb[zb, g, 0:1, :] - lt[g, 0:1, :])
            qs[g] = (qt[g].astype(F32) * scale).astype(BF16)

        def rows_of(r, carry):
            rr = pl.ds(pl.multiple_of(r * 256, 256), 256)
            acc = nt(prob[zb, 0, rr, :], qs[0])
            for g in range(1, 4):
                acc = acc + nt(prob[zb, g, rr, :], qs[g])
            ga[zb, rr, :] = acc[:, 0:256].astype(BF16)
            gb[zb, rr, :] = acc[:, 256:512].astype(BF16)
            return carry

        lax.fori_loop(0, 4, rows_of, 0)

    for k in (2, 1, 3):
        zb = lax.rem(z + k, NZ)
        neg_block(zb)
        rcopy(ga.at[zb], ra1.at[z], send.at[A1_S], recv.at[A1_S], (zb * 2 + c, shard))
    neg_block(z)

    def to_shard_b(j, carry):
        ss = lax.rem(shard + j, NS)
        rows = pl.ds(pl.multiple_of(ss * NEG_OWN, NEG_OWN), NEG_OWN)
        rcopy(gb.at[:, rows, :], rb1.at[shard], send.at[B1_S], recv.at[B1_S], (bucket, ss))
        return carry

    lax.fori_loop(1, NS, to_shard_b, 0)
    my_rows = pl.ds(pl.multiple_of(shard * NEG_OWN, NEG_OWN), NEG_OWN)
    rb1[shard] = gb[:, my_rows, :]

    wait_bytes(rp_in, recv.at[RC_S])
    r1b[...] = (rp[pl.ds(pl.multiple_of(c * 256, 256), 256), :] + rp_in[...]).astype(BF16)

    def to_shard_r(j, carry):
        ss = lax.rem(shard + j, NS)
        rows = r1b.at[pl.ds(pl.multiple_of(ss * 16, 16), 16)]
        rcopy(rows, r2in.at[shard], send.at[R2_S], recv.at[R2_S], (bucket, ss))
        return carry

    lax.fori_loop(1, NS, to_shard_r, 0)
    r2in[shard] = r1b[pl.ds(pl.multiple_of(shard * 16, 16), 16), :]
    wait_bytes(r2in.at[pl.ds(0, NS - 1)], recv.at[R2_S])
    r2 = r2in[0].astype(F32)
    for i in range(1, NS):
        r2 = r2 + r2in[i].astype(F32)
    r2all[z] = r2
    for k in (1, 3, 2):
        zz = lax.rem(z + k, NZ)
        rcopy(r2all.at[z], r2all.at[z], send.at[R3_S], recv.at[R3_S], (zz * 2 + c, shard))

    wait_bytes(ra1.at[pl.ds(0, 3)], recv.at[A1_S])

    def sum_a(r, carry):
        rr = pl.ds(pl.multiple_of(r * 128, 128), 128)
        total = ga[z, rr, :].astype(F32)
        for k in range(1, NZ):
            total = total + ra1[lax.rem(z + k, NZ), rr, :].astype(F32)
        a2[rr, :] = total.astype(BF16)
        return carry

    lax.fori_loop(0, 8, sum_a, 0)

    def to_shard_a(j, carry):
        ss = lax.rem(shard + j, NS)
        rows = a2.at[pl.ds(pl.multiple_of(ss * NEG_OWN, NEG_OWN), NEG_OWN)]
        rcopy(rows, ra2.at[shard], send.at[A2_S], recv.at[A2_S], (bucket, ss))
        return carry

    lax.fori_loop(1, NS, to_shard_a, 0)
    ra2[shard] = a2[my_rows, :]

    wait_bytes(r2all.at[pl.ds(0, 3)], recv.at[R3_S])
    rel_row = pl.ds(pl.multiple_of(c * 256 + shard * 16, 16), 16)
    rfin[rel_row, :] = ((r2all[0] + r2all[1]) + r2all[2]) + r2all[3]

    def to_shard_f(j, carry):
        ss = lax.rem(shard + j, NS)
        rcopy(rfin.at[rel_row], rfin.at[rel_row], send.at[R4_S], recv.at[R4_S], (bucket, ss))
        return carry

    lax.fori_loop(1, NS, to_shard_f, 0)

    wait_bytes(rb1.at[pl.ds(0, NS - 1)], recv.at[B1_S])

    def sum_b(zb, carry):
        total = rb1[0, zb].astype(F32)
        for i in range(1, NS):
            total = total + rb1[i, zb].astype(F32)
        b2[zb] = total
        return carry

    lax.fori_loop(0, NZ, sum_b, 0)
    for k in (1, 3, 2):
        zz = lax.rem(z + k, NZ)
        rcopy(b2.at[zz], rb2.at[z], send.at[B2_S], recv.at[B2_S], (zz * 2 + c, shard))
    rb2[z] = b2[z]

    wait_bytes(rfin.at[pl.ds(0, 240)], recv.at[R4_S])
    half_rel = rfin.at[pl.ds(pl.multiple_of(c * 256, 256), 256)]
    rcopy(half_rel, half_rel, send.at[R5_S], recv.at[R5_S], partner)

    wait_bytes(arrived, recv.at[ENT_S])
    lane = iota((8, DP), 1)
    unit = jnp.where(lane == D, 32.0, jnp.where(lane == D + 1, 1.0, 0.0)).astype(BF16)
    row_ids = nt(unit, arrived[...])[0:1, :]

    def scatter(r, carry):
        hot = ((iota((128, 2048), 0) + r * 128).astype(F32) == row_ids).astype(F32).astype(BF16)
        got = nn(hot, arrived[...])
        ent_out[pl.ds(pl.multiple_of(r * 128, 128), 128), :] = got[:, 0:D]
        return carry

    lax.fori_loop(0, 8, scatter, 0)

    wait_bytes(ra2.at[pl.ds(0, NS - 1)], recv.at[A2_S])
    total = ra2[0].astype(F32)
    for i in range(1, NS):
        total = total + ra2[i].astype(F32)
    neg_out[:, 0:256] = total
    wait_bytes(rb2.at[pl.ds(0, 3)], recv.at[B2_S])
    total = ((rb2[0] + rb2[1]) + rb2[2]) + rb2[3]
    neg_out[:, 256:D] = total[:, 0 : D - 256]

    wait_bytes(half_rel, recv.at[R5_S])
    rel_out[...] = rfin[...]

    wait_bytes(nb.at[0, pl.ds(0, 768)], send.at[Z_S])
    wait_bytes(arrived.at[pl.ds(0, 1152)], send.at[X_S])
    wait_bytes(arrived.at[pl.ds(0, 1152)], send.at[Y_S])
    wait_bytes(qt.at[mine], send.at[Q_S])
    wait_bytes(sq.at[mine], send.at[SL_S])
    wait_bytes(st.at[c], send.at[ST_S])
    wait_bytes(ot_in, send.at[O_S])
    wait_bytes(arrived.at[pl.ds(0, 2048 - SLOT)], send.at[ENT_S])
    wait_bytes(rp_in, send.at[RC_S])
    wait_bytes(r2in.at[pl.ds(0, NS - 1)], send.at[R2_S])
    wait_bytes(r2all.at[pl.ds(0, 3)], send.at[R3_S])
    wait_bytes(rfin.at[pl.ds(0, 240)], send.at[R4_S])
    wait_bytes(half_rel, send.at[R5_S])
    wait_bytes(ra1.at[pl.ds(0, 3)], send.at[A1_S])
    wait_bytes(rb1.at[pl.ds(0, NS - 1)], send.at[B1_S])
    wait_bytes(ra2.at[pl.ds(0, NS - 1)], send.at[A2_S])
    wait_bytes(rb2.at[pl.ds(0, 3)], send.at[B2_S])


SCRATCH = [
    ((NZ, NEG_DEV, DP), BF16),
    ((DP, NEG_DEV), BF16),
    ((NZ, 4, NEG_DEV, EC), BF16),
    ((4, DP, EC), BF16),
    ((4, 8, EC), F32),
    ((2, D, EC), F32),
    ((2, D, EC), F32),
    ((2, D, EC), F32),
    ((NZ, 4, 8, EC), F32),
    ((2, 4, 8, EC), F32),
    ((4, D, EC), F32),
    ((2, D, EC), F32),
    ((4, 8, EC), F32),
    ((4, DP, EC), BF16),
    ((DP, 2 * E_DEV), BF16),
    ((D, E_DEV), BF16),
    ((D, E_DEV), BF16),
    ((NB, 256, DP), BF16),
    ((2048, DP), BF16),
    ((NB, 256, 128), F32),
    ((NB, 256, 128), F32),
    ((NZ, NEG_DEV, 256), BF16),
    ((NZ, NEG_DEV, 256), BF16),
    ((NZ, NEG_DEV, 256), BF16),
    ((NS, NZ, NEG_OWN, 256), BF16),
    ((NEG_DEV, 256), BF16),
    ((NS, NEG_OWN, 256), BF16),
    ((NZ, NEG_OWN, 256), F32),
    ((NZ, NEG_OWN, 256), F32),
    ((REL, D), F32),
    ((REL // 2, D), F32),
    ((REL // 2, D), BF16),
    ((NS, 16, D), BF16),
    ((NZ, 16, D), F32),
    ((REL, D), F32),
]


def per_device(
    head_rows, tail_rows, rel_ids, relations, edge_weights, neg_rows, send_slots, dest_rows
):
    vmem = pl.BlockSpec(memory_space=pltpu.VMEM)
    return pl.pallas_call(
        kernel,
        out_shape=(
            jax.ShapeDtypeStruct((ENT_DEV, D), F32),
            jax.ShapeDtypeStruct((NEG_OWN, D), F32),
            jax.ShapeDtypeStruct((REL, D), F32),
        ),
        in_specs=[vmem] * 8,
        out_specs=(vmem,) * 3,
        scratch_shapes=[pltpu.VMEM(shape, dtype) for shape, dtype in SCRATCH]
        + [
            pltpu.SemaphoreType.DMA((17,)),
            pltpu.SemaphoreType.DMA((14,)),
            pltpu.SemaphoreType.DMA((NZ,)),
            pltpu.SemaphoreType.DMA((NZ,)),
            pltpu.SemaphoreType.DMA((NZ,)),
        ],
        compiler_params=pltpu.CompilerParams(
            collective_id=0, has_side_effects=True, vmem_limit_bytes=60 * 1024 * 1024
        ),
        cost_estimate=pl.CostEstimate(
            flops=2 * 3 * 1024 * 4096 * 400, bytes_accessed=8 * 1024 * 1024, transcendentals=1024 * 4096
        ),
        name="complex_backward",
    )(
        head_rows,
        tail_rows,
        rel_ids.reshape(1, E_DEV),
        relations,
        edge_weights.reshape(1, E_DEV),
        neg_rows,
        send_slots.reshape(NB, NS * SLOT),
        dest_rows.reshape(NB, NS * SLOT),
    )


def solution(mesh):
    return jax.shard_map(
        per_device,
        mesh=mesh,
        in_specs=(
            P(("bucket", "shard"), None),
            P(("bucket", "shard"), None),
            P(("bucket", "shard")),
            P(),
            P(("bucket", "shard")),
            P("bucket", None),
            P(("bucket", "shard"), None),
            P(("bucket", "shard"), None),
        ),
        out_specs=(P(("bucket", "shard"), None), P(("bucket", "shard"), None), P()),
        check_vma=False,
    )
```

```python
import functools

import jax
import jax.numpy as jnp
from jax import lax
from jax.experimental import pallas as pl
from jax.experimental.pallas import tpu as pltpu
from jax.sharding import PartitionSpec as P

D = 400
HALF = 200
DP = 512
E_DEV = 512
ENT_DEV = 1024
REL = 512
NEG_DEV = 1024
SLOT = 16
NB = 8
NS = 16
NZ = 4
EC = 256
NEG_OWN = 64

MESH = pl.DeviceIdType.MESH
F32 = jnp.float32
BF16 = jnp.bfloat16

(Q_S, SQ_S, ST_S, O_S, RC_S, R2_S, R3_S, R4_S, R5_S, ENT_S,
 Z1_S, X1_S, Y1_S, Z2_S, X2_S, Y2_S, GZ_S, GX_S, GY_S) = range(19)


def nt(a, b):
    return lax.dot_general(a, b, (((1,), (1,)), ((), ())), preferred_element_type=F32)


def nn(a, b):
    return jnp.dot(a, b, preferred_element_type=F32)


def iota(shape, dim):
    return lax.broadcasted_iota(jnp.int32, shape, dim)


def hot_where(mask):
    return mask.astype(F32).astype(BF16)


def wait_bytes(ref, sem):
    pltpu.make_async_copy(ref, ref, sem).wait()


def kernel(
    head, tail, ids, rel, wts, neg, slots, drows,
    ent_out, neg_out, rel_out,
    nbt, nb, prob, qt, sq, hts, tts, rts, mb, st, ot, ot_in, lt, qs, ends, rt_hi, rt_lo,
    packed, arrived, slot_col, dest_col,
    gz, gx, gy, rz1, rx1, ry1, az, ax, ay, rz2, rx2, ry2,
    rp, rp_in, r1b, r2in, r2all, rfin,
    send, recv, zrecv, xrecv, yrecv,
):
    bucket, shard = lax.axis_index("bucket"), lax.axis_index("shard")
    z, c = bucket // 2, bucket % 2
    x, y = shard // 4, shard % 4
    oc = 1 - c
    me = bucket * NS + shard
    partner = (z * 2 + oc, shard)

    def rcopy(src, dst, s_sem, r_sem, device):
        pltpu.make_async_remote_copy(
            src_ref=src, dst_ref=dst, send_sem=s_sem, recv_sem=r_sem,
            device_id=device, device_id_type=MESH,
        ).start()

    barrier = pltpu.get_barrier_semaphore()

    def greet(i, carry):
        d = lax.rem(me + i, NB * NS)
        pl.semaphore_signal(barrier, inc=1, device_id=(d // NS, d % NS), device_id_type=MESH)
        return carry

    lax.fori_loop(1, NB * NS, greet, 0)

    for i in range(8):
        nbt[z * 8 + i] = neg[:, i * 128 : (i + 1) * 128]

    rel_1 = rel[...].astype(BF16)
    rest = rel[...] - rel_1.astype(F32)
    rel_2 = rest.astype(BF16)
    rel_3 = (rest - rel_2.astype(F32)).astype(BF16)
    for j in range(2):
        cols = slice(j * EC, (j + 1) * EC)
        h_t = head[:, cols].astype(F32)
        t_t = tail[:, cols].astype(F32)
        hot = hot_where(iota((REL, EC), 0) == ids[0:1, cols])
        r_t = (nn(rel_1, hot) + nn(rel_2, hot)) + nn(rel_3, hot)
        hre, him = h_t[:HALF], h_t[HALF:]
        rre, rim = r_t[:HALF], r_t[HALF:]
        q = jnp.concatenate([hre * rre - him * rim, hre * rim + him * rre], axis=0).astype(BF16)
        qt[2 * c + j, 0:D, :] = q
        qt[2 * c + j, D:DP, :] = jnp.zeros((DP - D, EC), BF16)
        sq[2 * c + j, 0:1, :] = jnp.sum(q.astype(F32) * t_t, axis=0, keepdims=True)
        sq[2 * c + j, 1:2, :] = wts[0:1, cols]
        sq[2 * c + j, 2:8, :] = jnp.zeros((6, EC), F32)
        hts[j] = h_t
        tts[j] = t_t
        rts[j] = r_t

    pl.semaphore_wait(barrier, NB * NS - 1)

    for k in (1, 3, 2):
        zz = lax.rem(z + k, NZ)
        for part in (nbt.at[z * 8 + x], nbt.at[z * 8 + 4 + y]):
            rcopy(part, part, send.at[GZ_S], zrecv.at[k], (zz * 2 + c, shard))
    mine = pl.ds(2 * c, 2)
    rcopy(qt.at[mine], qt.at[mine], send.at[Q_S], recv.at[Q_S], partner)
    rcopy(sq.at[mine], sq.at[mine], send.at[SQ_S], recv.at[SQ_S], partner)

    ones = jnp.ones((SLOT, 128), BF16)
    tables = []
    for ref in (slots, drows):
        value = ref[...].astype(F32)
        high = jnp.floor(value * (1.0 / 32.0))
        tables.append((high.astype(BF16), (value - 32.0 * high).astype(BF16)))

    def columns(b, carry):
        owner_hot = hot_where(iota((256, 128), 1) == iota((256, 128), 0) // SLOT + b * NS)
        keep = iota((256, SLOT), 1) == iota((256, SLOT), 0) % SLOT
        for (high, low), out in zip(tables, (slot_col, dest_col)):
            h = jnp.where(keep, nt(owner_hot, high), 0.0).astype(BF16)
            l = jnp.where(keep, nt(owner_hot, low), 0.0).astype(BF16)
            out[b] = 32.0 * nn(h, ones) + nn(l, ones)
        return carry

    lax.fori_loop(0, NB, columns, 0)
    nb[:, 384:DP] = jnp.zeros((NEG_DEV, 128), BF16)

    wait_bytes(qt.at[mine], recv.at[Q_S])
    wait_bytes(sq.at[mine], recv.at[SQ_S])

    def forward(k):
        src = lax.rem(z + NZ - k, NZ)
        wait_bytes(nbt.at[pl.ds(src * 8, 2)], zrecv.at[k])
        part_x, part_y = nbt.at[src * 8 + x], nbt.at[src * 8 + 4 + y]
        for i in (1, 3, 2):
            xx, yy = lax.rem(x + i, 4), lax.rem(y + i, 4)
            rcopy(part_x, part_x, send.at[GX_S], xrecv.at[k], (bucket, xx * 4 + y))
            rcopy(part_y, part_y, send.at[GY_S], yrecv.at[k], (bucket, x * 4 + yy))

    def block(zb, first):
        for i in range(8):
            nb[i * 128 : (i + 1) * 128, 0:D] = nbt[zb * 8 + i].astype(F32).T.astype(BF16)

        def chunk(g):
            s = nn(nb[...], qt[g])
            m = jnp.max(s, axis=0, keepdims=True)
            p = jnp.exp(s - m)
            l = jnp.sum(p, axis=0, keepdims=True)
            pb = p.astype(BF16)
            prob[zb, g] = pb
            wide = jnp.concatenate([nbt[zb * 8 + i] for i in range(8)], axis=1)
            o = nn(wide, pb)
            mb[zb, g, 0:1, :] = m
            if first:
                st[c, g, 0:1, :] = m
                st[c, g, 1:2, :] = l
                st[c, g, 2:8, :] = jnp.zeros((6, EC), F32)
                ot[g] = o
            else:
                m_old = st[c, g, 0:1, :]
                m_new = jnp.maximum(m_old, m)
                f_old = jnp.exp(m_old - m_new)
                f_new = jnp.exp(m - m_new)
                st[c, g, 0:1, :] = m_new
                st[c, g, 1:2, :] = st[c, g, 1:2, :] * f_old + l * f_new
                ot[g] = ot[g] * f_old + o * f_new

        def two(h, carry):
            chunk(2 * h)
            chunk(2 * h + 1)
            return carry

        lax.fori_loop(0, 2, two, 0)

    block(z, True)
    for k in (1, 3, 2):
        forward(k)
    for k in (1, 3, 2):
        src = lax.rem(z + NZ - k, NZ)
        wait_bytes(nbt.at[pl.ds(src * 8, 3)], xrecv.at[k])
        wait_bytes(nbt.at[pl.ds(src * 8, 3)], yrecv.at[k])
        block(src, False)

    rcopy(st.at[c], st.at[c], send.at[ST_S], recv.at[ST_S], partner)
    rcopy(ot.at[pl.ds(2 * oc, 2)], ot_in, send.at[O_S], recv.at[O_S], partner)
    wait_bytes(st.at[c], recv.at[ST_S])
    for g in range(4):
        pos = sq[g, 0:1, :]
        m0, m1 = st[0, g, 0:1, :], st[1, g, 0:1, :]
        top = jnp.maximum(pos, jnp.maximum(m0, m1))
        total = (
            jnp.exp(pos - top)
            + st[0, g, 1:2, :] * jnp.exp(m0 - top)
            + st[1, g, 1:2, :] * jnp.exp(m1 - top)
        )
        lt[g, 0:1, :] = top + jnp.log(total)
    wait_bytes(ot_in, recv.at[O_S])

    ends[D:DP, :] = jnp.zeros((DP - D, 2 * E_DEV), BF16)
    for j in range(2):
        cols = slice(j * EC, (j + 1) * EC)
        tail_cols = slice(E_DEV + j * EC, E_DEV + (j + 1) * EC)
        g = 2 * c + j
        pos, w, ltot = sq[g, 0:1, :], sq[g, 1:2, :], lt[g, 0:1, :]
        pos_coef = w * (jnp.exp(pos - ltot) - 1.0)
        own = w * jnp.exp(st[c, g, 0:1, :] - ltot)
        other = w * jnp.exp(st[oc, g, 0:1, :] - ltot)
        grad = pos_coef * tts[j] + ot[g] * own + ot_in[j] * other
        gre, gim = grad[:HALF], grad[HALF:]
        rre, rim = rts[j, :HALF, :], rts[j, HALF:, :]
        hre, him = hts[j, :HALF, :], hts[j, HALF:, :]
        ends[0:D, cols] = jnp.concatenate(
            [gre * rre + gim * rim, gim * rre - gre * rim], axis=0
        ).astype(BF16)
        ends[0:D, tail_cols] = (pos_coef * qt[g, 0:D, :].astype(F32)).astype(BF16)
        term = jnp.concatenate([gre * hre + gim * him, gim * hre - gre * him], axis=0)
        hi = term.astype(BF16)
        rt_hi[:, cols] = hi
        rt_lo[:, cols] = (term - hi.astype(F32)).astype(BF16)

    my_slots = pl.ds(pl.multiple_of(me * SLOT, SLOT), SLOT)

    def pack(bb, first):
        sc = slot_col[bb]
        sel = jnp.concatenate(
            [hot_where(sc == (iota((256, 128), 1) + 128 * t).astype(F32)) for t in range(8)], axis=1
        )
        rows = nt(sel, ends[...])
        dc = dest_col[bb]
        high = jnp.floor(dc * (1.0 / 32.0))
        lane = iota((256, 128), 1)
        code = jnp.where(lane == 16, high, jnp.where(lane == 17, dc - 32.0 * high, 0.0))
        packed[bb, :, 0:384] = rows[:, 0:384].astype(BF16)
        packed[bb, :, 384:512] = (rows[:, 384:512] + code).astype(BF16)
        for j in range(NS):
            ss = lax.rem(shard + j, NS)
            src = packed.at[bb, pl.ds(pl.multiple_of(ss * SLOT, SLOT), SLOT)]
            if first and j == 0:
                pltpu.make_async_copy(src, arrived.at[my_slots], recv.at[ENT_S]).start()
            else:
                rcopy(src, arrived.at[my_slots], send.at[ENT_S], recv.at[ENT_S], (bb, ss))

    pack(bucket, True)

    def pack_other(k, carry):
        pack(lax.rem(bucket + k, NB), False)
        return carry

    lax.fori_loop(1, NB, pack_other, 0)

    def rel_chunk(r, carry):
        hot = hot_where(iota((128, E_DEV), 0) + r * 128 == ids[...])
        rp[pl.ds(pl.multiple_of(r * 128, 128), 128), :] = nt(hot, rt_hi[...]) + nt(hot, rt_lo[...])
        return carry

    lax.fori_loop(0, 4, rel_chunk, 0)
    rcopy(
        rp.at[pl.ds(pl.multiple_of(oc * 256, 256), 256)], rp_in, send.at[RC_S], recv.at[RC_S], partner
    )

    def neg_block(zb):
        for g in range(4):
            scale = sq[g, 1:2, :] * jnp.exp(mb[zb, g, 0:1, :] - lt[g, 0:1, :])
            qs[g] = (qt[g].astype(F32) * scale).astype(BF16)

        def rows_of(xx, carry):
            rr = pl.ds(pl.multiple_of(xx * 256, 256), 256)
            acc = nt(prob[zb, 0, rr, :], qs[0])
            for g in range(1, 4):
                acc = acc + nt(prob[zb, g, rr, :], qs[g])
            gx[zb, xx] = acc[:, 0:128].astype(BF16)
            for yy in range(4):
                gy[zb, yy, xx] = acc[yy * 64 : (yy + 1) * 64, 128:256].astype(BF16)
            gz[zb, :, rr] = acc[:, 256:512].T[0 : D - 256].astype(BF16)
            return carry

        lax.fori_loop(0, 4, rows_of, 0)
        for i in (1, 3, 2):
            xx, yy = lax.rem(x + i, 4), lax.rem(y + i, 4)
            rcopy(gx.at[zb, xx], rx1.at[x, zb], send.at[X1_S], recv.at[X1_S], (bucket, xx * 4 + y))
            rcopy(gy.at[zb, yy], ry1.at[y, zb], send.at[Y1_S], recv.at[Y1_S], (bucket, x * 4 + yy))

    for k in (2, 1, 3):
        zb = lax.rem(z + k, NZ)
        neg_block(zb)
        rcopy(gz.at[zb], rz1.at[z], send.at[Z1_S], recv.at[Z1_S], (zb * 2 + c, shard))
    neg_block(z)

    wait_bytes(rp_in, recv.at[RC_S])
    r1b[...] = (rp[pl.ds(pl.multiple_of(c * 256, 256), 256), :] + rp_in[...]).astype(BF16)
    for j in range(1, NS):
        ss = lax.rem(shard + j, NS)
        rows = r1b.at[pl.ds(pl.multiple_of(ss * 16, 16), 16)]
        rcopy(rows, r2in.at[shard], send.at[R2_S], recv.at[R2_S], (bucket, ss))
    r2in[shard] = r1b[pl.ds(pl.multiple_of(shard * 16, 16), 16), :]

    wait_bytes(rx1.at[pl.ds(0, 3)], recv.at[X1_S])

    def sum_x(zb, carry):
        total = gx[zb, x].astype(F32)
        for i in range(1, 4):
            total = total + rx1[lax.rem(x + i, 4), zb].astype(F32)
        ax[zb] = total.astype(BF16)
        return carry

    lax.fori_loop(0, NZ, sum_x, 0)
    for j in range(1, NS):
        other_zy = lax.rem(z * 4 + y + j, NS)
        zz, yy = other_zy // 4, other_zy % 4
        rows = ax.at[zz, pl.ds(pl.multiple_of(yy * NEG_OWN, NEG_OWN), NEG_OWN)]
        rcopy(rows, rx2.at[z * 4 + y], send.at[X2_S], recv.at[X2_S], (zz * 2 + c, x * 4 + yy))
    rx2[z * 4 + y] = ax[z, pl.ds(pl.multiple_of(y * NEG_OWN, NEG_OWN), NEG_OWN), :]

    wait_bytes(ry1.at[pl.ds(0, 3)], recv.at[Y1_S])

    def sum_y(zb, carry):
        for xx in range(4):
            total = gy[zb, y, xx].astype(F32)
            for i in range(1, 4):
                total = total + ry1[lax.rem(y + i, 4), zb, xx].astype(F32)
            ay[zb, xx] = total.astype(BF16)
        return carry

    lax.fori_loop(0, NZ, sum_y, 0)
    for j in range(1, NS):
        other_zx = lax.rem(z * 4 + x + j, NS)
        zz, xx = other_zx // 4, other_zx % 4
        rcopy(ay.at[zz, xx], ry2.at[z * 4 + x], send.at[Y2_S], recv.at[Y2_S], (zz * 2 + c, xx * 4 + y))
    ry2[z * 4 + x] = ay[z, x]

    wait_bytes(rz1.at[pl.ds(0, 3)], recv.at[Z1_S])

    def sum_z(r, carry):
        rr = pl.ds(pl.multiple_of(r * 256, 256), 256)
        total = gz[z, :, rr].astype(F32)
        for k in range(1, NZ):
            total = total + rz1[lax.rem(z + k, NZ), :, rr].astype(F32)
        wide = jnp.concatenate([total, jnp.zeros((256 - (D - 256), 256), F32)], axis=0)
        az[rr, :] = wide.T.astype(BF16)
        return carry

    lax.fori_loop(0, 4, sum_z, 0)
    for j in range(1, NS):
        ss = lax.rem(shard + j, NS)
        rows = az.at[pl.ds(pl.multiple_of(ss * NEG_OWN, NEG_OWN), NEG_OWN)]
        rcopy(rows, rz2.at[shard], send.at[Z2_S], recv.at[Z2_S], (bucket, ss))
    rz2[shard] = az[pl.ds(pl.multiple_of(shard * NEG_OWN, NEG_OWN), NEG_OWN), :]

    wait_bytes(r2in.at[pl.ds(0, NS - 1)], recv.at[R2_S])
    r2 = r2in[0].astype(F32)
    for i in range(1, NS):
        r2 = r2 + r2in[i].astype(F32)
    r2all[z] = r2
    for k in (1, 3, 2):
        zz = lax.rem(z + k, NZ)
        rcopy(r2all.at[z], r2all.at[z], send.at[R3_S], recv.at[R3_S], (zz * 2 + c, shard))
    wait_bytes(r2all.at[pl.ds(0, 3)], recv.at[R3_S])
    rel_row = pl.ds(pl.multiple_of(c * 256 + shard * 16, 16), 16)
    rfin[rel_row, :] = ((r2all[0] + r2all[1]) + r2all[2]) + r2all[3]
    for j in range(1, NS):
        ss = lax.rem(shard + j, NS)
        rcopy(rfin.at[rel_row], rfin.at[rel_row], send.at[R4_S], recv.at[R4_S], (bucket, ss))
    wait_bytes(rfin.at[pl.ds(0, 240)], recv.at[R4_S])
    half_rel = rfin.at[pl.ds(pl.multiple_of(c * 256, 256), 256)]
    rcopy(half_rel, half_rel, send.at[R5_S], recv.at[R5_S], partner)

    wait_bytes(arrived, recv.at[ENT_S])
    lane = iota((8, DP), 1)
    unit = jnp.where(lane == D, 32.0, jnp.where(lane == D + 1, 1.0, 0.0)).astype(BF16)
    row_ids = nt(unit, arrived[...])[0:1, :]

    def scatter(r, carry):
        hot = hot_where((iota((256, 2048), 0) + r * 256).astype(F32) == row_ids)
        got = nn(hot, arrived[...])
        ent_out[:, pl.ds(pl.multiple_of(r * 256, 256), 256)] = got.T[0:D]
        return carry

    lax.fori_loop(0, 4, scatter, 0)

    wait_bytes(half_rel, recv.at[R5_S])
    for r in range(4):
        rr = slice(r * 128, (r + 1) * 128)
        wide = jnp.concatenate([rfin[rr, :], jnp.zeros((128, DP - D), F32)], axis=1)
        rel_out[:, rr] = wide.T[0:D]

    def sum16(ref):
        total = ref[0].astype(F32)
        for i in range(1, NS):
            total = total + ref[i].astype(F32)
        return total

    wait_bytes(rx2.at[pl.ds(0, NS - 1)], recv.at[X2_S])
    neg_out[:, 0:128] = sum16(rx2)
    wait_bytes(ry2.at[pl.ds(0, NS - 1)], recv.at[Y2_S])
    neg_out[:, 128:256] = sum16(ry2)
    wait_bytes(rz2.at[pl.ds(0, NS - 1)], recv.at[Z2_S])
    neg_out[:, 256:D] = sum16(rz2)[:, 0 : D - 256]

    wait_bytes(nbt.at[pl.ds(0, 6)], send.at[GZ_S])
    wait_bytes(nbt.at[pl.ds(0, 9)], send.at[GX_S])
    wait_bytes(nbt.at[pl.ds(0, 9)], send.at[GY_S])
    wait_bytes(qt.at[mine], send.at[Q_S])
    wait_bytes(sq.at[mine], send.at[SQ_S])
    wait_bytes(st.at[c], send.at[ST_S])
    wait_bytes(ot_in, send.at[O_S])
    wait_bytes(arrived.at[pl.ds(0, 2048 - SLOT)], send.at[ENT_S])
    wait_bytes(rp_in, send.at[RC_S])
    wait_bytes(r2in.at[pl.ds(0, NS - 1)], send.at[R2_S])
    wait_bytes(r2all.at[pl.ds(0, 3)], send.at[R3_S])
    wait_bytes(rfin.at[pl.ds(0, 240)], send.at[R4_S])
    wait_bytes(half_rel, send.at[R5_S])
    wait_bytes(rz1.at[pl.ds(0, 3)], send.at[Z1_S])
    wait_bytes(rx1.at[pl.ds(0, 3)], send.at[X1_S])
    wait_bytes(ry1.at[pl.ds(0, 3)], send.at[Y1_S])
    wait_bytes(rx2.at[pl.ds(0, NS - 1)], send.at[X2_S])
    wait_bytes(ry2.at[pl.ds(0, NS - 1)], send.at[Y2_S])
    wait_bytes(rz2.at[pl.ds(0, NS - 1)], send.at[Z2_S])


SCRATCH = [
    ((NZ * 8, D, 128), BF16),
    ((NEG_DEV, DP), BF16),
    ((NZ, 4, NEG_DEV, EC), BF16),
    ((4, DP, EC), BF16),
    ((4, 8, EC), F32),
    ((2, D, EC), F32),
    ((2, D, EC), F32),
    ((2, D, EC), F32),
    ((NZ, 4, 8, EC), F32),
    ((2, 4, 8, EC), F32),
    ((4, D, EC), F32),
    ((2, D, EC), F32),
    ((4, 8, EC), F32),
    ((4, DP, EC), BF16),
    ((DP, 2 * E_DEV), BF16),
    ((D, E_DEV), BF16),
    ((D, E_DEV), BF16),
    ((NB, 256, DP), BF16),
    ((2048, DP), BF16),
    ((NB, 256, 128), F32),
    ((NB, 256, 128), F32),
    ((NZ, D - 256, NEG_DEV), BF16),
    ((NZ, 4, 256, 128), BF16),
    ((NZ, 4, 4, NEG_OWN, 128), BF16),
    ((NZ, D - 256, NEG_DEV), BF16),
    ((4, NZ, 256, 128), BF16),
    ((4, NZ, 4, NEG_OWN, 128), BF16),
    ((NEG_DEV, 256), BF16),
    ((NZ, 256, 128), BF16),
    ((NZ, 4, NEG_OWN, 128), BF16),
    ((NS, NEG_OWN, 256), BF16),
    ((NS, NEG_OWN, 128), BF16),
    ((NS, NEG_OWN, 128), BF16),
    ((REL, D), F32),
    ((REL // 2, D), F32),
    ((REL // 2, D), BF16),
    ((NS, 16, D), BF16),
    ((NZ, 16, D), F32),
    ((REL, D), F32),
]


def per_device(
    head_rows, tail_rows, rel_ids, relations, edge_weights, neg_rows, send_slots, dest_rows
):
    vmem = pl.BlockSpec(memory_space=pltpu.VMEM)
    ent_t, neg_grad, rel_t = pl.pallas_call(
        kernel,
        out_shape=(
            jax.ShapeDtypeStruct((D, ENT_DEV), F32),
            jax.ShapeDtypeStruct((NEG_OWN, D), F32),
            jax.ShapeDtypeStruct((D, REL), F32),
        ),
        in_specs=[vmem] * 8,
        out_specs=(vmem,) * 3,
        scratch_shapes=[pltpu.VMEM(shape, dtype) for shape, dtype in SCRATCH]
        + [
            pltpu.SemaphoreType.DMA((19,)),
            pltpu.SemaphoreType.DMA((16,)),
            pltpu.SemaphoreType.DMA((NZ,)),
            pltpu.SemaphoreType.DMA((NZ,)),
            pltpu.SemaphoreType.DMA((NZ,)),
        ],
        compiler_params=pltpu.CompilerParams(
            collective_id=0, has_side_effects=True, vmem_limit_bytes=60 * 1024 * 1024
        ),
        cost_estimate=pl.CostEstimate(
            flops=2 * 3 * 1024 * 4096 * 400, bytes_accessed=8 * 1024 * 1024, transcendentals=1024 * 4096
        ),
        name="complex_backward",
    )(
        head_rows.T,
        tail_rows.T,
        rel_ids.reshape(1, E_DEV),
        relations.T,
        edge_weights.reshape(1, E_DEV),
        neg_rows.T,
        send_slots.T,
        dest_rows.T,
    )
    return ent_t.T, neg_grad, rel_t.T


def solution(mesh):
    return jax.shard_map(
        per_device,
        mesh=mesh,
        in_specs=(
            P(("bucket", "shard"), None),
            P(("bucket", "shard"), None),
            P(("bucket", "shard")),
            P(),
            P(("bucket", "shard")),
            P("bucket", None),
            P(("bucket", "shard"), None),
            P(("bucket", "shard"), None),
        ),
        out_specs=(P(("bucket", "shard"), None), P(("bucket", "shard"), None), P()),
        check_vma=False,
    )
```

```python
import functools

import jax
import jax.numpy as jnp
from jax import lax
from jax.experimental import pallas as pl
from jax.experimental.pallas import tpu as pltpu
from jax.sharding import PartitionSpec as P

D = 400
HALF = 200
DP = 512
E_DEV = 512
ENT_DEV = 1024
REL = 512
NEG_DEV = 1024
SLOT = 16
NB = 8
NS = 16
NZ = 4
EC = 256
NEG_OWN = 64

MESH = pl.DeviceIdType.MESH
F32 = jnp.float32
BF16 = jnp.bfloat16

(Q_S, SQ_S, ST_S, O_S, RC_S, R2_S, R3_S, R4_S, R5_S, ENT_S,
 Z1_S, X1_S, Y1_S, Z2_S, X2_S, Y2_S, GZ_S, GX_S, GY_S) = range(19)


def nt(a, b):
    return lax.dot_general(a, b, (((1,), (1,)), ((), ())), preferred_element_type=F32)


def nn(a, b):
    return jnp.dot(a, b, preferred_element_type=F32)


def iota(shape, dim):
    return lax.broadcasted_iota(jnp.int32, shape, dim)


def hot_where(mask):
    return mask.astype(F32).astype(BF16)


def wait_bytes(ref, sem):
    pltpu.make_async_copy(ref, ref, sem).wait()


def kernel(
    head, tail, ids, rel, wts, neg, slots, drows,
    ent_out, neg_out, rel_out,
    nbt, nb, prob, qt, sq, hts, tts, rts, mb, st, ot, ot_in, lt, qs, ends, rt_hi, rt_lo,
    packed, arrived, slot_col, dest_col,
    gz, gx, gy, hz, hx, hy, rz1, rx1, ry1, az, ax, ay, rz2, rx2, ry2,
    rp, rp_in, r1b, r2in, r2all, rfin,
    send, recv, zrecv, xrecv, yrecv, hrecv,
):
    bucket, shard = lax.axis_index("bucket"), lax.axis_index("shard")
    z, c = bucket // 2, bucket % 2
    x, y = shard // 4, shard % 4
    oc = 1 - c
    me = bucket * NS + shard
    partner = (z * 2 + oc, shard)

    def rcopy(src, dst, s_sem, r_sem, device):
        pltpu.make_async_remote_copy(
            src_ref=src, dst_ref=dst, send_sem=s_sem, recv_sem=r_sem,
            device_id=device, device_id_type=MESH,
        ).start()

    barrier = pltpu.get_barrier_semaphore()

    def greet(i, carry):
        d = lax.rem(me + i, NB * NS)
        pl.semaphore_signal(barrier, inc=1, device_id=(d // NS, d % NS), device_id_type=MESH)
        return carry

    lax.fori_loop(1, NB * NS, greet, 0)

    for i in range(8):
        nbt[z * 8 + i] = neg[:, i * 128 : (i + 1) * 128]

    rel_1 = rel[...].astype(BF16)
    rest = rel[...] - rel_1.astype(F32)
    rel_2 = rest.astype(BF16)
    rel_3 = (rest - rel_2.astype(F32)).astype(BF16)
    for j in range(2):
        cols = slice(j * EC, (j + 1) * EC)
        h_t = head[:, cols].astype(F32)
        t_t = tail[:, cols].astype(F32)
        hot = hot_where(iota((REL, EC), 0) == ids[0:1, cols])
        r_t = (nn(rel_1, hot) + nn(rel_2, hot)) + nn(rel_3, hot)
        hre, him = h_t[:HALF], h_t[HALF:]
        rre, rim = r_t[:HALF], r_t[HALF:]
        q = jnp.concatenate([hre * rre - him * rim, hre * rim + him * rre], axis=0).astype(BF16)
        qt[2 * c + j, 0:D, :] = q
        qt[2 * c + j, D:DP, :] = jnp.zeros((DP - D, EC), BF16)
        sq[2 * c + j, 0:1, :] = jnp.sum(q.astype(F32) * t_t, axis=0, keepdims=True)
        sq[2 * c + j, 1:2, :] = wts[0:1, cols]
        sq[2 * c + j, 2:8, :] = jnp.zeros((6, EC), F32)
        hts[j] = h_t
        tts[j] = t_t
        rts[j] = r_t

    pl.semaphore_wait(barrier, NB * NS - 1)

    def ring(i, d):
        return lax.rem(i + d, 4)

    z_left, z_right, z_far = ring(z, 3), ring(z, 1), ring(z, 2)
    x_left, x_right, x_far = ring(x, 3), ring(x, 1), ring(x, 2)
    y_left, y_right, y_far = ring(y, 3), ring(y, 1), ring(y, 2)
    to_z_left, to_z_right = (z_left * 2 + c, shard), (z_right * 2 + c, shard)
    to_x_left, to_x_right = (bucket, x_left * 4 + y), (bucket, x_right * 4 + y)
    to_y_left, to_y_right = (bucket, x * 4 + y_left), (bucket, x * 4 + y_right)

    for part in (nbt.at[z * 8 + x], nbt.at[z * 8 + 4 + y]):
        rcopy(part, part, send.at[GZ_S], zrecv.at[1], to_z_right)
        rcopy(part, part, send.at[GZ_S], zrecv.at[3], to_z_left)
    mine = pl.ds(2 * c, 2)
    rcopy(qt.at[mine], qt.at[mine], send.at[Q_S], recv.at[Q_S], partner)
    rcopy(sq.at[mine], sq.at[mine], send.at[SQ_S], recv.at[SQ_S], partner)

    ones = jnp.ones((SLOT, 128), BF16)
    tables = []
    for ref in (slots, drows):
        value = ref[...].astype(F32)
        high = jnp.floor(value * (1.0 / 32.0))
        tables.append((high.astype(BF16), (value - 32.0 * high).astype(BF16)))

    def columns(b, carry):
        owner_hot = hot_where(iota((256, 128), 1) == iota((256, 128), 0) // SLOT + b * NS)
        keep = iota((256, SLOT), 1) == iota((256, SLOT), 0) % SLOT
        for (high, low), out in zip(tables, (slot_col, dest_col)):
            h = jnp.where(keep, nt(owner_hot, high), 0.0).astype(BF16)
            l = jnp.where(keep, nt(owner_hot, low), 0.0).astype(BF16)
            out[b] = 32.0 * nn(h, ones) + nn(l, ones)
        return carry

    lax.fori_loop(0, NB, columns, 0)
    nb[:, 384:DP] = jnp.zeros((NEG_DEV, 128), BF16)

    wait_bytes(qt.at[mine], recv.at[Q_S])
    wait_bytes(sq.at[mine], recv.at[SQ_S])

    LOW, HIGH = pl.ds(0, 208), pl.ds(208, 192)

    def ring_start_x(k, src):
        part = nbt.at[src * 8 + x]
        rcopy(part, part, send.at[GX_S], xrecv.at[k, 0], to_x_right)
        rcopy(part, part, send.at[GX_S], xrecv.at[k, 1], to_x_left)

    def ring_start_y(k, src):
        part = nbt.at[src * 8 + 4 + y]
        rcopy(part, part, send.at[GY_S], yrecv.at[k, 0], to_y_right)
        rcopy(part, part, send.at[GY_S], yrecv.at[k, 1], to_y_left)

    def ring_forward(k, src):
        for first, left, right, s_sem, r_sem, to_left, to_right in (
            (src * 8, x_left, x_right, send.at[GX_S], xrecv, to_x_left, to_x_right),
            (src * 8 + 4, y_left, y_right, send.at[GY_S], yrecv, to_y_left, to_y_right),
        ):
            wait_bytes(nbt.at[first + left], r_sem.at[k, 0])
            part = nbt.at[first + left, LOW]
            rcopy(part, part, s_sem, r_sem.at[k, 2], to_right)
            wait_bytes(nbt.at[first + right], r_sem.at[k, 1])
            part = nbt.at[first + right, HIGH]
            rcopy(part, part, s_sem, r_sem.at[k, 2], to_left)

    def ring_finish(k, src):
        wait_bytes(nbt.at[src * 8 + x_far], xrecv.at[k, 2])
        wait_bytes(nbt.at[src * 8 + 4 + y_far], yrecv.at[k, 2])

    def flip(zb):
        for i in range(8):
            nb[i * 128 : (i + 1) * 128, 0:D] = nbt[zb * 8 + i].astype(F32).T.astype(BF16)

    def block(zb, first, pair):

        def chunk(g):
            s = nn(nb[...], qt[g])
            m = jnp.max(s, axis=0, keepdims=True)
            p = jnp.exp(s - m)
            l = jnp.sum(p, axis=0, keepdims=True)
            pb = p.astype(BF16)
            prob[zb, g] = pb
            wide = jnp.concatenate([nbt[zb * 8 + i] for i in range(8)], axis=1)
            o = nn(wide, pb)
            mb[zb, g, 0:1, :] = m
            if first:
                st[c, g, 0:1, :] = m
                st[c, g, 1:2, :] = l
                st[c, g, 2:8, :] = jnp.zeros((6, EC), F32)
                ot[g] = o
            else:
                m_old = st[c, g, 0:1, :]
                m_new = jnp.maximum(m_old, m)
                f_old = jnp.exp(m_old - m_new)
                f_new = jnp.exp(m - m_new)
                st[c, g, 0:1, :] = m_new
                st[c, g, 1:2, :] = st[c, g, 1:2, :] * f_old + l * f_new
                ot[g] = ot[g] * f_old + o * f_new

        chunk(2 * pair)
        chunk(2 * pair + 1)

    def whole(zb, first):
        flip(zb)

        def two(pair, carry):
            block(zb, first, pair)
            return carry

        lax.fori_loop(0, 2, two, 0)

    whole(z, True)
    wait_bytes(nbt.at[pl.ds(z_left * 8, 2)], zrecv.at[1])
    part = nbt.at[z_left * 8 + x]
    rcopy(part, part, send.at[GZ_S], zrecv.at[2], to_z_right)
    ring_start_x(1, z_left)
    ring_start_y(1, z_left)
    wait_bytes(nbt.at[pl.ds(z_right * 8, 2)], zrecv.at[3])
    part = nbt.at[z_right * 8 + 4 + y]
    rcopy(part, part, send.at[GZ_S], zrecv.at[0], to_z_left)
    ring_start_x(3, z_right)
    ring_start_y(3, z_right)
    ring_forward(1, z_left)
    wait_bytes(nbt.at[z_far * 8 + x], zrecv.at[2])
    ring_start_x(2, z_far)
    wait_bytes(nbt.at[z_far * 8 + 4 + y], zrecv.at[0])
    ring_start_y(2, z_far)
    ring_forward(3, z_right)
    ring_finish(1, z_left)
    flip(z_left)
    block(z_left, False, 0)
    ring_forward(2, z_far)
    block(z_left, False, 1)
    ring_finish(3, z_right)
    whole(z_right, False)
    ring_finish(2, z_far)
    whole(z_far, False)

    rcopy(st.at[c], st.at[c], send.at[ST_S], recv.at[ST_S], partner)
    rcopy(ot.at[pl.ds(2 * oc, 2)], ot_in, send.at[O_S], recv.at[O_S], partner)
    wait_bytes(st.at[c], recv.at[ST_S])
    for g in range(4):
        pos = sq[g, 0:1, :]
        m0, m1 = st[0, g, 0:1, :], st[1, g, 0:1, :]
        top = jnp.maximum(pos, jnp.maximum(m0, m1))
        total = (
            jnp.exp(pos - top)
            + st[0, g, 1:2, :] * jnp.exp(m0 - top)
            + st[1, g, 1:2, :] * jnp.exp(m1 - top)
        )
        lt[g, 0:1, :] = top + jnp.log(total)
    wait_bytes(ot_in, recv.at[O_S])

    ends[D:DP, :] = jnp.zeros((DP - D, 2 * E_DEV), BF16)
    for j in range(2):
        cols = slice(j * EC, (j + 1) * EC)
        tail_cols = slice(E_DEV + j * EC, E_DEV + (j + 1) * EC)
        g = 2 * c + j
        pos, w, ltot = sq[g, 0:1, :], sq[g, 1:2, :], lt[g, 0:1, :]
        pos_coef = w * (jnp.exp(pos - ltot) - 1.0)
        own = w * jnp.exp(st[c, g, 0:1, :] - ltot)
        other = w * jnp.exp(st[oc, g, 0:1, :] - ltot)
        grad = pos_coef * tts[j] + ot[g] * own + ot_in[j] * other
        gre, gim = grad[:HALF], grad[HALF:]
        rre, rim = rts[j, :HALF, :], rts[j, HALF:, :]
        hre, him = hts[j, :HALF, :], hts[j, HALF:, :]
        ends[0:D, cols] = jnp.concatenate(
            [gre * rre + gim * rim, gim * rre - gre * rim], axis=0
        ).astype(BF16)
        ends[0:D, tail_cols] = (pos_coef * qt[g, 0:D, :].astype(F32)).astype(BF16)
        term = jnp.concatenate([gre * hre + gim * him, gim * hre - gre * him], axis=0)
        hi = term.astype(BF16)
        rt_hi[:, cols] = hi
        rt_lo[:, cols] = (term - hi.astype(F32)).astype(BF16)

    my_slots = pl.ds(pl.multiple_of(me * SLOT, SLOT), SLOT)

    def pack(bb, first):
        sc = slot_col[bb]
        sel = jnp.concatenate(
            [hot_where(sc == (iota((256, 128), 1) + 128 * t).astype(F32)) for t in range(8)], axis=1
        )
        rows = nt(sel, ends[...])
        dc = dest_col[bb]
        high = jnp.floor(dc * (1.0 / 32.0))
        lane = iota((256, 128), 1)
        code = jnp.where(lane == 16, high, jnp.where(lane == 17, dc - 32.0 * high, 0.0))
        packed[bb, :, 0:384] = rows[:, 0:384].astype(BF16)
        packed[bb, :, 384:512] = (rows[:, 384:512] + code).astype(BF16)
        for j in range(NS):
            ss = lax.rem(shard + j, NS)
            src = packed.at[bb, pl.ds(pl.multiple_of(ss * SLOT, SLOT), SLOT)]
            if first and j == 0:
                pltpu.make_async_copy(src, arrived.at[my_slots], recv.at[ENT_S]).start()
            else:
                rcopy(src, arrived.at[my_slots], send.at[ENT_S], recv.at[ENT_S], (bb, ss))

    def rel_chunk(r, carry):
        hot = hot_where(iota((128, E_DEV), 0) + r * 128 == ids[...])
        rp[pl.ds(pl.multiple_of(r * 128, 128), 128), :] = nt(hot, rt_hi[...]) + nt(hot, rt_lo[...])
        return carry

    lax.fori_loop(0, 4, rel_chunk, 0)
    rcopy(
        rp.at[pl.ds(pl.multiple_of(oc * 256, 256), 256)], rp_in, send.at[RC_S], recv.at[RC_S], partner
    )

    def pack_other(k, carry):
        pack(lax.rem(bucket + k, NB), False)
        return carry

    pack(bucket, True)
    lax.fori_loop(1, 3, pack_other, 0)

    wait_bytes(rp_in, recv.at[RC_S])
    r1b[...] = (rp[pl.ds(pl.multiple_of(c * 256, 256), 256), :] + rp_in[...]).astype(BF16)
    for j in range(1, NS):
        ss = lax.rem(shard + j, NS)
        rows = r1b.at[pl.ds(pl.multiple_of(ss * 16, 16), 16)]
        rcopy(rows, r2in.at[shard], send.at[R2_S], recv.at[R2_S], (bucket, ss))
    r2in[shard] = r1b[pl.ds(pl.multiple_of(shard * 16, 16), 16), :]
    lax.fori_loop(3, NB, pack_other, 0)

    def neg_block(zb):
        for g in range(4):
            scale = sq[g, 1:2, :] * jnp.exp(mb[zb, g, 0:1, :] - lt[g, 0:1, :])
            qs[g] = (qt[g].astype(F32) * scale).astype(BF16)

        def rows_of(xx, carry):
            rr = pl.ds(pl.multiple_of(xx * 256, 256), 256)
            acc = nt(prob[zb, 0, rr, :], qs[0])
            for g in range(1, 4):
                acc = acc + nt(prob[zb, g, rr, :], qs[g])
            gx[zb, xx] = acc[:, 0:128].astype(BF16)
            for yy in range(4):
                gy[zb, yy, xx] = acc[yy * 64 : (yy + 1) * 64, 128:256].astype(BF16)
            gz[zb, :, rr] = acc[:, 256:512].T[0 : D - 256].astype(BF16)
            return carry

        lax.fori_loop(0, 4, rows_of, 0)

    def far_xy(n, zb):
        low, high = pl.ds(0, 128), pl.ds(128, 128)
        rcopy(gx.at[zb, x_far, low], hx.at[0, zb], send.at[X1_S], hrecv.at[0, n], to_x_right)
        rcopy(gx.at[zb, x_far, high], hx.at[1, zb], send.at[X1_S], hrecv.at[1, n], to_x_left)
        low, high = pl.ds(0, 2), pl.ds(2, 2)
        rcopy(gy.at[zb, y_far, low], hy.at[0, zb], send.at[Y1_S], hrecv.at[2, n], to_y_right)
        rcopy(gy.at[zb, y_far, high], hy.at[1, zb], send.at[Y1_S], hrecv.at[3, n], to_y_left)

    def plus(a, b):
        return (a.astype(F32) + b.astype(F32)).astype(BF16)

    def near_xy(n, zb):
        wait_bytes(hx.at[0, zb], hrecv.at[0, n])
        gx[zb, x_right, 0:128, :] = plus(gx[zb, x_right, 0:128, :], hx[0, zb])
        rcopy(gx.at[zb, x_right], rx1.at[0, zb], send.at[X1_S], recv.at[X1_S], to_x_right)
        wait_bytes(hx.at[1, zb], hrecv.at[1, n])
        gx[zb, x_left, 128:256, :] = plus(gx[zb, x_left, 128:256, :], hx[1, zb])
        rcopy(gx.at[zb, x_left], rx1.at[1, zb], send.at[X1_S], recv.at[X1_S], to_x_left)
        wait_bytes(hy.at[0, zb], hrecv.at[2, n])
        gy[zb, y_right, 0:2] = plus(gy[zb, y_right, 0:2], hy[0, zb])
        rcopy(gy.at[zb, y_right], ry1.at[0, zb], send.at[Y1_S], recv.at[Y1_S], to_y_right)
        wait_bytes(hy.at[1, zb], hrecv.at[3, n])
        gy[zb, y_left, 2:4] = plus(gy[zb, y_left, 2:4], hy[1, zb])
        rcopy(gy.at[zb, y_left], ry1.at[1, zb], send.at[Y1_S], recv.at[Y1_S], to_y_left)

    neg_block(z_far)
    rcopy(gz.at[z_far, :, pl.ds(0, 512)], hz.at[0], send.at[Z1_S], hrecv.at[4, 0], to_z_right)
    rcopy(gz.at[z_far, :, pl.ds(512, 512)], hz.at[1], send.at[Z1_S], hrecv.at[5, 0], to_z_left)
    far_xy(0, z_far)

    neg_block(z_right)
    wait_bytes(hz.at[0], hrecv.at[4, 0])
    gz[z_right, :, 0:512] = plus(gz[z_right, :, 0:512], hz[0])
    rcopy(gz.at[z_right], rz1.at[0], send.at[Z1_S], recv.at[Z1_S], to_z_right)
    far_xy(1, z_right)
    near_xy(0, z_far)

    wait_bytes(r2in.at[pl.ds(0, NS - 1)], recv.at[R2_S])
    r2 = r2in[0].astype(F32)
    for i in range(1, NS):
        r2 = r2 + r2in[i].astype(F32)
    r2all[z] = r2
    for k in (1, 3, 2):
        zz = lax.rem(z + k, NZ)
        rcopy(r2all.at[z], r2all.at[z], send.at[R3_S], recv.at[R3_S], (zz * 2 + c, shard))

    neg_block(z_left)
    wait_bytes(hz.at[1], hrecv.at[5, 0])
    gz[z_left, :, 512:1024] = plus(gz[z_left, :, 512:1024], hz[1])
    rcopy(gz.at[z_left], rz1.at[1], send.at[Z1_S], recv.at[Z1_S], to_z_left)
    far_xy(2, z_left)
    near_xy(1, z_right)

    neg_block(z)
    far_xy(3, z)
    near_xy(2, z_left)

    wait_bytes(r2all.at[pl.ds(0, 3)], recv.at[R3_S])
    rel_row = pl.ds(pl.multiple_of(c * 256 + shard * 16, 16), 16)
    rfin[rel_row, :] = ((r2all[0] + r2all[1]) + r2all[2]) + r2all[3]
    for j in range(1, NS):
        ss = lax.rem(shard + j, NS)
        rcopy(rfin.at[rel_row], rfin.at[rel_row], send.at[R4_S], recv.at[R4_S], (bucket, ss))

    near_xy(3, z)

    wait_bytes(rx1, recv.at[X1_S])

    def sum_x(zb, carry):
        total = gx[zb, x].astype(F32) + rx1[0, zb].astype(F32) + rx1[1, zb].astype(F32)
        ax[zb] = total.astype(BF16)
        return carry

    lax.fori_loop(0, NZ, sum_x, 0)
    for j in range(1, NS):
        other_zy = lax.rem(z * 4 + y + j, NS)
        zz, yy = other_zy // 4, other_zy % 4
        rows = ax.at[zz, pl.ds(pl.multiple_of(yy * NEG_OWN, NEG_OWN), NEG_OWN)]
        rcopy(rows, rx2.at[z * 4 + y], send.at[X2_S], recv.at[X2_S], (zz * 2 + c, x * 4 + yy))
    rx2[z * 4 + y] = ax[z, pl.ds(pl.multiple_of(y * NEG_OWN, NEG_OWN), NEG_OWN), :]

    wait_bytes(ry1, recv.at[Y1_S])

    def sum_y(zb, carry):
        total = gy[zb, y].astype(F32) + ry1[0, zb].astype(F32) + ry1[1, zb].astype(F32)
        ay[zb] = total.astype(BF16)
        return carry

    lax.fori_loop(0, NZ, sum_y, 0)
    for j in range(1, NS):
        other_zx = lax.rem(z * 4 + x + j, NS)
        zz, xx = other_zx // 4, other_zx % 4
        rcopy(ay.at[zz, xx], ry2.at[z * 4 + x], send.at[Y2_S], recv.at[Y2_S], (zz * 2 + c, xx * 4 + y))
    ry2[z * 4 + x] = ay[z, x]

    wait_bytes(rz1, recv.at[Z1_S])

    def sum_z(r, carry):
        rr = pl.ds(pl.multiple_of(r * 256, 256), 256)
        total = gz[z, :, rr].astype(F32) + rz1[0, :, rr].astype(F32) + rz1[1, :, rr].astype(F32)
        wide = jnp.concatenate([total, jnp.zeros((256 - (D - 256), 256), F32)], axis=0)
        az[rr, :] = wide.T.astype(BF16)
        return carry

    lax.fori_loop(0, 4, sum_z, 0)
    for j in range(1, NS):
        ss = lax.rem(shard + j, NS)
        rows = az.at[pl.ds(pl.multiple_of(ss * NEG_OWN, NEG_OWN), NEG_OWN)]
        rcopy(rows, rz2.at[shard], send.at[Z2_S], recv.at[Z2_S], (bucket, ss))
    rz2[shard] = az[pl.ds(pl.multiple_of(shard * NEG_OWN, NEG_OWN), NEG_OWN), :]

    wait_bytes(arrived, recv.at[ENT_S])
    lane = iota((8, DP), 1)
    unit = jnp.where(lane == D, 32.0, jnp.where(lane == D + 1, 1.0, 0.0)).astype(BF16)
    row_ids = nt(unit, arrived[...])[0:1, :]

    def scatter(r, carry):
        hot = hot_where((iota((256, 2048), 0) + r * 256).astype(F32) == row_ids)
        got = nn(hot, arrived[...])
        ent_out[:, pl.ds(pl.multiple_of(r * 256, 256), 256)] = got.T[0:D]
        return carry

    lax.fori_loop(0, 4, scatter, 0)

    wait_bytes(rfin.at[pl.ds(0, 240)], recv.at[R4_S])
    half_rel = rfin.at[pl.ds(pl.multiple_of(c * 256, 256), 256)]
    rcopy(half_rel, half_rel, send.at[R5_S], recv.at[R5_S], partner)

    def sum16(ref):
        total = ref[0].astype(F32)
        for i in range(1, NS):
            total = total + ref[i].astype(F32)
        return total

    wait_bytes(rx2.at[pl.ds(0, NS - 1)], recv.at[X2_S])
    neg_out[:, 0:128] = sum16(rx2)
    wait_bytes(ry2.at[pl.ds(0, NS - 1)], recv.at[Y2_S])
    neg_out[:, 128:256] = sum16(ry2)
    wait_bytes(rz2.at[pl.ds(0, NS - 1)], recv.at[Z2_S])
    neg_out[:, 256:D] = sum16(rz2)[:, 0 : D - 256]

    wait_bytes(half_rel, recv.at[R5_S])
    for r in range(4):
        rr = slice(r * 128, (r + 1) * 128)
        wide = jnp.concatenate([rfin[rr, :], jnp.zeros((128, DP - D), F32)], axis=1)
        rel_out[:, rr] = wide.T[0:D]

    wait_bytes(nbt.at[pl.ds(0, 6)], send.at[GZ_S])
    wait_bytes(nbt.at[pl.ds(0, 9)], send.at[GX_S])
    wait_bytes(nbt.at[pl.ds(0, 9)], send.at[GY_S])
    wait_bytes(qt.at[mine], send.at[Q_S])
    wait_bytes(sq.at[mine], send.at[SQ_S])
    wait_bytes(st.at[c], send.at[ST_S])
    wait_bytes(ot_in, send.at[O_S])
    wait_bytes(arrived.at[pl.ds(0, 2048 - SLOT)], send.at[ENT_S])
    wait_bytes(rp_in, send.at[RC_S])
    wait_bytes(r2in.at[pl.ds(0, NS - 1)], send.at[R2_S])
    wait_bytes(r2all.at[pl.ds(0, 3)], send.at[R3_S])
    wait_bytes(rfin.at[pl.ds(0, 240)], send.at[R4_S])
    wait_bytes(half_rel, send.at[R5_S])
    wait_bytes(gz.at[pl.ds(0, 3)], send.at[Z1_S])
    wait_bytes(gx.at[pl.ds(0, 3)], send.at[X1_S])
    wait_bytes(gy.at[pl.ds(0, 3)], send.at[Y1_S])
    wait_bytes(rx2.at[pl.ds(0, NS - 1)], send.at[X2_S])
    wait_bytes(ry2.at[pl.ds(0, NS - 1)], send.at[Y2_S])
    wait_bytes(rz2.at[pl.ds(0, NS - 1)], send.at[Z2_S])


SCRATCH = [
    ((NZ * 8, D, 128), BF16),
    ((NEG_DEV, DP), BF16),
    ((NZ, 4, NEG_DEV, EC), BF16),
    ((4, DP, EC), BF16),
    ((4, 8, EC), F32),
    ((2, D, EC), F32),
    ((2, D, EC), F32),
    ((2, D, EC), F32),
    ((NZ, 4, 8, EC), F32),
    ((2, 4, 8, EC), F32),
    ((4, D, EC), F32),
    ((2, D, EC), F32),
    ((4, 8, EC), F32),
    ((4, DP, EC), BF16),
    ((DP, 2 * E_DEV), BF16),
    ((D, E_DEV), BF16),
    ((D, E_DEV), BF16),
    ((NB, 256, DP), BF16),
    ((2048, DP), BF16),
    ((NB, 256, 128), F32),
    ((NB, 256, 128), F32),
    ((NZ, D - 256, NEG_DEV), BF16),
    ((NZ, 4, 256, 128), BF16),
    ((NZ, 4, 4, NEG_OWN, 128), BF16),
    ((2, D - 256, 512), BF16),
    ((2, NZ, 128, 128), BF16),
    ((2, NZ, 2, NEG_OWN, 128), BF16),
    ((2, D - 256, NEG_DEV), BF16),
    ((2, NZ, 256, 128), BF16),
    ((2, NZ, 4, NEG_OWN, 128), BF16),
    ((NEG_DEV, 256), BF16),
    ((NZ, 256, 128), BF16),
    ((NZ, 4, NEG_OWN, 128), BF16),
    ((NS, NEG_OWN, 256), BF16),
    ((NS, NEG_OWN, 128), BF16),
    ((NS, NEG_OWN, 128), BF16),
    ((REL, D), F32),
    ((REL // 2, D), F32),
    ((REL // 2, D), BF16),
    ((NS, 16, D), BF16),
    ((NZ, 16, D), F32),
    ((REL, D), F32),
]


def per_device(
    head_rows, tail_rows, rel_ids, relations, edge_weights, neg_rows, send_slots, dest_rows
):
    vmem = pl.BlockSpec(memory_space=pltpu.VMEM)
    ent_t, neg_grad, rel_t = pl.pallas_call(
        kernel,
        out_shape=(
            jax.ShapeDtypeStruct((D, ENT_DEV), F32),
            jax.ShapeDtypeStruct((NEG_OWN, D), F32),
            jax.ShapeDtypeStruct((D, REL), F32),
        ),
        in_specs=[vmem] * 8,
        out_specs=(vmem,) * 3,
        scratch_shapes=[pltpu.VMEM(shape, dtype) for shape, dtype in SCRATCH]
        + [
            pltpu.SemaphoreType.DMA((19,)),
            pltpu.SemaphoreType.DMA((16,)),
            pltpu.SemaphoreType.DMA((NZ,)),
            pltpu.SemaphoreType.DMA((NZ, 3)),
            pltpu.SemaphoreType.DMA((NZ, 3)),
            pltpu.SemaphoreType.DMA((6, 4)),
        ],
        compiler_params=pltpu.CompilerParams(
            collective_id=0, has_side_effects=True, vmem_limit_bytes=60 * 1024 * 1024
        ),
        cost_estimate=pl.CostEstimate(
            flops=2 * 3 * 1024 * 4096 * 400, bytes_accessed=8 * 1024 * 1024, transcendentals=1024 * 4096
        ),
        name="complex_backward",
    )(
        head_rows.T,
        tail_rows.T,
        rel_ids.reshape(1, E_DEV),
        relations.T,
        edge_weights.reshape(1, E_DEV),
        neg_rows.T,
        send_slots.T,
        dest_rows.T,
    )
    return ent_t.T, neg_grad, rel_t.T


def solution(mesh):
    return jax.shard_map(
        per_device,
        mesh=mesh,
        in_specs=(
            P(("bucket", "shard"), None),
            P(("bucket", "shard"), None),
            P(("bucket", "shard")),
            P(),
            P(("bucket", "shard")),
            P("bucket", None),
            P(("bucket", "shard"), None),
            P(("bucket", "shard"), None),
        ),
        out_specs=(P(("bucket", "shard"), None), P(("bucket", "shard"), None), P()),
        check_vma=False,
    )
```

```python
import functools

import jax
import jax.numpy as jnp
from jax import lax
from jax.experimental import pallas as pl
from jax.experimental.pallas import tpu as pltpu
from jax.sharding import PartitionSpec as P

D = 400
HALF = 200
DP = 512
E_DEV = 512
ENT_DEV = 1024
REL = 512
NEG_DEV = 1024
SLOT = 16
NB = 8
NS = 16
NZ = 4
EC = 256
NEG_OWN = 64

MESH = pl.DeviceIdType.MESH
F32 = jnp.float32
BF16 = jnp.bfloat16

(Q_S, SQ_S, ST_S, O_S, RC_S, R2_S, R3_S, R4_S, R5_S, ENT_S,
 Z1_S, X1_S, Y1_S, Z2_S, X2_S, Y2_S, GZ_S, GX_S, GY_S) = range(19)


def nt(a, b):
    return lax.dot_general(a, b, (((1,), (1,)), ((), ())), preferred_element_type=F32)


def nn(a, b):
    return jnp.dot(a, b, preferred_element_type=F32)


def iota(shape, dim):
    return lax.broadcasted_iota(jnp.int32, shape, dim)


def hot_where(mask):
    return mask.astype(F32).astype(BF16)


def wait_bytes(ref, sem):
    pltpu.make_async_copy(ref, ref, sem).wait()


def kernel(
    head, tail, ids, rel, wts, neg, slots, drows,
    arrived_out, rx2_out, ry2_out, rz2_out, rel_sum_out,
    nbt, wide, nb, prob, qt, sq, hts, tts, rts, mb, st, ot, ot_in, lt, qs, ends, rt_hi, rt_lo,
    packed, arrived, slot_col, dest_col,
    gz, gx, gy, hz, hx, hy, rz1, rx1, ry1, az, ax, ay, rz2, rx2, ry2,
    rp, rp_in, r1b, r2in, r2all, rfin,
    send, recv, zrecv, xrecv, yrecv, hrecv, out_sem,
):
    bucket, shard = lax.axis_index("bucket"), lax.axis_index("shard")
    z, c = bucket // 2, bucket % 2
    x, y = shard // 4, shard % 4
    oc = 1 - c
    me = bucket * NS + shard
    partner = (z * 2 + oc, shard)

    def rcopy(src, dst, s_sem, r_sem, device):
        pltpu.make_async_remote_copy(
            src_ref=src, dst_ref=dst, send_sem=s_sem, recv_sem=r_sem,
            device_id=device, device_id_type=MESH,
        ).start()

    barrier = pltpu.get_barrier_semaphore()

    def greet(i, carry):
        d = lax.rem(me + i, NB * NS)
        pl.semaphore_signal(barrier, inc=1, device_id=(d // NS, d % NS), device_id_type=MESH)
        return carry

    lax.fori_loop(1, NB * NS, greet, 0)

    for i in range(8):
        nbt[z * 8 + i] = neg[:, i * 128 : (i + 1) * 128]

    rel_1 = rel[...].astype(BF16)
    rest = rel[...] - rel_1.astype(F32)
    rel_2 = rest.astype(BF16)
    rel_3 = (rest - rel_2.astype(F32)).astype(BF16)
    for j in range(2):
        cols = slice(j * EC, (j + 1) * EC)
        h_t = head[:, cols].astype(F32)
        t_t = tail[:, cols].astype(F32)
        hot = hot_where(iota((REL, EC), 0) == ids[0:1, cols])
        r_t = (nn(rel_1, hot) + nn(rel_2, hot)) + nn(rel_3, hot)
        hre, him = h_t[:HALF], h_t[HALF:]
        rre, rim = r_t[:HALF], r_t[HALF:]
        q = jnp.concatenate([hre * rre - him * rim, hre * rim + him * rre], axis=0).astype(BF16)
        qt[2 * c + j, 0:D, :] = q
        qt[2 * c + j, D:DP, :] = jnp.zeros((DP - D, EC), BF16)
        sq[2 * c + j, 0:1, :] = jnp.sum(q.astype(F32) * t_t, axis=0, keepdims=True)
        sq[2 * c + j, 1:2, :] = wts[0:1, cols]
        sq[2 * c + j, 2:8, :] = jnp.zeros((6, EC), F32)
        hts[j] = h_t
        tts[j] = t_t
        rts[j] = r_t

    pl.semaphore_wait(barrier, NB * NS - 1)

    def ring(i, d):
        return lax.rem(i + d, 4)

    z_left, z_right, z_far = ring(z, 3), ring(z, 1), ring(z, 2)
    x_left, x_right, x_far = ring(x, 3), ring(x, 1), ring(x, 2)
    y_left, y_right, y_far = ring(y, 3), ring(y, 1), ring(y, 2)
    to_z_left, to_z_right = (z_left * 2 + c, shard), (z_right * 2 + c, shard)
    to_x_left, to_x_right = (bucket, x_left * 4 + y), (bucket, x_right * 4 + y)
    to_y_left, to_y_right = (bucket, x * 4 + y_left), (bucket, x * 4 + y_right)

    for part in (nbt.at[z * 8 + x], nbt.at[z * 8 + 4 + y]):
        rcopy(part, part, send.at[GZ_S], zrecv.at[1], to_z_right)
        rcopy(part, part, send.at[GZ_S], zrecv.at[3], to_z_left)
    mine = pl.ds(2 * c, 2)
    rcopy(qt.at[mine], qt.at[mine], send.at[Q_S], recv.at[Q_S], partner)
    rcopy(sq.at[mine], sq.at[mine], send.at[SQ_S], recv.at[SQ_S], partner)

    ones = jnp.ones((SLOT, 128), BF16)
    tables = []
    for ref in (slots, drows):
        value = ref[...].astype(F32)
        high = jnp.floor(value * (1.0 / 32.0))
        tables.append((high.astype(BF16), (value - 32.0 * high).astype(BF16)))

    def columns(b, carry):
        owner_hot = hot_where(iota((256, 128), 1) == iota((256, 128), 0) // SLOT + b * NS)
        keep = iota((256, SLOT), 1) == iota((256, SLOT), 0) % SLOT
        for (high, low), out in zip(tables, (slot_col, dest_col)):
            h = jnp.where(keep, nt(owner_hot, high), 0.0).astype(BF16)
            l = jnp.where(keep, nt(owner_hot, low), 0.0).astype(BF16)
            out[b] = 32.0 * nn(h, ones) + nn(l, ones)
        return carry

    lax.fori_loop(0, NB, columns, 0)
    nb[:, 384:DP] = jnp.zeros((NEG_DEV, 128), BF16)

    wait_bytes(qt.at[mine], recv.at[Q_S])
    wait_bytes(sq.at[mine], recv.at[SQ_S])

    LOW, HIGH = pl.ds(0, 208), pl.ds(208, 192)

    def ring_start_x(k, src):
        part = nbt.at[src * 8 + x]
        rcopy(part, part, send.at[GX_S], xrecv.at[k, 0], to_x_right)
        rcopy(part, part, send.at[GX_S], xrecv.at[k, 1], to_x_left)

    def ring_start_y(k, src):
        part = nbt.at[src * 8 + 4 + y]
        rcopy(part, part, send.at[GY_S], yrecv.at[k, 0], to_y_right)
        rcopy(part, part, send.at[GY_S], yrecv.at[k, 1], to_y_left)

    def ring_forward(k, src):
        for first, left, right, s_sem, r_sem, to_left, to_right in (
            (src * 8, x_left, x_right, send.at[GX_S], xrecv, to_x_left, to_x_right),
            (src * 8 + 4, y_left, y_right, send.at[GY_S], yrecv, to_y_left, to_y_right),
        ):
            wait_bytes(nbt.at[first + left], r_sem.at[k, 0])
            part = nbt.at[first + left, LOW]
            rcopy(part, part, s_sem, r_sem.at[k, 2], to_right)
            wait_bytes(nbt.at[first + right], r_sem.at[k, 1])
            part = nbt.at[first + right, HIGH]
            rcopy(part, part, s_sem, r_sem.at[k, 2], to_left)

    def ring_finish(k, src):
        wait_bytes(nbt.at[src * 8 + x_far], xrecv.at[k, 2])
        wait_bytes(nbt.at[src * 8 + 4 + y_far], yrecv.at[k, 2])

    def flip(zb):
        for i in range(8):
            part = nbt[zb * 8 + i]
            wide[:, i * 128 : (i + 1) * 128] = part
            nb[i * 128 : (i + 1) * 128, 0:D] = part.astype(F32).T.astype(BF16)

    def block(zb, first, pair):

        def chunk(g):
            s = nn(nb[...], qt[g])
            m = jnp.max(s, axis=0, keepdims=True)
            p = jnp.exp(s - m)
            l = jnp.sum(p, axis=0, keepdims=True)
            pb = p.astype(BF16)
            prob[zb, g] = pb
            o = nn(wide[...], pb)
            mb[zb, g, 0:1, :] = m
            if first:
                st[c, g, 0:1, :] = m
                st[c, g, 1:2, :] = l
                st[c, g, 2:8, :] = jnp.zeros((6, EC), F32)
                ot[g] = o
            else:
                m_old = st[c, g, 0:1, :]
                m_new = jnp.maximum(m_old, m)
                f_old = jnp.exp(m_old - m_new)
                f_new = jnp.exp(m - m_new)
                st[c, g, 0:1, :] = m_new
                st[c, g, 1:2, :] = st[c, g, 1:2, :] * f_old + l * f_new
                ot[g] = ot[g] * f_old + o * f_new

        chunk(2 * pair)
        chunk(2 * pair + 1)

    def whole(zb, first):
        flip(zb)

        def two(pair, carry):
            block(zb, first, pair)
            return carry

        lax.fori_loop(0, 2, two, 0)

    whole(z, True)
    wait_bytes(nbt.at[pl.ds(z_left * 8, 2)], zrecv.at[1])
    part = nbt.at[z_left * 8 + x]
    rcopy(part, part, send.at[GZ_S], zrecv.at[2], to_z_right)
    ring_start_x(1, z_left)
    ring_start_y(1, z_left)
    wait_bytes(nbt.at[pl.ds(z_right * 8, 2)], zrecv.at[3])
    part = nbt.at[z_right * 8 + 4 + y]
    rcopy(part, part, send.at[GZ_S], zrecv.at[0], to_z_left)
    ring_start_x(3, z_right)
    ring_start_y(3, z_right)
    ring_forward(1, z_left)
    wait_bytes(nbt.at[z_far * 8 + x], zrecv.at[2])
    ring_start_x(2, z_far)
    wait_bytes(nbt.at[z_far * 8 + 4 + y], zrecv.at[0])
    ring_start_y(2, z_far)
    ring_forward(3, z_right)
    ring_finish(1, z_left)
    flip(z_left)
    block(z_left, False, 0)
    ring_forward(2, z_far)
    block(z_left, False, 1)
    ring_finish(3, z_right)
    whole(z_right, False)
    ring_finish(2, z_far)
    whole(z_far, False)

    rcopy(st.at[c], st.at[c], send.at[ST_S], recv.at[ST_S], partner)
    rcopy(ot.at[pl.ds(2 * oc, 2)], ot_in, send.at[O_S], recv.at[O_S], partner)
    wait_bytes(st.at[c], recv.at[ST_S])
    for g in range(4):
        pos = sq[g, 0:1, :]
        m0, m1 = st[0, g, 0:1, :], st[1, g, 0:1, :]
        top = jnp.maximum(pos, jnp.maximum(m0, m1))
        total = (
            jnp.exp(pos - top)
            + st[0, g, 1:2, :] * jnp.exp(m0 - top)
            + st[1, g, 1:2, :] * jnp.exp(m1 - top)
        )
        lt[g, 0:1, :] = top + jnp.log(total)
    wait_bytes(ot_in, recv.at[O_S])

    ends[D:DP, :] = jnp.zeros((DP - D, 2 * E_DEV), BF16)
    for j in range(2):
        cols = slice(j * EC, (j + 1) * EC)
        tail_cols = slice(E_DEV + j * EC, E_DEV + (j + 1) * EC)
        g = 2 * c + j
        pos, w, ltot = sq[g, 0:1, :], sq[g, 1:2, :], lt[g, 0:1, :]
        pos_coef = w * (jnp.exp(pos - ltot) - 1.0)
        own = w * jnp.exp(st[c, g, 0:1, :] - ltot)
        other = w * jnp.exp(st[oc, g, 0:1, :] - ltot)
        grad = pos_coef * tts[j] + ot[g] * own + ot_in[j] * other
        gre, gim = grad[:HALF], grad[HALF:]
        rre, rim = rts[j, :HALF, :], rts[j, HALF:, :]
        hre, him = hts[j, :HALF, :], hts[j, HALF:, :]
        ends[0:D, cols] = jnp.concatenate(
            [gre * rre + gim * rim, gim * rre - gre * rim], axis=0
        ).astype(BF16)
        ends[0:D, tail_cols] = (pos_coef * qt[g, 0:D, :].astype(F32)).astype(BF16)
        term = jnp.concatenate([gre * hre + gim * him, gim * hre - gre * him], axis=0)
        hi = term.astype(BF16)
        rt_hi[:, cols] = hi
        rt_lo[:, cols] = (term - hi.astype(F32)).astype(BF16)

    my_slots = pl.ds(pl.multiple_of(me * SLOT, SLOT), SLOT)

    def pack(bb, first):
        sc = slot_col[bb]
        sel = jnp.concatenate(
            [hot_where(sc == (iota((256, 128), 1) + 128 * t).astype(F32)) for t in range(8)], axis=1
        )
        rows = nt(sel, ends[...])
        dc = dest_col[bb]
        high = jnp.floor(dc * (1.0 / 32.0))
        lane = iota((256, 128), 1)
        code = jnp.where(lane == 16, high, jnp.where(lane == 17, dc - 32.0 * high, 0.0))
        packed[bb, :, 0:384] = rows[:, 0:384].astype(BF16)
        packed[bb, :, 384:512] = (rows[:, 384:512] + code).astype(BF16)
        for j in range(NS):
            ss = lax.rem(shard + j, NS)
            src = packed.at[bb, pl.ds(pl.multiple_of(ss * SLOT, SLOT), SLOT)]
            if first and j == 0:
                pltpu.make_async_copy(src, arrived.at[my_slots], recv.at[ENT_S]).start()
            else:
                rcopy(src, arrived.at[my_slots], send.at[ENT_S], recv.at[ENT_S], (bb, ss))

    def rel_chunk(r, carry):
        hot = hot_where(iota((128, E_DEV), 0) + r * 128 == ids[...])
        rp[pl.ds(pl.multiple_of(r * 128, 128), 128), :] = nt(hot, rt_hi[...]) + nt(hot, rt_lo[...])
        return carry

    lax.fori_loop(0, 4, rel_chunk, 0)
    rcopy(
        rp.at[pl.ds(pl.multiple_of(oc * 256, 256), 256)], rp_in, send.at[RC_S], recv.at[RC_S], partner
    )

    def pack_other(k, carry):
        pack(lax.rem(bucket + k, NB), False)
        return carry

    pack(bucket, True)
    lax.fori_loop(1, 3, pack_other, 0)

    wait_bytes(rp_in, recv.at[RC_S])
    r1b[...] = (rp[pl.ds(pl.multiple_of(c * 256, 256), 256), :] + rp_in[...]).astype(BF16)
    for j in range(1, NS):
        ss = lax.rem(shard + j, NS)
        rows = r1b.at[pl.ds(pl.multiple_of(ss * 16, 16), 16)]
        rcopy(rows, r2in.at[shard], send.at[R2_S], recv.at[R2_S], (bucket, ss))
    r2in[shard] = r1b[pl.ds(pl.multiple_of(shard * 16, 16), 16), :]
    lax.fori_loop(3, NB, pack_other, 0)

    def neg_block(zb):
        for g in range(4):
            scale = sq[g, 1:2, :] * jnp.exp(mb[zb, g, 0:1, :] - lt[g, 0:1, :])
            qs[g] = (qt[g].astype(F32) * scale).astype(BF16)

        def rows_of(xx, carry):
            rr = pl.ds(pl.multiple_of(xx * 256, 256), 256)
            acc = nt(prob[zb, 0, rr, :], qs[0])
            for g in range(1, 4):
                acc = acc + nt(prob[zb, g, rr, :], qs[g])
            gx[zb, xx] = acc[:, 0:128].astype(BF16)
            for yy in range(4):
                gy[zb, yy, xx] = acc[yy * 64 : (yy + 1) * 64, 128:256].astype(BF16)
            gz[zb, :, rr] = acc[:, 256:512].T[0 : D - 256].astype(BF16)
            return carry

        lax.fori_loop(0, 4, rows_of, 0)

    def far_xy(n, zb):
        low, high = pl.ds(0, 128), pl.ds(128, 128)
        rcopy(gx.at[zb, x_far, low], hx.at[0, zb], send.at[X1_S], hrecv.at[0, n], to_x_right)
        rcopy(gx.at[zb, x_far, high], hx.at[1, zb], send.at[X1_S], hrecv.at[1, n], to_x_left)
        low, high = pl.ds(0, 2), pl.ds(2, 2)
        rcopy(gy.at[zb, y_far, low], hy.at[0, zb], send.at[Y1_S], hrecv.at[2, n], to_y_right)
        rcopy(gy.at[zb, y_far, high], hy.at[1, zb], send.at[Y1_S], hrecv.at[3, n], to_y_left)

    def plus(a, b):
        return (a.astype(F32) + b.astype(F32)).astype(BF16)

    def near_xy(n, zb):
        wait_bytes(hx.at[0, zb], hrecv.at[0, n])
        gx[zb, x_right, 0:128, :] = plus(gx[zb, x_right, 0:128, :], hx[0, zb])
        rcopy(gx.at[zb, x_right], rx1.at[0, zb], send.at[X1_S], recv.at[X1_S], to_x_right)
        wait_bytes(hx.at[1, zb], hrecv.at[1, n])
        gx[zb, x_left, 128:256, :] = plus(gx[zb, x_left, 128:256, :], hx[1, zb])
        rcopy(gx.at[zb, x_left], rx1.at[1, zb], send.at[X1_S], recv.at[X1_S], to_x_left)
        wait_bytes(hy.at[0, zb], hrecv.at[2, n])
        gy[zb, y_right, 0:2] = plus(gy[zb, y_right, 0:2], hy[0, zb])
        rcopy(gy.at[zb, y_right], ry1.at[0, zb], send.at[Y1_S], recv.at[Y1_S], to_y_right)
        wait_bytes(hy.at[1, zb], hrecv.at[3, n])
        gy[zb, y_left, 2:4] = plus(gy[zb, y_left, 2:4], hy[1, zb])
        rcopy(gy.at[zb, y_left], ry1.at[1, zb], send.at[Y1_S], recv.at[Y1_S], to_y_left)

    neg_block(z_far)
    rcopy(gz.at[z_far, :, pl.ds(0, 512)], hz.at[0], send.at[Z1_S], hrecv.at[4, 0], to_z_right)
    rcopy(gz.at[z_far, :, pl.ds(512, 512)], hz.at[1], send.at[Z1_S], hrecv.at[5, 0], to_z_left)
    far_xy(0, z_far)

    neg_block(z_right)
    wait_bytes(hz.at[0], hrecv.at[4, 0])
    gz[z_right, :, 0:512] = plus(gz[z_right, :, 0:512], hz[0])
    rcopy(gz.at[z_right], rz1.at[0], send.at[Z1_S], recv.at[Z1_S], to_z_right)
    far_xy(1, z_right)
    near_xy(0, z_far)

    wait_bytes(r2in.at[pl.ds(0, NS - 1)], recv.at[R2_S])
    r2 = r2in[0].astype(F32)
    for i in range(1, NS):
        r2 = r2 + r2in[i].astype(F32)
    r2all[z] = r2
    for k in (1, 3, 2):
        zz = lax.rem(z + k, NZ)
        rcopy(r2all.at[z], r2all.at[z], send.at[R3_S], recv.at[R3_S], (zz * 2 + c, shard))

    neg_block(z_left)
    wait_bytes(hz.at[1], hrecv.at[5, 0])
    gz[z_left, :, 512:1024] = plus(gz[z_left, :, 512:1024], hz[1])
    rcopy(gz.at[z_left], rz1.at[1], send.at[Z1_S], recv.at[Z1_S], to_z_left)
    far_xy(2, z_left)
    near_xy(1, z_right)

    neg_block(z)
    far_xy(3, z)
    near_xy(2, z_left)

    wait_bytes(r2all.at[pl.ds(0, 3)], recv.at[R3_S])
    rel_row = pl.ds(pl.multiple_of(c * 256 + shard * 16, 16), 16)
    rfin[rel_row, :] = ((r2all[0] + r2all[1]) + r2all[2]) + r2all[3]
    for j in range(1, NS):
        ss = lax.rem(shard + j, NS)
        rcopy(rfin.at[rel_row], rfin.at[rel_row], send.at[R4_S], recv.at[R4_S], (bucket, ss))

    near_xy(3, z)

    wait_bytes(rx1, recv.at[X1_S])

    def sum_x(zb, carry):
        total = gx[zb, x].astype(F32) + rx1[0, zb].astype(F32) + rx1[1, zb].astype(F32)
        ax[zb] = total.astype(BF16)
        return carry

    lax.fori_loop(0, NZ, sum_x, 0)
    for j in range(1, NS):
        other_zy = lax.rem(z * 4 + y + j, NS)
        zz, yy = other_zy // 4, other_zy % 4
        rows = ax.at[zz, pl.ds(pl.multiple_of(yy * NEG_OWN, NEG_OWN), NEG_OWN)]
        rcopy(rows, rx2.at[z * 4 + y], send.at[X2_S], recv.at[X2_S], (zz * 2 + c, x * 4 + yy))
    rx2[z * 4 + y] = ax[z, pl.ds(pl.multiple_of(y * NEG_OWN, NEG_OWN), NEG_OWN), :]

    wait_bytes(ry1, recv.at[Y1_S])

    def sum_y(zb, carry):
        total = gy[zb, y].astype(F32) + ry1[0, zb].astype(F32) + ry1[1, zb].astype(F32)
        ay[zb] = total.astype(BF16)
        return carry

    lax.fori_loop(0, NZ, sum_y, 0)
    for j in range(1, NS):
        other_zx = lax.rem(z * 4 + x + j, NS)
        zz, xx = other_zx // 4, other_zx % 4
        rcopy(ay.at[zz, xx], ry2.at[z * 4 + x], send.at[Y2_S], recv.at[Y2_S], (zz * 2 + c, xx * 4 + y))
    ry2[z * 4 + x] = ay[z, x]

    wait_bytes(rz1, recv.at[Z1_S])

    def sum_z(r, carry):
        rr = pl.ds(pl.multiple_of(r * 256, 256), 256)
        total = gz[z, :, rr].astype(F32) + rz1[0, :, rr].astype(F32) + rz1[1, :, rr].astype(F32)
        wide = jnp.concatenate([total, jnp.zeros((256 - (D - 256), 256), F32)], axis=0)
        az[rr, :] = wide.T.astype(BF16)
        return carry

    lax.fori_loop(0, 4, sum_z, 0)
    for j in range(1, NS):
        ss = lax.rem(shard + j, NS)
        rows = az.at[pl.ds(pl.multiple_of(ss * NEG_OWN, NEG_OWN), NEG_OWN)]
        rcopy(rows, rz2.at[shard], send.at[Z2_S], recv.at[Z2_S], (bucket, ss))
    rz2[shard] = az[pl.ds(pl.multiple_of(shard * NEG_OWN, NEG_OWN), NEG_OWN), :]

    def give(src, dst, sem):
        pltpu.make_async_copy(src, dst, sem).start()

    wait_bytes(arrived, recv.at[ENT_S])
    give(arrived, arrived_out, out_sem.at[0])
    wait_bytes(rfin.at[pl.ds(0, 240)], recv.at[R4_S])
    half_rel = rfin.at[pl.ds(pl.multiple_of(c * 256, 256), 256)]
    rcopy(half_rel, half_rel, send.at[R5_S], recv.at[R5_S], partner)
    wait_bytes(rx2.at[pl.ds(0, NS - 1)], recv.at[X2_S])
    give(rx2, rx2_out, out_sem.at[1])
    wait_bytes(ry2.at[pl.ds(0, NS - 1)], recv.at[Y2_S])
    give(ry2, ry2_out, out_sem.at[2])
    wait_bytes(rz2.at[pl.ds(0, NS - 1)], recv.at[Z2_S])
    give(rz2, rz2_out, out_sem.at[3])
    wait_bytes(half_rel, recv.at[R5_S])
    give(rfin, rel_sum_out, out_sem.at[4])

    wait_bytes(nbt.at[pl.ds(0, 6)], send.at[GZ_S])
    wait_bytes(nbt.at[pl.ds(0, 9)], send.at[GX_S])
    wait_bytes(nbt.at[pl.ds(0, 9)], send.at[GY_S])
    wait_bytes(qt.at[mine], send.at[Q_S])
    wait_bytes(sq.at[mine], send.at[SQ_S])
    wait_bytes(st.at[c], send.at[ST_S])
    wait_bytes(ot_in, send.at[O_S])
    wait_bytes(arrived.at[pl.ds(0, 2048 - SLOT)], send.at[ENT_S])
    wait_bytes(rp_in, send.at[RC_S])
    wait_bytes(r2in.at[pl.ds(0, NS - 1)], send.at[R2_S])
    wait_bytes(r2all.at[pl.ds(0, 3)], send.at[R3_S])
    wait_bytes(rfin.at[pl.ds(0, 240)], send.at[R4_S])
    wait_bytes(half_rel, send.at[R5_S])
    wait_bytes(gz.at[pl.ds(0, 3)], send.at[Z1_S])
    wait_bytes(gx.at[pl.ds(0, 3)], send.at[X1_S])
    wait_bytes(gy.at[pl.ds(0, 3)], send.at[Y1_S])
    wait_bytes(rx2.at[pl.ds(0, NS - 1)], send.at[X2_S])
    wait_bytes(ry2.at[pl.ds(0, NS - 1)], send.at[Y2_S])
    wait_bytes(rz2.at[pl.ds(0, NS - 1)], send.at[Z2_S])
    wait_bytes(arrived, out_sem.at[0])
    wait_bytes(rx2, out_sem.at[1])
    wait_bytes(ry2, out_sem.at[2])
    wait_bytes(rz2, out_sem.at[3])
    wait_bytes(rfin, out_sem.at[4])


def finish(arrived, rx2, ry2, rz2, rel_sum, ent_out, neg_out, rel_out, row_ids):
    r = pl.program_id(0)

    @pl.when(r == 0)
    def _():
        lane = iota((8, DP), 1)
        unit = jnp.where(lane == D, 32.0, jnp.where(lane == D + 1, 1.0, 0.0)).astype(BF16)
        row_ids[...] = nt(unit, arrived[...])

        def sum16(ref):
            total = ref[0].astype(F32)
            for i in range(1, NS):
                total = total + ref[i].astype(F32)
            return total

        neg_out[:, 0:128] = sum16(rx2)
        neg_out[:, 128:256] = sum16(ry2)
        neg_out[:, 256:D] = sum16(rz2)[:, 0 : D - 256]

    hot = hot_where((iota((256, 2048), 0) + r * 256).astype(F32) == row_ids[0:1, :])
    ent_out[...] = nn(hot, arrived[...]).T[0:D]
    rows = rel_sum[...]
    wide = jnp.concatenate([rows, jnp.zeros((rows.shape[0], DP - D), F32)], axis=1)
    rel_out[...] = wide.T[0:D]


SCRATCH = [
    ((NZ * 8, D, 128), BF16),
    ((D, NEG_DEV), BF16),
    ((NEG_DEV, DP), BF16),
    ((NZ, 4, NEG_DEV, EC), BF16),
    ((4, DP, EC), BF16),
    ((4, 8, EC), F32),
    ((2, D, EC), F32),
    ((2, D, EC), F32),
    ((2, D, EC), F32),
    ((NZ, 4, 8, EC), F32),
    ((2, 4, 8, EC), F32),
    ((4, D, EC), F32),
    ((2, D, EC), F32),
    ((4, 8, EC), F32),
    ((4, DP, EC), BF16),
    ((DP, 2 * E_DEV), BF16),
    ((D, E_DEV), BF16),
    ((D, E_DEV), BF16),
    ((NB, 256, DP), BF16),
    ((2048, DP), BF16),
    ((NB, 256, 128), F32),
    ((NB, 256, 128), F32),
    ((NZ, D - 256, NEG_DEV), BF16),
    ((NZ, 4, 256, 128), BF16),
    ((NZ, 4, 4, NEG_OWN, 128), BF16),
    ((2, D - 256, 512), BF16),
    ((2, NZ, 128, 128), BF16),
    ((2, NZ, 2, NEG_OWN, 128), BF16),
    ((2, D - 256, NEG_DEV), BF16),
    ((2, NZ, 256, 128), BF16),
    ((2, NZ, 4, NEG_OWN, 128), BF16),
    ((NEG_DEV, 256), BF16),
    ((NZ, 256, 128), BF16),
    ((NZ, 4, NEG_OWN, 128), BF16),
    ((NS, NEG_OWN, 256), BF16),
    ((NS, NEG_OWN, 128), BF16),
    ((NS, NEG_OWN, 128), BF16),
    ((REL, D), F32),
    ((REL // 2, D), F32),
    ((REL // 2, D), BF16),
    ((NS, 16, D), BF16),
    ((NZ, 16, D), F32),
    ((REL, D), F32),
]


def per_device(
    head_rows, tail_rows, rel_ids, relations, edge_weights, neg_rows, send_slots, dest_rows
):
    vmem = pl.BlockSpec(memory_space=pltpu.VMEM)
    results = pl.pallas_call(
        kernel,
        out_shape=(
            jax.ShapeDtypeStruct((2048, DP), BF16),
            jax.ShapeDtypeStruct((NS, NEG_OWN, 128), BF16),
            jax.ShapeDtypeStruct((NS, NEG_OWN, 128), BF16),
            jax.ShapeDtypeStruct((NS, NEG_OWN, 256), BF16),
            jax.ShapeDtypeStruct((REL, D), F32),
        ),
        in_specs=[vmem] * 8,
        out_specs=(pl.BlockSpec(memory_space=pl.ANY),) * 5,
        scratch_shapes=[pltpu.VMEM(shape, dtype) for shape, dtype in SCRATCH]
        + [
            pltpu.SemaphoreType.DMA((19,)),
            pltpu.SemaphoreType.DMA((16,)),
            pltpu.SemaphoreType.DMA((NZ,)),
            pltpu.SemaphoreType.DMA((NZ, 3)),
            pltpu.SemaphoreType.DMA((NZ, 3)),
            pltpu.SemaphoreType.DMA((6, 4)),
            pltpu.SemaphoreType.DMA((5,)),
        ],
        compiler_params=pltpu.CompilerParams(
            collective_id=0, has_side_effects=True, vmem_limit_bytes=60 * 1024 * 1024
        ),
        cost_estimate=pl.CostEstimate(
            flops=2 * 3 * 1024 * 4096 * 400, bytes_accessed=8 * 1024 * 1024, transcendentals=1024 * 4096
        ),
        name="complex_backward",
    )(
        head_rows.T,
        tail_rows.T,
        rel_ids.reshape(1, E_DEV),
        relations.T,
        edge_weights.reshape(1, E_DEV),
        neg_rows.T,
        send_slots.T,
        dest_rows.T,
    )
    ent_t, neg_grad, rel_t = pl.pallas_call(
        finish,
        grid=(4,),
        out_shape=(
            jax.ShapeDtypeStruct((D, ENT_DEV), F32),
            jax.ShapeDtypeStruct((NEG_OWN, D), F32),
            jax.ShapeDtypeStruct((D, REL), F32),
        ),
        in_specs=[vmem] * 4 + [pl.BlockSpec((128, D), lambda r: (r, 0))],
        out_specs=(
            pl.BlockSpec((D, 256), lambda r: (0, r)),
            pl.BlockSpec((NEG_OWN, D), lambda r: (0, 0)),
            pl.BlockSpec((D, 128), lambda r: (0, r)),
        ),
        scratch_shapes=[pltpu.VMEM((8, 2048), F32)],
        compiler_params=pltpu.CompilerParams(vmem_limit_bytes=32 * 1024 * 1024),
        cost_estimate=pl.CostEstimate(
            flops=2 * 1024 * 2048 * 512, bytes_accessed=6 * 1024 * 1024, transcendentals=0
        ),
        name="make_outputs",
    )(*results)
    return ent_t.T, neg_grad, rel_t.T


def solution(mesh):
    return jax.shard_map(
        per_device,
        mesh=mesh,
        in_specs=(
            P(("bucket", "shard"), None),
            P(("bucket", "shard"), None),
            P(("bucket", "shard")),
            P(),
            P(("bucket", "shard")),
            P("bucket", None),
            P(("bucket", "shard"), None),
            P(("bucket", "shard"), None),
        ),
        out_specs=(P(("bucket", "shard"), None), P(("bucket", "shard"), None), P()),
        check_vma=False,
    )
```

```python
import functools

import jax
import jax.numpy as jnp
from jax import lax
from jax.experimental import pallas as pl
from jax.experimental.pallas import tpu as pltpu
from jax.sharding import PartitionSpec as P

D = 400
HALF = 200
DP = 512
E_DEV = 512
ENT_DEV = 1024
REL = 512
NEG_DEV = 1024
SLOT = 16
NB = 8
NS = 16
NZ = 4
EC = 256
NEG_OWN = 64

MESH = pl.DeviceIdType.MESH
F32 = jnp.float32
BF16 = jnp.bfloat16

(Q_S, SQ_S, ST_S, O_S, RC_S, R2_S, R3_S, R4_S, R5_S, ENT_S,
 Z1_S, X1_S, Y1_S, Z2_S, X2_S, Y2_S, GZ_S, GX_S, GY_S) = range(19)


def nt(a, b):
    return lax.dot_general(a, b, (((1,), (1,)), ((), ())), preferred_element_type=F32)


def nn(a, b):
    return jnp.dot(a, b, preferred_element_type=F32)


def iota(shape, dim):
    return lax.broadcasted_iota(jnp.int32, shape, dim)


def hot_where(mask):
    return mask.astype(F32).astype(BF16)


def wait_bytes(ref, sem):
    pltpu.make_async_copy(ref, ref, sem).wait()


def kernel(
    head, tail, ids, rel, wts, neg, slots, drows,
    ent_out, neg_out, rel_out,
    nbt, wide, nb, prob, qt, sq, hts, tts, rts, mb, st, ot, ot_in, lt, qs, ends, rt_hi, rt_lo,
    packed, arrived, slot_col, dest_col,
    gz, gx, gy, hz, hx, hy, rz1, rx1, ry1, az, ax, ay, rz2, rx2, ry2,
    rp, rp_in, r1b, r2in, r2all, rfin,
    send, recv, zrecv, xrecv, yrecv, hrecv,
):
    bucket, shard = lax.axis_index("bucket"), lax.axis_index("shard")
    z, c = bucket // 2, bucket % 2
    x, y = shard // 4, shard % 4
    oc = 1 - c
    me = bucket * NS + shard
    partner = (z * 2 + oc, shard)

    def rcopy(src, dst, s_sem, r_sem, device):
        pltpu.make_async_remote_copy(
            src_ref=src, dst_ref=dst, send_sem=s_sem, recv_sem=r_sem,
            device_id=device, device_id_type=MESH,
        ).start()

    barrier = pltpu.get_barrier_semaphore()

    def greet(i, carry):
        d = lax.rem(me + i, NB * NS)
        pl.semaphore_signal(barrier, inc=1, device_id=(d // NS, d % NS), device_id_type=MESH)
        return carry

    lax.fori_loop(1, NB * NS, greet, 0)

    for i in range(8):
        nbt[z * 8 + i] = neg[:, i * 128 : (i + 1) * 128]

    rel_1 = rel[...].astype(BF16)
    rest = rel[...] - rel_1.astype(F32)
    rel_2 = rest.astype(BF16)
    rel_3 = (rest - rel_2.astype(F32)).astype(BF16)
    for j in range(2):
        cols = slice(j * EC, (j + 1) * EC)
        h_t = head[:, cols].astype(F32)
        t_t = tail[:, cols].astype(F32)
        hot = hot_where(iota((REL, EC), 0) == ids[0:1, cols])
        r_t = (nn(rel_1, hot) + nn(rel_2, hot)) + nn(rel_3, hot)
        hre, him = h_t[:HALF], h_t[HALF:]
        rre, rim = r_t[:HALF], r_t[HALF:]
        q = jnp.concatenate([hre * rre - him * rim, hre * rim + him * rre], axis=0).astype(BF16)
        qt[2 * c + j, 0:D, :] = q
        qt[2 * c + j, D:DP, :] = jnp.zeros((DP - D, EC), BF16)
        sq[2 * c + j, 0:1, :] = jnp.sum(q.astype(F32) * t_t, axis=0, keepdims=True)
        sq[2 * c + j, 1:2, :] = wts[0:1, cols]
        sq[2 * c + j, 2:8, :] = jnp.zeros((6, EC), F32)
        hts[j] = h_t
        tts[j] = t_t
        rts[j] = r_t

    pl.semaphore_wait(barrier, NB * NS - 1)

    def ring(i, d):
        return lax.rem(i + d, 4)

    z_left, z_right, z_far = ring(z, 3), ring(z, 1), ring(z, 2)
    x_left, x_right, x_far = ring(x, 3), ring(x, 1), ring(x, 2)
    y_left, y_right, y_far = ring(y, 3), ring(y, 1), ring(y, 2)
    to_z_left, to_z_right = (z_left * 2 + c, shard), (z_right * 2 + c, shard)
    to_x_left, to_x_right = (bucket, x_left * 4 + y), (bucket, x_right * 4 + y)
    to_y_left, to_y_right = (bucket, x * 4 + y_left), (bucket, x * 4 + y_right)

    for part in (nbt.at[z * 8 + x], nbt.at[z * 8 + 4 + y]):
        rcopy(part, part, send.at[GZ_S], zrecv.at[1], to_z_right)
        rcopy(part, part, send.at[GZ_S], zrecv.at[3], to_z_left)
    mine = pl.ds(2 * c, 2)
    rcopy(qt.at[mine], qt.at[mine], send.at[Q_S], recv.at[Q_S], partner)
    rcopy(sq.at[mine], sq.at[mine], send.at[SQ_S], recv.at[SQ_S], partner)

    ones = jnp.ones((SLOT, 128), BF16)
    tables = []
    for ref in (slots, drows):
        value = ref[...].astype(F32)
        high = jnp.floor(value * (1.0 / 32.0))
        tables.append((high.astype(BF16), (value - 32.0 * high).astype(BF16)))

    def columns(b, carry):
        owner_hot = hot_where(iota((256, 128), 1) == iota((256, 128), 0) // SLOT + b * NS)
        keep = iota((256, SLOT), 1) == iota((256, SLOT), 0) % SLOT
        for (high, low), out in zip(tables, (slot_col, dest_col)):
            h = jnp.where(keep, nt(owner_hot, high), 0.0).astype(BF16)
            l = jnp.where(keep, nt(owner_hot, low), 0.0).astype(BF16)
            out[b] = 32.0 * nn(h, ones) + nn(l, ones)
        return carry

    lax.fori_loop(0, NB, columns, 0)
    nb[:, 384:DP] = jnp.zeros((NEG_DEV, 128), BF16)

    wait_bytes(qt.at[mine], recv.at[Q_S])
    wait_bytes(sq.at[mine], recv.at[SQ_S])

    LOW, HIGH = pl.ds(0, 208), pl.ds(208, 192)

    def ring_start_x(k, src):
        part = nbt.at[src * 8 + x]
        rcopy(part, part, send.at[GX_S], xrecv.at[k, 0], to_x_right)
        rcopy(part, part, send.at[GX_S], xrecv.at[k, 1], to_x_left)

    def ring_start_y(k, src):
        part = nbt.at[src * 8 + 4 + y]
        rcopy(part, part, send.at[GY_S], yrecv.at[k, 0], to_y_right)
        rcopy(part, part, send.at[GY_S], yrecv.at[k, 1], to_y_left)

    def ring_forward(k, src):
        for first, left, right, s_sem, r_sem, to_left, to_right in (
            (src * 8, x_left, x_right, send.at[GX_S], xrecv, to_x_left, to_x_right),
            (src * 8 + 4, y_left, y_right, send.at[GY_S], yrecv, to_y_left, to_y_right),
        ):
            wait_bytes(nbt.at[first + left], r_sem.at[k, 0])
            part = nbt.at[first + left, LOW]
            rcopy(part, part, s_sem, r_sem.at[k, 2], to_right)
            wait_bytes(nbt.at[first + right], r_sem.at[k, 1])
            part = nbt.at[first + right, HIGH]
            rcopy(part, part, s_sem, r_sem.at[k, 2], to_left)

    def ring_finish(k, src):
        wait_bytes(nbt.at[src * 8 + x_far], xrecv.at[k, 2])
        wait_bytes(nbt.at[src * 8 + 4 + y_far], yrecv.at[k, 2])

    def flip(zb):
        for i in range(8):
            part = nbt[zb * 8 + i]
            wide[:, i * 128 : (i + 1) * 128] = part
            nb[i * 128 : (i + 1) * 128, 0:D] = part.astype(F32).T.astype(BF16)

    def block(zb, first, pair):

        def chunk(g):
            s = nn(nb[...], qt[g])
            m = jnp.max(s, axis=0, keepdims=True)
            p = jnp.exp(s - m)
            l = jnp.sum(p, axis=0, keepdims=True)
            pb = p.astype(BF16)
            prob[zb, g] = pb
            o = nn(wide[...], pb)
            mb[zb, g, 0:1, :] = m
            if first:
                st[c, g, 0:1, :] = m
                st[c, g, 1:2, :] = l
                st[c, g, 2:8, :] = jnp.zeros((6, EC), F32)
                ot[g] = o
            else:
                m_old = st[c, g, 0:1, :]
                m_new = jnp.maximum(m_old, m)
                f_old = jnp.exp(m_old - m_new)
                f_new = jnp.exp(m - m_new)
                st[c, g, 0:1, :] = m_new
                st[c, g, 1:2, :] = st[c, g, 1:2, :] * f_old + l * f_new
                ot[g] = ot[g] * f_old + o * f_new

        chunk(2 * pair)
        chunk(2 * pair + 1)

    def whole(zb, first):
        flip(zb)

        def two(pair, carry):
            block(zb, first, pair)
            return carry

        lax.fori_loop(0, 2, two, 0)

    whole(z, True)
    wait_bytes(nbt.at[pl.ds(z_left * 8, 2)], zrecv.at[1])
    part = nbt.at[z_left * 8 + x]
    rcopy(part, part, send.at[GZ_S], zrecv.at[2], to_z_right)
    ring_start_x(1, z_left)
    ring_start_y(1, z_left)
    wait_bytes(nbt.at[pl.ds(z_right * 8, 2)], zrecv.at[3])
    part = nbt.at[z_right * 8 + 4 + y]
    rcopy(part, part, send.at[GZ_S], zrecv.at[0], to_z_left)
    ring_start_x(3, z_right)
    ring_start_y(3, z_right)
    ring_forward(1, z_left)
    wait_bytes(nbt.at[z_far * 8 + x], zrecv.at[2])
    ring_start_x(2, z_far)
    wait_bytes(nbt.at[z_far * 8 + 4 + y], zrecv.at[0])
    ring_start_y(2, z_far)
    ring_forward(3, z_right)
    ring_finish(1, z_left)
    flip(z_left)
    block(z_left, False, 0)
    ring_forward(2, z_far)
    block(z_left, False, 1)
    ring_finish(3, z_right)
    whole(z_right, False)
    ring_finish(2, z_far)
    whole(z_far, False)

    rcopy(st.at[c], st.at[c], send.at[ST_S], recv.at[ST_S], partner)
    rcopy(ot.at[pl.ds(2 * oc, 2)], ot_in, send.at[O_S], recv.at[O_S], partner)
    wait_bytes(st.at[c], recv.at[ST_S])
    for g in range(4):
        pos = sq[g, 0:1, :]
        m0, m1 = st[0, g, 0:1, :], st[1, g, 0:1, :]
        top = jnp.maximum(pos, jnp.maximum(m0, m1))
        total = (
            jnp.exp(pos - top)
            + st[0, g, 1:2, :] * jnp.exp(m0 - top)
            + st[1, g, 1:2, :] * jnp.exp(m1 - top)
        )
        lt[g, 0:1, :] = top + jnp.log(total)
    wait_bytes(ot_in, recv.at[O_S])

    ends[D:DP, :] = jnp.zeros((DP - D, 2 * E_DEV), BF16)
    for j in range(2):
        cols = slice(j * EC, (j + 1) * EC)
        tail_cols = slice(E_DEV + j * EC, E_DEV + (j + 1) * EC)
        g = 2 * c + j
        pos, w, ltot = sq[g, 0:1, :], sq[g, 1:2, :], lt[g, 0:1, :]
        pos_coef = w * (jnp.exp(pos - ltot) - 1.0)
        own = w * jnp.exp(st[c, g, 0:1, :] - ltot)
        other = w * jnp.exp(st[oc, g, 0:1, :] - ltot)
        grad = pos_coef * tts[j] + ot[g] * own + ot_in[j] * other
        gre, gim = grad[:HALF], grad[HALF:]
        rre, rim = rts[j, :HALF, :], rts[j, HALF:, :]
        hre, him = hts[j, :HALF, :], hts[j, HALF:, :]
        ends[0:D, cols] = jnp.concatenate(
            [gre * rre + gim * rim, gim * rre - gre * rim], axis=0
        ).astype(BF16)
        ends[0:D, tail_cols] = (pos_coef * qt[g, 0:D, :].astype(F32)).astype(BF16)
        term = jnp.concatenate([gre * hre + gim * him, gim * hre - gre * him], axis=0)
        hi = term.astype(BF16)
        rt_hi[:, cols] = hi
        rt_lo[:, cols] = (term - hi.astype(F32)).astype(BF16)

    my_slots = pl.ds(pl.multiple_of(me * SLOT, SLOT), SLOT)

    def pack(bb, first):
        sc = slot_col[bb]
        sel = jnp.concatenate(
            [hot_where(sc == (iota((256, 128), 1) + 128 * t).astype(F32)) for t in range(8)], axis=1
        )
        rows = nt(sel, ends[...])
        dc = dest_col[bb]
        high = jnp.floor(dc * (1.0 / 32.0))
        lane = iota((256, 128), 1)
        code = jnp.where(lane == 16, high, jnp.where(lane == 17, dc - 32.0 * high, 0.0))
        packed[bb, :, 0:384] = rows[:, 0:384].astype(BF16)
        packed[bb, :, 384:512] = (rows[:, 384:512] + code).astype(BF16)
        for j in range(NS):
            ss = lax.rem(shard + j, NS)
            src = packed.at[bb, pl.ds(pl.multiple_of(ss * SLOT, SLOT), SLOT)]
            if first and j == 0:
                pltpu.make_async_copy(src, arrived.at[my_slots], recv.at[ENT_S]).start()
            else:
                rcopy(src, arrived.at[my_slots], send.at[ENT_S], recv.at[ENT_S], (bb, ss))

    def rel_chunk(r, carry):
        hot = hot_where(iota((128, E_DEV), 0) + r * 128 == ids[...])
        rp[pl.ds(pl.multiple_of(r * 128, 128), 128), :] = nt(hot, rt_hi[...]) + nt(hot, rt_lo[...])
        return carry

    lax.fori_loop(0, 4, rel_chunk, 0)
    rcopy(
        rp.at[pl.ds(pl.multiple_of(oc * 256, 256), 256)], rp_in, send.at[RC_S], recv.at[RC_S], partner
    )

    def pack_other(k, carry):
        pack(lax.rem(bucket + k, NB), False)
        return carry


    def neg_block(zb):
        for g in range(4):
            scale = sq[g, 1:2, :] * jnp.exp(mb[zb, g, 0:1, :] - lt[g, 0:1, :])
            qs[g] = (qt[g].astype(F32) * scale).astype(BF16)

        def rows_of(xx, carry):
            rr = pl.ds(pl.multiple_of(xx * 256, 256), 256)
            acc = nt(prob[zb, 0, rr, :], qs[0])
            for g in range(1, 4):
                acc = acc + nt(prob[zb, g, rr, :], qs[g])
            gx[zb, xx] = acc[:, 0:128].astype(BF16)
            for yy in range(4):
                gy[zb, yy, xx] = acc[yy * 64 : (yy + 1) * 64, 128:256].astype(BF16)
            gz[zb, :, rr] = acc[:, 256:512].T[0 : D - 256].astype(BF16)
            return carry

        lax.fori_loop(0, 4, rows_of, 0)

    def far_xy(n, zb):
        low, high = pl.ds(0, 128), pl.ds(128, 128)
        rcopy(gx.at[zb, x_far, low], hx.at[0, zb], send.at[X1_S], hrecv.at[0, n], to_x_right)
        rcopy(gx.at[zb, x_far, high], hx.at[1, zb], send.at[X1_S], hrecv.at[1, n], to_x_left)
        low, high = pl.ds(0, 2), pl.ds(2, 2)
        rcopy(gy.at[zb, y_far, low], hy.at[0, zb], send.at[Y1_S], hrecv.at[2, n], to_y_right)
        rcopy(gy.at[zb, y_far, high], hy.at[1, zb], send.at[Y1_S], hrecv.at[3, n], to_y_left)

    def plus(a, b):
        return (a.astype(F32) + b.astype(F32)).astype(BF16)

    def near_xy(n, zb):
        wait_bytes(hx.at[0, zb], hrecv.at[0, n])
        gx[zb, x_right, 0:128, :] = plus(gx[zb, x_right, 0:128, :], hx[0, zb])
        rcopy(gx.at[zb, x_right], rx1.at[0, zb], send.at[X1_S], recv.at[X1_S], to_x_right)
        wait_bytes(hx.at[1, zb], hrecv.at[1, n])
        gx[zb, x_left, 128:256, :] = plus(gx[zb, x_left, 128:256, :], hx[1, zb])
        rcopy(gx.at[zb, x_left], rx1.at[1, zb], send.at[X1_S], recv.at[X1_S], to_x_left)
        wait_bytes(hy.at[0, zb], hrecv.at[2, n])
        gy[zb, y_right, 0:2] = plus(gy[zb, y_right, 0:2], hy[0, zb])
        rcopy(gy.at[zb, y_right], ry1.at[0, zb], send.at[Y1_S], recv.at[Y1_S], to_y_right)
        wait_bytes(hy.at[1, zb], hrecv.at[3, n])
        gy[zb, y_left, 2:4] = plus(gy[zb, y_left, 2:4], hy[1, zb])
        rcopy(gy.at[zb, y_left], ry1.at[1, zb], send.at[Y1_S], recv.at[Y1_S], to_y_left)

    neg_block(z_far)
    rcopy(gz.at[z_far, :, pl.ds(0, 512)], hz.at[0], send.at[Z1_S], hrecv.at[4, 0], to_z_right)
    rcopy(gz.at[z_far, :, pl.ds(512, 512)], hz.at[1], send.at[Z1_S], hrecv.at[5, 0], to_z_left)
    far_xy(0, z_far)

    wait_bytes(rp_in, recv.at[RC_S])
    r1b[...] = (rp[pl.ds(pl.multiple_of(c * 256, 256), 256), :] + rp_in[...]).astype(BF16)
    for j in range(1, NS):
        ss = lax.rem(shard + j, NS)
        rows = r1b.at[pl.ds(pl.multiple_of(ss * 16, 16), 16)]
        rcopy(rows, r2in.at[shard], send.at[R2_S], recv.at[R2_S], (bucket, ss))
    r2in[shard] = r1b[pl.ds(pl.multiple_of(shard * 16, 16), 16), :]

    neg_block(z_right)
    wait_bytes(hz.at[0], hrecv.at[4, 0])
    gz[z_right, :, 0:512] = plus(gz[z_right, :, 0:512], hz[0])
    rcopy(gz.at[z_right], rz1.at[0], send.at[Z1_S], recv.at[Z1_S], to_z_right)
    far_xy(1, z_right)
    near_xy(0, z_far)

    wait_bytes(r2in.at[pl.ds(0, NS - 1)], recv.at[R2_S])
    r2 = r2in[0].astype(F32)
    for i in range(1, NS):
        r2 = r2 + r2in[i].astype(F32)
    r2all[z] = r2
    for k in (1, 3, 2):
        zz = lax.rem(z + k, NZ)
        rcopy(r2all.at[z], r2all.at[z], send.at[R3_S], recv.at[R3_S], (zz * 2 + c, shard))

    neg_block(z_left)
    wait_bytes(hz.at[1], hrecv.at[5, 0])
    gz[z_left, :, 512:1024] = plus(gz[z_left, :, 512:1024], hz[1])
    rcopy(gz.at[z_left], rz1.at[1], send.at[Z1_S], recv.at[Z1_S], to_z_left)
    far_xy(2, z_left)
    near_xy(1, z_right)

    neg_block(z)
    far_xy(3, z)
    near_xy(2, z_left)

    wait_bytes(r2all.at[pl.ds(0, 3)], recv.at[R3_S])
    rel_row = pl.ds(pl.multiple_of(c * 256 + shard * 16, 16), 16)
    rfin[rel_row, :] = ((r2all[0] + r2all[1]) + r2all[2]) + r2all[3]
    for j in range(1, NS):
        ss = lax.rem(shard + j, NS)
        rcopy(rfin.at[rel_row], rfin.at[rel_row], send.at[R4_S], recv.at[R4_S], (bucket, ss))

    near_xy(3, z)

    pack(bucket, True)
    lax.fori_loop(1, NB, pack_other, 0)

    wait_bytes(rx1, recv.at[X1_S])

    def sum_x(zb, carry):
        total = gx[zb, x].astype(F32) + rx1[0, zb].astype(F32) + rx1[1, zb].astype(F32)
        ax[zb] = total.astype(BF16)
        return carry

    lax.fori_loop(0, NZ, sum_x, 0)
    for j in range(1, NS):
        other_zy = lax.rem(z * 4 + y + j, NS)
        zz, yy = other_zy // 4, other_zy % 4
        rows = ax.at[zz, pl.ds(pl.multiple_of(yy * NEG_OWN, NEG_OWN), NEG_OWN)]
        rcopy(rows, rx2.at[z * 4 + y], send.at[X2_S], recv.at[X2_S], (zz * 2 + c, x * 4 + yy))
    rx2[z * 4 + y] = ax[z, pl.ds(pl.multiple_of(y * NEG_OWN, NEG_OWN), NEG_OWN), :]

    wait_bytes(ry1, recv.at[Y1_S])

    def sum_y(zb, carry):
        total = gy[zb, y].astype(F32) + ry1[0, zb].astype(F32) + ry1[1, zb].astype(F32)
        ay[zb] = total.astype(BF16)
        return carry

    lax.fori_loop(0, NZ, sum_y, 0)
    for j in range(1, NS):
        other_zx = lax.rem(z * 4 + x + j, NS)
        zz, xx = other_zx // 4, other_zx % 4
        rcopy(ay.at[zz, xx], ry2.at[z * 4 + x], send.at[Y2_S], recv.at[Y2_S], (zz * 2 + c, xx * 4 + y))
    ry2[z * 4 + x] = ay[z, x]

    wait_bytes(rz1, recv.at[Z1_S])

    def sum_z(r, carry):
        rr = pl.ds(pl.multiple_of(r * 256, 256), 256)
        total = gz[z, :, rr].astype(F32) + rz1[0, :, rr].astype(F32) + rz1[1, :, rr].astype(F32)
        wide = jnp.concatenate([total, jnp.zeros((256 - (D - 256), 256), F32)], axis=0)
        az[rr, :] = wide.T.astype(BF16)
        return carry

    lax.fori_loop(0, 4, sum_z, 0)
    for j in range(1, NS):
        ss = lax.rem(shard + j, NS)
        rows = az.at[pl.ds(pl.multiple_of(ss * NEG_OWN, NEG_OWN), NEG_OWN)]
        rcopy(rows, rz2.at[shard], send.at[Z2_S], recv.at[Z2_S], (bucket, ss))
    rz2[shard] = az[pl.ds(pl.multiple_of(shard * NEG_OWN, NEG_OWN), NEG_OWN), :]

    wait_bytes(arrived, recv.at[ENT_S])
    lane = iota((8, DP), 1)
    unit = jnp.where(lane == D, 32.0, jnp.where(lane == D + 1, 1.0, 0.0)).astype(BF16)
    row_ids = nt(unit, arrived[...])[0:1, :]

    def scatter(r, carry):
        hot = hot_where((iota((256, 2048), 0) + r * 256).astype(F32) == row_ids)
        got = nn(hot, arrived[...])
        ent_out[:, pl.ds(pl.multiple_of(r * 256, 256), 256)] = got.T[0:D]
        return carry

    lax.fori_loop(0, 4, scatter, 0)

    wait_bytes(rfin.at[pl.ds(0, 240)], recv.at[R4_S])
    half_rel = rfin.at[pl.ds(pl.multiple_of(c * 256, 256), 256)]
    rcopy(half_rel, half_rel, send.at[R5_S], recv.at[R5_S], partner)

    def sum16(ref):
        total = ref[0].astype(F32)
        for i in range(1, NS):
            total = total + ref[i].astype(F32)
        return total

    wait_bytes(rx2.at[pl.ds(0, NS - 1)], recv.at[X2_S])
    neg_out[:, 0:128] = sum16(rx2)
    wait_bytes(ry2.at[pl.ds(0, NS - 1)], recv.at[Y2_S])
    neg_out[:, 128:256] = sum16(ry2)
    wait_bytes(rz2.at[pl.ds(0, NS - 1)], recv.at[Z2_S])
    neg_out[:, 256:D] = sum16(rz2)[:, 0 : D - 256]

    wait_bytes(half_rel, recv.at[R5_S])
    for r in range(4):
        rr = slice(r * 128, (r + 1) * 128)
        wide = jnp.concatenate([rfin[rr, :], jnp.zeros((128, DP - D), F32)], axis=1)
        rel_out[:, rr] = wide.T[0:D]

    wait_bytes(nbt.at[pl.ds(0, 6)], send.at[GZ_S])
    wait_bytes(nbt.at[pl.ds(0, 9)], send.at[GX_S])
    wait_bytes(nbt.at[pl.ds(0, 9)], send.at[GY_S])
    wait_bytes(qt.at[mine], send.at[Q_S])
    wait_bytes(sq.at[mine], send.at[SQ_S])
    wait_bytes(st.at[c], send.at[ST_S])
    wait_bytes(ot_in, send.at[O_S])
    wait_bytes(arrived.at[pl.ds(0, 2048 - SLOT)], send.at[ENT_S])
    wait_bytes(rp_in, send.at[RC_S])
    wait_bytes(r2in.at[pl.ds(0, NS - 1)], send.at[R2_S])
    wait_bytes(r2all.at[pl.ds(0, 3)], send.at[R3_S])
    wait_bytes(rfin.at[pl.ds(0, 240)], send.at[R4_S])
    wait_bytes(half_rel, send.at[R5_S])
    wait_bytes(gz.at[pl.ds(0, 3)], send.at[Z1_S])
    wait_bytes(gx.at[pl.ds(0, 3)], send.at[X1_S])
    wait_bytes(gy.at[pl.ds(0, 3)], send.at[Y1_S])
    wait_bytes(rx2.at[pl.ds(0, NS - 1)], send.at[X2_S])
    wait_bytes(ry2.at[pl.ds(0, NS - 1)], send.at[Y2_S])
    wait_bytes(rz2.at[pl.ds(0, NS - 1)], send.at[Z2_S])


SCRATCH = [
    ((NZ * 8, D, 128), BF16),
    ((D, NEG_DEV), BF16),
    ((NEG_DEV, DP), BF16),
    ((NZ, 4, NEG_DEV, EC), BF16),
    ((4, DP, EC), BF16),
    ((4, 8, EC), F32),
    ((2, D, EC), F32),
    ((2, D, EC), F32),
    ((2, D, EC), F32),
    ((NZ, 4, 8, EC), F32),
    ((2, 4, 8, EC), F32),
    ((4, D, EC), F32),
    ((2, D, EC), F32),
    ((4, 8, EC), F32),
    ((4, DP, EC), BF16),
    ((DP, 2 * E_DEV), BF16),
    ((D, E_DEV), BF16),
    ((D, E_DEV), BF16),
    ((NB, 256, DP), BF16),
    ((2048, DP), BF16),
    ((NB, 256, 128), F32),
    ((NB, 256, 128), F32),
    ((NZ, D - 256, NEG_DEV), BF16),
    ((NZ, 4, 256, 128), BF16),
    ((NZ, 4, 4, NEG_OWN, 128), BF16),
    ((2, D - 256, 512), BF16),
    ((2, NZ, 128, 128), BF16),
    ((2, NZ, 2, NEG_OWN, 128), BF16),
    ((2, D - 256, NEG_DEV), BF16),
    ((2, NZ, 256, 128), BF16),
    ((2, NZ, 4, NEG_OWN, 128), BF16),
    ((NEG_DEV, 256), BF16),
    ((NZ, 256, 128), BF16),
    ((NZ, 4, NEG_OWN, 128), BF16),
    ((NS, NEG_OWN, 256), BF16),
    ((NS, NEG_OWN, 128), BF16),
    ((NS, NEG_OWN, 128), BF16),
    ((REL, D), F32),
    ((REL // 2, D), F32),
    ((REL // 2, D), BF16),
    ((NS, 16, D), BF16),
    ((NZ, 16, D), F32),
    ((REL, D), F32),
]


def per_device(
    head_rows, tail_rows, rel_ids, relations, edge_weights, neg_rows, send_slots, dest_rows
):
    vmem = pl.BlockSpec(memory_space=pltpu.VMEM)
    ent_t, neg_grad, rel_t = pl.pallas_call(
        kernel,
        out_shape=(
            jax.ShapeDtypeStruct((D, ENT_DEV), F32),
            jax.ShapeDtypeStruct((NEG_OWN, D), F32),
            jax.ShapeDtypeStruct((D, REL), F32),
        ),
        in_specs=[vmem] * 8,
        out_specs=(vmem,) * 3,
        scratch_shapes=[pltpu.VMEM(shape, dtype) for shape, dtype in SCRATCH]
        + [
            pltpu.SemaphoreType.DMA((19,)),
            pltpu.SemaphoreType.DMA((16,)),
            pltpu.SemaphoreType.DMA((NZ,)),
            pltpu.SemaphoreType.DMA((NZ, 3)),
            pltpu.SemaphoreType.DMA((NZ, 3)),
            pltpu.SemaphoreType.DMA((6, 4)),
        ],
        compiler_params=pltpu.CompilerParams(
            collective_id=0, has_side_effects=True, vmem_limit_bytes=60 * 1024 * 1024
        ),
        cost_estimate=pl.CostEstimate(
            flops=2 * 3 * 1024 * 4096 * 400, bytes_accessed=8 * 1024 * 1024, transcendentals=1024 * 4096
        ),
        name="complex_backward",
    )(
        head_rows.T,
        tail_rows.T,
        rel_ids.reshape(1, E_DEV),
        relations.T,
        edge_weights.reshape(1, E_DEV),
        neg_rows.T,
        send_slots.T,
        dest_rows.T,
    )
    return ent_t.T, neg_grad, rel_t.T


def solution(mesh):
    return jax.shard_map(
        per_device,
        mesh=mesh,
        in_specs=(
            P(("bucket", "shard"), None),
            P(("bucket", "shard"), None),
            P(("bucket", "shard")),
            P(),
            P(("bucket", "shard")),
            P("bucket", None),
            P(("bucket", "shard"), None),
            P(("bucket", "shard"), None),
        ),
        out_specs=(P(("bucket", "shard"), None), P(("bucket", "shard"), None), P()),
        check_vma=False,
    )
```

```python
import functools

import jax
import jax.numpy as jnp
from jax import lax
from jax.experimental import pallas as pl
from jax.experimental.pallas import tpu as pltpu
from jax.sharding import PartitionSpec as P

D = 400
HALF = 200
DP = 512
E_DEV = 512
ENT_DEV = 1024
REL = 512
NEG_DEV = 1024
SLOT = 16
NB = 8
NS = 16
NZ = 4
EC = 256
NEG_OWN = 64

MESH = pl.DeviceIdType.MESH
F32 = jnp.float32
BF16 = jnp.bfloat16

(Q1_S, SQ1_S, Q2_S, SQ2_S, Q3_S, SQ3_S, ST1_S, O1_S, SC1_S, O2_S, ST2_S, O3_S, SC2_S,
 RC_S, R2_S, R3_S, R4_S, R5_S, ENT_S, Z1_S, X1_S, Y1_S, Z2_S, X2_S, Y2_S, GZ_S, GX_S, GY_S) = range(28)


def nt(a, b):
    return lax.dot_general(a, b, (((1,), (1,)), ((), ())), preferred_element_type=F32)


def nn(a, b):
    return jnp.dot(a, b, preferred_element_type=F32)


def iota(shape, dim):
    return lax.broadcasted_iota(jnp.int32, shape, dim)


def hot_where(mask):
    return mask.astype(F32).astype(BF16)


def wait_bytes(ref, sem):
    pltpu.make_async_copy(ref, ref, sem).wait()


def kernel(
    head, tail, ids, rel, wts, neg, slots, drows,
    ent_out, neg_out, rel_out,
    nbt, wide, nb, prob, qt, sq, hts, tts, rts, mb, st, st_in, sc, sc_in,
    ot, ot_pair, ot_own, o_sum, o_far, lt, qs, ends, rt_hi, rt_lo,
    packed, arrived, slot_col, dest_col,
    gz, gx, gy, rz1, rx1, ry1, az, ax, ay, rz2, rx2, ry2,
    rp, rp_in, r1b, r2in, r2all, rfin,
    send, recv,
):
    bucket, shard = lax.axis_index("bucket"), lax.axis_index("shard")
    z, c = bucket // 2, bucket % 2
    x, y = shard // 4, shard % 4
    oc = 1 - c
    me = bucket * NS + shard
    partner = (z * 2 + oc, shard)
    pair = ((z + 1 - 2 * (z % 2)) * 2 + c, shard)
    z_far = 3 - z
    far = (z_far * 2 + c, shard)

    def rcopy(src, dst, s_sem, r_sem, device):
        pltpu.make_async_remote_copy(
            src_ref=src, dst_ref=dst, send_sem=s_sem, recv_sem=r_sem,
            device_id=device, device_id_type=MESH,
        ).start()

    barrier = pltpu.get_barrier_semaphore()

    def greet(i, carry):
        d = lax.rem(me + i, NB * NS)
        pl.semaphore_signal(barrier, inc=1, device_id=(d // NS, d % NS), device_id_type=MESH)
        return carry

    lax.fori_loop(1, NB * NS, greet, 0)

    for i in range(8):
        nbt[i] = neg[:, i * 128 : (i + 1) * 128]

    rel_1 = rel[...].astype(BF16)
    rest = rel[...] - rel_1.astype(F32)
    rel_2 = rest.astype(BF16)
    rel_3 = (rest - rel_2.astype(F32)).astype(BF16)
    for j in range(2):
        cols = slice(j * EC, (j + 1) * EC)
        h_t = head[:, cols].astype(F32)
        t_t = tail[:, cols].astype(F32)
        hot = hot_where(iota((REL, EC), 0) == ids[0:1, cols])
        r_t = (nn(rel_1, hot) + nn(rel_2, hot)) + nn(rel_3, hot)
        hre, him = h_t[:HALF], h_t[HALF:]
        rre, rim = r_t[:HALF], r_t[HALF:]
        q = jnp.concatenate([hre * rre - him * rim, hre * rim + him * rre], axis=0).astype(BF16)
        qt[2 * c + j, 0:D, :] = q
        qt[2 * c + j, D:DP, :] = jnp.zeros((DP - D, EC), BF16)
        sq[2 * c + j, 0:1, :] = jnp.sum(q.astype(F32) * t_t, axis=0, keepdims=True)
        sq[2 * c + j, 1:2, :] = wts[0:1, cols]
        sq[2 * c + j, 2:8, :] = jnp.zeros((6, EC), F32)
        hts[j] = h_t
        tts[j] = t_t
        rts[j] = r_t

    pl.semaphore_wait(barrier, NB * NS - 1)

    for i in (x, 4 + y):
        rcopy(nbt.at[i], nbt.at[8 + i], send.at[GZ_S], recv.at[GZ_S], far)
    mine, theirs = pl.ds(2 * c, 2), pl.ds(4 + 2 * c, 2)
    rcopy(qt.at[mine], qt.at[mine], send.at[Q1_S], recv.at[Q1_S], partner)
    rcopy(sq.at[mine], sq.at[mine], send.at[SQ1_S], recv.at[SQ1_S], partner)
    rcopy(qt.at[mine], qt.at[theirs], send.at[Q2_S], recv.at[Q2_S], pair)
    rcopy(sq.at[mine], sq.at[theirs], send.at[SQ2_S], recv.at[SQ2_S], pair)

    ones = jnp.ones((SLOT, 128), BF16)
    tables = []
    for ref in (slots, drows):
        value = ref[...].astype(F32)
        high = jnp.floor(value * (1.0 / 32.0))
        tables.append((high.astype(BF16), (value - 32.0 * high).astype(BF16)))

    def columns(b, carry):
        owner_hot = hot_where(iota((256, 128), 1) == iota((256, 128), 0) // SLOT + b * NS)
        keep = iota((256, SLOT), 1) == iota((256, SLOT), 0) % SLOT
        for (high, low), out in zip(tables, (slot_col, dest_col)):
            h = jnp.where(keep, nt(owner_hot, high), 0.0).astype(BF16)
            l = jnp.where(keep, nt(owner_hot, low), 0.0).astype(BF16)
            out[b] = 32.0 * nn(h, ones) + nn(l, ones)
        return carry

    lax.fori_loop(0, NB, columns, 0)
    nb[:, 384:DP] = jnp.zeros((NEG_DEV, 128), BF16)

    def flip(b):
        for i in range(8):
            part = nbt[b * 8 + i]
            wide[:, i * 128 : (i + 1) * 128] = part
            nb[i * 128 : (i + 1) * 128, 0:D] = part.astype(F32).T.astype(BF16)

    def block(b, two):

        def chunk(g):
            s = nn(nb[...], qt[g])
            m = jnp.max(s, axis=0, keepdims=True)
            p = jnp.exp(s - m)
            l = jnp.sum(p, axis=0, keepdims=True)
            pb = p.astype(BF16)
            prob[b, g] = pb
            o = nn(wide[...], pb)
            mb[b, g, 0:1, :] = m
            if b == 0:
                st[g, 0:1, :] = m
                st[g, 1:2, :] = l
                st[g, 2:8, :] = jnp.zeros((6, EC), F32)
                ot[g] = o
            else:
                m_old = st[g, 0:1, :]
                m_new = jnp.maximum(m_old, m)
                f_old = jnp.exp(m_old - m_new)
                f_new = jnp.exp(m - m_new)
                st[g, 0:1, :] = m_new
                st[g, 1:2, :] = st[g, 1:2, :] * f_old + l * f_new
                ot[g] = ot[g] * f_old + o * f_new

        chunk(2 * two)
        chunk(2 * two + 1)

    flip(0)
    block(0, c)
    wait_bytes(nbt.at[pl.ds(8, 2)], recv.at[GZ_S])
    for i in (1, 3, 2):
        xx, yy = lax.rem(x + i, 4), lax.rem(y + i, 4)
        rcopy(nbt.at[8 + x], nbt.at[8 + x], send.at[GX_S], recv.at[GX_S], (bucket, xx * 4 + y))
        rcopy(nbt.at[12 + y], nbt.at[12 + y], send.at[GY_S], recv.at[GY_S], (bucket, x * 4 + yy))
    wait_bytes(qt.at[mine], recv.at[Q1_S])
    wait_bytes(sq.at[mine], recv.at[SQ1_S])
    block(0, oc)
    wait_bytes(qt.at[mine], recv.at[Q2_S])
    wait_bytes(sq.at[mine], recv.at[SQ2_S])
    rcopy(qt.at[theirs], qt.at[theirs], send.at[Q3_S], recv.at[Q3_S], partner)
    rcopy(sq.at[theirs], sq.at[theirs], send.at[SQ3_S], recv.at[SQ3_S], partner)
    block(0, 2 + c)
    wait_bytes(qt.at[mine], recv.at[Q3_S])
    wait_bytes(sq.at[mine], recv.at[SQ3_S])
    block(0, 2 + oc)
    wait_bytes(nbt.at[pl.ds(8, 3)], recv.at[GX_S])
    wait_bytes(nbt.at[pl.ds(8, 3)], recv.at[GY_S])
    flip(1)
    block(1, 2 + oc)
    rcopy(
        ot.at[pl.ds(4 + 2 * oc, 2)], ot_pair, send.at[O1_S], recv.at[O1_S], partner
    )
    block(1, 2 + c)
    own_half, pair_half = pl.ds(0, 4), pl.ds(4, 4)
    rcopy(st.at[pair_half], st_in.at[pair_half], send.at[ST1_S], recv.at[ST1_S], partner)

    def merge(g):
        m_a, m_b = st[g, 0:1, :], st_in[g, 0:1, :]
        m = jnp.maximum(m_a, m_b)
        f_a, f_b = jnp.exp(m_a - m), jnp.exp(m_b - m)
        sc[g, 0:1, :] = m
        sc[g, 1:2, :] = st[g, 1:2, :] * f_a + st_in[g, 1:2, :] * f_b
        sc[g, 2:8, :] = jnp.zeros((6, EC), F32)
        return f_a, f_b

    block(1, oc)
    rcopy(ot.at[pl.ds(2 * oc, 2)], ot_own, send.at[O3_S], recv.at[O3_S], partner)
    wait_bytes(st_in.at[pair_half], recv.at[ST1_S])
    wait_bytes(ot_pair, recv.at[O1_S])
    for g in range(4, 8):
        merge(g)
    for j in range(2):
        f_a, f_b = merge(4 + 2 * c + j)
        o_sum[j] = (ot[4 + 2 * c + j] * f_a + ot_pair[j] * f_b).astype(BF16)
    rcopy(o_sum, o_far, send.at[O2_S], recv.at[O2_S], pair)
    rcopy(sc.at[pair_half], sc_in.at[own_half], send.at[SC1_S], recv.at[SC1_S], pair)
    block(1, c)
    rcopy(st.at[own_half], st_in.at[own_half], send.at[ST2_S], recv.at[ST2_S], partner)
    wait_bytes(st_in.at[own_half], recv.at[ST2_S])
    for g in range(4):
        merge(g)
    rcopy(sc.at[own_half], sc_in.at[pair_half], send.at[SC2_S], recv.at[SC2_S], pair)
    wait_bytes(sc_in.at[own_half], recv.at[SC1_S])
    wait_bytes(sc_in.at[pair_half], recv.at[SC2_S])
    for g in range(8):
        pos = sq[g, 0:1, :]
        m0, m1 = sc[g, 0:1, :], sc_in[g, 0:1, :]
        top = jnp.maximum(pos, jnp.maximum(m0, m1))
        total = (
            jnp.exp(pos - top)
            + sc[g, 1:2, :] * jnp.exp(m0 - top)
            + sc_in[g, 1:2, :] * jnp.exp(m1 - top)
        )
        lt[g, 0:1, :] = top + jnp.log(total)

    def neg_block(b):
        for g in range(8):
            scale = sq[g, 1:2, :] * jnp.exp(mb[b, g, 0:1, :] - lt[g, 0:1, :])
            qs[g] = (qt[g].astype(F32) * scale).astype(BF16)

        def rows_of(xx, carry):
            rr = pl.ds(pl.multiple_of(xx * 256, 256), 256)
            acc = nt(prob[b, 0, rr, :], qs[0])
            for g in range(1, 8):
                acc = acc + nt(prob[b, g, rr, :], qs[g])
            gx[b, xx] = acc[:, 0:128].astype(BF16)
            for yy in range(4):
                gy[b, yy, xx] = acc[yy * 64 : (yy + 1) * 64, 128:256].astype(BF16)
            gz[b, :, rr] = acc[:, 256:512].T[0 : D - 256].astype(BF16)
            return carry

        lax.fori_loop(0, 4, rows_of, 0)
        for i in (1, 3, 2):
            xx, yy = lax.rem(x + i, 4), lax.rem(y + i, 4)
            rcopy(gx.at[b, xx], rx1.at[x, b], send.at[X1_S], recv.at[X1_S], (bucket, xx * 4 + y))
            rcopy(gy.at[b, yy], ry1.at[y, b], send.at[Y1_S], recv.at[Y1_S], (bucket, x * 4 + yy))

    neg_block(1)
    rcopy(gz.at[1], rz1, send.at[Z1_S], recv.at[Z1_S], far)
    neg_block(0)
    wait_bytes(ot_own, recv.at[O3_S])
    wait_bytes(o_far, recv.at[O2_S])
    ends[D:DP, :] = jnp.zeros((DP - D, 2 * E_DEV), BF16)
    for j in range(2):
        cols = slice(j * EC, (j + 1) * EC)
        tail_cols = slice(E_DEV + j * EC, E_DEV + (j + 1) * EC)
        g = 2 * c + j
        pos, w, ltot = sq[g, 0:1, :], sq[g, 1:2, :], lt[g, 0:1, :]
        pos_coef = w * (jnp.exp(pos - ltot) - 1.0)
        own = w * jnp.exp(st[g, 0:1, :] - ltot)
        other = w * jnp.exp(st_in[g, 0:1, :] - ltot)
        away = w * jnp.exp(sc_in[g, 0:1, :] - ltot)
        grad = pos_coef * tts[j] + ot[g] * own + ot_own[j] * other + o_far[j].astype(F32) * away
        gre, gim = grad[:HALF], grad[HALF:]
        rre, rim = rts[j, :HALF, :], rts[j, HALF:, :]
        hre, him = hts[j, :HALF, :], hts[j, HALF:, :]
        ends[0:D, cols] = jnp.concatenate(
            [gre * rre + gim * rim, gim * rre - gre * rim], axis=0
        ).astype(BF16)
        ends[0:D, tail_cols] = (pos_coef * qt[g, 0:D, :].astype(F32)).astype(BF16)
        term = jnp.concatenate([gre * hre + gim * him, gim * hre - gre * him], axis=0)
        hi = term.astype(BF16)
        rt_hi[:, cols] = hi
        rt_lo[:, cols] = (term - hi.astype(F32)).astype(BF16)

    my_slots = pl.ds(pl.multiple_of(me * SLOT, SLOT), SLOT)

    def pack(bb, first):
        sc = slot_col[bb]
        sel = jnp.concatenate(
            [hot_where(sc == (iota((256, 128), 1) + 128 * t).astype(F32)) for t in range(8)], axis=1
        )
        rows = nt(sel, ends[...])
        dc = dest_col[bb]
        high = jnp.floor(dc * (1.0 / 32.0))
        lane = iota((256, 128), 1)
        code = jnp.where(lane == 16, high, jnp.where(lane == 17, dc - 32.0 * high, 0.0))
        packed[bb, :, 0:384] = rows[:, 0:384].astype(BF16)
        packed[bb, :, 384:512] = (rows[:, 384:512] + code).astype(BF16)
        for j in range(NS):
            ss = lax.rem(shard + j, NS)
            src = packed.at[bb, pl.ds(pl.multiple_of(ss * SLOT, SLOT), SLOT)]
            if first and j == 0:
                pltpu.make_async_copy(src, arrived.at[my_slots], recv.at[ENT_S]).start()
            else:
                rcopy(src, arrived.at[my_slots], send.at[ENT_S], recv.at[ENT_S], (bb, ss))

    def rel_chunk(r, carry):
        hot = hot_where(iota((128, E_DEV), 0) + r * 128 == ids[...])
        rp[pl.ds(pl.multiple_of(r * 128, 128), 128), :] = nt(hot, rt_hi[...]) + nt(hot, rt_lo[...])
        return carry

    lax.fori_loop(0, 4, rel_chunk, 0)
    rcopy(
        rp.at[pl.ds(pl.multiple_of(oc * 256, 256), 256)], rp_in, send.at[RC_S], recv.at[RC_S], partner
    )

    def pack_other(k, carry):
        pack(lax.rem(bucket + k, NB), False)
        return carry

    pack(bucket, True)
    lax.fori_loop(1, 3, pack_other, 0)

    wait_bytes(rp_in, recv.at[RC_S])
    r1b[...] = (rp[pl.ds(pl.multiple_of(c * 256, 256), 256), :] + rp_in[...]).astype(BF16)
    for j in range(1, NS):
        ss = lax.rem(shard + j, NS)
        rows = r1b.at[pl.ds(pl.multiple_of(ss * 16, 16), 16)]
        rcopy(rows, r2in.at[shard], send.at[R2_S], recv.at[R2_S], (bucket, ss))
    r2in[shard] = r1b[pl.ds(pl.multiple_of(shard * 16, 16), 16), :]
    lax.fori_loop(3, NB, pack_other, 0)

    my_rows = pl.ds(pl.multiple_of(shard * NEG_OWN, NEG_OWN), NEG_OWN)
    wait_bytes(rx1.at[pl.ds(0, 3)], recv.at[X1_S])
    for b in range(2):
        total = gx[b, x].astype(F32)
        for i in range(1, 4):
            total = total + rx1[lax.rem(x + i, 4), b].astype(F32)
        ax[b] = total.astype(BF16)
    for i in range(4):
        yy = lax.rem(y + i, 4)
        rows = pl.ds(pl.multiple_of(yy * NEG_OWN, NEG_OWN), NEG_OWN)
        if i:
            rcopy(ax.at[0, rows], rx2.at[y], send.at[X2_S], recv.at[X2_S], (bucket, x * 4 + yy))
        else:
            rx2[y] = ax[0, rows, :]
        rcopy(
            ax.at[1, rows], rx2.at[4 + y], send.at[X2_S], recv.at[X2_S], (z_far * 2 + c, x * 4 + yy)
        )
    wait_bytes(ry1.at[pl.ds(0, 3)], recv.at[Y1_S])
    for b in range(2):
        total = gy[b, y].astype(F32)
        for i in range(1, 4):
            total = total + ry1[lax.rem(y + i, 4), b].astype(F32)
        ay[b] = total.astype(BF16)
    for i in range(4):
        xx = lax.rem(x + i, 4)
        if i:
            rcopy(ay.at[0, xx], ry2.at[x], send.at[Y2_S], recv.at[Y2_S], (bucket, xx * 4 + y))
        else:
            ry2[x] = ay[0, x]
        rcopy(
            ay.at[1, xx], ry2.at[4 + x], send.at[Y2_S], recv.at[Y2_S], (z_far * 2 + c, xx * 4 + y)
        )
    wait_bytes(rz1, recv.at[Z1_S])

    def sum_z(r, carry):
        rr = pl.ds(pl.multiple_of(r * 256, 256), 256)
        total = gz[0, :, rr].astype(F32) + rz1[:, rr].astype(F32)
        wide_sum = jnp.concatenate([total, jnp.zeros((256 - (D - 256), 256), F32)], axis=0)
        az[rr, :] = wide_sum.T.astype(BF16)
        return carry

    lax.fori_loop(0, 4, sum_z, 0)
    for j in range(1, NS):
        ss = lax.rem(shard + j, NS)
        rows = az.at[pl.ds(pl.multiple_of(ss * NEG_OWN, NEG_OWN), NEG_OWN)]
        rcopy(rows, rz2.at[shard], send.at[Z2_S], recv.at[Z2_S], (bucket, ss))
    rz2[shard] = az[my_rows, :]

    wait_bytes(r2in.at[pl.ds(0, NS - 1)], recv.at[R2_S])
    r2 = r2in[0].astype(F32)
    for i in range(1, NS):
        r2 = r2 + r2in[i].astype(F32)
    r2all[z] = r2
    for k in (1, 3, 2):
        zz = lax.rem(z + k, NZ)
        rcopy(r2all.at[z], r2all.at[z], send.at[R3_S], recv.at[R3_S], (zz * 2 + c, shard))
    wait_bytes(r2all.at[pl.ds(0, 3)], recv.at[R3_S])
    rel_row = pl.ds(pl.multiple_of(c * 256 + shard * 16, 16), 16)
    rfin[rel_row, :] = ((r2all[0] + r2all[1]) + r2all[2]) + r2all[3]
    for j in range(1, NS):
        ss = lax.rem(shard + j, NS)
        rcopy(rfin.at[rel_row], rfin.at[rel_row], send.at[R4_S], recv.at[R4_S], (bucket, ss))

    wait_bytes(arrived, recv.at[ENT_S])
    lane = iota((8, DP), 1)
    unit = jnp.where(lane == D, 32.0, jnp.where(lane == D + 1, 1.0, 0.0)).astype(BF16)
    row_ids = nt(unit, arrived[...])[0:1, :]

    def scatter(r, carry):
        hot = hot_where((iota((256, 2048), 0) + r * 256).astype(F32) == row_ids)
        got = nn(hot, arrived[...])
        ent_out[:, pl.ds(pl.multiple_of(r * 256, 256), 256)] = got.T[0:D]
        return carry

    lax.fori_loop(0, 4, scatter, 0)

    wait_bytes(rfin.at[pl.ds(0, 240)], recv.at[R4_S])
    half_rel = rfin.at[pl.ds(pl.multiple_of(c * 256, 256), 256)]
    rcopy(half_rel, half_rel, send.at[R5_S], recv.at[R5_S], partner)

    def sum16(ref):
        total = ref[0].astype(F32)
        for i in range(1, ref.shape[0]):
            total = total + ref[i].astype(F32)
        return total

    wait_bytes(rx2.at[pl.ds(0, 7)], recv.at[X2_S])
    neg_out[:, 0:128] = sum16(rx2)
    wait_bytes(ry2.at[pl.ds(0, 7)], recv.at[Y2_S])
    neg_out[:, 128:256] = sum16(ry2)
    wait_bytes(rz2.at[pl.ds(0, NS - 1)], recv.at[Z2_S])
    neg_out[:, 256:D] = sum16(rz2)[:, 0 : D - 256]

    wait_bytes(half_rel, recv.at[R5_S])
    for r in range(4):
        rr = slice(r * 128, (r + 1) * 128)
        wide = jnp.concatenate([rfin[rr, :], jnp.zeros((128, DP - D), F32)], axis=1)
        rel_out[:, rr] = wide.T[0:D]

    wait_bytes(nbt.at[pl.ds(0, 2)], send.at[GZ_S])
    wait_bytes(nbt.at[pl.ds(0, 3)], send.at[GX_S])
    wait_bytes(nbt.at[pl.ds(0, 3)], send.at[GY_S])
    for number in (Q1_S, Q2_S, Q3_S):
        wait_bytes(qt.at[mine], send.at[number])
    for number in (SQ1_S, SQ2_S, SQ3_S):
        wait_bytes(sq.at[mine], send.at[number])
    for number in (ST1_S, ST2_S, SC1_S, SC2_S):
        wait_bytes(st.at[own_half], send.at[number])
    wait_bytes(ot_pair, send.at[O1_S])
    wait_bytes(o_far, send.at[O2_S])
    wait_bytes(ot_own, send.at[O3_S])
    wait_bytes(arrived.at[pl.ds(0, 2048 - SLOT)], send.at[ENT_S])
    wait_bytes(rp_in, send.at[RC_S])
    wait_bytes(r2in.at[pl.ds(0, NS - 1)], send.at[R2_S])
    wait_bytes(r2all.at[pl.ds(0, 3)], send.at[R3_S])
    wait_bytes(rfin.at[pl.ds(0, 240)], send.at[R4_S])
    wait_bytes(half_rel, send.at[R5_S])
    wait_bytes(rz1, send.at[Z1_S])
    wait_bytes(rx1.at[pl.ds(0, 3)], send.at[X1_S])
    wait_bytes(ry1.at[pl.ds(0, 3)], send.at[Y1_S])
    wait_bytes(rx2.at[pl.ds(0, 7)], send.at[X2_S])
    wait_bytes(ry2.at[pl.ds(0, 7)], send.at[Y2_S])
    wait_bytes(rz2.at[pl.ds(0, NS - 1)], send.at[Z2_S])


SCRATCH = [
    ((16, D, 128), BF16),
    ((D, NEG_DEV), BF16),
    ((NEG_DEV, DP), BF16),
    ((2, 8, NEG_DEV, EC), BF16),
    ((8, DP, EC), BF16),
    ((8, 8, EC), F32),
    ((2, D, EC), F32),
    ((2, D, EC), F32),
    ((2, D, EC), F32),
    ((2, 8, 8, EC), F32),
    ((8, 8, EC), F32),
    ((8, 8, EC), F32),
    ((8, 8, EC), F32),
    ((8, 8, EC), F32),
    ((8, D, EC), F32),
    ((2, D, EC), F32),
    ((2, D, EC), F32),
    ((2, D, EC), BF16),
    ((2, D, EC), BF16),
    ((8, 8, EC), F32),
    ((8, DP, EC), BF16),
    ((DP, 2 * E_DEV), BF16),
    ((D, E_DEV), BF16),
    ((D, E_DEV), BF16),
    ((NB, 256, DP), BF16),
    ((2048, DP), BF16),
    ((NB, 256, 128), F32),
    ((NB, 256, 128), F32),
    ((2, D - 256, NEG_DEV), BF16),
    ((2, 4, 256, 128), BF16),
    ((2, 4, 4, NEG_OWN, 128), BF16),
    ((D - 256, NEG_DEV), BF16),
    ((4, 2, 256, 128), BF16),
    ((4, 2, 4, NEG_OWN, 128), BF16),
    ((NEG_DEV, 256), BF16),
    ((2, 256, 128), BF16),
    ((2, 4, NEG_OWN, 128), BF16),
    ((NS, NEG_OWN, 256), BF16),
    ((8, NEG_OWN, 128), BF16),
    ((8, NEG_OWN, 128), BF16),
    ((REL, D), F32),
    ((REL // 2, D), F32),
    ((REL // 2, D), BF16),
    ((NS, 16, D), BF16),
    ((NZ, 16, D), F32),
    ((REL, D), F32),
]


def per_device(
    head_rows, tail_rows, rel_ids, relations, edge_weights, neg_rows, send_slots, dest_rows
):
    vmem = pl.BlockSpec(memory_space=pltpu.VMEM)
    ent_t, neg_grad, rel_t = pl.pallas_call(
        kernel,
        out_shape=(
            jax.ShapeDtypeStruct((D, ENT_DEV), F32),
            jax.ShapeDtypeStruct((NEG_OWN, D), F32),
            jax.ShapeDtypeStruct((D, REL), F32),
        ),
        in_specs=[vmem] * 8,
        out_specs=(vmem,) * 3,
        scratch_shapes=[pltpu.VMEM(shape, dtype) for shape, dtype in SCRATCH]
        + [
            pltpu.SemaphoreType.DMA((28,)),
            pltpu.SemaphoreType.DMA((28,)),
        ],
        compiler_params=pltpu.CompilerParams(
            collective_id=0, has_side_effects=True, vmem_limit_bytes=60 * 1024 * 1024
        ),
        cost_estimate=pl.CostEstimate(
            flops=2 * 3 * 1024 * 4096 * 400, bytes_accessed=8 * 1024 * 1024, transcendentals=1024 * 4096
        ),
        name="complex_backward",
    )(
        head_rows.T,
        tail_rows.T,
        rel_ids.reshape(1, E_DEV),
        relations.T,
        edge_weights.reshape(1, E_DEV),
        neg_rows.T,
        send_slots.T,
        dest_rows.T,
    )
    return ent_t.T, neg_grad, rel_t.T


def solution(mesh):
    return jax.shard_map(
        per_device,
        mesh=mesh,
        in_specs=(
            P(("bucket", "shard"), None),
            P(("bucket", "shard"), None),
            P(("bucket", "shard")),
            P(),
            P(("bucket", "shard")),
            P("bucket", None),
            P(("bucket", "shard"), None),
            P(("bucket", "shard"), None),
        ),
        out_specs=(P(("bucket", "shard"), None), P(("bucket", "shard"), None), P()),
        check_vma=False,
    )
```

```python
import functools

import jax
import jax.numpy as jnp
from jax import lax
from jax.experimental import pallas as pl
from jax.experimental.pallas import tpu as pltpu
from jax.sharding import PartitionSpec as P

D = 400
HALF = 200
DP = 512
E_DEV = 512
ENT_DEV = 1024
REL = 512
NEG_DEV = 1024
SLOT = 16
NB = 8
NS = 16
NZ = 4
EC = 256
NEG_OWN = 64

MESH = pl.DeviceIdType.MESH
F32 = jnp.float32
BF16 = jnp.bfloat16

(Q1_S, SQ1_S, Q2_S, SQ2_S, Q3_S, SQ3_S, ST1_S, O1_S, SC1_S, O2_S, ST2_S, O3_S, SC2_S,
 RC_S, R2_S, R3_S, R4_S, R5_S, ENT_S, Z1_S, X1_S, Y1_S, Z2_S, X2_S, Y2_S, GZ_S, GX_S, GY_S) = range(28)


def nt(a, b):
    return lax.dot_general(a, b, (((1,), (1,)), ((), ())), preferred_element_type=F32)


def nn(a, b):
    return jnp.dot(a, b, preferred_element_type=F32)


def iota(shape, dim):
    return lax.broadcasted_iota(jnp.int32, shape, dim)


def hot_where(mask):
    return mask.astype(F32).astype(BF16)


def wait_bytes(ref, sem):
    pltpu.make_async_copy(ref, ref, sem).wait()


def kernel(
    head, tail, ids, rel, wts, neg, slots, drows,
    ent_out, neg_out, rel_out,
    nbt, wide, nb, prob, qt, sq, hts, tts, rts, mb, st, st_in, sc, sc_in,
    ot, ot_pair, ot_own, o_sum, o_far, lt, qs, ends, rt_hi, rt_lo,
    packed, arrived, slot_col, dest_col,
    gz, gx, gy, rz1, rx1, ry1, az, ax, ay, rz2, rx2, ry2,
    rp, rp_in, r1b, r2in, r2all, rfin,
    send, recv,
):
    bucket, shard = lax.axis_index("bucket"), lax.axis_index("shard")
    z, c = bucket // 2, bucket % 2
    x, y = shard // 4, shard % 4
    oc = 1 - c
    me = bucket * NS + shard
    partner = (z * 2 + oc, shard)
    pair = ((z + 1 - 2 * (z % 2)) * 2 + c, shard)
    z_far = 3 - z
    far = (z_far * 2 + c, shard)

    def rcopy(src, dst, s_sem, r_sem, device):
        pltpu.make_async_remote_copy(
            src_ref=src, dst_ref=dst, send_sem=s_sem, recv_sem=r_sem,
            device_id=device, device_id_type=MESH,
        ).start()

    def peer(k, i):
        a, b = i % 4, i // 4
        zz = (z + k + 3 * a + 2 * b) % 4
        cc = (c + k // 4) % 2
        return zz * 2 + cc, (x + a) % 4 * 4 + (y + a + b) % 4

    def shard_peer(i):
        return peer(0, i)[1]

    barrier = pltpu.get_barrier_semaphore()

    ones = jnp.ones((SLOT, 128), BF16)
    tables = []
    for ref in (slots, drows):
        value = ref[...].astype(F32)
        high = jnp.floor(value * (1.0 / 32.0))
        tables.append((high.astype(BF16), (value - 32.0 * high).astype(BF16)))

    def columns(k, first):
        peer_bucket, peer_shard = peer(k, iota((256, 128), 0) // SLOT)
        owner_hot = hot_where(iota((256, 128), 1) == peer_bucket * NS + peer_shard)
        keep = iota((256, SLOT), 1) == iota((256, SLOT), 0) % SLOT
        for (high, low), out in zip(tables, (slot_col, dest_col)):
            h = jnp.where(keep, nt(owner_hot, high), 0.0).astype(BF16)
            l = jnp.where(keep, nt(owner_hot, low), 0.0).astype(BF16)
            out[k] = 32.0 * nn(h, ones) + nn(l, ones)
        for i in range(first, NS):
            pl.semaphore_signal(barrier, inc=1, device_id=peer(k, i), device_id_type=MESH)

    columns(0, 1)

    def more_columns(k, carry):
        columns(k, 0)
        return carry

    lax.fori_loop(1, NB, more_columns, 0)

    for i in range(8):
        nbt[i] = neg[:, i * 128 : (i + 1) * 128]

    rel_1 = rel[...].astype(BF16)
    rest = rel[...] - rel_1.astype(F32)
    rel_2 = rest.astype(BF16)
    rel_3 = (rest - rel_2.astype(F32)).astype(BF16)
    for j in range(2):
        cols = slice(j * EC, (j + 1) * EC)
        h_t = head[:, cols].astype(F32)
        t_t = tail[:, cols].astype(F32)
        hot = hot_where(iota((REL, EC), 0) == ids[0:1, cols])
        r_t = (nn(rel_1, hot) + nn(rel_2, hot)) + nn(rel_3, hot)
        hre, him = h_t[:HALF], h_t[HALF:]
        rre, rim = r_t[:HALF], r_t[HALF:]
        q = jnp.concatenate([hre * rre - him * rim, hre * rim + him * rre], axis=0).astype(BF16)
        qt[2 * c + j, 0:D, :] = q
        qt[2 * c + j, D:DP, :] = jnp.zeros((DP - D, EC), BF16)
        sq[2 * c + j, 0:1, :] = jnp.sum(q.astype(F32) * t_t, axis=0, keepdims=True)
        sq[2 * c + j, 1:2, :] = wts[0:1, cols]
        sq[2 * c + j, 2:8, :] = jnp.zeros((6, EC), F32)
        hts[j] = h_t
        tts[j] = t_t
        rts[j] = r_t

    pl.semaphore_wait(barrier, NB * NS - 1)

    for i in (x, 4 + y):
        rcopy(nbt.at[i], nbt.at[8 + i], send.at[GZ_S], recv.at[GZ_S], far)
    mine, theirs = pl.ds(2 * c, 2), pl.ds(4 + 2 * c, 2)
    rcopy(qt.at[mine], qt.at[mine], send.at[Q1_S], recv.at[Q1_S], partner)
    rcopy(sq.at[mine], sq.at[mine], send.at[SQ1_S], recv.at[SQ1_S], partner)
    rcopy(qt.at[mine], qt.at[theirs], send.at[Q2_S], recv.at[Q2_S], pair)
    rcopy(sq.at[mine], sq.at[theirs], send.at[SQ2_S], recv.at[SQ2_S], pair)

    nb[:, 384:DP] = jnp.zeros((NEG_DEV, 128), BF16)

    def flip(b):
        for i in range(8):
            part = nbt[b * 8 + i]
            wide[:, i * 128 : (i + 1) * 128] = part
            nb[i * 128 : (i + 1) * 128, 0:D] = part.astype(F32).T.astype(BF16)

    def block(b, two):

        def chunk(g):
            s = nn(nb[...], qt[g])
            m = jnp.max(s, axis=0, keepdims=True)
            p = jnp.exp(s - m)
            l = jnp.sum(p, axis=0, keepdims=True)
            pb = p.astype(BF16)
            prob[b, g] = pb
            o = nn(wide[...], pb)
            mb[b, g, 0:1, :] = m
            if b == 0:
                st[g, 0:1, :] = m
                st[g, 1:2, :] = l
                st[g, 2:8, :] = jnp.zeros((6, EC), F32)
                ot[g] = o
            else:
                m_old = st[g, 0:1, :]
                m_new = jnp.maximum(m_old, m)
                f_old = jnp.exp(m_old - m_new)
                f_new = jnp.exp(m - m_new)
                st[g, 0:1, :] = m_new
                st[g, 1:2, :] = st[g, 1:2, :] * f_old + l * f_new
                ot[g] = ot[g] * f_old + o * f_new

        chunk(2 * two)
        chunk(2 * two + 1)

    flip(0)
    block(0, c)
    wait_bytes(nbt.at[pl.ds(8, 2)], recv.at[GZ_S])
    for i in (1, 3, 2):
        xx, yy = lax.rem(x + i, 4), lax.rem(y + i, 4)
        rcopy(nbt.at[8 + x], nbt.at[8 + x], send.at[GX_S], recv.at[GX_S], (bucket, xx * 4 + y))
        rcopy(nbt.at[12 + y], nbt.at[12 + y], send.at[GY_S], recv.at[GY_S], (bucket, x * 4 + yy))
    wait_bytes(qt.at[mine], recv.at[Q1_S])
    wait_bytes(sq.at[mine], recv.at[SQ1_S])
    block(0, oc)
    wait_bytes(qt.at[mine], recv.at[Q2_S])
    wait_bytes(sq.at[mine], recv.at[SQ2_S])
    rcopy(qt.at[theirs], qt.at[theirs], send.at[Q3_S], recv.at[Q3_S], partner)
    rcopy(sq.at[theirs], sq.at[theirs], send.at[SQ3_S], recv.at[SQ3_S], partner)
    block(0, 2 + c)
    wait_bytes(qt.at[mine], recv.at[Q3_S])
    wait_bytes(sq.at[mine], recv.at[SQ3_S])
    block(0, 2 + oc)
    wait_bytes(nbt.at[pl.ds(8, 3)], recv.at[GX_S])
    wait_bytes(nbt.at[pl.ds(8, 3)], recv.at[GY_S])
    flip(1)
    block(1, 2 + oc)
    rcopy(
        ot.at[pl.ds(4 + 2 * oc, 2)], ot_pair, send.at[O1_S], recv.at[O1_S], partner
    )
    block(1, 2 + c)
    own_half, pair_half = pl.ds(0, 4), pl.ds(4, 4)
    rcopy(st.at[pair_half], st_in.at[pair_half], send.at[ST1_S], recv.at[ST1_S], partner)

    def merge(g):
        m_a, m_b = st[g, 0:1, :], st_in[g, 0:1, :]
        m = jnp.maximum(m_a, m_b)
        f_a, f_b = jnp.exp(m_a - m), jnp.exp(m_b - m)
        sc[g, 0:1, :] = m
        sc[g, 1:2, :] = st[g, 1:2, :] * f_a + st_in[g, 1:2, :] * f_b
        sc[g, 2:8, :] = jnp.zeros((6, EC), F32)
        return f_a, f_b

    block(1, oc)
    rcopy(ot.at[pl.ds(2 * oc, 2)], ot_own, send.at[O3_S], recv.at[O3_S], partner)
    wait_bytes(st_in.at[pair_half], recv.at[ST1_S])
    wait_bytes(ot_pair, recv.at[O1_S])
    for g in range(4, 8):
        merge(g)
    for j in range(2):
        f_a, f_b = merge(4 + 2 * c + j)
        o_sum[j] = (ot[4 + 2 * c + j] * f_a + ot_pair[j] * f_b).astype(BF16)
    rcopy(o_sum, o_far, send.at[O2_S], recv.at[O2_S], pair)
    rcopy(sc.at[pair_half], sc_in.at[own_half], send.at[SC1_S], recv.at[SC1_S], pair)
    block(1, c)
    rcopy(st.at[own_half], st_in.at[own_half], send.at[ST2_S], recv.at[ST2_S], partner)
    wait_bytes(st_in.at[own_half], recv.at[ST2_S])
    for g in range(4):
        merge(g)
    rcopy(sc.at[own_half], sc_in.at[pair_half], send.at[SC2_S], recv.at[SC2_S], pair)
    wait_bytes(sc_in.at[own_half], recv.at[SC1_S])
    wait_bytes(sc_in.at[pair_half], recv.at[SC2_S])
    for g in range(8):
        pos = sq[g, 0:1, :]
        m0, m1 = sc[g, 0:1, :], sc_in[g, 0:1, :]
        top = jnp.maximum(pos, jnp.maximum(m0, m1))
        total = (
            jnp.exp(pos - top)
            + sc[g, 1:2, :] * jnp.exp(m0 - top)
            + sc_in[g, 1:2, :] * jnp.exp(m1 - top)
        )
        lt[g, 0:1, :] = top + jnp.log(total)

    def neg_block(b):
        for g in range(8):
            scale = sq[g, 1:2, :] * jnp.exp(mb[b, g, 0:1, :] - lt[g, 0:1, :])
            qs[g] = (qt[g].astype(F32) * scale).astype(BF16)

        def rows_of(xx, carry):
            rr = pl.ds(pl.multiple_of(xx * 256, 256), 256)
            acc = nt(prob[b, 0, rr, :], qs[0])
            for g in range(1, 8):
                acc = acc + nt(prob[b, g, rr, :], qs[g])
            gx[b, xx] = acc[:, 0:128].astype(BF16)
            for yy in range(4):
                gy[b, yy, xx] = acc[yy * 64 : (yy + 1) * 64, 128:256].astype(BF16)
            gz[b, :, rr] = acc[:, 256:512].T[0 : D - 256].astype(BF16)
            return carry

        lax.fori_loop(0, 4, rows_of, 0)
        for i in (1, 3, 2):
            xx, yy = lax.rem(x + i, 4), lax.rem(y + i, 4)
            rcopy(gx.at[b, xx], rx1.at[x, b], send.at[X1_S], recv.at[X1_S], (bucket, xx * 4 + y))
            rcopy(gy.at[b, yy], ry1.at[y, b], send.at[Y1_S], recv.at[Y1_S], (bucket, x * 4 + yy))

    neg_block(1)
    rcopy(gz.at[1], rz1, send.at[Z1_S], recv.at[Z1_S], far)
    neg_block(0)
    wait_bytes(ot_own, recv.at[O3_S])
    wait_bytes(o_far, recv.at[O2_S])
    ends[D:DP, :] = jnp.zeros((DP - D, 2 * E_DEV), BF16)
    for j in range(2):
        cols = slice(j * EC, (j + 1) * EC)
        tail_cols = slice(E_DEV + j * EC, E_DEV + (j + 1) * EC)
        g = 2 * c + j
        pos, w, ltot = sq[g, 0:1, :], sq[g, 1:2, :], lt[g, 0:1, :]
        pos_coef = w * (jnp.exp(pos - ltot) - 1.0)
        own = w * jnp.exp(st[g, 0:1, :] - ltot)
        other = w * jnp.exp(st_in[g, 0:1, :] - ltot)
        away = w * jnp.exp(sc_in[g, 0:1, :] - ltot)
        grad = pos_coef * tts[j] + ot[g] * own + ot_own[j] * other + o_far[j].astype(F32) * away
        gre, gim = grad[:HALF], grad[HALF:]
        rre, rim = rts[j, :HALF, :], rts[j, HALF:, :]
        hre, him = hts[j, :HALF, :], hts[j, HALF:, :]
        ends[0:D, cols] = jnp.concatenate(
            [gre * rre + gim * rim, gim * rre - gre * rim], axis=0
        ).astype(BF16)
        ends[0:D, tail_cols] = (pos_coef * qt[g, 0:D, :].astype(F32)).astype(BF16)
        term = jnp.concatenate([gre * hre + gim * him, gim * hre - gre * him], axis=0)
        hi = term.astype(BF16)
        rt_hi[:, cols] = hi
        rt_lo[:, cols] = (term - hi.astype(F32)).astype(BF16)

    my_slots = pl.ds(pl.multiple_of(me * SLOT, SLOT), SLOT)

    def pack(k, first):
        sc_k = slot_col[k]
        sel = jnp.concatenate(
            [hot_where(sc_k == (iota((256, 128), 1) + 128 * t).astype(F32)) for t in range(8)], axis=1
        )
        rows = nt(sel, ends[...])
        dc = dest_col[k]
        high = jnp.floor(dc * (1.0 / 32.0))
        lane = iota((256, 128), 1)
        code = jnp.where(lane == 16, high, jnp.where(lane == 17, dc - 32.0 * high, 0.0))
        packed[k, :, 0:384] = rows[:, 0:384].astype(BF16)
        packed[k, :, 384:512] = (rows[:, 384:512] + code).astype(BF16)
        for i in range(NS):
            src = packed.at[k, pl.ds(i * SLOT, SLOT)]
            if first and i == 0:
                pltpu.make_async_copy(src, arrived.at[my_slots], recv.at[ENT_S]).start()
            else:
                rcopy(src, arrived.at[my_slots], send.at[ENT_S], recv.at[ENT_S], peer(k, i))

    def rel_chunk(r, carry):
        hot = hot_where(iota((128, E_DEV), 0) + r * 128 == ids[...])
        rp[pl.ds(pl.multiple_of(r * 128, 128), 128), :] = nt(hot, rt_hi[...]) + nt(hot, rt_lo[...])
        return carry

    lax.fori_loop(0, 4, rel_chunk, 0)
    rcopy(
        rp.at[pl.ds(pl.multiple_of(oc * 256, 256), 256)], rp_in, send.at[RC_S], recv.at[RC_S], partner
    )

    def pack_other(k, carry):
        pack(k, False)
        return carry

    pack(0, True)
    lax.fori_loop(1, 3, pack_other, 0)

    wait_bytes(rp_in, recv.at[RC_S])
    r1b[...] = (rp[pl.ds(pl.multiple_of(c * 256, 256), 256), :] + rp_in[...]).astype(BF16)
    for j in range(1, NS):
        ss = shard_peer(j)
        rows = r1b.at[pl.ds(pl.multiple_of(ss * 16, 16), 16)]
        rcopy(rows, r2in.at[shard], send.at[R2_S], recv.at[R2_S], (bucket, ss))
    r2in[shard] = r1b[pl.ds(pl.multiple_of(shard * 16, 16), 16), :]
    lax.fori_loop(3, NB, pack_other, 0)

    my_rows = pl.ds(pl.multiple_of(shard * NEG_OWN, NEG_OWN), NEG_OWN)
    wait_bytes(rx1.at[pl.ds(0, 3)], recv.at[X1_S])
    for b in range(2):
        total = gx[b, x].astype(F32)
        for i in range(1, 4):
            total = total + rx1[lax.rem(x + i, 4), b].astype(F32)
        ax[b] = total.astype(BF16)
    for i in range(4):
        yy = lax.rem(y + i, 4)
        rows = pl.ds(pl.multiple_of(yy * NEG_OWN, NEG_OWN), NEG_OWN)
        if i:
            rcopy(ax.at[0, rows], rx2.at[y], send.at[X2_S], recv.at[X2_S], (bucket, x * 4 + yy))
        else:
            rx2[y] = ax[0, rows, :]
        rcopy(
            ax.at[1, rows], rx2.at[4 + y], send.at[X2_S], recv.at[X2_S], (z_far * 2 + c, x * 4 + yy)
        )
    wait_bytes(ry1.at[pl.ds(0, 3)], recv.at[Y1_S])
    for b in range(2):
        total = gy[b, y].astype(F32)
        for i in range(1, 4):
            total = total + ry1[lax.rem(y + i, 4), b].astype(F32)
        ay[b] = total.astype(BF16)
    for i in range(4):
        xx = lax.rem(x + i, 4)
        if i:
            rcopy(ay.at[0, xx], ry2.at[x], send.at[Y2_S], recv.at[Y2_S], (bucket, xx * 4 + y))
        else:
            ry2[x] = ay[0, x]
        rcopy(
            ay.at[1, xx], ry2.at[4 + x], send.at[Y2_S], recv.at[Y2_S], (z_far * 2 + c, xx * 4 + y)
        )
    wait_bytes(rz1, recv.at[Z1_S])

    def sum_z(r, carry):
        rr = pl.ds(pl.multiple_of(r * 256, 256), 256)
        total = gz[0, :, rr].astype(F32) + rz1[:, rr].astype(F32)
        wide_sum = jnp.concatenate([total, jnp.zeros((256 - (D - 256), 256), F32)], axis=0)
        az[rr, :] = wide_sum.T.astype(BF16)
        return carry

    lax.fori_loop(0, 4, sum_z, 0)
    for j in range(1, NS):
        ss = shard_peer(j)
        rows = az.at[pl.ds(pl.multiple_of(ss * NEG_OWN, NEG_OWN), NEG_OWN)]
        rcopy(rows, rz2.at[shard], send.at[Z2_S], recv.at[Z2_S], (bucket, ss))
    rz2[shard] = az[my_rows, :]

    wait_bytes(r2in.at[pl.ds(0, NS - 1)], recv.at[R2_S])
    r2 = r2in[0].astype(F32)
    for i in range(1, NS):
        r2 = r2 + r2in[i].astype(F32)
    r2all[z] = r2
    for k in (1, 3, 2):
        zz = lax.rem(z + k, NZ)
        rcopy(r2all.at[z], r2all.at[z], send.at[R3_S], recv.at[R3_S], (zz * 2 + c, shard))
    wait_bytes(r2all.at[pl.ds(0, 3)], recv.at[R3_S])
    rel_row = pl.ds(pl.multiple_of(c * 256 + shard * 16, 16), 16)
    rfin[rel_row, :] = ((r2all[0] + r2all[1]) + r2all[2]) + r2all[3]
    for j in range(1, NS):
        ss = shard_peer(j)
        rcopy(rfin.at[rel_row], rfin.at[rel_row], send.at[R4_S], recv.at[R4_S], (bucket, ss))

    wait_bytes(arrived, recv.at[ENT_S])
    lane = iota((8, DP), 1)
    unit = jnp.where(lane == D, 32.0, jnp.where(lane == D + 1, 1.0, 0.0)).astype(BF16)
    row_ids = nt(unit, arrived[...])[0:1, :]

    def scatter(r, carry):
        hot = hot_where((iota((256, 2048), 0) + r * 256).astype(F32) == row_ids)
        got = nn(hot, arrived[...])
        ent_out[:, pl.ds(pl.multiple_of(r * 256, 256), 256)] = got.T[0:D]
        return carry

    lax.fori_loop(0, 4, scatter, 0)

    wait_bytes(rfin.at[pl.ds(0, 240)], recv.at[R4_S])
    half_rel = rfin.at[pl.ds(pl.multiple_of(c * 256, 256), 256)]
    rcopy(half_rel, half_rel, send.at[R5_S], recv.at[R5_S], partner)

    def sum16(ref):
        total = ref[0].astype(F32)
        for i in range(1, ref.shape[0]):
            total = total + ref[i].astype(F32)
        return total

    wait_bytes(rx2.at[pl.ds(0, 7)], recv.at[X2_S])
    neg_out[:, 0:128] = sum16(rx2)
    wait_bytes(ry2.at[pl.ds(0, 7)], recv.at[Y2_S])
    neg_out[:, 128:256] = sum16(ry2)
    wait_bytes(rz2.at[pl.ds(0, NS - 1)], recv.at[Z2_S])
    neg_out[:, 256:D] = sum16(rz2)[:, 0 : D - 256]

    wait_bytes(half_rel, recv.at[R5_S])
    for r in range(4):
        rr = slice(r * 128, (r + 1) * 128)
        wide = jnp.concatenate([rfin[rr, :], jnp.zeros((128, DP - D), F32)], axis=1)
        rel_out[:, rr] = wide.T[0:D]

    wait_bytes(nbt.at[pl.ds(0, 2)], send.at[GZ_S])
    wait_bytes(nbt.at[pl.ds(0, 3)], send.at[GX_S])
    wait_bytes(nbt.at[pl.ds(0, 3)], send.at[GY_S])
    for number in (Q1_S, Q2_S, Q3_S):
        wait_bytes(qt.at[mine], send.at[number])
    for number in (SQ1_S, SQ2_S, SQ3_S):
        wait_bytes(sq.at[mine], send.at[number])
    for number in (ST1_S, ST2_S, SC1_S, SC2_S):
        wait_bytes(st.at[own_half], send.at[number])
    wait_bytes(ot_pair, send.at[O1_S])
    wait_bytes(o_far, send.at[O2_S])
    wait_bytes(ot_own, send.at[O3_S])
    wait_bytes(arrived.at[pl.ds(0, 2048 - SLOT)], send.at[ENT_S])
    wait_bytes(rp_in, send.at[RC_S])
    wait_bytes(r2in.at[pl.ds(0, NS - 1)], send.at[R2_S])
    wait_bytes(r2all.at[pl.ds(0, 3)], send.at[R3_S])
    wait_bytes(rfin.at[pl.ds(0, 240)], send.at[R4_S])
    wait_bytes(half_rel, send.at[R5_S])
    wait_bytes(rz1, send.at[Z1_S])
    wait_bytes(rx1.at[pl.ds(0, 3)], send.at[X1_S])
    wait_bytes(ry1.at[pl.ds(0, 3)], send.at[Y1_S])
    wait_bytes(rx2.at[pl.ds(0, 7)], send.at[X2_S])
    wait_bytes(ry2.at[pl.ds(0, 7)], send.at[Y2_S])
    wait_bytes(rz2.at[pl.ds(0, NS - 1)], send.at[Z2_S])


SCRATCH = [
    ((16, D, 128), BF16),
    ((D, NEG_DEV), BF16),
    ((NEG_DEV, DP), BF16),
    ((2, 8, NEG_DEV, EC), BF16),
    ((8, DP, EC), BF16),
    ((8, 8, EC), F32),
    ((2, D, EC), F32),
    ((2, D, EC), F32),
    ((2, D, EC), F32),
    ((2, 8, 8, EC), F32),
    ((8, 8, EC), F32),
    ((8, 8, EC), F32),
    ((8, 8, EC), F32),
    ((8, 8, EC), F32),
    ((8, D, EC), F32),
    ((2, D, EC), F32),
    ((2, D, EC), F32),
    ((2, D, EC), BF16),
    ((2, D, EC), BF16),
    ((8, 8, EC), F32),
    ((8, DP, EC), BF16),
    ((DP, 2 * E_DEV), BF16),
    ((D, E_DEV), BF16),
    ((D, E_DEV), BF16),
    ((NB, 256, DP), BF16),
    ((2048, DP), BF16),
    ((NB, 256, 128), F32),
    ((NB, 256, 128), F32),
    ((2, D - 256, NEG_DEV), BF16),
    ((2, 4, 256, 128), BF16),
    ((2, 4, 4, NEG_OWN, 128), BF16),
    ((D - 256, NEG_DEV), BF16),
    ((4, 2, 256, 128), BF16),
    ((4, 2, 4, NEG_OWN, 128), BF16),
    ((NEG_DEV, 256), BF16),
    ((2, 256, 128), BF16),
    ((2, 4, NEG_OWN, 128), BF16),
    ((NS, NEG_OWN, 256), BF16),
    ((8, NEG_OWN, 128), BF16),
    ((8, NEG_OWN, 128), BF16),
    ((REL, D), F32),
    ((REL // 2, D), F32),
    ((REL // 2, D), BF16),
    ((NS, 16, D), BF16),
    ((NZ, 16, D), F32),
    ((REL, D), F32),
]


def per_device(
    head_rows, tail_rows, rel_ids, relations, edge_weights, neg_rows, send_slots, dest_rows
):
    vmem = pl.BlockSpec(memory_space=pltpu.VMEM)
    ent_t, neg_grad, rel_t = pl.pallas_call(
        kernel,
        out_shape=(
            jax.ShapeDtypeStruct((D, ENT_DEV), F32),
            jax.ShapeDtypeStruct((NEG_OWN, D), F32),
            jax.ShapeDtypeStruct((D, REL), F32),
        ),
        in_specs=[vmem] * 8,
        out_specs=(vmem,) * 3,
        scratch_shapes=[pltpu.VMEM(shape, dtype) for shape, dtype in SCRATCH]
        + [
            pltpu.SemaphoreType.DMA((28,)),
            pltpu.SemaphoreType.DMA((28,)),
        ],
        compiler_params=pltpu.CompilerParams(
            collective_id=0, has_side_effects=True, vmem_limit_bytes=60 * 1024 * 1024
        ),
        cost_estimate=pl.CostEstimate(
            flops=2 * 3 * 1024 * 4096 * 400, bytes_accessed=8 * 1024 * 1024, transcendentals=1024 * 4096
        ),
        name="complex_backward",
    )(
        head_rows.T,
        tail_rows.T,
        rel_ids.reshape(1, E_DEV),
        relations.T,
        edge_weights.reshape(1, E_DEV),
        neg_rows.T,
        send_slots.T,
        dest_rows.T,
    )
    return ent_t.T, neg_grad, rel_t.T


def solution(mesh):
    return jax.shard_map(
        per_device,
        mesh=mesh,
        in_specs=(
            P(("bucket", "shard"), None),
            P(("bucket", "shard"), None),
            P(("bucket", "shard")),
            P(),
            P(("bucket", "shard")),
            P("bucket", None),
            P(("bucket", "shard"), None),
            P(("bucket", "shard"), None),
        ),
        out_specs=(P(("bucket", "shard"), None), P(("bucket", "shard"), None), P()),
        check_vma=False,
    )
```

```python
import functools

import jax
import jax.numpy as jnp
from jax import lax
from jax.experimental import pallas as pl
from jax.experimental.pallas import tpu as pltpu
from jax.sharding import PartitionSpec as P

D = 400
HALF = 200
DP = 512
E_DEV = 512
ENT_DEV = 1024
REL = 512
NEG_DEV = 1024
SLOT = 16
NB = 8
NS = 16
NZ = 4
EC = 256
NEG_OWN = 64

MESH = pl.DeviceIdType.MESH
F32 = jnp.float32
BF16 = jnp.bfloat16

(Q1_S, SQ1_S, Q2_S, SQ2_S, Q3_S, SQ3_S, ST1_S, O1_S, SC1_S, O2_S, ST2_S, O3_S, SC2_S,
 GZ_S, GX_S, GY_S) = range(16)
RC_S, R2_S, R3_S, R4_S, R5_S, Z1_S, X1_S, Y1_S, Z2_S, X2_S, Y2_S = range(11)


def nt(a, b):
    return lax.dot_general(a, b, (((1,), (1,)), ((), ())), preferred_element_type=F32)


def nn(a, b):
    return jnp.dot(a, b, preferred_element_type=F32)


def iota(shape, dim):
    return lax.broadcasted_iota(jnp.int32, shape, dim)


def hot_where(mask):
    return mask.astype(F32).astype(BF16)


def wait_bytes(ref, sem):
    pltpu.make_async_copy(ref, ref, sem).wait()


def edge_kernel(
    head, tail, ids, rel, wts, neg, slots, drows,
    packed_out, gx_out, gy_out, gz_out, rp_out,
    nbt, wide, nb, prob, qt, sq, hts, tts, rts, mb, st, st_in, sc, sc_in,
    ot, ot_pair, ot_own, o_sum, o_far, lt, qs, ends, rt_hi, rt_lo,
    packed, slot_col, dest_col, gz, gx, gy, rp,
    send, recv, out_sem,
):
    bucket, shard = lax.axis_index("bucket"), lax.axis_index("shard")
    z, c = bucket // 2, bucket % 2
    x, y = shard // 4, shard % 4
    oc = 1 - c
    partner = (z * 2 + oc, shard)
    pair = ((z + 1 - 2 * (z % 2)) * 2 + c, shard)
    z_far = 3 - z
    far = (z_far * 2 + c, shard)

    def rcopy(src, dst, s_sem, r_sem, device):
        pltpu.make_async_remote_copy(
            src_ref=src, dst_ref=dst, send_sem=s_sem, recv_sem=r_sem,
            device_id=device, device_id_type=MESH,
        ).start()

    def give(src, dst, sem):
        pltpu.make_async_copy(src, dst, sem).start()

    friends = [partner, pair, far]
    for i in (1, 2, 3):
        friends.append((bucket, lax.rem(x + i, 4) * 4 + y))
        friends.append((bucket, x * 4 + lax.rem(y + i, 4)))
    barrier = pltpu.get_barrier_semaphore()
    for friend in friends:
        pl.semaphore_signal(barrier, inc=1, device_id=friend, device_id_type=MESH)

    ones = jnp.ones((SLOT, 128), BF16)
    tables = []
    for ref in (slots, drows):
        value = ref[...].astype(F32)
        high = jnp.floor(value * (1.0 / 32.0))
        tables.append((high.astype(BF16), (value - 32.0 * high).astype(BF16)))

    def columns(k, carry):
        owner_hot = hot_where(iota((256, 128), 1) == iota((256, 128), 0) // SLOT + k * NS)
        keep = iota((256, SLOT), 1) == iota((256, SLOT), 0) % SLOT
        for (high, low), out in zip(tables, (slot_col, dest_col)):
            h = jnp.where(keep, nt(owner_hot, high), 0.0).astype(BF16)
            l = jnp.where(keep, nt(owner_hot, low), 0.0).astype(BF16)
            out[k] = 32.0 * nn(h, ones) + nn(l, ones)
        return carry

    lax.fori_loop(0, NB, columns, 0)

    for i in range(8):
        nbt[i] = neg[:, i * 128 : (i + 1) * 128]

    rel_1 = rel[...].astype(BF16)
    rest = rel[...] - rel_1.astype(F32)
    rel_2 = rest.astype(BF16)
    rel_3 = (rest - rel_2.astype(F32)).astype(BF16)
    for j in range(2):
        cols = slice(j * EC, (j + 1) * EC)
        h_t = head[:, cols].astype(F32)
        t_t = tail[:, cols].astype(F32)
        hot = hot_where(iota((REL, EC), 0) == ids[0:1, cols])
        r_t = (nn(rel_1, hot) + nn(rel_2, hot)) + nn(rel_3, hot)
        hre, him = h_t[:HALF], h_t[HALF:]
        rre, rim = r_t[:HALF], r_t[HALF:]
        q = jnp.concatenate([hre * rre - him * rim, hre * rim + him * rre], axis=0).astype(BF16)
        qt[2 * c + j, 0:D, :] = q
        qt[2 * c + j, D:DP, :] = jnp.zeros((DP - D, EC), BF16)
        sq[2 * c + j, 0:1, :] = jnp.sum(q.astype(F32) * t_t, axis=0, keepdims=True)
        sq[2 * c + j, 1:2, :] = wts[0:1, cols]
        sq[2 * c + j, 2:8, :] = jnp.zeros((6, EC), F32)
        hts[j] = h_t
        tts[j] = t_t
        rts[j] = r_t

    pl.semaphore_wait(barrier, len(friends))

    for i in (x, 4 + y):
        rcopy(nbt.at[i], nbt.at[8 + i], send.at[GZ_S], recv.at[GZ_S], far)
    mine, theirs = pl.ds(2 * c, 2), pl.ds(4 + 2 * c, 2)
    rcopy(qt.at[mine], qt.at[mine], send.at[Q1_S], recv.at[Q1_S], partner)
    rcopy(sq.at[mine], sq.at[mine], send.at[SQ1_S], recv.at[SQ1_S], partner)
    rcopy(qt.at[mine], qt.at[theirs], send.at[Q2_S], recv.at[Q2_S], pair)
    rcopy(sq.at[mine], sq.at[theirs], send.at[SQ2_S], recv.at[SQ2_S], pair)

    nb[:, 384:DP] = jnp.zeros((NEG_DEV, 128), BF16)

    def flip(b):
        for i in range(8):
            part = nbt[b * 8 + i]
            wide[:, i * 128 : (i + 1) * 128] = part
            nb[i * 128 : (i + 1) * 128, 0:D] = part.astype(F32).T.astype(BF16)

    def block(b, two):

        def chunk(g):
            s = nn(nb[...], qt[g])
            m = jnp.max(s, axis=0, keepdims=True)
            p = jnp.exp(s - m)
            l = jnp.sum(p, axis=0, keepdims=True)
            pb = p.astype(BF16)
            prob[b, g] = pb
            o = nn(wide[...], pb)
            mb[b, g, 0:1, :] = m
            if b == 0:
                st[g, 0:1, :] = m
                st[g, 1:2, :] = l
                st[g, 2:8, :] = jnp.zeros((6, EC), F32)
                ot[g] = o
            else:
                m_old = st[g, 0:1, :]
                m_new = jnp.maximum(m_old, m)
                f_old = jnp.exp(m_old - m_new)
                f_new = jnp.exp(m - m_new)
                st[g, 0:1, :] = m_new
                st[g, 1:2, :] = st[g, 1:2, :] * f_old + l * f_new
                ot[g] = ot[g] * f_old + o * f_new

        chunk(2 * two)
        chunk(2 * two + 1)

    flip(0)
    block(0, c)
    wait_bytes(nbt.at[pl.ds(8, 2)], recv.at[GZ_S])
    for i in (1, 3, 2):
        xx, yy = lax.rem(x + i, 4), lax.rem(y + i, 4)
        rcopy(nbt.at[8 + x], nbt.at[8 + x], send.at[GX_S], recv.at[GX_S], (bucket, xx * 4 + y))
        rcopy(nbt.at[12 + y], nbt.at[12 + y], send.at[GY_S], recv.at[GY_S], (bucket, x * 4 + yy))
    wait_bytes(qt.at[mine], recv.at[Q1_S])
    wait_bytes(sq.at[mine], recv.at[SQ1_S])
    block(0, oc)
    wait_bytes(qt.at[mine], recv.at[Q2_S])
    wait_bytes(sq.at[mine], recv.at[SQ2_S])
    rcopy(qt.at[theirs], qt.at[theirs], send.at[Q3_S], recv.at[Q3_S], partner)
    rcopy(sq.at[theirs], sq.at[theirs], send.at[SQ3_S], recv.at[SQ3_S], partner)
    block(0, 2 + c)
    wait_bytes(qt.at[mine], recv.at[Q3_S])
    wait_bytes(sq.at[mine], recv.at[SQ3_S])
    block(0, 2 + oc)
    wait_bytes(nbt.at[pl.ds(8, 3)], recv.at[GX_S])
    wait_bytes(nbt.at[pl.ds(8, 3)], recv.at[GY_S])
    flip(1)
    block(1, 2 + oc)
    rcopy(
        ot.at[pl.ds(4 + 2 * oc, 2)], ot_pair, send.at[O1_S], recv.at[O1_S], partner
    )
    block(1, 2 + c)
    own_half, pair_half = pl.ds(0, 4), pl.ds(4, 4)
    rcopy(st.at[pair_half], st_in.at[pair_half], send.at[ST1_S], recv.at[ST1_S], partner)

    def merge(g):
        m_a, m_b = st[g, 0:1, :], st_in[g, 0:1, :]
        m = jnp.maximum(m_a, m_b)
        f_a, f_b = jnp.exp(m_a - m), jnp.exp(m_b - m)
        sc[g, 0:1, :] = m
        sc[g, 1:2, :] = st[g, 1:2, :] * f_a + st_in[g, 1:2, :] * f_b
        sc[g, 2:8, :] = jnp.zeros((6, EC), F32)
        return f_a, f_b

    block(1, oc)
    rcopy(ot.at[pl.ds(2 * oc, 2)], ot_own, send.at[O3_S], recv.at[O3_S], partner)
    wait_bytes(st_in.at[pair_half], recv.at[ST1_S])
    wait_bytes(ot_pair, recv.at[O1_S])
    for g in range(4, 8):
        merge(g)
    for j in range(2):
        f_a, f_b = merge(4 + 2 * c + j)
        o_sum[j] = (ot[4 + 2 * c + j] * f_a + ot_pair[j] * f_b).astype(BF16)
    rcopy(o_sum, o_far, send.at[O2_S], recv.at[O2_S], pair)
    rcopy(sc.at[pair_half], sc_in.at[own_half], send.at[SC1_S], recv.at[SC1_S], pair)
    block(1, c)
    rcopy(st.at[own_half], st_in.at[own_half], send.at[ST2_S], recv.at[ST2_S], partner)
    wait_bytes(st_in.at[own_half], recv.at[ST2_S])
    for g in range(4):
        merge(g)
    rcopy(sc.at[own_half], sc_in.at[pair_half], send.at[SC2_S], recv.at[SC2_S], pair)
    wait_bytes(sc_in.at[own_half], recv.at[SC1_S])
    wait_bytes(sc_in.at[pair_half], recv.at[SC2_S])
    for g in range(8):
        pos = sq[g, 0:1, :]
        m0, m1 = sc[g, 0:1, :], sc_in[g, 0:1, :]
        top = jnp.maximum(pos, jnp.maximum(m0, m1))
        total = (
            jnp.exp(pos - top)
            + sc[g, 1:2, :] * jnp.exp(m0 - top)
            + sc_in[g, 1:2, :] * jnp.exp(m1 - top)
        )
        lt[g, 0:1, :] = top + jnp.log(total)

    def neg_block(b):
        for g in range(8):
            scale = sq[g, 1:2, :] * jnp.exp(mb[b, g, 0:1, :] - lt[g, 0:1, :])
            qs[g] = (qt[g].astype(F32) * scale).astype(BF16)

        def rows_of(xx, carry):
            rr = pl.ds(pl.multiple_of(xx * 256, 256), 256)
            acc = nt(prob[b, 0, rr, :], qs[0])
            for g in range(1, 8):
                acc = acc + nt(prob[b, g, rr, :], qs[g])
            gx[b, xx] = acc[:, 0:128].astype(BF16)
            for yy in range(4):
                gy[b, yy, xx] = acc[yy * 64 : (yy + 1) * 64, 128:256].astype(BF16)
            gz[b, :, rr] = acc[:, 256:512].T[0 : D - 256].astype(BF16)
            return carry

        lax.fori_loop(0, 4, rows_of, 0)
        give(gx.at[b], gx_out.at[b], out_sem.at[b])
        give(gy.at[b], gy_out.at[b], out_sem.at[2 + b])
        give(gz.at[b], gz_out.at[b], out_sem.at[4 + b])

    neg_block(1)
    neg_block(0)
    wait_bytes(ot_own, recv.at[O3_S])
    wait_bytes(o_far, recv.at[O2_S])
    ends[D:DP, :] = jnp.zeros((DP - D, 2 * E_DEV), BF16)
    for j in range(2):
        cols = slice(j * EC, (j + 1) * EC)
        tail_cols = slice(E_DEV + j * EC, E_DEV + (j + 1) * EC)
        g = 2 * c + j
        pos, w, ltot = sq[g, 0:1, :], sq[g, 1:2, :], lt[g, 0:1, :]
        pos_coef = w * (jnp.exp(pos - ltot) - 1.0)
        own = w * jnp.exp(st[g, 0:1, :] - ltot)
        other = w * jnp.exp(st_in[g, 0:1, :] - ltot)
        away = w * jnp.exp(sc_in[g, 0:1, :] - ltot)
        grad = pos_coef * tts[j] + ot[g] * own + ot_own[j] * other + o_far[j].astype(F32) * away
        gre, gim = grad[:HALF], grad[HALF:]
        rre, rim = rts[j, :HALF, :], rts[j, HALF:, :]
        hre, him = hts[j, :HALF, :], hts[j, HALF:, :]
        ends[0:D, cols] = jnp.concatenate(
            [gre * rre + gim * rim, gim * rre - gre * rim], axis=0
        ).astype(BF16)
        ends[0:D, tail_cols] = (pos_coef * qt[g, 0:D, :].astype(F32)).astype(BF16)
        term = jnp.concatenate([gre * hre + gim * him, gim * hre - gre * him], axis=0)
        hi = term.astype(BF16)
        rt_hi[:, cols] = hi
        rt_lo[:, cols] = (term - hi.astype(F32)).astype(BF16)

    def pack(k, carry):
        sc_k = slot_col[k]
        sel = jnp.concatenate(
            [hot_where(sc_k == (iota((256, 128), 1) + 128 * t).astype(F32)) for t in range(8)], axis=1
        )
        rows = nt(sel, ends[...])
        dc = dest_col[k]
        high = jnp.floor(dc * (1.0 / 32.0))
        lane = iota((256, 128), 1)
        code = jnp.where(lane == 16, high, jnp.where(lane == 17, dc - 32.0 * high, 0.0))
        packed[k, :, 0:384] = rows[:, 0:384].astype(BF16)
        packed[k, :, 384:512] = (rows[:, 384:512] + code).astype(BF16)
        give(packed.at[k], packed_out.at[k], out_sem.at[6])
        return carry

    lax.fori_loop(0, NB, pack, 0)

    def rel_chunk(r, carry):
        hot = hot_where(iota((128, E_DEV), 0) + r * 128 == ids[...])
        rp[pl.ds(pl.multiple_of(r * 128, 128), 128), :] = nt(hot, rt_hi[...]) + nt(hot, rt_lo[...])
        return carry

    lax.fori_loop(0, 4, rel_chunk, 0)
    give(rp, rp_out, out_sem.at[7])

    wait_bytes(packed, out_sem.at[6])
    wait_bytes(rp, out_sem.at[7])
    for b in range(2):
        wait_bytes(gx.at[b], out_sem.at[b])
        wait_bytes(gy.at[b], out_sem.at[2 + b])
        wait_bytes(gz.at[b], out_sem.at[4 + b])
    wait_bytes(nbt.at[pl.ds(0, 2)], send.at[GZ_S])
    wait_bytes(nbt.at[pl.ds(0, 3)], send.at[GX_S])
    wait_bytes(nbt.at[pl.ds(0, 3)], send.at[GY_S])
    for number in (Q1_S, Q2_S, Q3_S):
        wait_bytes(qt.at[mine], send.at[number])
    for number in (SQ1_S, SQ2_S, SQ3_S):
        wait_bytes(sq.at[mine], send.at[number])
    for number in (ST1_S, ST2_S, SC1_S, SC2_S):
        wait_bytes(st.at[own_half], send.at[number])
    wait_bytes(ot_pair, send.at[O1_S])
    wait_bytes(o_far, send.at[O2_S])
    wait_bytes(ot_own, send.at[O3_S])


def sum_kernel(
    gx, gy, gz, rp,
    neg_out, rel_out,
    gx_own, gy_own, gz_own, rp_own,
    rz1, rx1, ry1, az, ax, ay, rz2, rx2, ry2, rp_in, r1b, r2in, r2all, rfin,
    send, recv, own_sem,
):
    bucket, shard = lax.axis_index("bucket"), lax.axis_index("shard")
    z, c = bucket // 2, bucket % 2
    x, y = shard // 4, shard % 4
    oc = 1 - c
    partner = (z * 2 + oc, shard)
    z_far = 3 - z
    far = (z_far * 2 + c, shard)

    def rcopy(src, dst, s_sem, r_sem, device):
        pltpu.make_async_remote_copy(
            src_ref=src, dst_ref=dst, send_sem=s_sem, recv_sem=r_sem,
            device_id=device, device_id_type=MESH,
        ).start()

    def shard_peer(i):
        return (x + i % 4) % 4 * 4 + (y + i // 4 + i % 4) % 4

    friends = [partner]
    for i in range(1, NS):
        friends.append((bucket, shard_peer(i)))
    for i in range(1, 4):
        friends.append((lax.rem(z + i, 4) * 2 + c, shard))
        friends.append((z_far * 2 + c, lax.rem(x + i, 4) * 4 + y))
        friends.append((z_far * 2 + c, x * 4 + lax.rem(y + i, 4)))
    barrier = pltpu.get_barrier_semaphore()
    for friend in friends:
        pl.semaphore_signal(barrier, inc=1, device_id=friend, device_id_type=MESH)
    half = pl.ds(pl.multiple_of(c * 256, 256), 256)
    own_copies = [
        pltpu.make_async_copy(rp.at[half], rp_own, own_sem.at[0]),
        pltpu.make_async_copy(gz.at[0], gz_own, own_sem.at[1]),
    ]
    for b in range(2):
        own_copies.append(pltpu.make_async_copy(gx.at[b, x], gx_own.at[b], own_sem.at[2 + b]))
        own_copies.append(pltpu.make_async_copy(gy.at[b, y], gy_own.at[b], own_sem.at[4 + b]))
    for copy in own_copies:
        copy.start()
    pl.semaphore_wait(barrier, len(friends))

    rcopy(
        rp.at[pl.ds(pl.multiple_of(oc * 256, 256), 256)], rp_in, send.at[RC_S], recv.at[RC_S], partner
    )
    rcopy(gz.at[1], rz1, send.at[Z1_S], recv.at[Z1_S], far)
    for b in range(2):
        for i in (1, 3, 2):
            xx, yy = lax.rem(x + i, 4), lax.rem(y + i, 4)
            rcopy(gx.at[b, xx], rx1.at[x, b], send.at[X1_S], recv.at[X1_S], (bucket, xx * 4 + y))
            rcopy(gy.at[b, yy], ry1.at[y, b], send.at[Y1_S], recv.at[Y1_S], (bucket, x * 4 + yy))
    for copy in own_copies:
        copy.wait()

    wait_bytes(rp_in, recv.at[RC_S])
    r1b[...] = (rp_own[...] + rp_in[...]).astype(BF16)
    for j in range(1, NS):
        ss = shard_peer(j)
        rows = r1b.at[pl.ds(pl.multiple_of(ss * 16, 16), 16)]
        rcopy(rows, r2in.at[shard], send.at[R2_S], recv.at[R2_S], (bucket, ss))
    r2in[shard] = r1b[pl.ds(pl.multiple_of(shard * 16, 16), 16), :]
    my_rows = pl.ds(pl.multiple_of(shard * NEG_OWN, NEG_OWN), NEG_OWN)
    wait_bytes(rx1.at[pl.ds(0, 3)], recv.at[X1_S])
    for b in range(2):
        total = gx_own[b].astype(F32)
        for i in range(1, 4):
            total = total + rx1[lax.rem(x + i, 4), b].astype(F32)
        ax[b] = total.astype(BF16)
    for i in range(4):
        yy = lax.rem(y + i, 4)
        rows = pl.ds(pl.multiple_of(yy * NEG_OWN, NEG_OWN), NEG_OWN)
        if i:
            rcopy(ax.at[0, rows], rx2.at[y], send.at[X2_S], recv.at[X2_S], (bucket, x * 4 + yy))
        else:
            rx2[y] = ax[0, rows, :]
        rcopy(
            ax.at[1, rows], rx2.at[4 + y], send.at[X2_S], recv.at[X2_S], (z_far * 2 + c, x * 4 + yy)
        )
    wait_bytes(ry1.at[pl.ds(0, 3)], recv.at[Y1_S])
    for b in range(2):
        total = gy_own[b].astype(F32)
        for i in range(1, 4):
            total = total + ry1[lax.rem(y + i, 4), b].astype(F32)
        ay[b] = total.astype(BF16)
    for i in range(4):
        xx = lax.rem(x + i, 4)
        if i:
            rcopy(ay.at[0, xx], ry2.at[x], send.at[Y2_S], recv.at[Y2_S], (bucket, xx * 4 + y))
        else:
            ry2[x] = ay[0, x]
        rcopy(
            ay.at[1, xx], ry2.at[4 + x], send.at[Y2_S], recv.at[Y2_S], (z_far * 2 + c, xx * 4 + y)
        )
    wait_bytes(rz1, recv.at[Z1_S])

    def sum_z(r, carry):
        rr = pl.ds(pl.multiple_of(r * 256, 256), 256)
        total = gz_own[:, rr].astype(F32) + rz1[:, rr].astype(F32)
        wide_sum = jnp.concatenate([total, jnp.zeros((256 - (D - 256), 256), F32)], axis=0)
        az[rr, :] = wide_sum.T.astype(BF16)
        return carry

    lax.fori_loop(0, 4, sum_z, 0)
    for j in range(1, NS):
        ss = shard_peer(j)
        rows = az.at[pl.ds(pl.multiple_of(ss * NEG_OWN, NEG_OWN), NEG_OWN)]
        rcopy(rows, rz2.at[shard], send.at[Z2_S], recv.at[Z2_S], (bucket, ss))
    rz2[shard] = az[my_rows, :]

    wait_bytes(r2in.at[pl.ds(0, NS - 1)], recv.at[R2_S])
    r2 = r2in[0].astype(F32)
    for i in range(1, NS):
        r2 = r2 + r2in[i].astype(F32)
    r2all[z] = r2
    for k in (1, 3, 2):
        zz = lax.rem(z + k, NZ)
        rcopy(r2all.at[z], r2all.at[z], send.at[R3_S], recv.at[R3_S], (zz * 2 + c, shard))
    wait_bytes(r2all.at[pl.ds(0, 3)], recv.at[R3_S])
    rel_row = pl.ds(pl.multiple_of(c * 256 + shard * 16, 16), 16)
    rfin[rel_row, :] = ((r2all[0] + r2all[1]) + r2all[2]) + r2all[3]
    for j in range(1, NS):
        ss = shard_peer(j)
        rcopy(rfin.at[rel_row], rfin.at[rel_row], send.at[R4_S], recv.at[R4_S], (bucket, ss))

    wait_bytes(rfin.at[pl.ds(0, 240)], recv.at[R4_S])
    half_rel = rfin.at[half]
    rcopy(half_rel, half_rel, send.at[R5_S], recv.at[R5_S], partner)

    def sum16(ref):
        total = ref[0].astype(F32)
        for i in range(1, ref.shape[0]):
            total = total + ref[i].astype(F32)
        return total

    wait_bytes(rx2.at[pl.ds(0, 7)], recv.at[X2_S])
    neg_out[:, 0:128] = sum16(rx2)
    wait_bytes(ry2.at[pl.ds(0, 7)], recv.at[Y2_S])
    neg_out[:, 128:256] = sum16(ry2)
    wait_bytes(rz2.at[pl.ds(0, NS - 1)], recv.at[Z2_S])
    neg_out[:, 256:D] = sum16(rz2)[:, 0 : D - 256]

    wait_bytes(half_rel, recv.at[R5_S])
    for r in range(4):
        rr = slice(r * 128, (r + 1) * 128)
        wide = jnp.concatenate([rfin[rr, :], jnp.zeros((128, DP - D), F32)], axis=1)
        rel_out[:, rr] = wide.T[0:D]

    wait_bytes(rp_in, send.at[RC_S])
    wait_bytes(r2in.at[pl.ds(0, NS - 1)], send.at[R2_S])
    wait_bytes(r2all.at[pl.ds(0, 3)], send.at[R3_S])
    wait_bytes(rfin.at[pl.ds(0, 240)], send.at[R4_S])
    wait_bytes(half_rel, send.at[R5_S])
    wait_bytes(rz1, send.at[Z1_S])
    wait_bytes(rx1.at[pl.ds(0, 3)], send.at[X1_S])
    wait_bytes(ry1.at[pl.ds(0, 3)], send.at[Y1_S])
    wait_bytes(rx2.at[pl.ds(0, 7)], send.at[X2_S])
    wait_bytes(ry2.at[pl.ds(0, 7)], send.at[Y2_S])
    wait_bytes(rz2.at[pl.ds(0, NS - 1)], send.at[Z2_S])


def scatter_kernel(arrived, ent_out, row_ids):
    r = pl.program_id(0)

    @pl.when(r == 0)
    def _():
        lane = iota((8, 128), 1)
        unit = jnp.where(lane == D - 384, 32.0, jnp.where(lane == D - 383, 1.0, 0.0)).astype(BF16)
        row_ids[...] = nt(unit, arrived[:, 384:DP])

    hot = hot_where((iota((256, 2048), 0) + r * 256).astype(F32) == row_ids[0:1, :])
    ent_out[...] = nn(hot, arrived[...]).T[0:D]


EDGE_SCRATCH = [
    ((16, D, 128), BF16),
    ((D, NEG_DEV), BF16),
    ((NEG_DEV, DP), BF16),
    ((2, 8, NEG_DEV, EC), BF16),
    ((8, DP, EC), BF16),
    ((8, 8, EC), F32),
    ((2, D, EC), F32),
    ((2, D, EC), F32),
    ((2, D, EC), F32),
    ((2, 8, 8, EC), F32),
    ((8, 8, EC), F32),
    ((8, 8, EC), F32),
    ((8, 8, EC), F32),
    ((8, 8, EC), F32),
    ((8, D, EC), F32),
    ((2, D, EC), F32),
    ((2, D, EC), F32),
    ((2, D, EC), BF16),
    ((2, D, EC), BF16),
    ((8, 8, EC), F32),
    ((8, DP, EC), BF16),
    ((DP, 2 * E_DEV), BF16),
    ((D, E_DEV), BF16),
    ((D, E_DEV), BF16),
    ((NB, 256, DP), BF16),
    ((NB, 256, 128), F32),
    ((NB, 256, 128), F32),
    ((2, D - 256, NEG_DEV), BF16),
    ((2, 4, 256, 128), BF16),
    ((2, 4, 4, NEG_OWN, 128), BF16),
    ((REL, D), F32),
]
SUM_SCRATCH = [
    ((2, 256, 128), BF16),
    ((2, 4, NEG_OWN, 128), BF16),
    ((D - 256, NEG_DEV), BF16),
    ((REL // 2, D), F32),
    ((D - 256, NEG_DEV), BF16),
    ((4, 2, 256, 128), BF16),
    ((4, 2, 4, NEG_OWN, 128), BF16),
    ((NEG_DEV, 256), BF16),
    ((2, 256, 128), BF16),
    ((2, 4, NEG_OWN, 128), BF16),
    ((NS, NEG_OWN, 256), BF16),
    ((8, NEG_OWN, 128), BF16),
    ((8, NEG_OWN, 128), BF16),
    ((REL // 2, D), F32),
    ((REL // 2, D), BF16),
    ((NS, 16, D), BF16),
    ((NZ, 16, D), F32),
    ((REL, D), F32),
]


def per_device(
    head_rows, tail_rows, rel_ids, relations, edge_weights, neg_rows, send_slots, dest_rows
):
    vmem = pl.BlockSpec(memory_space=pltpu.VMEM)
    anywhere = pl.BlockSpec(memory_space=pl.ANY)
    packed, gx, gy, gz, rp = pl.pallas_call(
        edge_kernel,
        out_shape=(
            jax.ShapeDtypeStruct((NB, 256, DP), BF16),
            jax.ShapeDtypeStruct((2, 4, 256, 128), BF16),
            jax.ShapeDtypeStruct((2, 4, 4, NEG_OWN, 128), BF16),
            jax.ShapeDtypeStruct((2, D - 256, NEG_DEV), BF16),
            jax.ShapeDtypeStruct((REL, D), F32),
        ),
        in_specs=[vmem] * 8,
        out_specs=(anywhere,) * 5,
        scratch_shapes=[pltpu.VMEM(shape, dtype) for shape, dtype in EDGE_SCRATCH]
        + [
            pltpu.SemaphoreType.DMA((16,)),
            pltpu.SemaphoreType.DMA((16,)),
            pltpu.SemaphoreType.DMA((8,)),
        ],
        compiler_params=pltpu.CompilerParams(
            collective_id=0, has_side_effects=True, vmem_limit_bytes=60 * 1024 * 1024
        ),
        cost_estimate=pl.CostEstimate(
            flops=2 * 3 * 1024 * 4096 * 400, bytes_accessed=8 * 1024 * 1024, transcendentals=1024 * 4096
        ),
        name="edge_part",
    )(
        head_rows.T,
        tail_rows.T,
        rel_ids.reshape(1, E_DEV),
        relations.T,
        edge_weights.reshape(1, E_DEV),
        neg_rows.T,
        send_slots.T,
        dest_rows.T,
    )
    arrived = lax.all_to_all(
        packed.reshape(NB * NS, SLOT, DP), ("bucket", "shard"), split_axis=0, concat_axis=0, tiled=True
    )
    neg_grad, rel_t = pl.pallas_call(
        sum_kernel,
        out_shape=(
            jax.ShapeDtypeStruct((NEG_OWN, D), F32),
            jax.ShapeDtypeStruct((D, REL), F32),
        ),
        in_specs=[anywhere] * 4,
        out_specs=(vmem,) * 2,
        scratch_shapes=[pltpu.VMEM(shape, dtype) for shape, dtype in SUM_SCRATCH]
        + [
            pltpu.SemaphoreType.DMA((11,)),
            pltpu.SemaphoreType.DMA((11,)),
            pltpu.SemaphoreType.DMA((6,)),
        ],
        compiler_params=pltpu.CompilerParams(
            collective_id=1, has_side_effects=True, vmem_limit_bytes=32 * 1024 * 1024
        ),
        cost_estimate=pl.CostEstimate(flops=0, bytes_accessed=64 * 1024 * 1024, transcendentals=0),
        name="sum_part",
    )(gx, gy, gz, rp)
    ent_t = pl.pallas_call(
        scatter_kernel,
        grid=(4,),
        out_shape=jax.ShapeDtypeStruct((D, ENT_DEV), F32),
        in_specs=[vmem],
        out_specs=pl.BlockSpec((D, 256), lambda r: (0, r)),
        scratch_shapes=[pltpu.VMEM((8, 2048), F32)],
        compiler_params=pltpu.CompilerParams(vmem_limit_bytes=32 * 1024 * 1024),
        cost_estimate=pl.CostEstimate(
            flops=2 * 1024 * 2048 * 512, bytes_accessed=4 * 1024 * 1024, transcendentals=0
        ),
        name="scatter_part",
    )(arrived.reshape(2048, DP))
    return ent_t.T, neg_grad, rel_t.T


def solution(mesh):
    return jax.shard_map(
        per_device,
        mesh=mesh,
        in_specs=(
            P(("bucket", "shard"), None),
            P(("bucket", "shard"), None),
            P(("bucket", "shard")),
            P(),
            P(("bucket", "shard")),
            P("bucket", None),
            P(("bucket", "shard"), None),
            P(("bucket", "shard"), None),
        ),
        out_specs=(P(("bucket", "shard"), None), P(("bucket", "shard"), None), P()),
        check_vma=False,
    )
```

```python
import functools

import jax
import jax.numpy as jnp
from jax import lax
from jax.experimental import pallas as pl
from jax.experimental.pallas import tpu as pltpu
from jax.sharding import PartitionSpec as P

D = 400
HALF = 200
DP = 512
E_DEV = 512
ENT_DEV = 1024
REL = 512
NEG_DEV = 1024
SLOT = 16
NB = 8
NS = 16
NZ = 4
EC = 256
NEG_OWN = 64

MESH = pl.DeviceIdType.MESH
F32 = jnp.float32
BF16 = jnp.bfloat16

(Q1_S, SQ1_S, Q2_S, SQ2_S, Q3_S, SQ3_S, ST1_S, O1_S, SC1_S, O2_S, ST2_S, O3_S, SC2_S,
 RC_S, R2_S, R3_S, R4_S, R5_S, ENT_S, Z1_S, X1_S, Y1_S, Z2_S, X2_S, Y2_S, GZ_S, GX_S, GY_S) = range(28)


def nt(a, b):
    return lax.dot_general(a, b, (((1,), (1,)), ((), ())), preferred_element_type=F32)


def nn(a, b):
    return jnp.dot(a, b, preferred_element_type=F32)


def iota(shape, dim):
    return lax.broadcasted_iota(jnp.int32, shape, dim)


def hot_where(mask):
    return mask.astype(F32).astype(BF16)


def wait_bytes(ref, sem):
    pltpu.make_async_copy(ref, ref, sem).wait()


def kernel(
    head, tail, ids, rel, wts, neg, slots, drows,
    ent_out, neg_out, rel_out,
    nbt, wide, nb, prob, qt, sq, hts, tts, rts, mb, st, st_in, sc, sc_in,
    ot, ot_pair, ot_own, o_sum, o_far, lt, qs, ends, rt_hi, rt_lo,
    packed, arrived, slot_col, dest_col,
    gz, gx, gy, rz1, rx1, ry1, az, ax, ay, rz2, rx2, ry2,
    rp, rp_in, r1b, r2in, r2all, rfin,
    send, recv,
):
    bucket, shard = lax.axis_index("bucket"), lax.axis_index("shard")
    z, c = bucket // 2, bucket % 2
    x, y = shard // 4, shard % 4
    oc = 1 - c
    me = bucket * NS + shard
    partner = (z * 2 + oc, shard)
    pair = ((z + 1 - 2 * (z % 2)) * 2 + c, shard)
    z_far = 3 - z
    far = (z_far * 2 + c, shard)

    def rcopy(src, dst, s_sem, r_sem, device):
        pltpu.make_async_remote_copy(
            src_ref=src, dst_ref=dst, send_sem=s_sem, recv_sem=r_sem,
            device_id=device, device_id_type=MESH,
        ).start()

    barrier = pltpu.get_barrier_semaphore()

    def greet(i, carry):
        d = lax.rem(me + i, NB * NS)
        pl.semaphore_signal(barrier, inc=1, device_id=(d // NS, d % NS), device_id_type=MESH)
        return carry

    lax.fori_loop(1, NB * NS, greet, 0)

    for g in range(8):
        qt[g, D:DP, :] = jnp.zeros((DP - D, EC), BF16)
    wide[D:, :] = jnp.ones((16, NEG_DEV), BF16)

    for i in range(8):
        nbt[i] = neg[:, i * 128 : (i + 1) * 128]

    rel_1 = rel[...].astype(BF16)
    rest = rel[...] - rel_1.astype(F32)
    rel_2 = rest.astype(BF16)
    rel_3 = (rest - rel_2.astype(F32)).astype(BF16)
    for j in range(2):
        cols = slice(j * EC, (j + 1) * EC)
        h_t = head[:, cols].astype(F32)
        t_t = tail[:, cols].astype(F32)
        hot = hot_where(iota((REL, EC), 0) == ids[0:1, cols])
        r_t = (nn(rel_1, hot) + nn(rel_2, hot)) + nn(rel_3, hot)
        hre, him = h_t[:HALF], h_t[HALF:]
        rre, rim = r_t[:HALF], r_t[HALF:]
        q = jnp.concatenate([hre * rre - him * rim, hre * rim + him * rre], axis=0).astype(BF16)
        qt[2 * c + j, 0:D, :] = q
        sq[2 * c + j, 0:1, :] = jnp.sum(q.astype(F32) * t_t, axis=0, keepdims=True)
        sq[2 * c + j, 1:2, :] = wts[0:1, cols]
        sq[2 * c + j, 2:8, :] = jnp.zeros((6, EC), F32)
        hts[j] = h_t
        tts[j] = t_t
        rts[j] = r_t

    pl.semaphore_wait(barrier, NB * NS - 1)

    for i in (x, 4 + y):
        rcopy(nbt.at[i], nbt.at[8 + i], send.at[GZ_S], recv.at[GZ_S], far)
    mine, theirs, real = pl.ds(2 * c, 2), pl.ds(4 + 2 * c, 2), pl.ds(0, D)
    rcopy(qt.at[mine, real], qt.at[mine, real], send.at[Q1_S], recv.at[Q1_S], partner)
    rcopy(sq.at[mine], sq.at[mine], send.at[SQ1_S], recv.at[SQ1_S], partner)
    rcopy(qt.at[mine, real], qt.at[theirs, real], send.at[Q2_S], recv.at[Q2_S], pair)
    rcopy(sq.at[mine], sq.at[theirs], send.at[SQ2_S], recv.at[SQ2_S], pair)

    ones = jnp.ones((SLOT, 128), BF16)
    tables = []
    for ref in (slots, drows):
        value = ref[...].astype(F32)
        high = jnp.floor(value * (1.0 / 32.0))
        tables.append((high.astype(BF16), (value - 32.0 * high).astype(BF16)))

    def columns(b, carry):
        owner_hot = hot_where(iota((256, 128), 1) == iota((256, 128), 0) // SLOT + b * NS)
        keep = iota((256, SLOT), 1) == iota((256, SLOT), 0) % SLOT
        for (high, low), out in zip(tables, (slot_col, dest_col)):
            h = jnp.where(keep, nt(owner_hot, high), 0.0).astype(BF16)
            l = jnp.where(keep, nt(owner_hot, low), 0.0).astype(BF16)
            out[b] = 32.0 * nn(h, ones) + nn(l, ones)
        return carry

    lax.fori_loop(0, NB, columns, 0)
    nb[:, 384:DP] = jnp.zeros((NEG_DEV, 128), BF16)

    def flip(b):
        for i in range(8):
            part = nbt[b * 8 + i]
            wide[0:D, i * 128 : (i + 1) * 128] = part
            nb[i * 128 : (i + 1) * 128, 0:D] = part.astype(F32).T.astype(BF16)

    def block(b, two):

        chunks = (2 * two, 2 * two + 1)
        scores = [nn(nb[...], qt[g]) for g in chunks]
        for g, s in zip(chunks, scores):
            m = jnp.max(s, axis=0, keepdims=True)
            pb = jnp.exp(s - m).astype(BF16)
            prob[b, :, pl.ds(pl.multiple_of(g * EC, EC), EC)] = pb
            o = nn(wide[...], pb)
            l = o[D : D + 1]
            o = o[0:D]
            mb[b, g, 0:1, :] = m
            if b == 0:
                st[g, 0:1, :] = m
                st[g, 1:2, :] = l
                st[g, 2:8, :] = jnp.zeros((6, EC), F32)
                ot[g] = o
            else:
                m_old = st[g, 0:1, :]
                m_new = jnp.maximum(m_old, m)
                f_old = jnp.exp(m_old - m_new)
                f_new = jnp.exp(m - m_new)
                st[g, 0:1, :] = m_new
                st[g, 1:2, :] = st[g, 1:2, :] * f_old + l * f_new
                ot[g] = ot[g] * f_old + o * f_new

    flip(0)
    block(0, c)
    wait_bytes(nbt.at[pl.ds(8, 2)], recv.at[GZ_S])
    for i in (1, 3, 2):
        xx, yy = lax.rem(x + i, 4), lax.rem(y + i, 4)
        rcopy(nbt.at[8 + x], nbt.at[8 + x], send.at[GX_S], recv.at[GX_S], (bucket, xx * 4 + y))
        rcopy(nbt.at[12 + y], nbt.at[12 + y], send.at[GY_S], recv.at[GY_S], (bucket, x * 4 + yy))
    wait_bytes(qt.at[mine, real], recv.at[Q1_S])
    wait_bytes(sq.at[mine], recv.at[SQ1_S])
    block(0, oc)
    wait_bytes(qt.at[mine, real], recv.at[Q2_S])
    wait_bytes(sq.at[mine], recv.at[SQ2_S])
    rcopy(qt.at[theirs, real], qt.at[theirs, real], send.at[Q3_S], recv.at[Q3_S], partner)
    rcopy(sq.at[theirs], sq.at[theirs], send.at[SQ3_S], recv.at[SQ3_S], partner)
    block(0, 2 + c)
    wait_bytes(qt.at[mine, real], recv.at[Q3_S])
    wait_bytes(sq.at[mine], recv.at[SQ3_S])
    block(0, 2 + oc)
    wait_bytes(nbt.at[pl.ds(8, 3)], recv.at[GX_S])
    wait_bytes(nbt.at[pl.ds(8, 3)], recv.at[GY_S])
    flip(1)
    block(1, 2 + oc)
    rcopy(
        ot.at[pl.ds(4 + 2 * oc, 2)], ot_pair, send.at[O1_S], recv.at[O1_S], partner
    )
    block(1, 2 + c)
    own_half, pair_half = pl.ds(0, 4), pl.ds(4, 4)
    rcopy(st.at[pair_half], st_in.at[pair_half], send.at[ST1_S], recv.at[ST1_S], partner)

    def merge(g):
        m_a, m_b = st[g, 0:1, :], st_in[g, 0:1, :]
        m = jnp.maximum(m_a, m_b)
        f_a, f_b = jnp.exp(m_a - m), jnp.exp(m_b - m)
        sc[g, 0:1, :] = m
        sc[g, 1:2, :] = st[g, 1:2, :] * f_a + st_in[g, 1:2, :] * f_b
        sc[g, 2:8, :] = jnp.zeros((6, EC), F32)
        return f_a, f_b

    block(1, oc)
    rcopy(ot.at[pl.ds(2 * oc, 2)], ot_own, send.at[O3_S], recv.at[O3_S], partner)
    wait_bytes(st_in.at[pair_half], recv.at[ST1_S])
    wait_bytes(ot_pair, recv.at[O1_S])
    for g in range(4, 8):
        merge(g)
    for j in range(2):
        f_a, f_b = merge(4 + 2 * c + j)
        o_sum[j] = (ot[4 + 2 * c + j] * f_a + ot_pair[j] * f_b).astype(BF16)
    rcopy(sc.at[pair_half], sc_in.at[own_half], send.at[SC1_S], recv.at[SC1_S], pair)
    block(1, c)
    rcopy(st.at[own_half], st_in.at[own_half], send.at[ST2_S], recv.at[ST2_S], partner)
    wait_bytes(st_in.at[own_half], recv.at[ST2_S])
    for g in range(4):
        merge(g)
    rcopy(sc.at[own_half], sc_in.at[pair_half], send.at[SC2_S], recv.at[SC2_S], pair)
    rcopy(o_sum, o_far, send.at[O2_S], recv.at[O2_S], pair)
    wait_bytes(sc_in.at[own_half], recv.at[SC1_S])
    wait_bytes(sc_in.at[pair_half], recv.at[SC2_S])
    for g in range(8):
        pos = sq[g, 0:1, :]
        m0, m1 = sc[g, 0:1, :], sc_in[g, 0:1, :]
        top = jnp.maximum(pos, jnp.maximum(m0, m1))
        total = (
            jnp.exp(pos - top)
            + sc[g, 1:2, :] * jnp.exp(m0 - top)
            + sc_in[g, 1:2, :] * jnp.exp(m1 - top)
        )
        lt[g, 0:1, :] = top + jnp.log(total)

    def neg_block(b):
        for g in range(8):
            scale = sq[g, 1:2, :] * jnp.exp(mb[b, g, 0:1, :] - lt[g, 0:1, :])
            qs[:, g * EC : (g + 1) * EC] = (qt[g].astype(F32) * scale).astype(BF16)

        def rows_of(h, carry):
            rr = pl.ds(pl.multiple_of(h * 512, 512), 512)
            acc = nt(prob[b, rr, :], qs[...])
            for u in range(2):
                part = acc[u * 256 : (u + 1) * 256]
                gx[b, 2 * h + u] = part[:, 0:128].astype(BF16)
                for yy in range(4):
                    gy[b, yy, 2 * h + u] = part[yy * 64 : (yy + 1) * 64, 128:256].astype(BF16)
            gz[b, :, rr] = acc[:, 256:512].T[0 : D - 256].astype(BF16)
            return carry

        lax.fori_loop(0, 2, rows_of, 0)
        for i in (1, 3, 2):
            xx, yy = lax.rem(x + i, 4), lax.rem(y + i, 4)
            rcopy(gx.at[b, xx], rx1.at[x, b], send.at[X1_S], recv.at[X1_S], (bucket, xx * 4 + y))
            rcopy(gy.at[b, yy], ry1.at[y, b], send.at[Y1_S], recv.at[Y1_S], (bucket, x * 4 + yy))

    neg_block(1)
    rcopy(gz.at[1], rz1, send.at[Z1_S], recv.at[Z1_S], far)
    wait_bytes(ot_own, recv.at[O3_S])
    wait_bytes(o_far, recv.at[O2_S])
    ends[D:DP, :] = jnp.zeros((DP - D, 2 * E_DEV), BF16)
    for j in range(2):
        cols = slice(j * EC, (j + 1) * EC)
        tail_cols = slice(E_DEV + j * EC, E_DEV + (j + 1) * EC)
        g = 2 * c + j
        pos, w, ltot = sq[g, 0:1, :], sq[g, 1:2, :], lt[g, 0:1, :]
        pos_coef = w * (jnp.exp(pos - ltot) - 1.0)
        own = w * jnp.exp(st[g, 0:1, :] - ltot)
        other = w * jnp.exp(st_in[g, 0:1, :] - ltot)
        away = w * jnp.exp(sc_in[g, 0:1, :] - ltot)
        grad = pos_coef * tts[j] + ot[g] * own + ot_own[j] * other + o_far[j].astype(F32) * away
        gre, gim = grad[:HALF], grad[HALF:]
        rre, rim = rts[j, :HALF, :], rts[j, HALF:, :]
        hre, him = hts[j, :HALF, :], hts[j, HALF:, :]
        ends[0:D, cols] = jnp.concatenate(
            [gre * rre + gim * rim, gim * rre - gre * rim], axis=0
        ).astype(BF16)
        ends[0:D, tail_cols] = (pos_coef * qt[g, 0:D, :].astype(F32)).astype(BF16)
        term = jnp.concatenate([gre * hre + gim * him, gim * hre - gre * him], axis=0)
        hi = term.astype(BF16)
        rt_hi[:, cols] = hi
        rt_lo[:, cols] = (term - hi.astype(F32)).astype(BF16)

    my_slots = pl.ds(pl.multiple_of(me * SLOT, SLOT), SLOT)

    def pack(k, first):
        sel = []
        for u in range(2):
            sc_b = slot_col[lax.rem(bucket + 2 * k + u, NB)]
            sel.append(jnp.concatenate(
                [hot_where(sc_b == (iota((256, 128), 1) + 128 * t).astype(F32)) for t in range(8)],
                axis=1,
            ))
        rows = nt(jnp.concatenate(sel, axis=0), ends[...])
        for u in range(2):
            bb = lax.rem(bucket + 2 * k + u, NB)
            part = rows[u * 256 : (u + 1) * 256]
            dc = dest_col[bb]
            high = jnp.floor(dc * (1.0 / 32.0))
            lane = iota((256, 128), 1)
            code = jnp.where(lane == 16, high, jnp.where(lane == 17, dc - 32.0 * high, 0.0))
            packed[bb, :, 0:384] = part[:, 0:384].astype(BF16)
            packed[bb, :, 384:512] = (part[:, 384:512] + code).astype(BF16)
            for j in range(NS):
                ss = lax.rem(shard + j, NS)
                src = packed.at[bb, pl.ds(pl.multiple_of(ss * SLOT, SLOT), SLOT)]
                if first and u == 0 and j == 0:
                    pltpu.make_async_copy(src, arrived.at[my_slots], recv.at[ENT_S]).start()
                else:
                    rcopy(src, arrived.at[my_slots], send.at[ENT_S], recv.at[ENT_S], (bb, ss))

    def rel_chunk(r, carry):
        hot = hot_where(iota((128, E_DEV), 0) + r * 128 == ids[...])
        rp[pl.ds(pl.multiple_of(r * 128, 128), 128), :] = nt(hot, rt_hi[...]) + nt(hot, rt_lo[...])
        return carry

    lax.fori_loop(0, 4, rel_chunk, 0)
    rcopy(
        rp.at[pl.ds(pl.multiple_of(oc * 256, 256), 256)], rp_in, send.at[RC_S], recv.at[RC_S], partner
    )

    def pack_other(k, carry):
        pack(k, False)
        return carry

    pack(0, True)
    lax.fori_loop(1, 2, pack_other, 0)

    wait_bytes(rp_in, recv.at[RC_S])
    r1b[...] = (rp[pl.ds(pl.multiple_of(c * 256, 256), 256), :] + rp_in[...]).astype(BF16)
    for j in range(1, NS):
        ss = lax.rem(shard + j, NS)
        rows = r1b.at[pl.ds(pl.multiple_of(ss * 16, 16), 16)]
        rcopy(rows, r2in.at[shard], send.at[R2_S], recv.at[R2_S], (bucket, ss))
    r2in[shard] = r1b[pl.ds(pl.multiple_of(shard * 16, 16), 16), :]
    lax.fori_loop(2, NB // 2, pack_other, 0)

    neg_block(0)


    wait_bytes(r2in.at[pl.ds(0, NS - 1)], recv.at[R2_S])
    r2 = r2in[0].astype(F32)
    for i in range(1, NS):
        r2 = r2 + r2in[i].astype(F32)
    r2all[z] = r2
    for k in (1, 3, 2):
        zz = lax.rem(z + k, NZ)
        rcopy(r2all.at[z], r2all.at[z], send.at[R3_S], recv.at[R3_S], (zz * 2 + c, shard))

    my_rows = pl.ds(pl.multiple_of(shard * NEG_OWN, NEG_OWN), NEG_OWN)
    wait_bytes(rx1.at[pl.ds(0, 3)], recv.at[X1_S])
    for b in range(2):
        total = gx[b, x].astype(F32)
        for i in range(1, 4):
            total = total + rx1[lax.rem(x + i, 4), b].astype(F32)
        ax[b] = total.astype(BF16)
    for i in range(4):
        yy = lax.rem(y + i, 4)
        rows = pl.ds(pl.multiple_of(yy * NEG_OWN, NEG_OWN), NEG_OWN)
        if i:
            rcopy(ax.at[0, rows], rx2.at[y], send.at[X2_S], recv.at[X2_S], (bucket, x * 4 + yy))
        else:
            rx2[y] = ax[0, rows, :]
        rcopy(
            ax.at[1, rows], rx2.at[4 + y], send.at[X2_S], recv.at[X2_S], (z_far * 2 + c, x * 4 + yy)
        )
    wait_bytes(r2all.at[pl.ds(0, 3)], recv.at[R3_S])
    rel_row = pl.ds(pl.multiple_of(c * 256 + shard * 16, 16), 16)
    rfin[rel_row, :] = (((r2all[0] + r2all[1]) + r2all[2]) + r2all[3]).astype(BF16)
    for j in range(1, NS):
        ss = lax.rem(shard + j, NS)
        rcopy(rfin.at[rel_row], rfin.at[rel_row], send.at[R4_S], recv.at[R4_S], (bucket, ss))

    wait_bytes(ry1.at[pl.ds(0, 3)], recv.at[Y1_S])
    for b in range(2):
        total = gy[b, y].astype(F32)
        for i in range(1, 4):
            total = total + ry1[lax.rem(y + i, 4), b].astype(F32)
        ay[b] = total.astype(BF16)
    for i in range(4):
        xx = lax.rem(x + i, 4)
        if i:
            rcopy(ay.at[0, xx], ry2.at[x], send.at[Y2_S], recv.at[Y2_S], (bucket, xx * 4 + y))
        else:
            ry2[x] = ay[0, x]
        rcopy(
            ay.at[1, xx], ry2.at[4 + x], send.at[Y2_S], recv.at[Y2_S], (z_far * 2 + c, xx * 4 + y)
        )
    wait_bytes(rz1, recv.at[Z1_S])

    def sum_z(r, carry):
        rr = pl.ds(pl.multiple_of(r * 256, 256), 256)
        total = gz[0, :, rr].astype(F32) + rz1[:, rr].astype(F32)
        wide_sum = jnp.concatenate([total, jnp.zeros((256 - (D - 256), 256), F32)], axis=0)
        az[rr, :] = wide_sum.T.astype(BF16)
        return carry

    lax.fori_loop(0, 4, sum_z, 0)
    for j in range(1, NS):
        ss = lax.rem(shard + j, NS)
        rows = az.at[pl.ds(pl.multiple_of(ss * NEG_OWN, NEG_OWN), NEG_OWN)]
        rcopy(rows, rz2.at[shard], send.at[Z2_S], recv.at[Z2_S], (bucket, ss))
    rz2[shard] = az[my_rows, :]

    wait_bytes(arrived, recv.at[ENT_S])
    lane = iota((8, DP), 1)
    unit = jnp.where(lane == D, 32.0, jnp.where(lane == D + 1, 1.0, 0.0)).astype(BF16)
    row_ids = nt(unit, arrived[...])[0:1, :]

    def scatter(r, carry):
        hot = hot_where((iota((512, 2048), 0) + r * 512).astype(F32) == row_ids)
        got = nn(hot, arrived[...])
        ent_out[:, pl.ds(pl.multiple_of(r * 512, 512), 512)] = got.T[0:D]
        return carry

    lax.fori_loop(0, 2, scatter, 0)

    wait_bytes(rfin.at[pl.ds(0, 240)], recv.at[R4_S])
    half_rel = rfin.at[pl.ds(pl.multiple_of(c * 256, 256), 256)]
    rcopy(half_rel, half_rel, send.at[R5_S], recv.at[R5_S], partner)

    def sum16(ref):
        total = ref[0].astype(F32)
        for i in range(1, ref.shape[0]):
            total = total + ref[i].astype(F32)
        return total

    wait_bytes(rx2.at[pl.ds(0, 7)], recv.at[X2_S])
    neg_out[:, 0:128] = sum16(rx2)
    wait_bytes(ry2.at[pl.ds(0, 7)], recv.at[Y2_S])
    neg_out[:, 128:256] = sum16(ry2)
    wait_bytes(rz2.at[pl.ds(0, NS - 1)], recv.at[Z2_S])
    neg_out[:, 256:D] = sum16(rz2)[:, 0 : D - 256]

    wait_bytes(half_rel, recv.at[R5_S])
    for r in range(4):
        rr = slice(r * 128, (r + 1) * 128)
        wide_rel = jnp.concatenate([rfin[rr, :].astype(F32), jnp.zeros((128, DP - D), F32)], axis=1)
        rel_out[:, rr] = wide_rel.T[0:D]

    wait_bytes(nbt.at[pl.ds(0, 2)], send.at[GZ_S])
    wait_bytes(nbt.at[pl.ds(0, 3)], send.at[GX_S])
    wait_bytes(nbt.at[pl.ds(0, 3)], send.at[GY_S])
    for number in (Q1_S, Q2_S, Q3_S):
        wait_bytes(qt.at[mine, real], send.at[number])
    for number in (SQ1_S, SQ2_S, SQ3_S):
        wait_bytes(sq.at[mine], send.at[number])
    for number in (ST1_S, ST2_S, SC1_S, SC2_S):
        wait_bytes(st.at[own_half], send.at[number])
    wait_bytes(ot_pair, send.at[O1_S])
    wait_bytes(o_far, send.at[O2_S])
    wait_bytes(ot_own, send.at[O3_S])
    wait_bytes(arrived.at[pl.ds(0, 2048 - SLOT)], send.at[ENT_S])
    wait_bytes(rp_in, send.at[RC_S])
    wait_bytes(r2in.at[pl.ds(0, NS - 1)], send.at[R2_S])
    wait_bytes(r2all.at[pl.ds(0, 3)], send.at[R3_S])
    wait_bytes(rfin.at[pl.ds(0, 240)], send.at[R4_S])
    wait_bytes(half_rel, send.at[R5_S])
    wait_bytes(rz1, send.at[Z1_S])
    wait_bytes(rx1.at[pl.ds(0, 3)], send.at[X1_S])
    wait_bytes(ry1.at[pl.ds(0, 3)], send.at[Y1_S])
    wait_bytes(rx2.at[pl.ds(0, 7)], send.at[X2_S])
    wait_bytes(ry2.at[pl.ds(0, 7)], send.at[Y2_S])
    wait_bytes(rz2.at[pl.ds(0, NS - 1)], send.at[Z2_S])


SCRATCH = [
    ((16, D, 128), BF16),
    ((D + 16, NEG_DEV), BF16),
    ((NEG_DEV, DP), BF16),
    ((2, NEG_DEV, 8 * EC), BF16),
    ((8, DP, EC), BF16),
    ((8, 8, EC), F32),
    ((2, D, EC), F32),
    ((2, D, EC), F32),
    ((2, D, EC), F32),
    ((2, 8, 8, EC), F32),
    ((8, 8, EC), F32),
    ((8, 8, EC), F32),
    ((8, 8, EC), F32),
    ((8, 8, EC), F32),
    ((8, D, EC), F32),
    ((2, D, EC), F32),
    ((2, D, EC), F32),
    ((2, D, EC), BF16),
    ((2, D, EC), BF16),
    ((8, 8, EC), F32),
    ((DP, 8 * EC), BF16),
    ((DP, 2 * E_DEV), BF16),
    ((D, E_DEV), BF16),
    ((D, E_DEV), BF16),
    ((NB, 256, DP), BF16),
    ((2048, DP), BF16),
    ((NB, 256, 128), F32),
    ((NB, 256, 128), F32),
    ((2, D - 256, NEG_DEV), BF16),
    ((2, 4, 256, 128), BF16),
    ((2, 4, 4, NEG_OWN, 128), BF16),
    ((D - 256, NEG_DEV), BF16),
    ((4, 2, 256, 128), BF16),
    ((4, 2, 4, NEG_OWN, 128), BF16),
    ((NEG_DEV, 256), BF16),
    ((2, 256, 128), BF16),
    ((2, 4, NEG_OWN, 128), BF16),
    ((NS, NEG_OWN, 256), BF16),
    ((8, NEG_OWN, 128), BF16),
    ((8, NEG_OWN, 128), BF16),
    ((REL, D), F32),
    ((REL // 2, D), F32),
    ((REL // 2, D), BF16),
    ((NS, 16, D), BF16),
    ((NZ, 16, D), F32),
    ((REL, D), BF16),
]


def per_device(
    head_rows, tail_rows, rel_ids, relations, edge_weights, neg_rows, send_slots, dest_rows
):
    vmem = pl.BlockSpec(memory_space=pltpu.VMEM)
    ent_t, neg_grad, rel_t = pl.pallas_call(
        kernel,
        out_shape=(
            jax.ShapeDtypeStruct((D, ENT_DEV), F32),
            jax.ShapeDtypeStruct((NEG_OWN, D), F32),
            jax.ShapeDtypeStruct((D, REL), F32),
        ),
        in_specs=[vmem] * 8,
        out_specs=(vmem,) * 3,
        scratch_shapes=[pltpu.VMEM(shape, dtype) for shape, dtype in SCRATCH]
        + [
            pltpu.SemaphoreType.DMA((28,)),
            pltpu.SemaphoreType.DMA((28,)),
        ],
        compiler_params=pltpu.CompilerParams(
            collective_id=0, has_side_effects=True, vmem_limit_bytes=60 * 1024 * 1024
        ),
        cost_estimate=pl.CostEstimate(
            flops=2 * 3 * 1024 * 4096 * 400, bytes_accessed=8 * 1024 * 1024, transcendentals=1024 * 4096
        ),
        name="complex_backward",
    )(
        head_rows.T,
        tail_rows.T,
        rel_ids.reshape(1, E_DEV),
        relations.T,
        edge_weights.reshape(1, E_DEV),
        neg_rows.T,
        send_slots.T,
        dest_rows.T,
    )
    return ent_t.T, neg_grad, rel_t.T


def solution(mesh):
    return jax.shard_map(
        per_device,
        mesh=mesh,
        in_specs=(
            P(("bucket", "shard"), None),
            P(("bucket", "shard"), None),
            P(("bucket", "shard")),
            P(),
            P(("bucket", "shard")),
            P("bucket", None),
            P(("bucket", "shard"), None),
            P(("bucket", "shard"), None),
        ),
        out_specs=(P(("bucket", "shard"), None), P(("bucket", "shard"), None), P()),
        check_vma=False,
    )
```

```python
import functools

import jax
import jax.numpy as jnp
from jax import lax
from jax.experimental import pallas as pl
from jax.experimental.pallas import tpu as pltpu
from jax.sharding import PartitionSpec as P

D = 400
HALF = 200
DP = 512
E_DEV = 512
ENT_DEV = 1024
REL = 512
NEG_DEV = 1024
SLOT = 16
NB = 8
NS = 16
NZ = 4
EC = 256
NEG_OWN = 64

MESH = pl.DeviceIdType.MESH
F32 = jnp.float32
BF16 = jnp.bfloat16

(Q1_S, SQ1_S, Q2_S, SQ2_S, Q3_S, SQ3_S, ST1_S, O1_S, SC1_S, O2_S, ST2_S, O3_S, SC2_S,
 RC_S, R2_S, R3_S, R4_S, R5_S, ENT_S, Z1_S, X1_S, Y1_S, Z2_S, X2_S, Y2_S, GZ_S, GX_S, GY_S,
 O4_S, PX_S, PY_S) = range(31)


def nt(a, b):
    return lax.dot_general(a, b, (((1,), (1,)), ((), ())), preferred_element_type=F32)


def nn(a, b):
    return jnp.dot(a, b, preferred_element_type=F32)


def iota(shape, dim):
    return lax.broadcasted_iota(jnp.int32, shape, dim)


def hot_where(mask):
    return mask.astype(F32).astype(BF16)


def wait_bytes(ref, sem):
    pltpu.make_async_copy(ref, ref, sem).wait()


def kernel(
    head, tail, ids, rel, wts, neg, slots, drows,
    ent_out, neg_out, rel_out,
    nbt, wide, nb, prob, qt, sq, hts, tts, rts, mb, st, st_in, sc, sc_in,
    ot, ot_pair, ot_own, o_sum, o_far, lt, qs, ends, rt_hi, rt_lo,
    packed, px, arrived, slot_col, dest_col,
    gz, gx, gy, rz1, rx1, ry1, az, ax, ay, rz2, rx2, ry2,
    rp, rp_in, r1b, r2in, r2all, rfin,
    send, recv, known,
):
    bucket, shard = lax.axis_index("bucket"), lax.axis_index("shard")
    z, c = bucket // 2, bucket % 2
    x, y = shard // 4, shard % 4
    oc = 1 - c
    partner = (z * 2 + oc, shard)
    pair = ((z + 1 - 2 * (z % 2)) * 2 + c, shard)
    z_far = 3 - z
    far = (z_far * 2 + c, shard)

    def rcopy(src, dst, s_sem, r_sem, device):
        pltpu.make_async_remote_copy(
            src_ref=src, dst_ref=dst, send_sem=s_sem, recv_sem=r_sem,
            device_id=device, device_id_type=MESH,
        ).start()

    barrier = pltpu.get_barrier_semaphore()

    x_peers = [(bucket, lax.rem(x + i, 4) * 4 + y) for i in (1, 2, 3)]
    y_peers = [(bucket, x * 4 + lax.rem(y + i, 4)) for i in (1, 2, 3)]
    friends = [partner, pair, far] + x_peers + y_peers

    def tell(sem, devices):
        for device in devices:
            pl.semaphore_signal(sem, inc=1, device_id=device, device_id_type=MESH)

    tell(barrier, friends)

    for g in range(8):
        qt[g, D:DP, :] = jnp.zeros((DP - D, EC), BF16)
    wide[D:, :] = jnp.ones((16, NEG_DEV), BF16)

    for i in range(8):
        nbt[i] = neg[:, i * 128 : (i + 1) * 128]

    rel_1 = rel[...].astype(BF16)
    rest = rel[...] - rel_1.astype(F32)
    rel_2 = rest.astype(BF16)
    rel_3 = (rest - rel_2.astype(F32)).astype(BF16)
    for j in range(2):
        cols = slice(j * EC, (j + 1) * EC)
        h_t = head[:, cols].astype(F32)
        t_t = tail[:, cols].astype(F32)
        hot = hot_where(iota((REL, EC), 0) == ids[0:1, cols])
        r_t = (nn(rel_1, hot) + nn(rel_2, hot)) + nn(rel_3, hot)
        hre, him = h_t[:HALF], h_t[HALF:]
        rre, rim = r_t[:HALF], r_t[HALF:]
        q = jnp.concatenate([hre * rre - him * rim, hre * rim + him * rre], axis=0).astype(BF16)
        qt[2 * c + j, 0:D, :] = q
        sq[2 * c + j, 0:1, :] = jnp.sum(q.astype(F32) * t_t, axis=0, keepdims=True)
        sq[2 * c + j, 1:2, :] = wts[0:1, cols]
        sq[2 * c + j, 2:8, :] = jnp.zeros((6, EC), F32)
        hts[j] = h_t
        tts[j] = t_t
        rts[j] = r_t

    pl.semaphore_wait(barrier, len(friends))
    tell(known.at[0], y_peers)

    for i in (x, 4 + y):
        rcopy(nbt.at[i], nbt.at[8 + i], send.at[GZ_S], recv.at[GZ_S], far)
    mine, theirs, real = pl.ds(2 * c, 2), pl.ds(4 + 2 * c, 2), pl.ds(0, D)
    rcopy(qt.at[mine, real], qt.at[mine, real], send.at[Q1_S], recv.at[Q1_S], partner)
    rcopy(sq.at[mine], sq.at[mine], send.at[SQ1_S], recv.at[SQ1_S], partner)
    rcopy(qt.at[mine, real], qt.at[theirs, real], send.at[Q2_S], recv.at[Q2_S], pair)
    rcopy(sq.at[mine], sq.at[theirs], send.at[SQ2_S], recv.at[SQ2_S], pair)

    ones = jnp.ones((SLOT, 128), BF16)
    tables = []
    for ref in (slots, drows):
        value = ref[...].astype(F32)
        high = jnp.floor(value * (1.0 / 32.0))
        tables.append((high.astype(BF16), (value - 32.0 * high).astype(BF16)))

    def columns(b, carry):
        owner_hot = hot_where(iota((256, 128), 1) == iota((256, 128), 0) // SLOT + b * NS)
        keep = iota((256, SLOT), 1) == iota((256, SLOT), 0) % SLOT
        for (high, low), out in zip(tables, (slot_col, dest_col)):
            h = jnp.where(keep, nt(owner_hot, high), 0.0).astype(BF16)
            l = jnp.where(keep, nt(owner_hot, low), 0.0).astype(BF16)
            out[b] = 32.0 * nn(h, ones) + nn(l, ones)
        return carry

    lax.fori_loop(0, NB, columns, 0)
    nb[:, 384:DP] = jnp.zeros((NEG_DEV, 128), BF16)

    def flip(b):
        for i in range(8):
            part = nbt[b * 8 + i]
            wide[0:D, i * 128 : (i + 1) * 128] = part
            nb[i * 128 : (i + 1) * 128, 0:D] = part.astype(F32).T.astype(BF16)

    def block(b, two):

        chunks = (2 * two, 2 * two + 1)
        scores = [nn(nb[...], qt[g]) for g in chunks]
        for g, s in zip(chunks, scores):
            m = jnp.max(s, axis=0, keepdims=True)
            pb = jnp.exp(s - m).astype(BF16)
            prob[b, :, pl.ds(pl.multiple_of(g * EC, EC), EC)] = pb
            o = nn(wide[...], pb)
            l = o[D : D + 1]
            o = o[0:D]
            mb[b, g, 0:1, :] = m
            if b == 0:
                st[g, 0:1, :] = m
                st[g, 1:2, :] = l
                st[g, 2:8, :] = jnp.zeros((6, EC), F32)
                ot[g] = o
            else:
                m_old = st[g, 0:1, :]
                m_new = jnp.maximum(m_old, m)
                f_old = jnp.exp(m_old - m_new)
                f_new = jnp.exp(m - m_new)
                st[g, 0:1, :] = m_new
                st[g, 1:2, :] = st[g, 1:2, :] * f_old + l * f_new
                ot[g] = ot[g] * f_old + o * f_new

    flip(0)
    block(0, c)
    pl.semaphore_wait(known.at[0], 3)
    tell(known.at[1], (pair, far))
    wait_bytes(nbt.at[pl.ds(8, 2)], recv.at[GZ_S])
    for i in (1, 3, 2):
        xx, yy = lax.rem(x + i, 4), lax.rem(y + i, 4)
        rcopy(nbt.at[8 + x], nbt.at[8 + x], send.at[GX_S], recv.at[GX_S], (bucket, xx * 4 + y))
        rcopy(nbt.at[12 + y], nbt.at[12 + y], send.at[GY_S], recv.at[GY_S], (bucket, x * 4 + yy))
    wait_bytes(qt.at[mine, real], recv.at[Q1_S])
    wait_bytes(sq.at[mine], recv.at[SQ1_S])
    block(0, oc)
    pl.semaphore_wait(known.at[1], 2)
    tell(known.at[2], (pair, far))
    wait_bytes(qt.at[mine, real], recv.at[Q2_S])
    wait_bytes(sq.at[mine], recv.at[SQ2_S])
    rcopy(qt.at[theirs, real], qt.at[theirs, real], send.at[Q3_S], recv.at[Q3_S], partner)
    rcopy(sq.at[theirs], sq.at[theirs], send.at[SQ3_S], recv.at[SQ3_S], partner)
    block(0, 2 + c)
    wait_bytes(qt.at[mine, real], recv.at[Q3_S])
    wait_bytes(sq.at[mine], recv.at[SQ3_S])
    block(0, 2 + oc)
    wait_bytes(nbt.at[pl.ds(8, 3)], recv.at[GX_S])
    wait_bytes(nbt.at[pl.ds(8, 3)], recv.at[GY_S])
    flip(1)
    block(1, 2 + oc)
    pl.semaphore_wait(known.at[2], 2)
    rcopy(
        ot.at[pl.ds(4 + 2 * oc, 2)], ot_pair, send.at[O1_S], recv.at[O1_S], partner
    )
    block(1, 2 + c)
    own_half, pair_half = pl.ds(0, 4), pl.ds(4, 4)
    rcopy(st.at[pair_half], st_in.at[pair_half], send.at[ST1_S], recv.at[ST1_S], partner)

    def merge(g):
        m_a, m_b = st[g, 0:1, :], st_in[g, 0:1, :]
        m = jnp.maximum(m_a, m_b)
        f_a, f_b = jnp.exp(m_a - m), jnp.exp(m_b - m)
        sc[g, 0:1, :] = m
        sc[g, 1:2, :] = st[g, 1:2, :] * f_a + st_in[g, 1:2, :] * f_b
        sc[g, 2:8, :] = jnp.zeros((6, EC), F32)
        return f_a, f_b

    block(1, oc)
    rcopy(ot.at[pl.ds(2 * oc, 2)], ot_own, send.at[O3_S], recv.at[O3_S], partner)
    wait_bytes(st_in.at[pair_half], recv.at[ST1_S])
    wait_bytes(ot_pair, recv.at[O1_S])
    for g in range(4, 8):
        merge(g)
    for j in range(2):
        f_a, f_b = merge(4 + 2 * c + j)
        o_sum[j] = (ot[4 + 2 * c + j] * f_a + ot_pair[j] * f_b).astype(BF16)
    rcopy(o_sum.at[0], o_far.at[0], send.at[O4_S], recv.at[O4_S], pair)
    rcopy(sc.at[pair_half], sc_in.at[own_half], send.at[SC1_S], recv.at[SC1_S], pair)
    block(1, c)
    rcopy(st.at[own_half], st_in.at[own_half], send.at[ST2_S], recv.at[ST2_S], partner)
    wait_bytes(st_in.at[own_half], recv.at[ST2_S])
    for g in range(4):
        merge(g)
    rcopy(sc.at[own_half], sc_in.at[pair_half], send.at[SC2_S], recv.at[SC2_S], pair)
    rcopy(o_sum.at[1], o_far.at[1], send.at[O2_S], recv.at[O2_S], pair)
    wait_bytes(sc_in.at[own_half], recv.at[SC1_S])
    wait_bytes(sc_in.at[pair_half], recv.at[SC2_S])
    for g in range(8):
        pos = sq[g, 0:1, :]
        m0, m1 = sc[g, 0:1, :], sc_in[g, 0:1, :]
        top = jnp.maximum(pos, jnp.maximum(m0, m1))
        total = (
            jnp.exp(pos - top)
            + sc[g, 1:2, :] * jnp.exp(m0 - top)
            + sc_in[g, 1:2, :] * jnp.exp(m1 - top)
        )
        lt[g, 0:1, :] = top + jnp.log(total)

    def neg_block(b):
        for g in range(8):
            scale = sq[g, 1:2, :] * jnp.exp(mb[b, g, 0:1, :] - lt[g, 0:1, :])
            qs[:, g * EC : (g + 1) * EC] = (qt[g].astype(F32) * scale).astype(BF16)

        def rows_of(h, carry):
            rr = pl.ds(pl.multiple_of(h * 512, 512), 512)
            acc = nt(prob[b, rr, :], qs[...])
            for u in range(2):
                part = acc[u * 256 : (u + 1) * 256]
                gx[b, 2 * h + u] = part[:, 0:128].astype(BF16)
                for yy in range(4):
                    gy[b, yy, 2 * h + u] = part[yy * 64 : (yy + 1) * 64, 128:256].astype(BF16)
            gz[b, :, rr] = acc[:, 256:512].T[0 : D - 256].astype(BF16)
            return carry

        lax.fori_loop(0, 2, rows_of, 0)
        for i in (1, 3, 2):
            xx, yy = lax.rem(x + i, 4), lax.rem(y + i, 4)
            rcopy(gx.at[b, xx], rx1.at[x, b], send.at[X1_S], recv.at[X1_S], (bucket, xx * 4 + y))
            rcopy(gy.at[b, yy], ry1.at[y, b], send.at[Y1_S], recv.at[Y1_S], (bucket, x * 4 + yy))

    neg_block(1)
    rcopy(gz.at[1], rz1, send.at[Z1_S], recv.at[Z1_S], far)
    neg_block(0)
    wait_bytes(ot_own, recv.at[O3_S])
    wait_bytes(o_far.at[0], recv.at[O4_S])
    wait_bytes(o_far.at[1], recv.at[O2_S])
    ends[D:DP, :] = jnp.zeros((DP - D, 2 * E_DEV), BF16)
    for j in range(2):
        cols = slice(j * EC, (j + 1) * EC)
        tail_cols = slice(E_DEV + j * EC, E_DEV + (j + 1) * EC)
        g = 2 * c + j
        pos, w, ltot = sq[g, 0:1, :], sq[g, 1:2, :], lt[g, 0:1, :]
        pos_coef = w * (jnp.exp(pos - ltot) - 1.0)
        own = w * jnp.exp(st[g, 0:1, :] - ltot)
        other = w * jnp.exp(st_in[g, 0:1, :] - ltot)
        away = w * jnp.exp(sc_in[g, 0:1, :] - ltot)
        grad = pos_coef * tts[j] + ot[g] * own + ot_own[j] * other + o_far[j].astype(F32) * away
        gre, gim = grad[:HALF], grad[HALF:]
        rre, rim = rts[j, :HALF, :], rts[j, HALF:, :]
        hre, him = hts[j, :HALF, :], hts[j, HALF:, :]
        ends[0:D, cols] = jnp.concatenate(
            [gre * rre + gim * rim, gim * rre - gre * rim], axis=0
        ).astype(BF16)
        ends[0:D, tail_cols] = (pos_coef * qt[g, 0:D, :].astype(F32)).astype(BF16)
        term = jnp.concatenate([gre * hre + gim * him, gim * hre - gre * him], axis=0)
        hi = term.astype(BF16)
        rt_hi[:, cols] = hi
        rt_lo[:, cols] = (term - hi.astype(F32)).astype(BF16)

    half = pl.ds(pl.multiple_of(c * SLOT, SLOT), SLOT)
    src_chip = z * NS + shard

    def pack(h, core):
        planes = [lax.rem(z + 2 * h + u, NZ) for u in range(2)]
        sel = []
        for zz in planes:
            sc_b = slot_col[zz * 2 + core]
            sel.append(jnp.concatenate(
                [hot_where(sc_b == (iota((256, 128), 1) + 128 * t).astype(F32)) for t in range(8)],
                axis=1,
            ))
        rows = nt(jnp.concatenate(sel, axis=0), ends[...])
        for u, zz in enumerate(planes):
            part = rows[u * 256 : (u + 1) * 256]
            dc = dest_col[zz * 2 + core]
            high = jnp.floor(dc * (1.0 / 32.0))
            lane = iota((256, 128), 1)
            code = jnp.where(lane == 16, high, jnp.where(lane == 17, dc - 32.0 * high, 0.0))
            last = part[:, 384:512] + code
            full = jnp.concatenate([part[:, 0:384], last], axis=1).astype(BF16)
            yield zz, full.reshape(NS, SLOT, DP)

    def pack_away(h):
        for zz, rows in pack(h, oc):
            owners = pl.ds(pl.multiple_of(zz * NS, NS), NS)
            px[owners] = rows
            rcopy(px.at[owners], packed.at[owners, half], send.at[PX_S + h], recv.at[PX_S + h], partner)

    def pack_own(h):
        for zz, rows in pack(h, c):
            packed[pl.ds(pl.multiple_of(zz * NS, NS), NS), half, :] = rows
        wait_bytes(px.at[pl.ds(0, 2 * NS)], recv.at[PX_S + h])
        dst = arrived.at[pl.ds(pl.multiple_of(src_chip * 2 * SLOT, 2 * SLOT), 2 * SLOT)]
        for u in range(2):
            zz = lax.rem(z + 2 * h + u, NZ)
            for j in range(NS):
                ss = lax.rem(shard + j, NS)
                src = packed.at[zz * NS + ss]
                if h == 0 and u == 0 and j == 0:
                    pltpu.make_async_copy(src, dst, recv.at[ENT_S]).start()
                else:
                    rcopy(src, dst, send.at[ENT_S], recv.at[ENT_S], (zz * 2 + c, ss))

    def rel_chunk(r, carry):
        hot = hot_where(iota((128, E_DEV), 0) + r * 128 == ids[...])
        rp[pl.ds(pl.multiple_of(r * 128, 128), 128), :] = nt(hot, rt_hi[...]) + nt(hot, rt_lo[...])
        return carry

    lax.fori_loop(0, 4, rel_chunk, 0)
    rcopy(
        rp.at[pl.ds(pl.multiple_of(oc * 256, 256), 256)], rp_in, send.at[RC_S], recv.at[RC_S], partner
    )

    pack_away(0)
    pack_away(1)
    pack_own(0)

    wait_bytes(rp_in, recv.at[RC_S])
    r1b[...] = (rp[pl.ds(pl.multiple_of(c * 256, 256), 256), :] + rp_in[...]).astype(BF16)
    for j in range(1, NS):
        ss = lax.rem(shard + j, NS)
        rows = r1b.at[pl.ds(pl.multiple_of(ss * 16, 16), 16)]
        rcopy(rows, r2in.at[shard], send.at[R2_S], recv.at[R2_S], (bucket, ss))
    r2in[shard] = r1b[pl.ds(pl.multiple_of(shard * 16, 16), 16), :]
    pack_own(1)


    wait_bytes(r2in.at[pl.ds(0, NS - 1)], recv.at[R2_S])
    r2 = r2in[0].astype(F32)
    for i in range(1, NS):
        r2 = r2 + r2in[i].astype(F32)
    r2all[z] = r2
    for k in (1, 3, 2):
        zz = lax.rem(z + k, NZ)
        rcopy(r2all.at[z], r2all.at[z], send.at[R3_S], recv.at[R3_S], (zz * 2 + c, shard))

    my_rows = pl.ds(pl.multiple_of(shard * NEG_OWN, NEG_OWN), NEG_OWN)
    wait_bytes(rx1.at[pl.ds(0, 3)], recv.at[X1_S])
    for b in range(2):
        total = gx[b, x].astype(F32)
        for i in range(1, 4):
            total = total + rx1[lax.rem(x + i, 4), b].astype(F32)
        ax[b] = total.astype(BF16)
    for i in range(4):
        yy = lax.rem(y + i, 4)
        rows = pl.ds(pl.multiple_of(yy * NEG_OWN, NEG_OWN), NEG_OWN)
        if i:
            rcopy(ax.at[0, rows], rx2.at[y], send.at[X2_S], recv.at[X2_S], (bucket, x * 4 + yy))
        else:
            rx2[y] = ax[0, rows, :]
        rcopy(
            ax.at[1, rows], rx2.at[4 + y], send.at[X2_S], recv.at[X2_S], (z_far * 2 + c, x * 4 + yy)
        )
    wait_bytes(r2all.at[pl.ds(0, 3)], recv.at[R3_S])
    rel_row = pl.ds(pl.multiple_of(c * 256 + shard * 16, 16), 16)
    rfin[rel_row, :] = (((r2all[0] + r2all[1]) + r2all[2]) + r2all[3]).astype(BF16)
    for j in range(1, NS):
        ss = lax.rem(shard + j, NS)
        rcopy(rfin.at[rel_row], rfin.at[rel_row], send.at[R4_S], recv.at[R4_S], (bucket, ss))

    wait_bytes(ry1.at[pl.ds(0, 3)], recv.at[Y1_S])
    for b in range(2):
        total = gy[b, y].astype(F32)
        for i in range(1, 4):
            total = total + ry1[lax.rem(y + i, 4), b].astype(F32)
        ay[b] = total.astype(BF16)
    for i in range(4):
        xx = lax.rem(x + i, 4)
        if i:
            rcopy(ay.at[0, xx], ry2.at[x], send.at[Y2_S], recv.at[Y2_S], (bucket, xx * 4 + y))
        else:
            ry2[x] = ay[0, x]
        rcopy(
            ay.at[1, xx], ry2.at[4 + x], send.at[Y2_S], recv.at[Y2_S], (z_far * 2 + c, xx * 4 + y)
        )
    wait_bytes(rz1, recv.at[Z1_S])

    def sum_z(r, carry):
        rr = pl.ds(pl.multiple_of(r * 256, 256), 256)
        total = gz[0, :, rr].astype(F32) + rz1[:, rr].astype(F32)
        wide_sum = jnp.concatenate([total, jnp.zeros((256 - (D - 256), 256), F32)], axis=0)
        az[rr, :] = wide_sum.T.astype(BF16)
        return carry

    lax.fori_loop(0, 4, sum_z, 0)
    for j in range(1, NS):
        ss = lax.rem(shard + j, NS)
        rows = az.at[pl.ds(pl.multiple_of(ss * NEG_OWN, NEG_OWN), NEG_OWN)]
        rcopy(rows, rz2.at[shard], send.at[Z2_S], recv.at[Z2_S], (bucket, ss))
    rz2[shard] = az[my_rows, :]

    wait_bytes(arrived, recv.at[ENT_S])
    lane = iota((8, DP), 1)
    unit = jnp.where(lane == D, 32.0, jnp.where(lane == D + 1, 1.0, 0.0)).astype(BF16)
    row_ids = nt(unit, arrived[...])[0:1, :]

    def scatter(r, carry):
        hot = hot_where((iota((512, 2048), 0) + r * 512).astype(F32) == row_ids)
        got = nn(hot, arrived[...])
        ent_out[pl.ds(pl.multiple_of(r * 512, 512), 512), :] = got[:, 0:D]
        return carry

    lax.fori_loop(0, 2, scatter, 0)

    wait_bytes(rfin.at[pl.ds(0, 240)], recv.at[R4_S])
    half_rel = rfin.at[pl.ds(pl.multiple_of(c * 256, 256), 256)]
    rcopy(half_rel, half_rel, send.at[R5_S], recv.at[R5_S], partner)

    def sum16(ref):
        total = ref[0].astype(F32)
        for i in range(1, ref.shape[0]):
            total = total + ref[i].astype(F32)
        return total

    wait_bytes(rx2.at[pl.ds(0, 7)], recv.at[X2_S])
    neg_out[:, 0:128] = sum16(rx2)
    wait_bytes(ry2.at[pl.ds(0, 7)], recv.at[Y2_S])
    neg_out[:, 128:256] = sum16(ry2)
    wait_bytes(rz2.at[pl.ds(0, NS - 1)], recv.at[Z2_S])
    neg_out[:, 256:D] = sum16(rz2)[:, 0 : D - 256]

    wait_bytes(half_rel, recv.at[R5_S])
    for r in range(4):
        rr = slice(r * 128, (r + 1) * 128)
        wide_rel = jnp.concatenate([rfin[rr, :].astype(F32), jnp.zeros((128, DP - D), F32)], axis=1)
        rel_out[:, rr] = wide_rel.T[0:D]

    wait_bytes(nbt.at[pl.ds(0, 2)], send.at[GZ_S])
    wait_bytes(nbt.at[pl.ds(0, 3)], send.at[GX_S])
    wait_bytes(nbt.at[pl.ds(0, 3)], send.at[GY_S])
    for number in (Q1_S, Q2_S, Q3_S):
        wait_bytes(qt.at[mine, real], send.at[number])
    for number in (SQ1_S, SQ2_S, SQ3_S):
        wait_bytes(sq.at[mine], send.at[number])
    for number in (ST1_S, ST2_S, SC1_S, SC2_S):
        wait_bytes(st.at[own_half], send.at[number])
    wait_bytes(ot_pair, send.at[O1_S])
    wait_bytes(o_far.at[0], send.at[O4_S])
    wait_bytes(o_far.at[1], send.at[O2_S])
    wait_bytes(ot_own, send.at[O3_S])
    wait_bytes(px.at[pl.ds(0, 2 * NS)], send.at[PX_S])
    wait_bytes(px.at[pl.ds(0, 2 * NS)], send.at[PY_S])
    wait_bytes(arrived.at[pl.ds(0, 2048 - 2 * SLOT)], send.at[ENT_S])
    wait_bytes(rp_in, send.at[RC_S])
    wait_bytes(r2in.at[pl.ds(0, NS - 1)], send.at[R2_S])
    wait_bytes(r2all.at[pl.ds(0, 3)], send.at[R3_S])
    wait_bytes(rfin.at[pl.ds(0, 240)], send.at[R4_S])
    wait_bytes(half_rel, send.at[R5_S])
    wait_bytes(rz1, send.at[Z1_S])
    wait_bytes(rx1.at[pl.ds(0, 3)], send.at[X1_S])
    wait_bytes(ry1.at[pl.ds(0, 3)], send.at[Y1_S])
    wait_bytes(rx2.at[pl.ds(0, 7)], send.at[X2_S])
    wait_bytes(ry2.at[pl.ds(0, 7)], send.at[Y2_S])
    wait_bytes(rz2.at[pl.ds(0, NS - 1)], send.at[Z2_S])


SCRATCH = [
    ((16, D, 128), BF16),
    ((D + 16, NEG_DEV), BF16),
    ((NEG_DEV, DP), BF16),
    ((2, NEG_DEV, 8 * EC), BF16),
    ((8, DP, EC), BF16),
    ((8, 8, EC), F32),
    ((2, D, EC), F32),
    ((2, D, EC), F32),
    ((2, D, EC), F32),
    ((2, 8, 8, EC), F32),
    ((8, 8, EC), F32),
    ((8, 8, EC), F32),
    ((8, 8, EC), F32),
    ((8, 8, EC), F32),
    ((8, D, EC), F32),
    ((2, D, EC), F32),
    ((2, D, EC), F32),
    ((2, D, EC), BF16),
    ((2, D, EC), BF16),
    ((8, 8, EC), F32),
    ((DP, 8 * EC), BF16),
    ((DP, 2 * E_DEV), BF16),
    ((D, E_DEV), BF16),
    ((D, E_DEV), BF16),
    ((NZ * NS, 2 * SLOT, DP), BF16),
    ((NZ * NS, SLOT, DP), BF16),
    ((2048, DP), BF16),
    ((NB, 256, 128), F32),
    ((NB, 256, 128), F32),
    ((2, D - 256, NEG_DEV), BF16),
    ((2, 4, 256, 128), BF16),
    ((2, 4, 4, NEG_OWN, 128), BF16),
    ((D - 256, NEG_DEV), BF16),
    ((4, 2, 256, 128), BF16),
    ((4, 2, 4, NEG_OWN, 128), BF16),
    ((NEG_DEV, 256), BF16),
    ((2, 256, 128), BF16),
    ((2, 4, NEG_OWN, 128), BF16),
    ((NS, NEG_OWN, 256), BF16),
    ((8, NEG_OWN, 128), BF16),
    ((8, NEG_OWN, 128), BF16),
    ((REL, D), F32),
    ((REL // 2, D), F32),
    ((REL // 2, D), BF16),
    ((NS, 16, D), BF16),
    ((NZ, 16, D), F32),
    ((REL, D), BF16),
]


def per_device(
    head_rows, tail_rows, rel_ids, relations, edge_weights, neg_rows, send_slots, dest_rows
):
    vmem = pl.BlockSpec(memory_space=pltpu.VMEM)
    ent_grad, neg_grad, rel_t = pl.pallas_call(
        kernel,
        out_shape=(
            jax.ShapeDtypeStruct((ENT_DEV, D), F32),
            jax.ShapeDtypeStruct((NEG_OWN, D), F32),
            jax.ShapeDtypeStruct((D, REL), F32),
        ),
        in_specs=[vmem] * 8,
        out_specs=(vmem,) * 3,
        scratch_shapes=[pltpu.VMEM(shape, dtype) for shape, dtype in SCRATCH]
        + [
            pltpu.SemaphoreType.DMA((31,)),
            pltpu.SemaphoreType.DMA((31,)),
            pltpu.SemaphoreType.REGULAR((3,)),
        ],
        compiler_params=pltpu.CompilerParams(
            collective_id=0, has_side_effects=True, vmem_limit_bytes=60 * 1024 * 1024
        ),
        cost_estimate=pl.CostEstimate(
            flops=2 * 3 * 1024 * 4096 * 400, bytes_accessed=8 * 1024 * 1024, transcendentals=1024 * 4096
        ),
        name="complex_backward",
    )(
        head_rows.T,
        tail_rows.T,
        rel_ids.reshape(1, E_DEV),
        relations.T,
        edge_weights.reshape(1, E_DEV),
        neg_rows.T,
        send_slots.T,
        dest_rows.T,
    )
    return ent_grad, neg_grad, rel_t.T


def solution(mesh):
    return jax.shard_map(
        per_device,
        mesh=mesh,
        in_specs=(
            P(("bucket", "shard"), None),
            P(("bucket", "shard"), None),
            P(("bucket", "shard")),
            P(),
            P(("bucket", "shard")),
            P("bucket", None),
            P(("bucket", "shard"), None),
            P(("bucket", "shard"), None),
        ),
        out_specs=(P(("bucket", "shard"), None), P(("bucket", "shard"), None), P()),
        check_vma=False,
    )
```

```python
import functools

import jax
import jax.numpy as jnp
from jax import lax
from jax.experimental import pallas as pl
from jax.experimental.pallas import tpu as pltpu
from jax.sharding import PartitionSpec as P

D = 400
HALF = 200
DP = 512
E_DEV = 512
ENT_DEV = 1024
REL = 512
NEG_DEV = 1024
SLOT = 16
NB = 8
NS = 16
NZ = 4
EC = 256
NEG_OWN = 64

MESH = pl.DeviceIdType.MESH
F32 = jnp.float32
BF16 = jnp.bfloat16

(Q1_S, SQ1_S, Q2_S, SQ2_S, Q3_S, SQ3_S, ST1_S, O1_S, SC1_S, O2_S, ST2_S, O3_S, SC2_S,
 RC_S, R2_S, R3_S, R4_S, R5_S, ENT_S, Z1_S, X1_S, Y1_S, Z2_S, X2_S, Y2_S, GZ_S, GX_S, GY_S, O4_S) = range(29)


def nt(a, b):
    return lax.dot_general(a, b, (((1,), (1,)), ((), ())), preferred_element_type=F32)


def nn(a, b):
    return jnp.dot(a, b, preferred_element_type=F32)


def iota(shape, dim):
    return lax.broadcasted_iota(jnp.int32, shape, dim)


def hot_where(mask):
    return mask.astype(F32).astype(BF16)


def wait_bytes(ref, sem):
    pltpu.make_async_copy(ref, ref, sem).wait()


def kernel(
    head, tail, ids, rel, wts, neg, slots, drows,
    arrived_out, rx2_out, ry2_out, rz2_out, rel_sum_out,
    nbt, wide, nb, prob, qt, sq, hts, tts, rts, mb, st, st_in, sc, sc_in,
    ot, ot_pair, ot_own, o_sum, o_far, lt, qs, ends, rt_hi, rt_lo,
    packed, arrived, slot_col, dest_col,
    gz, gx, gy, rz1, rx1, ry1, az, ax, ay, rz2, rx2, ry2,
    rp, rp_in, r1b, r2in, r2all, rfin,
    send, recv, known, out_sem,
):
    bucket, shard = lax.axis_index("bucket"), lax.axis_index("shard")
    z, c = bucket // 2, bucket % 2
    x, y = shard // 4, shard % 4
    oc = 1 - c
    me = bucket * NS + shard
    partner = (z * 2 + oc, shard)
    pair = ((z + 1 - 2 * (z % 2)) * 2 + c, shard)
    z_far = 3 - z
    far = (z_far * 2 + c, shard)

    def rcopy(src, dst, s_sem, r_sem, device):
        pltpu.make_async_remote_copy(
            src_ref=src, dst_ref=dst, send_sem=s_sem, recv_sem=r_sem,
            device_id=device, device_id_type=MESH,
        ).start()

    barrier = pltpu.get_barrier_semaphore()

    x_peers = [(bucket, lax.rem(x + i, 4) * 4 + y) for i in (1, 2, 3)]
    y_peers = [(bucket, x * 4 + lax.rem(y + i, 4)) for i in (1, 2, 3)]
    friends = [partner, pair, far] + x_peers + y_peers

    def tell(sem, devices):
        for device in devices:
            pl.semaphore_signal(sem, inc=1, device_id=device, device_id_type=MESH)

    tell(barrier, friends)

    for g in range(8):
        qt[g, D:DP, :] = jnp.zeros((DP - D, EC), BF16)
    wide[D:, :] = jnp.ones((16, NEG_DEV), BF16)

    for i in range(8):
        nbt[i] = neg[:, i * 128 : (i + 1) * 128]

    rel_1 = rel[...].astype(BF16)
    rest = rel[...] - rel_1.astype(F32)
    rel_2 = rest.astype(BF16)
    rel_3 = (rest - rel_2.astype(F32)).astype(BF16)
    for j in range(2):
        cols = slice(j * EC, (j + 1) * EC)
        h_t = head[:, cols].astype(F32)
        t_t = tail[:, cols].astype(F32)
        hot = hot_where(iota((REL, EC), 0) == ids[0:1, cols])
        r_t = (nn(rel_1, hot) + nn(rel_2, hot)) + nn(rel_3, hot)
        hre, him = h_t[:HALF], h_t[HALF:]
        rre, rim = r_t[:HALF], r_t[HALF:]
        q = jnp.concatenate([hre * rre - him * rim, hre * rim + him * rre], axis=0).astype(BF16)
        qt[2 * c + j, 0:D, :] = q
        sq[2 * c + j, 0:1, :] = jnp.sum(q.astype(F32) * t_t, axis=0, keepdims=True)
        sq[2 * c + j, 1:2, :] = wts[0:1, cols]
        sq[2 * c + j, 2:8, :] = jnp.zeros((6, EC), F32)
        hts[j] = h_t
        tts[j] = t_t
        rts[j] = r_t

    pl.semaphore_wait(barrier, len(friends))
    tell(known.at[0], y_peers)

    for i in (x, 4 + y):
        rcopy(nbt.at[i], nbt.at[8 + i], send.at[GZ_S], recv.at[GZ_S], far)
    mine, theirs, real = pl.ds(2 * c, 2), pl.ds(4 + 2 * c, 2), pl.ds(0, D)
    rcopy(qt.at[mine, real], qt.at[mine, real], send.at[Q1_S], recv.at[Q1_S], partner)
    rcopy(sq.at[mine], sq.at[mine], send.at[SQ1_S], recv.at[SQ1_S], partner)
    rcopy(qt.at[mine, real], qt.at[theirs, real], send.at[Q2_S], recv.at[Q2_S], pair)
    rcopy(sq.at[mine], sq.at[theirs], send.at[SQ2_S], recv.at[SQ2_S], pair)

    ones = jnp.ones((SLOT, 128), BF16)
    tables = []
    for ref in (slots, drows):
        value = ref[...].astype(F32)
        high = jnp.floor(value * (1.0 / 32.0))
        tables.append((high.astype(BF16), (value - 32.0 * high).astype(BF16)))

    def columns(b, carry):
        owner_hot = hot_where(iota((256, 128), 1) == iota((256, 128), 0) // SLOT + b * NS)
        keep = iota((256, SLOT), 1) == iota((256, SLOT), 0) % SLOT
        for (high, low), out in zip(tables, (slot_col, dest_col)):
            h = jnp.where(keep, nt(owner_hot, high), 0.0).astype(BF16)
            l = jnp.where(keep, nt(owner_hot, low), 0.0).astype(BF16)
            out[b] = 32.0 * nn(h, ones) + nn(l, ones)
        return carry

    lax.fori_loop(0, NB, columns, 0)
    nb[:, 384:DP] = jnp.zeros((NEG_DEV, 128), BF16)

    def flip(b):
        for i in range(8):
            part = nbt[b * 8 + i]
            wide[0:D, i * 128 : (i + 1) * 128] = part
            nb[i * 128 : (i + 1) * 128, 0:D] = part.astype(F32).T.astype(BF16)

    def block(b, two):

        chunks = (2 * two, 2 * two + 1)
        scores = [nn(nb[...], qt[g]) for g in chunks]
        for g, s in zip(chunks, scores):
            m = jnp.max(s, axis=0, keepdims=True)
            pb = jnp.exp(s - m).astype(BF16)
            prob[b, :, pl.ds(pl.multiple_of(g * EC, EC), EC)] = pb
            o = nn(wide[...], pb)
            l = o[D : D + 1]
            o = o[0:D]
            mb[b, g, 0:1, :] = m
            if b == 0:
                st[g, 0:1, :] = m
                st[g, 1:2, :] = l
                st[g, 2:8, :] = jnp.zeros((6, EC), F32)
                ot[g] = o
            else:
                m_old = st[g, 0:1, :]
                m_new = jnp.maximum(m_old, m)
                f_old = jnp.exp(m_old - m_new)
                f_new = jnp.exp(m - m_new)
                st[g, 0:1, :] = m_new
                st[g, 1:2, :] = st[g, 1:2, :] * f_old + l * f_new
                ot[g] = ot[g] * f_old + o * f_new

    flip(0)
    block(0, c)
    pl.semaphore_wait(known.at[0], 3)
    tell(known.at[1], (pair, far))
    wait_bytes(nbt.at[pl.ds(8, 2)], recv.at[GZ_S])
    for i in (1, 3, 2):
        xx, yy = lax.rem(x + i, 4), lax.rem(y + i, 4)
        rcopy(nbt.at[8 + x], nbt.at[8 + x], send.at[GX_S], recv.at[GX_S], (bucket, xx * 4 + y))
        rcopy(nbt.at[12 + y], nbt.at[12 + y], send.at[GY_S], recv.at[GY_S], (bucket, x * 4 + yy))
    wait_bytes(qt.at[mine, real], recv.at[Q1_S])
    wait_bytes(sq.at[mine], recv.at[SQ1_S])
    block(0, oc)
    pl.semaphore_wait(known.at[1], 2)
    tell(known.at[2], (pair, far))
    wait_bytes(qt.at[mine, real], recv.at[Q2_S])
    wait_bytes(sq.at[mine], recv.at[SQ2_S])
    rcopy(qt.at[theirs, real], qt.at[theirs, real], send.at[Q3_S], recv.at[Q3_S], partner)
    rcopy(sq.at[theirs], sq.at[theirs], send.at[SQ3_S], recv.at[SQ3_S], partner)
    block(0, 2 + c)
    wait_bytes(qt.at[mine, real], recv.at[Q3_S])
    wait_bytes(sq.at[mine], recv.at[SQ3_S])
    block(0, 2 + oc)
    wait_bytes(nbt.at[pl.ds(8, 3)], recv.at[GX_S])
    wait_bytes(nbt.at[pl.ds(8, 3)], recv.at[GY_S])
    flip(1)
    block(1, 2 + oc)
    pl.semaphore_wait(known.at[2], 2)
    tell(known.at[3], (partner,))
    rcopy(
        ot.at[pl.ds(4 + 2 * oc, 2)], ot_pair, send.at[O1_S], recv.at[O1_S], partner
    )
    block(1, 2 + c)
    own_half, pair_half = pl.ds(0, 4), pl.ds(4, 4)
    rcopy(st.at[pair_half], st_in.at[pair_half], send.at[ST1_S], recv.at[ST1_S], partner)

    def merge(g):
        m_a, m_b = st[g, 0:1, :], st_in[g, 0:1, :]
        m = jnp.maximum(m_a, m_b)
        f_a, f_b = jnp.exp(m_a - m), jnp.exp(m_b - m)
        sc[g, 0:1, :] = m
        sc[g, 1:2, :] = st[g, 1:2, :] * f_a + st_in[g, 1:2, :] * f_b
        sc[g, 2:8, :] = jnp.zeros((6, EC), F32)
        return f_a, f_b

    block(1, oc)
    pl.semaphore_wait(known.at[3], 1)
    rcopy(ot.at[pl.ds(2 * oc, 2)], ot_own, send.at[O3_S], recv.at[O3_S], partner)
    wait_bytes(st_in.at[pair_half], recv.at[ST1_S])
    wait_bytes(ot_pair, recv.at[O1_S])
    for g in range(4, 8):
        merge(g)
    for j in range(2):
        f_a, f_b = merge(4 + 2 * c + j)
        o_sum[j] = (ot[4 + 2 * c + j] * f_a + ot_pair[j] * f_b).astype(BF16)
    rcopy(o_sum.at[0], o_far.at[0], send.at[O4_S], recv.at[O4_S], pair)
    rcopy(sc.at[pair_half], sc_in.at[own_half], send.at[SC1_S], recv.at[SC1_S], pair)
    block(1, c)
    rcopy(st.at[own_half], st_in.at[own_half], send.at[ST2_S], recv.at[ST2_S], partner)
    wait_bytes(st_in.at[own_half], recv.at[ST2_S])
    for g in range(4):
        merge(g)
    rcopy(sc.at[own_half], sc_in.at[pair_half], send.at[SC2_S], recv.at[SC2_S], pair)
    rcopy(o_sum.at[1], o_far.at[1], send.at[O2_S], recv.at[O2_S], pair)
    wait_bytes(sc_in.at[own_half], recv.at[SC1_S])
    wait_bytes(sc_in.at[pair_half], recv.at[SC2_S])
    for g in range(8):
        pos = sq[g, 0:1, :]
        m0, m1 = sc[g, 0:1, :], sc_in[g, 0:1, :]
        top = jnp.maximum(pos, jnp.maximum(m0, m1))
        total = (
            jnp.exp(pos - top)
            + sc[g, 1:2, :] * jnp.exp(m0 - top)
            + sc_in[g, 1:2, :] * jnp.exp(m1 - top)
        )
        lt[g, 0:1, :] = top + jnp.log(total)

    def neg_block(b):
        for g in range(8):
            scale = sq[g, 1:2, :] * jnp.exp(mb[b, g, 0:1, :] - lt[g, 0:1, :])
            qs[:, g * EC : (g + 1) * EC] = (qt[g].astype(F32) * scale).astype(BF16)

        def rows_of(h, carry):
            rr = pl.ds(pl.multiple_of(h * 512, 512), 512)
            acc = nt(prob[b, rr, :], qs[...])
            for u in range(2):
                part = acc[u * 256 : (u + 1) * 256]
                gx[b, 2 * h + u] = part[:, 0:128].astype(BF16)
                for yy in range(4):
                    gy[b, yy, 2 * h + u] = part[yy * 64 : (yy + 1) * 64, 128:256].astype(BF16)
            gz[b, :, rr] = acc[:, 256:512].T[0 : D - 256].astype(BF16)
            return carry

        lax.fori_loop(0, 2, rows_of, 0)
        for i in (1, 3, 2):
            xx, yy = lax.rem(x + i, 4), lax.rem(y + i, 4)
            rcopy(gx.at[b, xx], rx1.at[x, b], send.at[X1_S], recv.at[X1_S], (bucket, xx * 4 + y))
            rcopy(gy.at[b, yy], ry1.at[y, b], send.at[Y1_S], recv.at[Y1_S], (bucket, x * 4 + yy))

    neg_block(1)
    rcopy(gz.at[1], rz1, send.at[Z1_S], recv.at[Z1_S], far)
    wait_bytes(ot_own, recv.at[O3_S])
    wait_bytes(o_far.at[0], recv.at[O4_S])
    wait_bytes(o_far.at[1], recv.at[O2_S])
    ends[D:DP, :] = jnp.zeros((DP - D, 2 * E_DEV), BF16)
    for j in range(2):
        cols = slice(j * EC, (j + 1) * EC)
        tail_cols = slice(E_DEV + j * EC, E_DEV + (j + 1) * EC)
        g = 2 * c + j
        pos, w, ltot = sq[g, 0:1, :], sq[g, 1:2, :], lt[g, 0:1, :]
        pos_coef = w * (jnp.exp(pos - ltot) - 1.0)
        own = w * jnp.exp(st[g, 0:1, :] - ltot)
        other = w * jnp.exp(st_in[g, 0:1, :] - ltot)
        away = w * jnp.exp(sc_in[g, 0:1, :] - ltot)
        grad = pos_coef * tts[j] + ot[g] * own + ot_own[j] * other + o_far[j].astype(F32) * away
        gre, gim = grad[:HALF], grad[HALF:]
        rre, rim = rts[j, :HALF, :], rts[j, HALF:, :]
        hre, him = hts[j, :HALF, :], hts[j, HALF:, :]
        ends[0:D, cols] = jnp.concatenate(
            [gre * rre + gim * rim, gim * rre - gre * rim], axis=0
        ).astype(BF16)
        ends[0:D, tail_cols] = (pos_coef * qt[g, 0:D, :].astype(F32)).astype(BF16)
        term = jnp.concatenate([gre * hre + gim * him, gim * hre - gre * him], axis=0)
        hi = term.astype(BF16)
        rt_hi[:, cols] = hi
        rt_lo[:, cols] = (term - hi.astype(F32)).astype(BF16)

    my_slots = pl.ds(pl.multiple_of(me * SLOT, SLOT), SLOT)

    def pack(k, first):
        sel = []
        for u in range(2):
            sc_b = slot_col[lax.rem(bucket + 2 * k + u, NB)]
            sel.append(jnp.concatenate(
                [hot_where(sc_b == (iota((256, 128), 1) + 128 * t).astype(F32)) for t in range(8)],
                axis=1,
            ))
        rows = nt(jnp.concatenate(sel, axis=0), ends[...])
        for u in range(2):
            bb = lax.rem(bucket + 2 * k + u, NB)
            part = rows[u * 256 : (u + 1) * 256]
            dc = dest_col[bb]
            high = jnp.floor(dc * (1.0 / 32.0))
            lane = iota((256, 128), 1)
            code = jnp.where(lane == 16, high, jnp.where(lane == 17, dc - 32.0 * high, 0.0))
            packed[bb, :, 0:384] = part[:, 0:384].astype(BF16)
            packed[bb, :, 384:512] = (part[:, 384:512] + code).astype(BF16)
            for j in range(NS):
                ss = lax.rem(shard + j, NS)
                src = packed.at[bb, pl.ds(pl.multiple_of(ss * SLOT, SLOT), SLOT)]
                if first and u == 0 and j == 0:
                    pltpu.make_async_copy(src, arrived.at[my_slots], recv.at[ENT_S]).start()
                else:
                    rcopy(src, arrived.at[my_slots], send.at[ENT_S], recv.at[ENT_S], (bb, ss))

    def rel_chunk(r, carry):
        hot = hot_where(iota((128, E_DEV), 0) + r * 128 == ids[...])
        rp[pl.ds(pl.multiple_of(r * 128, 128), 128), :] = nt(hot, rt_hi[...]) + nt(hot, rt_lo[...])
        return carry

    lax.fori_loop(0, 4, rel_chunk, 0)
    rcopy(
        rp.at[pl.ds(pl.multiple_of(oc * 256, 256), 256)], rp_in, send.at[RC_S], recv.at[RC_S], partner
    )

    def pack_other(k, carry):
        pack(k, False)
        return carry

    pack(0, True)
    lax.fori_loop(1, 2, pack_other, 0)

    wait_bytes(rp_in, recv.at[RC_S])
    r1b[...] = (rp[pl.ds(pl.multiple_of(c * 256, 256), 256), :] + rp_in[...]).astype(BF16)
    for j in range(1, NS):
        ss = lax.rem(shard + j, NS)
        rows = r1b.at[pl.ds(pl.multiple_of(ss * 16, 16), 16)]
        rcopy(rows, r2in.at[shard], send.at[R2_S], recv.at[R2_S], (bucket, ss))
    r2in[shard] = r1b[pl.ds(pl.multiple_of(shard * 16, 16), 16), :]
    neg_block(0)
    lax.fori_loop(2, NB // 2, pack_other, 0)


    wait_bytes(r2in.at[pl.ds(0, NS - 1)], recv.at[R2_S])
    r2 = r2in[0].astype(F32)
    for i in range(1, NS):
        r2 = r2 + r2in[i].astype(F32)
    r2all[z] = r2
    for k in (1, 3, 2):
        zz = lax.rem(z + k, NZ)
        rcopy(r2all.at[z], r2all.at[z], send.at[R3_S], recv.at[R3_S], (zz * 2 + c, shard))

    my_rows = pl.ds(pl.multiple_of(shard * NEG_OWN, NEG_OWN), NEG_OWN)
    wait_bytes(rx1.at[pl.ds(0, 3)], recv.at[X1_S])
    for b in range(2):
        total = gx[b, x].astype(F32)
        for i in range(1, 4):
            total = total + rx1[lax.rem(x + i, 4), b].astype(F32)
        ax[b] = total.astype(BF16)
    for i in range(4):
        yy = lax.rem(y + i, 4)
        rows = pl.ds(pl.multiple_of(yy * NEG_OWN, NEG_OWN), NEG_OWN)
        if i:
            rcopy(ax.at[0, rows], rx2.at[y], send.at[X2_S], recv.at[X2_S], (bucket, x * 4 + yy))
        else:
            rx2[y] = ax[0, rows, :]
        rcopy(
            ax.at[1, rows], rx2.at[4 + y], send.at[X2_S], recv.at[X2_S], (z_far * 2 + c, x * 4 + yy)
        )
    wait_bytes(r2all.at[pl.ds(0, 3)], recv.at[R3_S])
    rel_row = pl.ds(pl.multiple_of(c * 256 + shard * 16, 16), 16)
    rfin[rel_row, :] = (((r2all[0] + r2all[1]) + r2all[2]) + r2all[3]).astype(BF16)
    for j in range(1, NS):
        ss = lax.rem(shard + j, NS)
        rcopy(rfin.at[rel_row], rfin.at[rel_row], send.at[R4_S], recv.at[R4_S], (bucket, ss))

    wait_bytes(ry1.at[pl.ds(0, 3)], recv.at[Y1_S])
    for b in range(2):
        total = gy[b, y].astype(F32)
        for i in range(1, 4):
            total = total + ry1[lax.rem(y + i, 4), b].astype(F32)
        ay[b] = total.astype(BF16)
    for i in range(4):
        xx = lax.rem(x + i, 4)
        if i:
            rcopy(ay.at[0, xx], ry2.at[x], send.at[Y2_S], recv.at[Y2_S], (bucket, xx * 4 + y))
        else:
            ry2[x] = ay[0, x]
        rcopy(
            ay.at[1, xx], ry2.at[4 + x], send.at[Y2_S], recv.at[Y2_S], (z_far * 2 + c, xx * 4 + y)
        )
    wait_bytes(rz1, recv.at[Z1_S])

    def sum_z(r, carry):
        rr = pl.ds(pl.multiple_of(r * 256, 256), 256)
        total = gz[0, :, rr].astype(F32) + rz1[:, rr].astype(F32)
        wide_sum = jnp.concatenate([total, jnp.zeros((256 - (D - 256), 256), F32)], axis=0)
        az[rr, :] = wide_sum.T.astype(BF16)
        return carry

    lax.fori_loop(0, 4, sum_z, 0)
    for j in range(1, NS):
        ss = lax.rem(shard + j, NS)
        rows = az.at[pl.ds(pl.multiple_of(ss * NEG_OWN, NEG_OWN), NEG_OWN)]
        rcopy(rows, rz2.at[shard], send.at[Z2_S], recv.at[Z2_S], (bucket, ss))
    rz2[shard] = az[my_rows, :]

    def give(src, dst, sem):
        pltpu.make_async_copy(src, dst, sem).start()

    wait_bytes(arrived, recv.at[ENT_S])
    give(arrived, arrived_out, out_sem.at[0])
    wait_bytes(rfin.at[pl.ds(0, 240)], recv.at[R4_S])
    half_rel = rfin.at[pl.ds(pl.multiple_of(c * 256, 256), 256)]
    rcopy(half_rel, half_rel, send.at[R5_S], recv.at[R5_S], partner)
    wait_bytes(rx2.at[pl.ds(0, 7)], recv.at[X2_S])
    give(rx2, rx2_out, out_sem.at[1])
    wait_bytes(ry2.at[pl.ds(0, 7)], recv.at[Y2_S])
    give(ry2, ry2_out, out_sem.at[2])
    wait_bytes(rz2.at[pl.ds(0, NS - 1)], recv.at[Z2_S])
    give(rz2, rz2_out, out_sem.at[3])
    wait_bytes(half_rel, recv.at[R5_S])
    give(rfin, rel_sum_out, out_sem.at[4])

    wait_bytes(nbt.at[pl.ds(0, 2)], send.at[GZ_S])
    wait_bytes(nbt.at[pl.ds(0, 3)], send.at[GX_S])
    wait_bytes(nbt.at[pl.ds(0, 3)], send.at[GY_S])
    for number in (Q1_S, Q2_S, Q3_S):
        wait_bytes(qt.at[mine, real], send.at[number])
    for number in (SQ1_S, SQ2_S, SQ3_S):
        wait_bytes(sq.at[mine], send.at[number])
    for number in (ST1_S, ST2_S, SC1_S, SC2_S):
        wait_bytes(st.at[own_half], send.at[number])
    wait_bytes(ot_pair, send.at[O1_S])
    wait_bytes(o_far.at[0], send.at[O4_S])
    wait_bytes(o_far.at[1], send.at[O2_S])
    wait_bytes(ot_own, send.at[O3_S])
    wait_bytes(arrived.at[pl.ds(0, 2048 - SLOT)], send.at[ENT_S])
    wait_bytes(rp_in, send.at[RC_S])
    wait_bytes(r2in.at[pl.ds(0, NS - 1)], send.at[R2_S])
    wait_bytes(r2all.at[pl.ds(0, 3)], send.at[R3_S])
    wait_bytes(rfin.at[pl.ds(0, 240)], send.at[R4_S])
    wait_bytes(half_rel, send.at[R5_S])
    wait_bytes(rz1, send.at[Z1_S])
    wait_bytes(rx1.at[pl.ds(0, 3)], send.at[X1_S])
    wait_bytes(ry1.at[pl.ds(0, 3)], send.at[Y1_S])
    wait_bytes(rx2.at[pl.ds(0, 7)], send.at[X2_S])
    wait_bytes(ry2.at[pl.ds(0, 7)], send.at[Y2_S])
    wait_bytes(rz2.at[pl.ds(0, NS - 1)], send.at[Z2_S])
    wait_bytes(arrived, out_sem.at[0])
    wait_bytes(rx2, out_sem.at[1])
    wait_bytes(ry2, out_sem.at[2])
    wait_bytes(rz2, out_sem.at[3])
    wait_bytes(rfin, out_sem.at[4])


def finish(
    arrived_in, rx2_in, ry2_in, rz2_in, rel_in, ent_out, neg_out, rel_out,
    arrived, rx2, ry2, rz2, rel_sum, ent, neg_sum, rel_t, in_sem, out_sem,
):
    loads = [
        pltpu.make_async_copy(src, dst, in_sem.at[i])
        for i, (src, dst) in enumerate((
            (rel_in, rel_sum), (arrived_in, arrived), (rx2_in, rx2), (ry2_in, ry2), (rz2_in, rz2)
        ))
    ]
    for load in loads:
        load.start()
    loads[0].wait()
    for r in range(4):
        rows = rel_sum[r * 128 : (r + 1) * 128, :].astype(F32)
        wide = jnp.concatenate([rows, jnp.zeros((128, DP - D), F32)], axis=1)
        rel_t[:, r * 128 : (r + 1) * 128] = wide.T[0:D]
    stores = [pltpu.make_async_copy(rel_t, rel_out, out_sem.at[0])]
    stores[0].start()

    loads[1].wait()
    lane = iota((8, 128), 1)
    unit = jnp.where(lane == D - 384, 32.0, jnp.where(lane == D - 383, 1.0, 0.0)).astype(BF16)
    row_ids = nt(unit, arrived[:, 384:DP])[0:1, :]
    for r in range(2):
        hot = hot_where((iota((512, 2048), 0) + r * 512).astype(F32) == row_ids)
        ent[r] = nn(hot, arrived[...]).T[0:D]
        store = pltpu.make_async_copy(ent.at[r], ent_out.at[:, pl.ds(r * 512, 512)], out_sem.at[1 + r])
        store.start()
        stores.append(store)

    def sum_all(ref):
        total = ref[0].astype(F32)
        for i in range(1, ref.shape[0]):
            total = total + ref[i].astype(F32)
        return total

    for load in loads[2:]:
        load.wait()
    neg_sum[:, 0:128] = sum_all(rx2)
    neg_sum[:, 128:256] = sum_all(ry2)
    neg_sum[:, 256:D] = sum_all(rz2)[:, 0 : D - 256]
    stores.append(pltpu.make_async_copy(neg_sum, neg_out, out_sem.at[3]))
    stores[-1].start()
    for store in stores:
        store.wait()


SCRATCH = [
    ((16, D, 128), BF16),
    ((D + 16, NEG_DEV), BF16),
    ((NEG_DEV, DP), BF16),
    ((2, NEG_DEV, 8 * EC), BF16),
    ((8, DP, EC), BF16),
    ((8, 8, EC), F32),
    ((2, D, EC), F32),
    ((2, D, EC), F32),
    ((2, D, EC), F32),
    ((2, 8, 8, EC), F32),
    ((8, 8, EC), F32),
    ((8, 8, EC), F32),
    ((8, 8, EC), F32),
    ((8, 8, EC), F32),
    ((8, D, EC), F32),
    ((2, D, EC), F32),
    ((2, D, EC), F32),
    ((2, D, EC), BF16),
    ((2, D, EC), BF16),
    ((8, 8, EC), F32),
    ((DP, 8 * EC), BF16),
    ((DP, 2 * E_DEV), BF16),
    ((D, E_DEV), BF16),
    ((D, E_DEV), BF16),
    ((NB, 256, DP), BF16),
    ((2048, DP), BF16),
    ((NB, 256, 128), F32),
    ((NB, 256, 128), F32),
    ((2, D - 256, NEG_DEV), BF16),
    ((2, 4, 256, 128), BF16),
    ((2, 4, 4, NEG_OWN, 128), BF16),
    ((D - 256, NEG_DEV), BF16),
    ((4, 2, 256, 128), BF16),
    ((4, 2, 4, NEG_OWN, 128), BF16),
    ((NEG_DEV, 256), BF16),
    ((2, 256, 128), BF16),
    ((2, 4, NEG_OWN, 128), BF16),
    ((NS, NEG_OWN, 256), BF16),
    ((8, NEG_OWN, 128), BF16),
    ((8, NEG_OWN, 128), BF16),
    ((REL, D), F32),
    ((REL // 2, D), F32),
    ((REL // 2, D), BF16),
    ((NS, 16, D), BF16),
    ((NZ, 16, D), F32),
    ((REL, D), BF16),
]


def per_device(
    head_rows, tail_rows, rel_ids, relations, edge_weights, neg_rows, send_slots, dest_rows
):
    vmem = pl.BlockSpec(memory_space=pltpu.VMEM)
    anywhere = pl.BlockSpec(memory_space=pl.ANY)
    results = pl.pallas_call(
        kernel,
        out_shape=(
            jax.ShapeDtypeStruct((2048, DP), BF16),
            jax.ShapeDtypeStruct((8, NEG_OWN, 128), BF16),
            jax.ShapeDtypeStruct((8, NEG_OWN, 128), BF16),
            jax.ShapeDtypeStruct((NS, NEG_OWN, 256), BF16),
            jax.ShapeDtypeStruct((REL, D), BF16),
        ),
        in_specs=[vmem] * 8,
        out_specs=(anywhere,) * 5,
        scratch_shapes=[pltpu.VMEM(shape, dtype) for shape, dtype in SCRATCH]
        + [
            pltpu.SemaphoreType.DMA((29,)),
            pltpu.SemaphoreType.DMA((29,)),
            pltpu.SemaphoreType.REGULAR((4,)),
            pltpu.SemaphoreType.DMA((5,)),
        ],
        compiler_params=pltpu.CompilerParams(
            collective_id=0, has_side_effects=True, vmem_limit_bytes=60 * 1024 * 1024
        ),
        cost_estimate=pl.CostEstimate(
            flops=2 * 3 * 1024 * 4096 * 400, bytes_accessed=8 * 1024 * 1024, transcendentals=1024 * 4096
        ),
        name="complex_backward",
    )(
        head_rows.T,
        tail_rows.T,
        rel_ids.reshape(1, E_DEV),
        relations.T,
        edge_weights.reshape(1, E_DEV),
        neg_rows.T,
        send_slots.T,
        dest_rows.T,
    )
    ent_t, neg_grad, rel_t = pl.pallas_call(
        finish,
        out_shape=(
            jax.ShapeDtypeStruct((D, ENT_DEV), F32),
            jax.ShapeDtypeStruct((NEG_OWN, D), F32),
            jax.ShapeDtypeStruct((D, REL), F32),
        ),
        in_specs=[anywhere] * 5,
        out_specs=(anywhere,) * 3,
        scratch_shapes=[
            pltpu.VMEM((2048, DP), BF16),
            pltpu.VMEM((8, NEG_OWN, 128), BF16),
            pltpu.VMEM((8, NEG_OWN, 128), BF16),
            pltpu.VMEM((NS, NEG_OWN, 256), BF16),
            pltpu.VMEM((REL, D), BF16),
            pltpu.VMEM((2, D, 512), F32),
            pltpu.VMEM((NEG_OWN, D), F32),
            pltpu.VMEM((D, REL), F32),
            pltpu.SemaphoreType.DMA((5,)),
            pltpu.SemaphoreType.DMA((4,)),
        ],
        compiler_params=pltpu.CompilerParams(vmem_limit_bytes=60 * 1024 * 1024),
        cost_estimate=pl.CostEstimate(
            flops=2 * 1024 * 2048 * 512, bytes_accessed=6 * 1024 * 1024, transcendentals=0
        ),
        name="make_outputs",
    )(*results)
    return ent_t.T, neg_grad, rel_t.T


def solution(mesh):
    return jax.shard_map(
        per_device,
        mesh=mesh,
        in_specs=(
            P(("bucket", "shard"), None),
            P(("bucket", "shard"), None),
            P(("bucket", "shard")),
            P(),
            P(("bucket", "shard")),
            P("bucket", None),
            P(("bucket", "shard"), None),
            P(("bucket", "shard"), None),
        ),
        out_specs=(P(("bucket", "shard"), None), P(("bucket", "shard"), None), P()),
        check_vma=False,
    )
```

```python
import functools

import jax
import jax.numpy as jnp
from jax import lax
from jax.experimental import pallas as pl
from jax.experimental.pallas import tpu as pltpu
from jax.sharding import PartitionSpec as P

D = 400
HALF = 200
DP = 512
E_DEV = 512
ENT_DEV = 1024
REL = 512
NEG_DEV = 1024
SLOT = 16
NB = 8
NS = 16
NZ = 4
EC = 256
NEG_OWN = 64

MESH = pl.DeviceIdType.MESH
F32 = jnp.float32
BF16 = jnp.bfloat16

(Q1_S, SQ1_S, Q2_S, SQ2_S, Q3_S, SQ3_S, ST1_S, O1_S, SC1_S, O2_S, ST2_S, O3_S, SC2_S,
 RC_S, R2_S, R3_S, R4_S, R5_S, ENT_S, Z1_S, X1_S, Y1_S, Z2_S, X2_S, Y2_S, GZ_S, GX_S, GY_S, O4_S) = range(29)


def nt(a, b):
    return lax.dot_general(a, b, (((1,), (1,)), ((), ())), preferred_element_type=F32)


def nn(a, b):
    return jnp.dot(a, b, preferred_element_type=F32)


def iota(shape, dim):
    return lax.broadcasted_iota(jnp.int32, shape, dim)


def hot_where(mask):
    return mask.astype(F32).astype(BF16)


def wait_bytes(ref, sem):
    pltpu.make_async_copy(ref, ref, sem).wait()


def kernel(
    head, tail, ids, rel, wts, neg, slots, drows,
    arrived_out, rx2_out, ry2_out, rz2_out, rel_sum_out,
    nbt, wide, nb, prob, qt, sq, hts, tts, rts, mb, st, st_in, sc, sc_in,
    ot, ot_pair, ot_own, o_sum, o_far, lt, qs, ends, rt_hi, rt_lo,
    packed, arrived, slot_col, dest_col,
    gz, gx, gy, rz1, rx1, ry1, az, ax, ay, rz2, rx2, ry2,
    rp, rp_in, r1b, r2in, r2all, rfin,
    send, recv, known, out_sem,
):
    bucket, shard = lax.axis_index("bucket"), lax.axis_index("shard")
    z, c = bucket // 2, bucket % 2
    x, y = shard // 4, shard % 4
    oc = 1 - c
    me = bucket * NS + shard
    partner = (z * 2 + oc, shard)
    pair = ((z + 1 - 2 * (z % 2)) * 2 + c, shard)
    z_far = 3 - z
    far = (z_far * 2 + c, shard)

    def rcopy(src, dst, s_sem, r_sem, device):
        pltpu.make_async_remote_copy(
            src_ref=src, dst_ref=dst, send_sem=s_sem, recv_sem=r_sem,
            device_id=device, device_id_type=MESH,
        ).start()

    barrier = pltpu.get_barrier_semaphore()

    x_peers = [(bucket, lax.rem(x + i, 4) * 4 + y) for i in (1, 2, 3)]
    y_peers = [(bucket, x * 4 + lax.rem(y + i, 4)) for i in (1, 2, 3)]
    friends = [partner, pair, far] + x_peers + y_peers

    def tell(sem, devices):
        for device in devices:
            pl.semaphore_signal(sem, inc=1, device_id=device, device_id_type=MESH)

    tell(barrier, friends)

    for g in range(8):
        qt[g, D:DP, :] = jnp.zeros((DP - D, EC), BF16)

    for i in range(8):
        nbt[i] = neg[:, i * 128 : (i + 1) * 128]

    rel_1 = rel[...].astype(BF16)
    rest = rel[...] - rel_1.astype(F32)
    rel_2 = rest.astype(BF16)
    rel_3 = (rest - rel_2.astype(F32)).astype(BF16)
    for j in range(2):
        cols = slice(j * EC, (j + 1) * EC)
        h_t = head[:, cols].astype(F32)
        t_t = tail[:, cols].astype(F32)
        hot = hot_where(iota((REL, EC), 0) == ids[0:1, cols])
        r_t = (nn(rel_1, hot) + nn(rel_2, hot)) + nn(rel_3, hot)
        hre, him = h_t[:HALF], h_t[HALF:]
        rre, rim = r_t[:HALF], r_t[HALF:]
        q = jnp.concatenate([hre * rre - him * rim, hre * rim + him * rre], axis=0).astype(BF16)
        qt[2 * c + j, 0:D, :] = q
        sq[2 * c + j, 0:1, :] = jnp.sum(q.astype(F32) * t_t, axis=0, keepdims=True)
        sq[2 * c + j, 1:2, :] = wts[0:1, cols]
        sq[2 * c + j, 2:8, :] = jnp.zeros((6, EC), F32)
        hts[j] = h_t
        tts[j] = t_t
        rts[j] = r_t

    pl.semaphore_wait(barrier, len(friends))
    tell(known.at[0], y_peers)

    for i in (x, 4 + y):
        rcopy(nbt.at[i], nbt.at[8 + i], send.at[GZ_S], recv.at[GZ_S], far)
    mine, theirs, real = pl.ds(2 * c, 2), pl.ds(4 + 2 * c, 2), pl.ds(0, D)
    rcopy(qt.at[mine, real], qt.at[mine, real], send.at[Q1_S], recv.at[Q1_S], partner)
    rcopy(sq.at[mine], sq.at[mine], send.at[SQ1_S], recv.at[SQ1_S], partner)
    rcopy(qt.at[mine, real], qt.at[theirs, real], send.at[Q2_S], recv.at[Q2_S], pair)
    rcopy(sq.at[mine], sq.at[theirs], send.at[SQ2_S], recv.at[SQ2_S], pair)

    ones = jnp.ones((SLOT, 128), BF16)
    tables = []
    for ref in (slots, drows):
        value = ref[...].astype(F32)
        high = jnp.floor(value * (1.0 / 32.0))
        tables.append((high.astype(BF16), (value - 32.0 * high).astype(BF16)))

    def columns(b, carry):
        owner_hot = hot_where(iota((256, 128), 1) == iota((256, 128), 0) // SLOT + b * NS)
        keep = iota((256, SLOT), 1) == iota((256, SLOT), 0) % SLOT
        for (high, low), out in zip(tables, (slot_col, dest_col)):
            h = jnp.where(keep, nt(owner_hot, high), 0.0).astype(BF16)
            l = jnp.where(keep, nt(owner_hot, low), 0.0).astype(BF16)
            out[b] = 32.0 * nn(h, ones) + nn(l, ones)
        return carry

    lax.fori_loop(0, NB, columns, 0)
    nb[:, 384:DP] = jnp.zeros((NEG_DEV, 128), BF16)

    def flip(b):
        for i in range(8):
            part = nbt[b * 8 + i]
            wide[b, :, i * 128 : (i + 1) * 128] = part
            nb[i * 128 : (i + 1) * 128, 0:D] = part.astype(F32).T.astype(BF16)

    def score(b, two):
        chunks = (2 * two, 2 * two + 1)
        scores = [nn(nb[...], qt[g]) for g in chunks]
        for g, s in zip(chunks, scores):
            m = jnp.max(s, axis=0, keepdims=True)
            p = jnp.exp(s - m)
            prob[b, :, pl.ds(pl.multiple_of(g * EC, EC), EC)] = p.astype(BF16)
            mb[b, g, 0:1, :] = m
            mb[b, g, 1:2, :] = jnp.sum(p, axis=0, keepdims=True)

    def raw_sum(b, g):
        return nn(wide[b], prob[b, :, pl.ds(pl.multiple_of(g * EC, EC), EC)])

    def raw_first(two):
        for g in (2 * two, 2 * two + 1):
            ot[g] = raw_sum(0, g)

    def share(b, g):
        return sq[g, 1:2, :] * jnp.exp(mb[b, g, 0:1, :] - lt[g, 0:1, :])

    def both_sums(two):
        for g in (2 * two, 2 * two + 1):
            ot[g] = ot[g] * share(0, g) + raw_sum(1, g) * share(1, g)

    def merge(out, g, a, b):
        m = jnp.maximum(a[0:1, :], b[0:1, :])
        out[g, 0:1, :] = m
        out[g, 1:2, :] = a[1:2, :] * jnp.exp(a[0:1, :] - m) + b[1:2, :] * jnp.exp(b[0:1, :] - m)
        out[g, 2:8, :] = jnp.zeros((6, EC), F32)

    flip(0)
    score(0, c)
    pl.semaphore_wait(known.at[0], 3)
    tell(known.at[1], (pair, far))
    wait_bytes(nbt.at[pl.ds(8, 2)], recv.at[GZ_S])
    for i in (1, 3, 2):
        xx, yy = lax.rem(x + i, 4), lax.rem(y + i, 4)
        rcopy(nbt.at[8 + x], nbt.at[8 + x], send.at[GX_S], recv.at[GX_S], (bucket, xx * 4 + y))
        rcopy(nbt.at[12 + y], nbt.at[12 + y], send.at[GY_S], recv.at[GY_S], (bucket, x * 4 + yy))
    wait_bytes(qt.at[mine, real], recv.at[Q1_S])
    wait_bytes(sq.at[mine], recv.at[SQ1_S])
    score(0, oc)
    pl.semaphore_wait(known.at[1], 2)
    tell(known.at[2], (pair, far))
    raw_first(c)
    wait_bytes(qt.at[mine, real], recv.at[Q2_S])
    wait_bytes(sq.at[mine], recv.at[SQ2_S])
    rcopy(qt.at[theirs, real], qt.at[theirs, real], send.at[Q3_S], recv.at[Q3_S], partner)
    rcopy(sq.at[theirs], sq.at[theirs], send.at[SQ3_S], recv.at[SQ3_S], partner)
    score(0, 2 + c)
    raw_first(oc)
    wait_bytes(qt.at[mine, real], recv.at[Q3_S])
    wait_bytes(sq.at[mine], recv.at[SQ3_S])
    score(0, 2 + oc)
    pl.semaphore_wait(known.at[2], 2)
    tell(known.at[3], (partner,))
    wait_bytes(nbt.at[pl.ds(8, 3)], recv.at[GX_S])
    wait_bytes(nbt.at[pl.ds(8, 3)], recv.at[GY_S])
    flip(1)

    def score_far(two, carry):
        score(1, two)
        return carry

    lax.fori_loop(0, 4, score_far, 0)
    pl.semaphore_wait(known.at[3], 1)

    for g in range(8):
        merge(st, g, mb[0, g], mb[1, g])
    rcopy(st, st_in, send.at[ST1_S], recv.at[ST1_S], partner)
    raw_first(2 + oc)
    wait_bytes(st_in, recv.at[ST1_S])
    for g in range(8):
        merge(sc, g, st[g], st_in[g])
    own_half, pair_half = pl.ds(0, 4), pl.ds(4, 4)
    rcopy(sc.at[pair_half], sc_in.at[own_half], send.at[SC1_S], recv.at[SC1_S], pair)
    rcopy(sc.at[own_half], sc_in.at[pair_half], send.at[SC2_S], recv.at[SC2_S], pair)
    raw_first(2 + c)
    wait_bytes(sc_in.at[own_half], recv.at[SC1_S])
    wait_bytes(sc_in.at[pair_half], recv.at[SC2_S])
    for g in range(8):
        pos = sq[g, 0:1, :]
        m0, m1 = sc[g, 0:1, :], sc_in[g, 0:1, :]
        top = jnp.maximum(pos, jnp.maximum(m0, m1))
        total = (
            jnp.exp(pos - top)
            + sc[g, 1:2, :] * jnp.exp(m0 - top)
            + sc_in[g, 1:2, :] * jnp.exp(m1 - top)
        )
        lt[g, 0:1, :] = top + jnp.log(total)

    def neg_block(b):
        for g in range(8):
            qs[:, g * EC : (g + 1) * EC] = (qt[g].astype(F32) * share(b, g)).astype(BF16)

        def rows_of(h, carry):
            rr = pl.ds(pl.multiple_of(h * 512, 512), 512)
            acc = nt(prob[b, rr, :], qs[...])
            for u in range(2):
                part = acc[u * 256 : (u + 1) * 256]
                gx[b, 2 * h + u] = part[:, 0:128].astype(BF16)
                for yy in range(4):
                    gy[b, yy, 2 * h + u] = part[yy * 64 : (yy + 1) * 64, 128:256].astype(BF16)
            gz[b, :, rr] = acc[:, 256:512].T[0 : D - 256].astype(BF16)
            return carry

        lax.fori_loop(0, 2, rows_of, 0)
        for i in (1, 3, 2):
            xx, yy = lax.rem(x + i, 4), lax.rem(y + i, 4)
            rcopy(gx.at[b, xx], rx1.at[x, b], send.at[X1_S], recv.at[X1_S], (bucket, xx * 4 + y))
            rcopy(gy.at[b, yy], ry1.at[y, b], send.at[Y1_S], recv.at[Y1_S], (bucket, x * 4 + yy))

    neg_block(1)
    rcopy(gz.at[1], rz1, send.at[Z1_S], recv.at[Z1_S], far)
    both_sums(2 + oc)
    rcopy(ot.at[pl.ds(4 + 2 * oc, 2)], ot_pair, send.at[O1_S], recv.at[O1_S], partner)
    both_sums(2 + c)
    wait_bytes(ot_pair, recv.at[O1_S])
    for j in range(2):
        o_sum[j] = (ot[4 + 2 * c + j] + ot_pair[j]).astype(BF16)
    rcopy(o_sum, o_far, send.at[O2_S], recv.at[O2_S], pair)
    neg_block(0)
    both_sums(oc)
    rcopy(ot.at[pl.ds(2 * oc, 2)], ot_own, send.at[O3_S], recv.at[O3_S], partner)
    both_sums(c)

    my_rows = pl.ds(pl.multiple_of(shard * NEG_OWN, NEG_OWN), NEG_OWN)
    wait_bytes(rx1.at[pl.ds(0, 3)], recv.at[X1_S])
    for b in range(2):
        total = gx[b, x].astype(F32)
        for i in range(1, 4):
            total = total + rx1[lax.rem(x + i, 4), b].astype(F32)
        ax[b] = total.astype(BF16)
    for i in range(4):
        yy = lax.rem(y + i, 4)
        rows = pl.ds(pl.multiple_of(yy * NEG_OWN, NEG_OWN), NEG_OWN)
        if i:
            rcopy(ax.at[0, rows], rx2.at[y], send.at[X2_S], recv.at[X2_S], (bucket, x * 4 + yy))
        else:
            rx2[y] = ax[0, rows, :]
        rcopy(
            ax.at[1, rows], rx2.at[4 + y], send.at[X2_S], recv.at[X2_S], (z_far * 2 + c, x * 4 + yy)
        )
    wait_bytes(ry1.at[pl.ds(0, 3)], recv.at[Y1_S])
    for b in range(2):
        total = gy[b, y].astype(F32)
        for i in range(1, 4):
            total = total + ry1[lax.rem(y + i, 4), b].astype(F32)
        ay[b] = total.astype(BF16)
    for i in range(4):
        xx = lax.rem(x + i, 4)
        if i:
            rcopy(ay.at[0, xx], ry2.at[x], send.at[Y2_S], recv.at[Y2_S], (bucket, xx * 4 + y))
        else:
            ry2[x] = ay[0, x]
        rcopy(
            ay.at[1, xx], ry2.at[4 + x], send.at[Y2_S], recv.at[Y2_S], (z_far * 2 + c, xx * 4 + y)
        )
    wait_bytes(rz1, recv.at[Z1_S])

    def sum_z(r, carry):
        rr = pl.ds(pl.multiple_of(r * 256, 256), 256)
        total = gz[0, :, rr].astype(F32) + rz1[:, rr].astype(F32)
        wide_sum = jnp.concatenate([total, jnp.zeros((256 - (D - 256), 256), F32)], axis=0)
        az[rr, :] = wide_sum.T.astype(BF16)
        return carry

    lax.fori_loop(0, 4, sum_z, 0)
    for j in range(1, NS):
        ss = lax.rem(shard + j, NS)
        rows = az.at[pl.ds(pl.multiple_of(ss * NEG_OWN, NEG_OWN), NEG_OWN)]
        rcopy(rows, rz2.at[shard], send.at[Z2_S], recv.at[Z2_S], (bucket, ss))
    rz2[shard] = az[my_rows, :]

    wait_bytes(ot_own, recv.at[O3_S])
    wait_bytes(o_far, recv.at[O2_S])
    ends[D:DP, :] = jnp.zeros((DP - D, 2 * E_DEV), BF16)
    for j in range(2):
        cols = slice(j * EC, (j + 1) * EC)
        tail_cols = slice(E_DEV + j * EC, E_DEV + (j + 1) * EC)
        g = 2 * c + j
        pos, ltot = sq[g, 0:1, :], lt[g, 0:1, :]
        pos_coef = sq[g, 1:2, :] * (jnp.exp(pos - ltot) - 1.0)
        grad = pos_coef * tts[j] + ot[g] + ot_own[j] + o_far[j].astype(F32)
        gre, gim = grad[:HALF], grad[HALF:]
        rre, rim = rts[j, :HALF, :], rts[j, HALF:, :]
        hre, him = hts[j, :HALF, :], hts[j, HALF:, :]
        ends[0:D, cols] = jnp.concatenate(
            [gre * rre + gim * rim, gim * rre - gre * rim], axis=0
        ).astype(BF16)
        ends[0:D, tail_cols] = (pos_coef * qt[g, 0:D, :].astype(F32)).astype(BF16)
        term = jnp.concatenate([gre * hre + gim * him, gim * hre - gre * him], axis=0)
        hi = term.astype(BF16)
        rt_hi[:, cols] = hi
        rt_lo[:, cols] = (term - hi.astype(F32)).astype(BF16)

    my_slots = pl.ds(pl.multiple_of(me * SLOT, SLOT), SLOT)

    def pack(k, first):
        sel = []
        for u in range(2):
            sc_b = slot_col[lax.rem(bucket + 2 * k + u, NB)]
            sel.append(jnp.concatenate(
                [hot_where(sc_b == (iota((256, 128), 1) + 128 * t).astype(F32)) for t in range(8)],
                axis=1,
            ))
        rows = nt(jnp.concatenate(sel, axis=0), ends[...])
        for u in range(2):
            bb = lax.rem(bucket + 2 * k + u, NB)
            part = rows[u * 256 : (u + 1) * 256]
            dc = dest_col[bb]
            high = jnp.floor(dc * (1.0 / 32.0))
            lane = iota((256, 128), 1)
            code = jnp.where(lane == 16, high, jnp.where(lane == 17, dc - 32.0 * high, 0.0))
            packed[bb, :, 0:384] = part[:, 0:384].astype(BF16)
            packed[bb, :, 384:512] = (part[:, 384:512] + code).astype(BF16)
            for j in range(NS):
                ss = lax.rem(shard + j, NS)
                src = packed.at[bb, pl.ds(pl.multiple_of(ss * SLOT, SLOT), SLOT)]
                if first and u == 0 and j == 0:
                    pltpu.make_async_copy(src, arrived.at[my_slots], recv.at[ENT_S]).start()
                else:
                    rcopy(src, arrived.at[my_slots], send.at[ENT_S], recv.at[ENT_S], (bb, ss))

    def rel_chunk(r, carry):
        hot = hot_where(iota((128, E_DEV), 0) + r * 128 == ids[...])
        rp[pl.ds(pl.multiple_of(r * 128, 128), 128), :] = nt(hot, rt_hi[...]) + nt(hot, rt_lo[...])
        return carry

    lax.fori_loop(0, 4, rel_chunk, 0)
    rcopy(
        rp.at[pl.ds(pl.multiple_of(oc * 256, 256), 256)], rp_in, send.at[RC_S], recv.at[RC_S], partner
    )

    pack(0, True)

    wait_bytes(rp_in, recv.at[RC_S])
    r1b[...] = (rp[pl.ds(pl.multiple_of(c * 256, 256), 256), :] + rp_in[...]).astype(BF16)
    for j in range(1, NS):
        ss = lax.rem(shard + j, NS)
        rows = r1b.at[pl.ds(pl.multiple_of(ss * 16, 16), 16)]
        rcopy(rows, r2in.at[shard], send.at[R2_S], recv.at[R2_S], (bucket, ss))
    r2in[shard] = r1b[pl.ds(pl.multiple_of(shard * 16, 16), 16), :]

    pack(1, False)

    wait_bytes(r2in.at[pl.ds(0, NS - 1)], recv.at[R2_S])
    r2 = r2in[0].astype(F32)
    for i in range(1, NS):
        r2 = r2 + r2in[i].astype(F32)
    r2all[z] = r2
    for k in (1, 3, 2):
        zz = lax.rem(z + k, NZ)
        rcopy(r2all.at[z], r2all.at[z], send.at[R3_S], recv.at[R3_S], (zz * 2 + c, shard))


    pack(2, False)

    wait_bytes(r2all.at[pl.ds(0, 3)], recv.at[R3_S])
    rel_row = pl.ds(pl.multiple_of(c * 256 + shard * 16, 16), 16)
    rfin[rel_row, :] = (((r2all[0] + r2all[1]) + r2all[2]) + r2all[3]).astype(BF16)
    for j in range(1, NS):
        ss = lax.rem(shard + j, NS)
        rcopy(rfin.at[rel_row], rfin.at[rel_row], send.at[R4_S], recv.at[R4_S], (bucket, ss))

    pack(3, False)

    def give(src, dst, sem):
        pltpu.make_async_copy(src, dst, sem).start()

    wait_bytes(arrived, recv.at[ENT_S])
    give(arrived, arrived_out, out_sem.at[0])
    wait_bytes(rfin.at[pl.ds(0, 240)], recv.at[R4_S])
    half_rel = rfin.at[pl.ds(pl.multiple_of(c * 256, 256), 256)]
    rcopy(half_rel, half_rel, send.at[R5_S], recv.at[R5_S], partner)
    wait_bytes(rx2.at[pl.ds(0, 7)], recv.at[X2_S])
    give(rx2, rx2_out, out_sem.at[1])
    wait_bytes(ry2.at[pl.ds(0, 7)], recv.at[Y2_S])
    give(ry2, ry2_out, out_sem.at[2])
    wait_bytes(rz2.at[pl.ds(0, NS - 1)], recv.at[Z2_S])
    give(rz2, rz2_out, out_sem.at[3])
    wait_bytes(half_rel, recv.at[R5_S])
    give(rfin, rel_sum_out, out_sem.at[4])

    wait_bytes(nbt.at[pl.ds(0, 2)], send.at[GZ_S])
    wait_bytes(nbt.at[pl.ds(0, 3)], send.at[GX_S])
    wait_bytes(nbt.at[pl.ds(0, 3)], send.at[GY_S])
    for number in (Q1_S, Q2_S, Q3_S):
        wait_bytes(qt.at[mine, real], send.at[number])
    for number in (SQ1_S, SQ2_S, SQ3_S):
        wait_bytes(sq.at[mine], send.at[number])
    wait_bytes(st, send.at[ST1_S])
    for number in (SC1_S, SC2_S):
        wait_bytes(st.at[own_half], send.at[number])
    wait_bytes(ot_pair, send.at[O1_S])
    wait_bytes(o_far, send.at[O2_S])
    wait_bytes(ot_own, send.at[O3_S])
    wait_bytes(arrived.at[pl.ds(0, 2048 - SLOT)], send.at[ENT_S])
    wait_bytes(rp_in, send.at[RC_S])
    wait_bytes(r2in.at[pl.ds(0, NS - 1)], send.at[R2_S])
    wait_bytes(r2all.at[pl.ds(0, 3)], send.at[R3_S])
    wait_bytes(rfin.at[pl.ds(0, 240)], send.at[R4_S])
    wait_bytes(half_rel, send.at[R5_S])
    wait_bytes(rz1, send.at[Z1_S])
    wait_bytes(rx1.at[pl.ds(0, 3)], send.at[X1_S])
    wait_bytes(ry1.at[pl.ds(0, 3)], send.at[Y1_S])
    wait_bytes(rx2.at[pl.ds(0, 7)], send.at[X2_S])
    wait_bytes(ry2.at[pl.ds(0, 7)], send.at[Y2_S])
    wait_bytes(rz2.at[pl.ds(0, NS - 1)], send.at[Z2_S])
    wait_bytes(arrived, out_sem.at[0])
    wait_bytes(rx2, out_sem.at[1])
    wait_bytes(ry2, out_sem.at[2])
    wait_bytes(rz2, out_sem.at[3])
    wait_bytes(rfin, out_sem.at[4])


def finish(
    arrived_in, rx2_in, ry2_in, rz2_in, rel_in, ent_out, neg_out, rel_out,
    arrived, rx2, ry2, rz2, rel_sum, ent, neg_sum, rel_t, in_sem, out_sem,
):
    loads = [
        pltpu.make_async_copy(src, dst, in_sem.at[i])
        for i, (src, dst) in enumerate((
            (rel_in, rel_sum), (arrived_in, arrived), (rx2_in, rx2), (ry2_in, ry2), (rz2_in, rz2)
        ))
    ]
    for load in loads:
        load.start()
    loads[0].wait()
    for r in range(4):
        rows = rel_sum[r * 128 : (r + 1) * 128, :].astype(F32)
        wide = jnp.concatenate([rows, jnp.zeros((128, DP - D), F32)], axis=1)
        rel_t[:, r * 128 : (r + 1) * 128] = wide.T[0:D]
    stores = [pltpu.make_async_copy(rel_t, rel_out, out_sem.at[0])]
    stores[0].start()

    loads[1].wait()
    lane = iota((8, 128), 1)
    unit = jnp.where(lane == D - 384, 32.0, jnp.where(lane == D - 383, 1.0, 0.0)).astype(BF16)
    row_ids = nt(unit, arrived[:, 384:DP])[0:1, :]
    for r in range(2):
        hot = hot_where((iota((512, 2048), 0) + r * 512).astype(F32) == row_ids)
        ent[r] = nn(hot, arrived[...]).T[0:D]
        store = pltpu.make_async_copy(ent.at[r], ent_out.at[:, pl.ds(r * 512, 512)], out_sem.at[1 + r])
        store.start()
        stores.append(store)

    def sum_all(ref):
        total = ref[0].astype(F32)
        for i in range(1, ref.shape[0]):
            total = total + ref[i].astype(F32)
        return total

    for load in loads[2:]:
        load.wait()
    neg_sum[:, 0:128] = sum_all(rx2)
    neg_sum[:, 128:256] = sum_all(ry2)
    neg_sum[:, 256:D] = sum_all(rz2)[:, 0 : D - 256]
    stores.append(pltpu.make_async_copy(neg_sum, neg_out, out_sem.at[3]))
    stores[-1].start()
    for store in stores:
        store.wait()


SCRATCH = [
    ((16, D, 128), BF16),
    ((2, D, NEG_DEV), BF16),
    ((NEG_DEV, DP), BF16),
    ((2, NEG_DEV, 8 * EC), BF16),
    ((8, DP, EC), BF16),
    ((8, 8, EC), F32),
    ((2, D, EC), F32),
    ((2, D, EC), F32),
    ((2, D, EC), F32),
    ((2, 8, 8, EC), F32),
    ((8, 8, EC), F32),
    ((8, 8, EC), F32),
    ((8, 8, EC), F32),
    ((8, 8, EC), F32),
    ((8, D, EC), F32),
    ((2, D, EC), F32),
    ((2, D, EC), F32),
    ((2, D, EC), BF16),
    ((2, D, EC), BF16),
    ((8, 8, EC), F32),
    ((DP, 8 * EC), BF16),
    ((DP, 2 * E_DEV), BF16),
    ((D, E_DEV), BF16),
    ((D, E_DEV), BF16),
    ((NB, 256, DP), BF16),
    ((2048, DP), BF16),
    ((NB, 256, 128), F32),
    ((NB, 256, 128), F32),
    ((2, D - 256, NEG_DEV), BF16),
    ((2, 4, 256, 128), BF16),
    ((2, 4, 4, NEG_OWN, 128), BF16),
    ((D - 256, NEG_DEV), BF16),
    ((4, 2, 256, 128), BF16),
    ((4, 2, 4, NEG_OWN, 128), BF16),
    ((NEG_DEV, 256), BF16),
    ((2, 256, 128), BF16),
    ((2, 4, NEG_OWN, 128), BF16),
    ((NS, NEG_OWN, 256), BF16),
    ((8, NEG_OWN, 128), BF16),
    ((8, NEG_OWN, 128), BF16),
    ((REL, D), F32),
    ((REL // 2, D), F32),
    ((REL // 2, D), BF16),
    ((NS, 16, D), BF16),
    ((NZ, 16, D), F32),
    ((REL, D), BF16),
]


def per_device(
    head_rows, tail_rows, rel_ids, relations, edge_weights, neg_rows, send_slots, dest_rows
):
    vmem = pl.BlockSpec(memory_space=pltpu.VMEM)
    anywhere = pl.BlockSpec(memory_space=pl.ANY)
    results = pl.pallas_call(
        kernel,
        out_shape=(
            jax.ShapeDtypeStruct((2048, DP), BF16),
            jax.ShapeDtypeStruct((8, NEG_OWN, 128), BF16),
            jax.ShapeDtypeStruct((8, NEG_OWN, 128), BF16),
            jax.ShapeDtypeStruct((NS, NEG_OWN, 256), BF16),
            jax.ShapeDtypeStruct((REL, D), BF16),
        ),
        in_specs=[vmem] * 8,
        out_specs=(anywhere,) * 5,
        scratch_shapes=[pltpu.VMEM(shape, dtype) for shape, dtype in SCRATCH]
        + [
            pltpu.SemaphoreType.DMA((29,)),
            pltpu.SemaphoreType.DMA((29,)),
            pltpu.SemaphoreType.REGULAR((4,)),
            pltpu.SemaphoreType.DMA((5,)),
        ],
        compiler_params=pltpu.CompilerParams(
            collective_id=0, has_side_effects=True, vmem_limit_bytes=60 * 1024 * 1024
        ),
        cost_estimate=pl.CostEstimate(
            flops=2 * 3 * 1024 * 4096 * 400, bytes_accessed=8 * 1024 * 1024, transcendentals=1024 * 4096
        ),
        name="complex_backward",
    )(
        head_rows.T,
        tail_rows.T,
        rel_ids.reshape(1, E_DEV),
        relations.T,
        edge_weights.reshape(1, E_DEV),
        neg_rows.T,
        send_slots.T,
        dest_rows.T,
    )
    ent_t, neg_grad, rel_t = pl.pallas_call(
        finish,
        out_shape=(
            jax.ShapeDtypeStruct((D, ENT_DEV), F32),
            jax.ShapeDtypeStruct((NEG_OWN, D), F32),
            jax.ShapeDtypeStruct((D, REL), F32),
        ),
        in_specs=[anywhere] * 5,
        out_specs=(anywhere,) * 3,
        scratch_shapes=[
            pltpu.VMEM((2048, DP), BF16),
            pltpu.VMEM((8, NEG_OWN, 128), BF16),
            pltpu.VMEM((8, NEG_OWN, 128), BF16),
            pltpu.VMEM((NS, NEG_OWN, 256), BF16),
            pltpu.VMEM((REL, D), BF16),
            pltpu.VMEM((2, D, 512), F32),
            pltpu.VMEM((NEG_OWN, D), F32),
            pltpu.VMEM((D, REL), F32),
            pltpu.SemaphoreType.DMA((5,)),
            pltpu.SemaphoreType.DMA((4,)),
        ],
        compiler_params=pltpu.CompilerParams(vmem_limit_bytes=60 * 1024 * 1024),
        cost_estimate=pl.CostEstimate(
            flops=2 * 1024 * 2048 * 512, bytes_accessed=6 * 1024 * 1024, transcendentals=0
        ),
        name="make_outputs",
    )(*results)
    return ent_t.T, neg_grad, rel_t.T


def solution(mesh):
    return jax.shard_map(
        per_device,
        mesh=mesh,
        in_specs=(
            P(("bucket", "shard"), None),
            P(("bucket", "shard"), None),
            P(("bucket", "shard")),
            P(),
            P(("bucket", "shard")),
            P("bucket", None),
            P(("bucket", "shard"), None),
            P(("bucket", "shard"), None),
        ),
        out_specs=(P(("bucket", "shard"), None), P(("bucket", "shard"), None), P()),
        check_vma=False,
    )
```

```python
import functools

import jax
import jax.numpy as jnp
from jax import lax
from jax.experimental import pallas as pl
from jax.experimental.pallas import tpu as pltpu
from jax.sharding import PartitionSpec as P

D = 400
HALF = 200
DP = 512
E_DEV = 512
ENT_DEV = 1024
REL = 512
NEG_DEV = 1024
SLOT = 16
NB = 8
NS = 16
NZ = 4
EC = 256
NEG_OWN = 64

MESH = pl.DeviceIdType.MESH
F32 = jnp.float32
BF16 = jnp.bfloat16

(Q1_S, SQ1_S, Q2_S, SQ2_S, Q3_S, SQ3_S, ST1_S, O1_S, SC1_S, O2_S, ST2_S, O3_S, SC2_S,
 RC_S, R2_S, R3_S, R4_S, R5_S, ENT_S, Z1_S, X1_S, Y1_S, Z2_S, X2_S, Y2_S, GZ_S, GX_S, GY_S, O4_S,
 PX_S, PY_S) = range(31)


def nt(a, b):
    return lax.dot_general(a, b, (((1,), (1,)), ((), ())), preferred_element_type=F32)


def nn(a, b):
    return jnp.dot(a, b, preferred_element_type=F32)


def iota(shape, dim):
    return lax.broadcasted_iota(jnp.int32, shape, dim)


def hot_where(mask):
    return mask.astype(F32).astype(BF16)


def wait_bytes(ref, sem):
    pltpu.make_async_copy(ref, ref, sem).wait()


def kernel(
    head, tail, ids, rel, wts, neg, slots, drows,
    main_out, last_out, far_main_out, far_last_out, rx2_out, ry2_out, rz2_out, rel_sum_out,
    nbt, wide, nb, prob, qt, sq, hts, tts, rts, mb, st, st_in, sc, sc_in,
    ot, ot_pair, ot_own, o_sum, o_far, lt, qs, ends, rt_hi, rt_lo,
    packed, arrived, far_main, far_last, slot_col, dest_col,
    gz, gx, gy, rz1, rx1, ry1, az, ax, ay, rz2, rx2, ry2,
    rp, rp_in, r1b, r2in, r2all, rfin,
    send, recv, known, out_sem, ent_recv,
):
    bucket, shard = lax.axis_index("bucket"), lax.axis_index("shard")
    z, c = bucket // 2, bucket % 2
    x, y = shard // 4, shard % 4
    oc = 1 - c
    partner = (z * 2 + oc, shard)
    pair = ((z + 1 - 2 * (z % 2)) * 2 + c, shard)
    z_far = 3 - z
    far = (z_far * 2 + c, shard)

    def rcopy(src, dst, s_sem, r_sem, device):
        pltpu.make_async_remote_copy(
            src_ref=src, dst_ref=dst, send_sem=s_sem, recv_sem=r_sem,
            device_id=device, device_id_type=MESH,
        ).start()

    barrier = pltpu.get_barrier_semaphore()

    x_peers = [(bucket, lax.rem(x + i, 4) * 4 + y) for i in (1, 2, 3)]
    y_peers = [(bucket, x * 4 + lax.rem(y + i, 4)) for i in (1, 2, 3)]
    friends = [partner, pair, far] + x_peers + y_peers

    def tell(sem, devices):
        for device in devices:
            pl.semaphore_signal(sem, inc=1, device_id=device, device_id_type=MESH)

    tell(barrier, friends)

    for g in range(8):
        qt[g, D:DP, :] = jnp.zeros((DP - D, EC), BF16)
    wide[D:, :] = jnp.ones((16, NEG_DEV), BF16)

    for i in range(8):
        nbt[i] = neg[:, i * 128 : (i + 1) * 128]

    rel_1 = rel[...].astype(BF16)
    rest = rel[...] - rel_1.astype(F32)
    rel_2 = rest.astype(BF16)
    rel_3 = (rest - rel_2.astype(F32)).astype(BF16)
    for j in range(2):
        cols = slice(j * EC, (j + 1) * EC)
        h_t = head[:, cols].astype(F32)
        t_t = tail[:, cols].astype(F32)
        hot = hot_where(iota((REL, EC), 0) == ids[0:1, cols])
        r_t = (nn(rel_1, hot) + nn(rel_2, hot)) + nn(rel_3, hot)
        hre, him = h_t[:HALF], h_t[HALF:]
        rre, rim = r_t[:HALF], r_t[HALF:]
        q = jnp.concatenate([hre * rre - him * rim, hre * rim + him * rre], axis=0).astype(BF16)
        qt[2 * c + j, 0:D, :] = q
        sq[2 * c + j, 0:1, :] = jnp.sum(q.astype(F32) * t_t, axis=0, keepdims=True)
        sq[2 * c + j, 1:2, :] = wts[0:1, cols]
        sq[2 * c + j, 2:8, :] = jnp.zeros((6, EC), F32)
        hts[j] = h_t
        tts[j] = t_t
        rts[j] = r_t

    pl.semaphore_wait(barrier, len(friends))
    tell(known.at[0], y_peers)

    for i in (x, 4 + y):
        rcopy(nbt.at[i], nbt.at[8 + i], send.at[GZ_S], recv.at[GZ_S], far)
    mine, theirs, real = pl.ds(2 * c, 2), pl.ds(4 + 2 * c, 2), pl.ds(0, D)
    rcopy(qt.at[mine, real], qt.at[mine, real], send.at[Q1_S], recv.at[Q1_S], partner)
    rcopy(sq.at[mine], sq.at[mine], send.at[SQ1_S], recv.at[SQ1_S], partner)
    rcopy(qt.at[mine, real], qt.at[theirs, real], send.at[Q2_S], recv.at[Q2_S], pair)
    rcopy(sq.at[mine], sq.at[theirs], send.at[SQ2_S], recv.at[SQ2_S], pair)

    ones = jnp.ones((SLOT, 128), BF16)
    tables = []
    for ref in (slots, drows):
        value = ref[...].astype(F32)
        high = jnp.floor(value * (1.0 / 32.0))
        tables.append((high.astype(BF16), (value - 32.0 * high).astype(BF16)))

    def columns(b, carry):
        owner_hot = hot_where(iota((256, 128), 1) == iota((256, 128), 0) // SLOT + b * NS)
        keep = iota((256, SLOT), 1) == iota((256, SLOT), 0) % SLOT
        for (high, low), out in zip(tables, (slot_col, dest_col)):
            h = jnp.where(keep, nt(owner_hot, high), 0.0).astype(BF16)
            l = jnp.where(keep, nt(owner_hot, low), 0.0).astype(BF16)
            out[b] = 32.0 * nn(h, ones) + nn(l, ones)
        return carry

    lax.fori_loop(0, NB, columns, 0)
    nb[:, 384:DP] = jnp.zeros((NEG_DEV, 128), BF16)

    def flip(b):
        for i in range(8):
            part = nbt[b * 8 + i]
            wide[0:D, i * 128 : (i + 1) * 128] = part
            nb[i * 128 : (i + 1) * 128, 0:D] = part.astype(F32).T.astype(BF16)

    def block(b, two):

        chunks = (2 * two, 2 * two + 1)
        scores = [nn(nb[...], qt[g]) for g in chunks]
        for g, s in zip(chunks, scores):
            m = jnp.max(s, axis=0, keepdims=True)
            pb = jnp.exp(s - m).astype(BF16)
            prob[b, :, pl.ds(pl.multiple_of(g * EC, EC), EC)] = pb
            o = nn(wide[...], pb)
            l = o[D : D + 1]
            o = o[0:D]
            mb[b, g, 0:1, :] = m
            if b == 0:
                st[g, 0:1, :] = m
                st[g, 1:2, :] = l
                st[g, 2:8, :] = jnp.zeros((6, EC), F32)
                ot[g] = o
            else:
                m_old = st[g, 0:1, :]
                m_new = jnp.maximum(m_old, m)
                f_old = jnp.exp(m_old - m_new)
                f_new = jnp.exp(m - m_new)
                st[g, 0:1, :] = m_new
                st[g, 1:2, :] = st[g, 1:2, :] * f_old + l * f_new
                ot[g] = ot[g] * f_old + o * f_new

    flip(0)
    block(0, c)
    pl.semaphore_wait(known.at[0], 3)
    tell(known.at[1], (pair, far))
    wait_bytes(nbt.at[pl.ds(8, 2)], recv.at[GZ_S])
    for i in (1, 3, 2):
        xx, yy = lax.rem(x + i, 4), lax.rem(y + i, 4)
        rcopy(nbt.at[8 + x], nbt.at[8 + x], send.at[GX_S], recv.at[GX_S], (bucket, xx * 4 + y))
        rcopy(nbt.at[12 + y], nbt.at[12 + y], send.at[GY_S], recv.at[GY_S], (bucket, x * 4 + yy))
    wait_bytes(qt.at[mine, real], recv.at[Q1_S])
    wait_bytes(sq.at[mine], recv.at[SQ1_S])
    block(0, oc)
    pl.semaphore_wait(known.at[1], 2)
    tell(known.at[2], (pair, far))
    wait_bytes(qt.at[mine, real], recv.at[Q2_S])
    wait_bytes(sq.at[mine], recv.at[SQ2_S])
    rcopy(qt.at[theirs, real], qt.at[theirs, real], send.at[Q3_S], recv.at[Q3_S], partner)
    rcopy(sq.at[theirs], sq.at[theirs], send.at[SQ3_S], recv.at[SQ3_S], partner)
    block(0, 2 + c)
    wait_bytes(qt.at[mine, real], recv.at[Q3_S])
    wait_bytes(sq.at[mine], recv.at[SQ3_S])
    block(0, 2 + oc)
    wait_bytes(nbt.at[pl.ds(8, 3)], recv.at[GX_S])
    wait_bytes(nbt.at[pl.ds(8, 3)], recv.at[GY_S])
    flip(1)
    block(1, 2 + oc)
    pl.semaphore_wait(known.at[2], 2)
    tell(known.at[3], (partner,))
    rcopy(
        ot.at[pl.ds(4 + 2 * oc, 2)], ot_pair, send.at[O1_S], recv.at[O1_S], partner
    )
    block(1, 2 + c)
    own_half, pair_half = pl.ds(0, 4), pl.ds(4, 4)
    rcopy(st.at[pair_half], st_in.at[pair_half], send.at[ST1_S], recv.at[ST1_S], partner)

    def merge(g):
        m_a, m_b = st[g, 0:1, :], st_in[g, 0:1, :]
        m = jnp.maximum(m_a, m_b)
        f_a, f_b = jnp.exp(m_a - m), jnp.exp(m_b - m)
        sc[g, 0:1, :] = m
        sc[g, 1:2, :] = st[g, 1:2, :] * f_a + st_in[g, 1:2, :] * f_b
        sc[g, 2:8, :] = jnp.zeros((6, EC), F32)
        return f_a, f_b

    block(1, oc)
    pl.semaphore_wait(known.at[3], 1)
    rcopy(ot.at[pl.ds(2 * oc, 2)], ot_own, send.at[O3_S], recv.at[O3_S], partner)
    wait_bytes(st_in.at[pair_half], recv.at[ST1_S])
    wait_bytes(ot_pair, recv.at[O1_S])
    for g in range(4, 8):
        merge(g)
    for j in range(2):
        f_a, f_b = merge(4 + 2 * c + j)
        o_sum[j] = (ot[4 + 2 * c + j] * f_a + ot_pair[j] * f_b).astype(BF16)
    rcopy(o_sum.at[0], o_far.at[0], send.at[O4_S], recv.at[O4_S], pair)
    rcopy(sc.at[pair_half], sc_in.at[own_half], send.at[SC1_S], recv.at[SC1_S], pair)
    block(1, c)
    rcopy(st.at[own_half], st_in.at[own_half], send.at[ST2_S], recv.at[ST2_S], partner)
    wait_bytes(st_in.at[own_half], recv.at[ST2_S])
    for g in range(4):
        merge(g)
    rcopy(sc.at[own_half], sc_in.at[pair_half], send.at[SC2_S], recv.at[SC2_S], pair)
    rcopy(o_sum.at[1], o_far.at[1], send.at[O2_S], recv.at[O2_S], pair)
    wait_bytes(sc_in.at[own_half], recv.at[SC1_S])
    wait_bytes(sc_in.at[pair_half], recv.at[SC2_S])
    for g in range(8):
        pos = sq[g, 0:1, :]
        m0, m1 = sc[g, 0:1, :], sc_in[g, 0:1, :]
        top = jnp.maximum(pos, jnp.maximum(m0, m1))
        total = (
            jnp.exp(pos - top)
            + sc[g, 1:2, :] * jnp.exp(m0 - top)
            + sc_in[g, 1:2, :] * jnp.exp(m1 - top)
        )
        lt[g, 0:1, :] = top + jnp.log(total)

    def neg_block(b):
        for g in range(8):
            scale = sq[g, 1:2, :] * jnp.exp(mb[b, g, 0:1, :] - lt[g, 0:1, :])
            qs[:, g * EC : (g + 1) * EC] = (qt[g].astype(F32) * scale).astype(BF16)

        def rows_of(h, carry):
            rr = pl.ds(pl.multiple_of(h * 512, 512), 512)
            acc = nt(prob[b, rr, :], qs[...])
            for u in range(2):
                part = acc[u * 256 : (u + 1) * 256]
                gx[b, 2 * h + u] = part[:, 0:128].astype(BF16)
                for yy in range(4):
                    gy[b, yy, 2 * h + u] = part[yy * 64 : (yy + 1) * 64, 128:256].astype(BF16)
            gz[b, :, rr] = acc[:, 256:512].T[0 : D - 256].astype(BF16)
            return carry

        lax.fori_loop(0, 2, rows_of, 0)
        for i in (1, 3, 2):
            xx, yy = lax.rem(x + i, 4), lax.rem(y + i, 4)
            rcopy(gx.at[b, xx], rx1.at[x, b], send.at[X1_S], recv.at[X1_S], (bucket, xx * 4 + y))
            rcopy(gy.at[b, yy], ry1.at[y, b], send.at[Y1_S], recv.at[Y1_S], (bucket, x * 4 + yy))

    neg_block(1)
    rcopy(gz.at[1], rz1, send.at[Z1_S], recv.at[Z1_S], far)
    wait_bytes(ot_own, recv.at[O3_S])
    wait_bytes(o_far.at[0], recv.at[O4_S])
    wait_bytes(o_far.at[1], recv.at[O2_S])
    ends[D:DP, :] = jnp.zeros((DP - D, 2 * E_DEV), BF16)
    for j in range(2):
        cols = slice(j * EC, (j + 1) * EC)
        tail_cols = slice(E_DEV + j * EC, E_DEV + (j + 1) * EC)
        g = 2 * c + j
        pos, w, ltot = sq[g, 0:1, :], sq[g, 1:2, :], lt[g, 0:1, :]
        pos_coef = w * (jnp.exp(pos - ltot) - 1.0)
        own = w * jnp.exp(st[g, 0:1, :] - ltot)
        other = w * jnp.exp(st_in[g, 0:1, :] - ltot)
        away = w * jnp.exp(sc_in[g, 0:1, :] - ltot)
        grad = pos_coef * tts[j] + ot[g] * own + ot_own[j] * other + o_far[j].astype(F32) * away
        gre, gim = grad[:HALF], grad[HALF:]
        rre, rim = rts[j, :HALF, :], rts[j, HALF:, :]
        hre, him = hts[j, :HALF, :], hts[j, HALF:, :]
        head_grad = jnp.concatenate(
            [gre * rre + gim * rim, gim * rre - gre * rim], axis=0
        ).astype(BF16)
        tail_grad = (pos_coef * qt[g, 0:D, :].astype(F32)).astype(BF16)
        for part, where_to in ((head_grad, cols), (tail_grad, tail_cols)):
            ends[0:D, where_to] = part
            ends[416:432, where_to] = part[384:D]
        term = jnp.concatenate([gre * hre + gim * him, gim * hre - gre * him], axis=0)
        hi = term.astype(BF16)
        rt_hi[:, cols] = hi
        rt_lo[:, cols] = (term - hi.astype(F32)).astype(BF16)

    src_chip = z * NS + shard

    def pack(k, first):
        zz = lax.rem(z + k, NZ)
        chips = pl.ds(pl.multiple_of(zz * NS, NS), NS)
        sel = []
        for d in range(2):
            sc_b = slot_col[zz * 2 + d]
            sel.append(jnp.concatenate(
                [hot_where(sc_b == (iota((256, 128), 1) + 128 * t).astype(F32)) for t in range(8)],
                axis=1,
            ))
        rows = nt(jnp.concatenate(sel, axis=0), ends[...])
        lane = iota((256, 128), 1)
        last = []
        for d in range(2):
            part = rows[d * 256 : (d + 1) * 256]
            for t in range(3):
                first_row = (d * 3 + t) * SLOT
                tile = part[:, t * 128 : (t + 1) * 128].astype(BF16).reshape(NS, SLOT, 128)
                packed[chips, first_row : first_row + SLOT, :] = tile
            dc = dest_col[zz * 2 + d]
            high = jnp.floor(dc * (1.0 / 32.0))
            code = jnp.where(lane == 32 * d + 16, high, jnp.where(lane == 32 * d + 17, dc - 32.0 * high, 0.0))
            last.append(part[:, 384:512] + code)
        tile = jnp.where(lane < 32, last[0], last[1]).astype(BF16).reshape(NS, SLOT, 128)
        packed[chips, 96:112, :] = tile
        for j in range(NS):
            ss = lax.rem(shard + j, NS)
            src = packed.at[zz * NS + ss]
            if first and j == 0:
                pltpu.make_async_copy(src, arrived.at[src_chip], ent_recv.at[k]).start()
            else:
                rcopy(src, arrived.at[src_chip], send.at[ENT_S], ent_recv.at[k], (zz * 2 + c, ss))

    def rel_chunk(r, carry):
        hot = hot_where(iota((128, E_DEV), 0) + r * 128 == ids[...])
        rp[pl.ds(pl.multiple_of(r * 128, 128), 128), :] = nt(hot, rt_hi[...]) + nt(hot, rt_lo[...])
        return carry

    lax.fori_loop(0, 4, rel_chunk, 0)
    rcopy(
        rp.at[pl.ds(pl.multiple_of(oc * 256, 256), 256)], rp_in, send.at[RC_S], recv.at[RC_S], partner
    )

    def pack_other(k, carry):
        pack(k, False)
        return carry

    pack(0, True)
    lax.fori_loop(1, 2, pack_other, 0)

    wait_bytes(rp_in, recv.at[RC_S])
    r1b[...] = (rp[pl.ds(pl.multiple_of(c * 256, 256), 256), :] + rp_in[...]).astype(BF16)
    for j in range(1, NS):
        ss = lax.rem(shard + j, NS)
        rows = r1b.at[pl.ds(pl.multiple_of(ss * 16, 16), 16)]
        rcopy(rows, r2in.at[shard], send.at[R2_S], recv.at[R2_S], (bucket, ss))
    r2in[shard] = r1b[pl.ds(pl.multiple_of(shard * 16, 16), 16), :]
    neg_block(0)
    lax.fori_loop(2, NB // 2, pack_other, 0)


    wait_bytes(r2in.at[pl.ds(0, NS - 1)], recv.at[R2_S])
    r2 = r2in[0].astype(F32)
    for i in range(1, NS):
        r2 = r2 + r2in[i].astype(F32)
    r2all[z] = r2
    for k in (1, 3, 2):
        zz = lax.rem(z + k, NZ)
        rcopy(r2all.at[z], r2all.at[z], send.at[R3_S], recv.at[R3_S], (zz * 2 + c, shard))

    my_rows = pl.ds(pl.multiple_of(shard * NEG_OWN, NEG_OWN), NEG_OWN)
    wait_bytes(rx1.at[pl.ds(0, 3)], recv.at[X1_S])
    for b in range(2):
        total = gx[b, x].astype(F32)
        for i in range(1, 4):
            total = total + rx1[lax.rem(x + i, 4), b].astype(F32)
        ax[b] = total.astype(BF16)
    for i in range(4):
        yy = lax.rem(y + i, 4)
        rows = pl.ds(pl.multiple_of(yy * NEG_OWN, NEG_OWN), NEG_OWN)
        if i:
            rcopy(ax.at[0, rows], rx2.at[y], send.at[X2_S], recv.at[X2_S], (bucket, x * 4 + yy))
        else:
            rx2[y] = ax[0, rows, :]
        rcopy(
            ax.at[1, rows], rx2.at[4 + y], send.at[X2_S], recv.at[X2_S], (z_far * 2 + c, x * 4 + yy)
        )
    wait_bytes(r2all.at[pl.ds(0, 3)], recv.at[R3_S])
    rel_row = pl.ds(pl.multiple_of(c * 256 + shard * 16, 16), 16)
    rfin[rel_row, :] = (((r2all[0] + r2all[1]) + r2all[2]) + r2all[3]).astype(BF16)
    for j in range(1, NS):
        ss = lax.rem(shard + j, NS)
        rcopy(rfin.at[rel_row], rfin.at[rel_row], send.at[R4_S], recv.at[R4_S], (bucket, ss))

    wait_bytes(ry1.at[pl.ds(0, 3)], recv.at[Y1_S])
    for b in range(2):
        total = gy[b, y].astype(F32)
        for i in range(1, 4):
            total = total + ry1[lax.rem(y + i, 4), b].astype(F32)
        ay[b] = total.astype(BF16)
    for i in range(4):
        xx = lax.rem(x + i, 4)
        if i:
            rcopy(ay.at[0, xx], ry2.at[x], send.at[Y2_S], recv.at[Y2_S], (bucket, xx * 4 + y))
        else:
            ry2[x] = ay[0, x]
        rcopy(
            ay.at[1, xx], ry2.at[4 + x], send.at[Y2_S], recv.at[Y2_S], (z_far * 2 + c, xx * 4 + y)
        )
    wait_bytes(rz1, recv.at[Z1_S])

    def sum_z(r, carry):
        rr = pl.ds(pl.multiple_of(r * 256, 256), 256)
        total = gz[0, :, rr].astype(F32) + rz1[:, rr].astype(F32)
        wide_sum = jnp.concatenate([total, jnp.zeros((256 - (D - 256), 256), F32)], axis=0)
        az[rr, :] = wide_sum.T.astype(BF16)
        return carry

    lax.fori_loop(0, 4, sum_z, 0)
    for j in range(1, NS):
        ss = lax.rem(shard + j, NS)
        rows = az.at[pl.ds(pl.multiple_of(ss * NEG_OWN, NEG_OWN), NEG_OWN)]
        rcopy(rows, rz2.at[shard], send.at[Z2_S], recv.at[Z2_S], (bucket, ss))
    rz2[shard] = az[my_rows, :]

    def give(src, dst, sem):
        pltpu.make_async_copy(src, dst, sem).start()

    other_rows, last_rows = pl.ds(pl.multiple_of(oc * 48, 16), 48), pl.ds(96, SLOT)
    for k in range(NZ):
        chips = pl.ds(pl.multiple_of(lax.rem(z + NZ - k, NZ) * NS, NS), NS)
        wait_bytes(arrived.at[chips], ent_recv.at[k])
        rcopy(arrived.at[chips, other_rows], far_main.at[chips], send.at[PX_S], recv.at[PX_S], partner)
        rcopy(arrived.at[chips, last_rows], far_last.at[chips], send.at[PY_S], recv.at[PY_S], partner)
    give(arrived.at[:, pl.ds(pl.multiple_of(c * 48, 16), 48)], main_out, out_sem.at[0])
    give(arrived.at[:, last_rows], last_out, out_sem.at[5])
    wait_bytes(rfin.at[pl.ds(0, 240)], recv.at[R4_S])
    half_rel = rfin.at[pl.ds(pl.multiple_of(c * 256, 256), 256)]
    rcopy(half_rel, half_rel, send.at[R5_S], recv.at[R5_S], partner)
    wait_bytes(rx2.at[pl.ds(0, 7)], recv.at[X2_S])
    give(rx2, rx2_out, out_sem.at[1])
    wait_bytes(ry2.at[pl.ds(0, 7)], recv.at[Y2_S])
    give(ry2, ry2_out, out_sem.at[2])
    wait_bytes(rz2.at[pl.ds(0, NS - 1)], recv.at[Z2_S])
    give(rz2, rz2_out, out_sem.at[3])
    wait_bytes(half_rel, recv.at[R5_S])
    give(rfin, rel_sum_out, out_sem.at[4])
    wait_bytes(far_main, recv.at[PX_S])
    give(far_main, far_main_out, out_sem.at[6])
    wait_bytes(far_last, recv.at[PY_S])
    give(far_last, far_last_out, out_sem.at[7])

    wait_bytes(nbt.at[pl.ds(0, 2)], send.at[GZ_S])
    wait_bytes(nbt.at[pl.ds(0, 3)], send.at[GX_S])
    wait_bytes(nbt.at[pl.ds(0, 3)], send.at[GY_S])
    for number in (Q1_S, Q2_S, Q3_S):
        wait_bytes(qt.at[mine, real], send.at[number])
    for number in (SQ1_S, SQ2_S, SQ3_S):
        wait_bytes(sq.at[mine], send.at[number])
    for number in (ST1_S, ST2_S, SC1_S, SC2_S):
        wait_bytes(st.at[own_half], send.at[number])
    wait_bytes(ot_pair, send.at[O1_S])
    wait_bytes(o_far.at[0], send.at[O4_S])
    wait_bytes(o_far.at[1], send.at[O2_S])
    wait_bytes(ot_own, send.at[O3_S])
    wait_bytes(arrived.at[pl.ds(0, 63)], send.at[ENT_S])
    wait_bytes(far_main, send.at[PX_S])
    wait_bytes(far_last, send.at[PY_S])
    wait_bytes(rp_in, send.at[RC_S])
    wait_bytes(r2in.at[pl.ds(0, NS - 1)], send.at[R2_S])
    wait_bytes(r2all.at[pl.ds(0, 3)], send.at[R3_S])
    wait_bytes(rfin.at[pl.ds(0, 240)], send.at[R4_S])
    wait_bytes(half_rel, send.at[R5_S])
    wait_bytes(rz1, send.at[Z1_S])
    wait_bytes(rx1.at[pl.ds(0, 3)], send.at[X1_S])
    wait_bytes(ry1.at[pl.ds(0, 3)], send.at[Y1_S])
    wait_bytes(rx2.at[pl.ds(0, 7)], send.at[X2_S])
    wait_bytes(ry2.at[pl.ds(0, 7)], send.at[Y2_S])
    wait_bytes(rz2.at[pl.ds(0, NS - 1)], send.at[Z2_S])
    for number in (0, 6):
        wait_bytes(far_main, out_sem.at[number])
    for number in (5, 7):
        wait_bytes(far_last, out_sem.at[number])
    wait_bytes(rx2, out_sem.at[1])
    wait_bytes(ry2, out_sem.at[2])
    wait_bytes(rz2, out_sem.at[3])
    wait_bytes(rfin, out_sem.at[4])


def finish(
    main_in, last_in, far_main_in, far_last_in, rx2_in, ry2_in, rz2_in, rel_in,
    ent_out, neg_out, rel_out,
    main, last, far_main, far_last, rx2, ry2, rz2, rel_sum, ent, neg_sum, rel_t, in_sem, out_sem,
):
    loads = [
        pltpu.make_async_copy(src, dst, in_sem.at[i])
        for i, (src, dst) in enumerate((
            (rel_in, rel_sum), (last_in, last), (far_last_in, far_last), (main_in, main),
            (far_main_in, far_main), (rx2_in, rx2), (ry2_in, ry2), (rz2_in, rz2),
        ))
    ]
    for load in loads:
        load.start()
    loads[0].wait()
    for r in range(4):
        rows = rel_sum[r * 128 : (r + 1) * 128, :].astype(F32)
        wide = jnp.concatenate([rows, jnp.zeros((128, DP - D), F32)], axis=1)
        rel_t[:, r * 128 : (r + 1) * 128] = wide.T[0:D]
    stores = [pltpu.make_async_copy(rel_t, rel_out, out_sem.at[0])]
    stores[0].start()

    c = lax.axis_index("bucket") % 2
    lane = iota((8, 128), 1) - 32 * c
    unit = jnp.where(lane == 16, 32.0, jnp.where(lane == 17, 1.0, 0.0)).astype(BF16)
    for load in loads[1:5]:
        load.wait()
    slots, row_ids = [], []
    for tiles, tail in ((main, last), (far_main, far_last)):
        tail_rows = tail[...].reshape(1024, 128)
        columns = [tiles[:, t * SLOT : (t + 1) * SLOT, :].reshape(1024, 128) for t in range(3)]
        slots.append(jnp.concatenate(columns + [tail_rows], axis=1))
        row_ids.append(nt(unit, tail_rows)[0:1, :])
    for r in range(2):
        numbers = (iota((512, 1024), 0) + r * 512).astype(F32)
        got = nn(hot_where(numbers == row_ids[0]), slots[0]) + nn(hot_where(numbers == row_ids[1]), slots[1])
        turned = got.T
        ent[r, 0:384] = turned[0:384]
        ent[r, 384:D] = jnp.where(c == 0, turned[384:400], turned[416:432])
        store = pltpu.make_async_copy(ent.at[r], ent_out.at[:, pl.ds(r * 512, 512)], out_sem.at[1 + r])
        store.start()
        stores.append(store)

    def sum_all(ref):
        total = ref[0].astype(F32)
        for i in range(1, ref.shape[0]):
            total = total + ref[i].astype(F32)
        return total

    for load in loads[5:]:
        load.wait()
    neg_sum[:, 0:128] = sum_all(rx2)
    neg_sum[:, 128:256] = sum_all(ry2)
    neg_sum[:, 256:D] = sum_all(rz2)[:, 0 : D - 256]
    stores.append(pltpu.make_async_copy(neg_sum, neg_out, out_sem.at[3]))
    stores[-1].start()
    for store in stores:
        store.wait()


SCRATCH = [
    ((16, D, 128), BF16),
    ((D + 16, NEG_DEV), BF16),
    ((NEG_DEV, DP), BF16),
    ((2, NEG_DEV, 8 * EC), BF16),
    ((8, DP, EC), BF16),
    ((8, 8, EC), F32),
    ((2, D, EC), F32),
    ((2, D, EC), F32),
    ((2, D, EC), F32),
    ((2, 8, 8, EC), F32),
    ((8, 8, EC), F32),
    ((8, 8, EC), F32),
    ((8, 8, EC), F32),
    ((8, 8, EC), F32),
    ((8, D, EC), F32),
    ((2, D, EC), F32),
    ((2, D, EC), F32),
    ((2, D, EC), BF16),
    ((2, D, EC), BF16),
    ((8, 8, EC), F32),
    ((DP, 8 * EC), BF16),
    ((DP, 2 * E_DEV), BF16),
    ((D, E_DEV), BF16),
    ((D, E_DEV), BF16),
    ((NZ * NS, 112, 128), BF16),
    ((NZ * NS, 112, 128), BF16),
    ((NZ * NS, 48, 128), BF16),
    ((NZ * NS, SLOT, 128), BF16),
    ((NB, 256, 128), F32),
    ((NB, 256, 128), F32),
    ((2, D - 256, NEG_DEV), BF16),
    ((2, 4, 256, 128), BF16),
    ((2, 4, 4, NEG_OWN, 128), BF16),
    ((D - 256, NEG_DEV), BF16),
    ((4, 2, 256, 128), BF16),
    ((4, 2, 4, NEG_OWN, 128), BF16),
    ((NEG_DEV, 256), BF16),
    ((2, 256, 128), BF16),
    ((2, 4, NEG_OWN, 128), BF16),
    ((NS, NEG_OWN, 256), BF16),
    ((8, NEG_OWN, 128), BF16),
    ((8, NEG_OWN, 128), BF16),
    ((REL, D), F32),
    ((REL // 2, D), F32),
    ((REL // 2, D), BF16),
    ((NS, 16, D), BF16),
    ((NZ, 16, D), F32),
    ((REL, D), BF16),
]


def per_device(
    head_rows, tail_rows, rel_ids, relations, edge_weights, neg_rows, send_slots, dest_rows
):
    vmem = pl.BlockSpec(memory_space=pltpu.VMEM)
    anywhere = pl.BlockSpec(memory_space=pl.ANY)
    results = pl.pallas_call(
        kernel,
        out_shape=(
            jax.ShapeDtypeStruct((NZ * NS, 48, 128), BF16),
            jax.ShapeDtypeStruct((NZ * NS, SLOT, 128), BF16),
            jax.ShapeDtypeStruct((NZ * NS, 48, 128), BF16),
            jax.ShapeDtypeStruct((NZ * NS, SLOT, 128), BF16),
            jax.ShapeDtypeStruct((8, NEG_OWN, 128), BF16),
            jax.ShapeDtypeStruct((8, NEG_OWN, 128), BF16),
            jax.ShapeDtypeStruct((NS, NEG_OWN, 256), BF16),
            jax.ShapeDtypeStruct((REL, D), BF16),
        ),
        in_specs=[vmem] * 8,
        out_specs=(anywhere,) * 8,
        scratch_shapes=[pltpu.VMEM(shape, dtype) for shape, dtype in SCRATCH]
        + [
            pltpu.SemaphoreType.DMA((31,)),
            pltpu.SemaphoreType.DMA((31,)),
            pltpu.SemaphoreType.REGULAR((4,)),
            pltpu.SemaphoreType.DMA((8,)),
            pltpu.SemaphoreType.DMA((NZ,)),
        ],
        compiler_params=pltpu.CompilerParams(
            collective_id=0, has_side_effects=True, vmem_limit_bytes=60 * 1024 * 1024
        ),
        cost_estimate=pl.CostEstimate(
            flops=2 * 3 * 1024 * 4096 * 400, bytes_accessed=8 * 1024 * 1024, transcendentals=1024 * 4096
        ),
        name="complex_backward",
    )(
        head_rows.T,
        tail_rows.T,
        rel_ids.reshape(1, E_DEV),
        relations.T,
        edge_weights.reshape(1, E_DEV),
        neg_rows.T,
        send_slots.T,
        dest_rows.T,
    )
    ent_t, neg_grad, rel_t = pl.pallas_call(
        finish,
        out_shape=(
            jax.ShapeDtypeStruct((D, ENT_DEV), F32),
            jax.ShapeDtypeStruct((NEG_OWN, D), F32),
            jax.ShapeDtypeStruct((D, REL), F32),
        ),
        in_specs=[anywhere] * 8,
        out_specs=(anywhere,) * 3,
        scratch_shapes=[
            pltpu.VMEM((NZ * NS, 48, 128), BF16),
            pltpu.VMEM((NZ * NS, SLOT, 128), BF16),
            pltpu.VMEM((NZ * NS, 48, 128), BF16),
            pltpu.VMEM((NZ * NS, SLOT, 128), BF16),
            pltpu.VMEM((8, NEG_OWN, 128), BF16),
            pltpu.VMEM((8, NEG_OWN, 128), BF16),
            pltpu.VMEM((NS, NEG_OWN, 256), BF16),
            pltpu.VMEM((REL, D), BF16),
            pltpu.VMEM((2, D, 512), F32),
            pltpu.VMEM((NEG_OWN, D), F32),
            pltpu.VMEM((D, REL), F32),
            pltpu.SemaphoreType.DMA((8,)),
            pltpu.SemaphoreType.DMA((4,)),
        ],
        compiler_params=pltpu.CompilerParams(vmem_limit_bytes=60 * 1024 * 1024),
        cost_estimate=pl.CostEstimate(
            flops=2 * 1024 * 2048 * 512, bytes_accessed=6 * 1024 * 1024, transcendentals=0
        ),
        name="make_outputs",
    )(*results)
    return ent_t.T, neg_grad, rel_t.T


def solution(mesh):
    return jax.shard_map(
        per_device,
        mesh=mesh,
        in_specs=(
            P(("bucket", "shard"), None),
            P(("bucket", "shard"), None),
            P(("bucket", "shard")),
            P(),
            P(("bucket", "shard")),
            P("bucket", None),
            P(("bucket", "shard"), None),
            P(("bucket", "shard"), None),
        ),
        out_specs=(P(("bucket", "shard"), None), P(("bucket", "shard"), None), P()),
        check_vma=False,
    )
```

```python
import functools

import jax
import jax.numpy as jnp
from jax import lax
from jax.experimental import pallas as pl
from jax.experimental.pallas import tpu as pltpu
from jax.sharding import PartitionSpec as P

D = 400
HALF = 200
DP = 512
E_DEV = 512
ENT_DEV = 1024
REL = 512
NEG_DEV = 1024
SLOT = 16
NB = 8
NS = 16
NZ = 4
EC = 256
NEG_OWN = 64

MESH = pl.DeviceIdType.MESH
F32 = jnp.float32
BF16 = jnp.bfloat16

FAR_OFFSETS = [
    (dx, dy, dz) for dz in range(4) for dx in range(4) for dy in range(4) if 2 in (dx, dy, dz)
]
FORWARDED = [(dx, dy, dz) for dx, dy, dz in FAR_OFFSETS if (dy + dz) % 4 < 2]


def steps_back(offset):
    return tuple(int(d == 2) for d in offset)


(Q1_S, SQ1_S, Q2_S, SQ2_S, Q3_S, SQ3_S, ST1_S, O1_S, SC1_S, O2_S, ST2_S, O3_S, SC2_S,
 RC_S, R2_S, R3_S, R4_S, R5_S, ENT_S, Z1_S, X1_S, Y1_S, Z2_S, X2_S, Y2_S, GZ_S, GX_S, GY_S, O4_S,
 PX_S, PY_S, FW_S) = range(32)


def nt(a, b):
    return lax.dot_general(a, b, (((1,), (1,)), ((), ())), preferred_element_type=F32)


def nn(a, b):
    return jnp.dot(a, b, preferred_element_type=F32)


def iota(shape, dim):
    return lax.broadcasted_iota(jnp.int32, shape, dim)


def hot_where(mask):
    return mask.astype(F32).astype(BF16)


def wait_bytes(ref, sem):
    pltpu.make_async_copy(ref, ref, sem).wait()


def kernel(
    head, tail, ids, rel, wts, neg, slots, drows,
    main_out, last_out, far_main_out, far_last_out, rx2_out, ry2_out, rz2_out, rel_sum_out,
    nbt, wide, nb, prob, qt, sq, hts, tts, rts, mb, st, st_in, sc, sc_in,
    ot, ot_pair, ot_own, o_sum, o_far, lt, qs, ends, rt_hi, rt_lo,
    packed, arrived, passing, far_main, far_last, slot_col, dest_col,
    gz, gx, gy, rz1, rx1, ry1, az, ax, ay, rz2, rx2, ry2,
    rp, rp_in, r1b, r2in, r2all, rfin,
    send, recv, known, out_sem, ent_recv,
):
    bucket, shard = lax.axis_index("bucket"), lax.axis_index("shard")
    z, c = bucket // 2, bucket % 2
    x, y = shard // 4, shard % 4
    oc = 1 - c
    partner = (z * 2 + oc, shard)
    pair = ((z + 1 - 2 * (z % 2)) * 2 + c, shard)
    z_far = 3 - z
    far = (z_far * 2 + c, shard)

    def rcopy(src, dst, s_sem, r_sem, device):
        pltpu.make_async_remote_copy(
            src_ref=src, dst_ref=dst, send_sem=s_sem, recv_sem=r_sem,
            device_id=device, device_id_type=MESH,
        ).start()

    barrier = pltpu.get_barrier_semaphore()

    x_peers = [(bucket, lax.rem(x + i, 4) * 4 + y) for i in (1, 2, 3)]
    y_peers = [(bucket, x * 4 + lax.rem(y + i, 4)) for i in (1, 2, 3)]
    friends = [partner, pair, far] + x_peers + y_peers

    def tell(sem, devices):
        for device in devices:
            pl.semaphore_signal(sem, inc=1, device_id=device, device_id_type=MESH)

    tell(barrier, friends)

    for g in range(8):
        qt[g, D:DP, :] = jnp.zeros((DP - D, EC), BF16)
    wide[D:, :] = jnp.ones((16, NEG_DEV), BF16)

    for i in range(8):
        nbt[i] = neg[:, i * 128 : (i + 1) * 128]

    rel_1 = rel[...].astype(BF16)
    rest = rel[...] - rel_1.astype(F32)
    rel_2 = rest.astype(BF16)
    rel_3 = (rest - rel_2.astype(F32)).astype(BF16)
    for j in range(2):
        cols = slice(j * EC, (j + 1) * EC)
        h_t = head[:, cols].astype(F32)
        t_t = tail[:, cols].astype(F32)
        hot = hot_where(iota((REL, EC), 0) == ids[0:1, cols])
        r_t = (nn(rel_1, hot) + nn(rel_2, hot)) + nn(rel_3, hot)
        hre, him = h_t[:HALF], h_t[HALF:]
        rre, rim = r_t[:HALF], r_t[HALF:]
        q = jnp.concatenate([hre * rre - him * rim, hre * rim + him * rre], axis=0).astype(BF16)
        qt[2 * c + j, 0:D, :] = q
        sq[2 * c + j, 0:1, :] = jnp.sum(q.astype(F32) * t_t, axis=0, keepdims=True)
        sq[2 * c + j, 1:2, :] = wts[0:1, cols]
        sq[2 * c + j, 2:8, :] = jnp.zeros((6, EC), F32)
        hts[j] = h_t
        tts[j] = t_t
        rts[j] = r_t

    pl.semaphore_wait(barrier, len(friends))
    tell(known.at[0], y_peers)

    for i in (x, 4 + y):
        rcopy(nbt.at[i], nbt.at[8 + i], send.at[GZ_S], recv.at[GZ_S], far)
    mine, theirs, real = pl.ds(2 * c, 2), pl.ds(4 + 2 * c, 2), pl.ds(0, D)
    rcopy(qt.at[mine, real], qt.at[mine, real], send.at[Q1_S], recv.at[Q1_S], partner)
    rcopy(sq.at[mine], sq.at[mine], send.at[SQ1_S], recv.at[SQ1_S], partner)
    rcopy(qt.at[mine, real], qt.at[theirs, real], send.at[Q2_S], recv.at[Q2_S], pair)
    rcopy(sq.at[mine], sq.at[theirs], send.at[SQ2_S], recv.at[SQ2_S], pair)

    ones = jnp.ones((SLOT, 128), BF16)
    tables = []
    for ref in (slots, drows):
        value = ref[...].astype(F32)
        high = jnp.floor(value * (1.0 / 32.0))
        tables.append((high.astype(BF16), (value - 32.0 * high).astype(BF16)))

    def columns(b, carry):
        owner_hot = hot_where(iota((256, 128), 1) == iota((256, 128), 0) // SLOT + b * NS)
        keep = iota((256, SLOT), 1) == iota((256, SLOT), 0) % SLOT
        for (high, low), out in zip(tables, (slot_col, dest_col)):
            h = jnp.where(keep, nt(owner_hot, high), 0.0).astype(BF16)
            l = jnp.where(keep, nt(owner_hot, low), 0.0).astype(BF16)
            out[b] = 32.0 * nn(h, ones) + nn(l, ones)
        return carry

    lax.fori_loop(0, NB, columns, 0)
    nb[:, 384:DP] = jnp.zeros((NEG_DEV, 128), BF16)

    def flip(b):
        for i in range(8):
            part = nbt[b * 8 + i]
            wide[0:D, i * 128 : (i + 1) * 128] = part
            nb[i * 128 : (i + 1) * 128, 0:D] = part.astype(F32).T.astype(BF16)

    def block(b, two):

        chunks = (2 * two, 2 * two + 1)
        scores = [nn(nb[...], qt[g]) for g in chunks]
        for g, s in zip(chunks, scores):
            m = jnp.max(s, axis=0, keepdims=True)
            pb = jnp.exp(s - m).astype(BF16)
            prob[b, :, pl.ds(pl.multiple_of(g * EC, EC), EC)] = pb
            o = nn(wide[...], pb)
            l = o[D : D + 1]
            o = o[0:D]
            mb[b, g, 0:1, :] = m
            if b == 0:
                st[g, 0:1, :] = m
                st[g, 1:2, :] = l
                st[g, 2:8, :] = jnp.zeros((6, EC), F32)
                ot[g] = o
            else:
                m_old = st[g, 0:1, :]
                m_new = jnp.maximum(m_old, m)
                f_old = jnp.exp(m_old - m_new)
                f_new = jnp.exp(m - m_new)
                st[g, 0:1, :] = m_new
                st[g, 1:2, :] = st[g, 1:2, :] * f_old + l * f_new
                ot[g] = ot[g] * f_old + o * f_new

    flip(0)
    block(0, c)
    pl.semaphore_wait(known.at[0], 3)
    tell(known.at[1], (pair, far))
    wait_bytes(nbt.at[pl.ds(8, 2)], recv.at[GZ_S])
    for i in (1, 3, 2):
        xx, yy = lax.rem(x + i, 4), lax.rem(y + i, 4)
        rcopy(nbt.at[8 + x], nbt.at[8 + x], send.at[GX_S], recv.at[GX_S], (bucket, xx * 4 + y))
        rcopy(nbt.at[12 + y], nbt.at[12 + y], send.at[GY_S], recv.at[GY_S], (bucket, x * 4 + yy))
    wait_bytes(qt.at[mine, real], recv.at[Q1_S])
    wait_bytes(sq.at[mine], recv.at[SQ1_S])
    block(0, oc)
    pl.semaphore_wait(known.at[1], 2)
    tell(known.at[2], (pair, far))
    wait_bytes(qt.at[mine, real], recv.at[Q2_S])
    wait_bytes(sq.at[mine], recv.at[SQ2_S])
    rcopy(qt.at[theirs, real], qt.at[theirs, real], send.at[Q3_S], recv.at[Q3_S], partner)
    rcopy(sq.at[theirs], sq.at[theirs], send.at[SQ3_S], recv.at[SQ3_S], partner)
    block(0, 2 + c)
    wait_bytes(qt.at[mine, real], recv.at[Q3_S])
    wait_bytes(sq.at[mine], recv.at[SQ3_S])
    block(0, 2 + oc)
    wait_bytes(nbt.at[pl.ds(8, 3)], recv.at[GX_S])
    wait_bytes(nbt.at[pl.ds(8, 3)], recv.at[GY_S])
    flip(1)
    block(1, 2 + oc)
    pl.semaphore_wait(known.at[2], 2)
    tell(known.at[3], (partner,))
    rcopy(
        ot.at[pl.ds(4 + 2 * oc, 2)], ot_pair, send.at[O1_S], recv.at[O1_S], partner
    )
    block(1, 2 + c)
    own_half, pair_half = pl.ds(0, 4), pl.ds(4, 4)
    rcopy(st.at[pair_half], st_in.at[pair_half], send.at[ST1_S], recv.at[ST1_S], partner)

    def merge(g):
        m_a, m_b = st[g, 0:1, :], st_in[g, 0:1, :]
        m = jnp.maximum(m_a, m_b)
        f_a, f_b = jnp.exp(m_a - m), jnp.exp(m_b - m)
        sc[g, 0:1, :] = m
        sc[g, 1:2, :] = st[g, 1:2, :] * f_a + st_in[g, 1:2, :] * f_b
        sc[g, 2:8, :] = jnp.zeros((6, EC), F32)
        return f_a, f_b

    block(1, oc)
    pl.semaphore_wait(known.at[3], 1)
    rcopy(ot.at[pl.ds(2 * oc, 2)], ot_own, send.at[O3_S], recv.at[O3_S], partner)
    wait_bytes(st_in.at[pair_half], recv.at[ST1_S])
    wait_bytes(ot_pair, recv.at[O1_S])
    for g in range(4, 8):
        merge(g)
    for j in range(2):
        f_a, f_b = merge(4 + 2 * c + j)
        o_sum[j] = (ot[4 + 2 * c + j] * f_a + ot_pair[j] * f_b).astype(BF16)
    rcopy(o_sum.at[0], o_far.at[0], send.at[O4_S], recv.at[O4_S], pair)
    rcopy(sc.at[pair_half], sc_in.at[own_half], send.at[SC1_S], recv.at[SC1_S], pair)
    block(1, c)
    rcopy(st.at[own_half], st_in.at[own_half], send.at[ST2_S], recv.at[ST2_S], partner)
    wait_bytes(st_in.at[own_half], recv.at[ST2_S])
    for g in range(4):
        merge(g)
    rcopy(sc.at[own_half], sc_in.at[pair_half], send.at[SC2_S], recv.at[SC2_S], pair)
    rcopy(o_sum.at[1], o_far.at[1], send.at[O2_S], recv.at[O2_S], pair)
    wait_bytes(sc_in.at[own_half], recv.at[SC1_S])
    wait_bytes(sc_in.at[pair_half], recv.at[SC2_S])
    for g in range(8):
        pos = sq[g, 0:1, :]
        m0, m1 = sc[g, 0:1, :], sc_in[g, 0:1, :]
        top = jnp.maximum(pos, jnp.maximum(m0, m1))
        total = (
            jnp.exp(pos - top)
            + sc[g, 1:2, :] * jnp.exp(m0 - top)
            + sc_in[g, 1:2, :] * jnp.exp(m1 - top)
        )
        lt[g, 0:1, :] = top + jnp.log(total)

    def neg_block(b):
        for g in range(8):
            scale = sq[g, 1:2, :] * jnp.exp(mb[b, g, 0:1, :] - lt[g, 0:1, :])
            qs[:, g * EC : (g + 1) * EC] = (qt[g].astype(F32) * scale).astype(BF16)

        def rows_of(h, carry):
            rr = pl.ds(pl.multiple_of(h * 512, 512), 512)
            acc = nt(prob[b, rr, :], qs[...])
            for u in range(2):
                part = acc[u * 256 : (u + 1) * 256]
                gx[b, 2 * h + u] = part[:, 0:128].astype(BF16)
                for yy in range(4):
                    gy[b, yy, 2 * h + u] = part[yy * 64 : (yy + 1) * 64, 128:256].astype(BF16)
            gz[b, :, rr] = acc[:, 256:512].T[0 : D - 256].astype(BF16)
            return carry

        lax.fori_loop(0, 2, rows_of, 0)
        for i in (1, 3, 2):
            xx, yy = lax.rem(x + i, 4), lax.rem(y + i, 4)
            rcopy(gx.at[b, xx], rx1.at[x, b], send.at[X1_S], recv.at[X1_S], (bucket, xx * 4 + y))
            rcopy(gy.at[b, yy], ry1.at[y, b], send.at[Y1_S], recv.at[Y1_S], (bucket, x * 4 + yy))

    neg_block(1)
    rcopy(gz.at[1], rz1, send.at[Z1_S], recv.at[Z1_S], far)
    wait_bytes(ot_own, recv.at[O3_S])
    wait_bytes(o_far.at[0], recv.at[O4_S])
    wait_bytes(o_far.at[1], recv.at[O2_S])
    ends[D:DP, :] = jnp.zeros((DP - D, 2 * E_DEV), BF16)
    for j in range(2):
        cols = slice(j * EC, (j + 1) * EC)
        tail_cols = slice(E_DEV + j * EC, E_DEV + (j + 1) * EC)
        g = 2 * c + j
        pos, w, ltot = sq[g, 0:1, :], sq[g, 1:2, :], lt[g, 0:1, :]
        pos_coef = w * (jnp.exp(pos - ltot) - 1.0)
        own = w * jnp.exp(st[g, 0:1, :] - ltot)
        other = w * jnp.exp(st_in[g, 0:1, :] - ltot)
        away = w * jnp.exp(sc_in[g, 0:1, :] - ltot)
        grad = pos_coef * tts[j] + ot[g] * own + ot_own[j] * other + o_far[j].astype(F32) * away
        gre, gim = grad[:HALF], grad[HALF:]
        rre, rim = rts[j, :HALF, :], rts[j, HALF:, :]
        hre, him = hts[j, :HALF, :], hts[j, HALF:, :]
        head_grad = jnp.concatenate(
            [gre * rre + gim * rim, gim * rre - gre * rim], axis=0
        ).astype(BF16)
        tail_grad = (pos_coef * qt[g, 0:D, :].astype(F32)).astype(BF16)
        for part, where_to in ((head_grad, cols), (tail_grad, tail_cols)):
            ends[0:D, where_to] = part
            ends[416:432, where_to] = part[384:D]
        term = jnp.concatenate([gre * hre + gim * him, gim * hre - gre * him], axis=0)
        hi = term.astype(BF16)
        rt_hi[:, cols] = hi
        rt_lo[:, cols] = (term - hi.astype(F32)).astype(BF16)

    src_chip = z * NS + shard

    def chip_at(offset):
        dx, dy, dz = offset
        return (z + dz + 4) % 4, (x + dx + 4) % 4 * 4 + (y + dy + 4) % 4

    def pack(k):
        zz = lax.rem(z + k, NZ)
        chips = pl.ds(pl.multiple_of(zz * NS, NS), NS)
        sel = []
        for d in range(2):
            sc_b = slot_col[zz * 2 + d]
            sel.append(jnp.concatenate(
                [hot_where(sc_b == (iota((256, 128), 1) + 128 * t).astype(F32)) for t in range(8)],
                axis=1,
            ))
        rows = nt(jnp.concatenate(sel, axis=0), ends[...])
        lane = iota((256, 128), 1)
        last = []
        for d in range(2):
            part = rows[d * 256 : (d + 1) * 256]
            for t in range(3):
                first_row = (d * 3 + t) * SLOT
                tile = part[:, t * 128 : (t + 1) * 128].astype(BF16).reshape(NS, SLOT, 128)
                packed[chips, first_row : first_row + SLOT, :] = tile
            dc = dest_col[zz * 2 + d]
            high = jnp.floor(dc * (1.0 / 32.0))
            code = jnp.where(lane == 32 * d + 16, high, jnp.where(lane == 32 * d + 17, dc - 32.0 * high, 0.0))
            last.append(part[:, 384:512] + code)
        tile = jnp.where(lane < 32, last[0], last[1]).astype(BF16).reshape(NS, SLOT, 128)
        packed[chips, 96:112, :] = tile
        offsets = [(dx, dy, k) for dx in range(4) for dy in range(4)]
        for offset in sorted(offsets, key=lambda o: o not in FORWARDED):
            ss = chip_at(offset)[1]
            src = packed.at[zz * NS + ss]
            if offset == (0, 0, 0):
                pltpu.make_async_copy(src, arrived.at[src_chip], ent_recv.at[k]).start()
            elif offset in FORWARDED:
                bx, by, bz = steps_back(offset)
                way_z, way_shard = chip_at((-bx, -by, -bz))
                number = FORWARDED.index(offset)
                rcopy(src, passing.at[number], send.at[ENT_S], recv.at[FW_S], (way_z * 2 + c, way_shard))
            else:
                rcopy(src, arrived.at[src_chip], send.at[ENT_S], ent_recv.at[k], (zz * 2 + c, ss))

    def pass_on():
        wait_bytes(passing, recv.at[FW_S])
        for number, offset in enumerate(FORWARDED):
            back = steps_back(offset)
            from_z, from_shard = chip_at(back)
            to_z, to_shard = chip_at(tuple(d + b for d, b in zip(offset, back)))
            rcopy(
                passing.at[number], arrived.at[from_z * NS + from_shard], send.at[FW_S],
                ent_recv.at[offset[2]], (to_z * 2 + c, to_shard),
            )


    def rel_chunk(r, carry):
        hot = hot_where(iota((128, E_DEV), 0) + r * 128 == ids[...])
        rp[pl.ds(pl.multiple_of(r * 128, 128), 128), :] = nt(hot, rt_hi[...]) + nt(hot, rt_lo[...])
        return carry

    lax.fori_loop(0, 4, rel_chunk, 0)
    rcopy(
        rp.at[pl.ds(pl.multiple_of(oc * 256, 256), 256)], rp_in, send.at[RC_S], recv.at[RC_S], partner
    )

    pack(0)
    pack(1)

    wait_bytes(rp_in, recv.at[RC_S])
    r1b[...] = (rp[pl.ds(pl.multiple_of(c * 256, 256), 256), :] + rp_in[...]).astype(BF16)
    for j in range(1, NS):
        ss = lax.rem(shard + j, NS)
        rows = r1b.at[pl.ds(pl.multiple_of(ss * 16, 16), 16)]
        rcopy(rows, r2in.at[shard], send.at[R2_S], recv.at[R2_S], (bucket, ss))
    r2in[shard] = r1b[pl.ds(pl.multiple_of(shard * 16, 16), 16), :]
    neg_block(0)
    pack(2)
    pack(3)


    wait_bytes(r2in.at[pl.ds(0, NS - 1)], recv.at[R2_S])
    r2 = r2in[0].astype(F32)
    for i in range(1, NS):
        r2 = r2 + r2in[i].astype(F32)
    r2all[z] = r2
    for k in (1, 3, 2):
        zz = lax.rem(z + k, NZ)
        rcopy(r2all.at[z], r2all.at[z], send.at[R3_S], recv.at[R3_S], (zz * 2 + c, shard))

    my_rows = pl.ds(pl.multiple_of(shard * NEG_OWN, NEG_OWN), NEG_OWN)
    wait_bytes(rx1.at[pl.ds(0, 3)], recv.at[X1_S])
    for b in range(2):
        total = gx[b, x].astype(F32)
        for i in range(1, 4):
            total = total + rx1[lax.rem(x + i, 4), b].astype(F32)
        ax[b] = total.astype(BF16)
    for i in range(4):
        yy = lax.rem(y + i, 4)
        rows = pl.ds(pl.multiple_of(yy * NEG_OWN, NEG_OWN), NEG_OWN)
        if i:
            rcopy(ax.at[0, rows], rx2.at[y], send.at[X2_S], recv.at[X2_S], (bucket, x * 4 + yy))
        else:
            rx2[y] = ax[0, rows, :]
        rcopy(
            ax.at[1, rows], rx2.at[4 + y], send.at[X2_S], recv.at[X2_S], (z_far * 2 + c, x * 4 + yy)
        )
    pass_on()
    wait_bytes(r2all.at[pl.ds(0, 3)], recv.at[R3_S])
    rel_row = pl.ds(pl.multiple_of(c * 256 + shard * 16, 16), 16)
    rfin[rel_row, :] = (((r2all[0] + r2all[1]) + r2all[2]) + r2all[3]).astype(BF16)
    for j in range(1, NS):
        ss = lax.rem(shard + j, NS)
        rcopy(rfin.at[rel_row], rfin.at[rel_row], send.at[R4_S], recv.at[R4_S], (bucket, ss))

    wait_bytes(ry1.at[pl.ds(0, 3)], recv.at[Y1_S])
    for b in range(2):
        total = gy[b, y].astype(F32)
        for i in range(1, 4):
            total = total + ry1[lax.rem(y + i, 4), b].astype(F32)
        ay[b] = total.astype(BF16)
    for i in range(4):
        xx = lax.rem(x + i, 4)
        if i:
            rcopy(ay.at[0, xx], ry2.at[x], send.at[Y2_S], recv.at[Y2_S], (bucket, xx * 4 + y))
        else:
            ry2[x] = ay[0, x]
        rcopy(
            ay.at[1, xx], ry2.at[4 + x], send.at[Y2_S], recv.at[Y2_S], (z_far * 2 + c, xx * 4 + y)
        )
    wait_bytes(rz1, recv.at[Z1_S])

    def sum_z(r, carry):
        rr = pl.ds(pl.multiple_of(r * 256, 256), 256)
        total = gz[0, :, rr].astype(F32) + rz1[:, rr].astype(F32)
        wide_sum = jnp.concatenate([total, jnp.zeros((256 - (D - 256), 256), F32)], axis=0)
        az[rr, :] = wide_sum.T.astype(BF16)
        return carry

    lax.fori_loop(0, 4, sum_z, 0)
    for j in range(1, NS):
        ss = lax.rem(shard + j, NS)
        rows = az.at[pl.ds(pl.multiple_of(ss * NEG_OWN, NEG_OWN), NEG_OWN)]
        rcopy(rows, rz2.at[shard], send.at[Z2_S], recv.at[Z2_S], (bucket, ss))
    rz2[shard] = az[my_rows, :]

    def give(src, dst, sem):
        pltpu.make_async_copy(src, dst, sem).start()

    other_rows, last_rows = pl.ds(pl.multiple_of(oc * 48, 16), 48), pl.ds(96, SLOT)
    for k in range(NZ):
        chips = pl.ds(pl.multiple_of(lax.rem(z + NZ - k, NZ) * NS, NS), NS)
        wait_bytes(arrived.at[chips], ent_recv.at[k])
        rcopy(arrived.at[chips, other_rows], far_main.at[chips], send.at[PX_S], recv.at[PX_S], partner)
        rcopy(arrived.at[chips, last_rows], far_last.at[chips], send.at[PY_S], recv.at[PY_S], partner)
    give(arrived.at[:, pl.ds(pl.multiple_of(c * 48, 16), 48)], main_out, out_sem.at[0])
    give(arrived.at[:, last_rows], last_out, out_sem.at[5])
    wait_bytes(rfin.at[pl.ds(0, 240)], recv.at[R4_S])
    half_rel = rfin.at[pl.ds(pl.multiple_of(c * 256, 256), 256)]
    rcopy(half_rel, half_rel, send.at[R5_S], recv.at[R5_S], partner)
    wait_bytes(rx2.at[pl.ds(0, 7)], recv.at[X2_S])
    give(rx2, rx2_out, out_sem.at[1])
    wait_bytes(ry2.at[pl.ds(0, 7)], recv.at[Y2_S])
    give(ry2, ry2_out, out_sem.at[2])
    wait_bytes(rz2.at[pl.ds(0, NS - 1)], recv.at[Z2_S])
    give(rz2, rz2_out, out_sem.at[3])
    wait_bytes(half_rel, recv.at[R5_S])
    give(rfin, rel_sum_out, out_sem.at[4])
    wait_bytes(far_main, recv.at[PX_S])
    give(far_main, far_main_out, out_sem.at[6])
    wait_bytes(far_last, recv.at[PY_S])
    give(far_last, far_last_out, out_sem.at[7])

    wait_bytes(nbt.at[pl.ds(0, 2)], send.at[GZ_S])
    wait_bytes(nbt.at[pl.ds(0, 3)], send.at[GX_S])
    wait_bytes(nbt.at[pl.ds(0, 3)], send.at[GY_S])
    for number in (Q1_S, Q2_S, Q3_S):
        wait_bytes(qt.at[mine, real], send.at[number])
    for number in (SQ1_S, SQ2_S, SQ3_S):
        wait_bytes(sq.at[mine], send.at[number])
    for number in (ST1_S, ST2_S, SC1_S, SC2_S):
        wait_bytes(st.at[own_half], send.at[number])
    wait_bytes(ot_pair, send.at[O1_S])
    wait_bytes(o_far.at[0], send.at[O4_S])
    wait_bytes(o_far.at[1], send.at[O2_S])
    wait_bytes(ot_own, send.at[O3_S])
    wait_bytes(arrived.at[pl.ds(0, 63)], send.at[ENT_S])
    wait_bytes(passing, send.at[FW_S])
    wait_bytes(far_main, send.at[PX_S])
    wait_bytes(far_last, send.at[PY_S])
    wait_bytes(rp_in, send.at[RC_S])
    wait_bytes(r2in.at[pl.ds(0, NS - 1)], send.at[R2_S])
    wait_bytes(r2all.at[pl.ds(0, 3)], send.at[R3_S])
    wait_bytes(rfin.at[pl.ds(0, 240)], send.at[R4_S])
    wait_bytes(half_rel, send.at[R5_S])
    wait_bytes(rz1, send.at[Z1_S])
    wait_bytes(rx1.at[pl.ds(0, 3)], send.at[X1_S])
    wait_bytes(ry1.at[pl.ds(0, 3)], send.at[Y1_S])
    wait_bytes(rx2.at[pl.ds(0, 7)], send.at[X2_S])
    wait_bytes(ry2.at[pl.ds(0, 7)], send.at[Y2_S])
    wait_bytes(rz2.at[pl.ds(0, NS - 1)], send.at[Z2_S])
    for number in (0, 6):
        wait_bytes(far_main, out_sem.at[number])
    for number in (5, 7):
        wait_bytes(far_last, out_sem.at[number])
    wait_bytes(rx2, out_sem.at[1])
    wait_bytes(ry2, out_sem.at[2])
    wait_bytes(rz2, out_sem.at[3])
    wait_bytes(rfin, out_sem.at[4])


def finish(
    main_in, last_in, far_main_in, far_last_in, rx2_in, ry2_in, rz2_in, rel_in,
    ent_out, neg_out, rel_out,
    main, last, far_main, far_last, rx2, ry2, rz2, rel_sum, ent, neg_sum, rel_t, in_sem, out_sem,
):
    loads = [
        pltpu.make_async_copy(src, dst, in_sem.at[i])
        for i, (src, dst) in enumerate((
            (rel_in, rel_sum), (last_in, last), (far_last_in, far_last), (main_in, main),
            (far_main_in, far_main), (rx2_in, rx2), (ry2_in, ry2), (rz2_in, rz2),
        ))
    ]
    for load in loads:
        load.start()
    loads[0].wait()
    for r in range(4):
        rows = rel_sum[r * 128 : (r + 1) * 128, :].astype(F32)
        wide = jnp.concatenate([rows, jnp.zeros((128, DP - D), F32)], axis=1)
        rel_t[:, r * 128 : (r + 1) * 128] = wide.T[0:D]
    stores = [pltpu.make_async_copy(rel_t, rel_out, out_sem.at[0])]
    stores[0].start()

    c = lax.axis_index("bucket") % 2
    lane = iota((8, 128), 1) - 32 * c
    unit = jnp.where(lane == 16, 32.0, jnp.where(lane == 17, 1.0, 0.0)).astype(BF16)
    for load in loads[1:5]:
        load.wait()
    slots, row_ids = [], []
    for tiles, tail in ((main, last), (far_main, far_last)):
        tail_rows = tail[...].reshape(1024, 128)
        columns = [tiles[:, t * SLOT : (t + 1) * SLOT, :].reshape(1024, 128) for t in range(3)]
        slots.append(jnp.concatenate(columns + [tail_rows], axis=1))
        row_ids.append(nt(unit, tail_rows)[0:1, :])
    for r in range(2):
        numbers = (iota((512, 1024), 0) + r * 512).astype(F32)
        got = nn(hot_where(numbers == row_ids[0]), slots[0]) + nn(hot_where(numbers == row_ids[1]), slots[1])
        turned = got.T
        ent[r, 0:384] = turned[0:384]
        ent[r, 384:D] = jnp.where(c == 0, turned[384:400], turned[416:432])
        store = pltpu.make_async_copy(ent.at[r], ent_out.at[:, pl.ds(r * 512, 512)], out_sem.at[1 + r])
        store.start()
        stores.append(store)

    def sum_all(ref):
        total = ref[0].astype(F32)
        for i in range(1, ref.shape[0]):
            total = total + ref[i].astype(F32)
        return total

    for load in loads[5:]:
        load.wait()
    neg_sum[:, 0:128] = sum_all(rx2)
    neg_sum[:, 128:256] = sum_all(ry2)
    neg_sum[:, 256:D] = sum_all(rz2)[:, 0 : D - 256]
    stores.append(pltpu.make_async_copy(neg_sum, neg_out, out_sem.at[3]))
    stores[-1].start()
    for store in stores:
        store.wait()


SCRATCH = [
    ((16, D, 128), BF16),
    ((D + 16, NEG_DEV), BF16),
    ((NEG_DEV, DP), BF16),
    ((2, NEG_DEV, 8 * EC), BF16),
    ((8, DP, EC), BF16),
    ((8, 8, EC), F32),
    ((2, D, EC), F32),
    ((2, D, EC), F32),
    ((2, D, EC), F32),
    ((2, 8, 8, EC), F32),
    ((8, 8, EC), F32),
    ((8, 8, EC), F32),
    ((8, 8, EC), F32),
    ((8, 8, EC), F32),
    ((8, D, EC), F32),
    ((2, D, EC), F32),
    ((2, D, EC), F32),
    ((2, D, EC), BF16),
    ((2, D, EC), BF16),
    ((8, 8, EC), F32),
    ((DP, 8 * EC), BF16),
    ((DP, 2 * E_DEV), BF16),
    ((D, E_DEV), BF16),
    ((D, E_DEV), BF16),
    ((NZ * NS, 112, 128), BF16),
    ((NZ * NS, 112, 128), BF16),
    ((len(FORWARDED), 112, 128), BF16),
    ((NZ * NS, 48, 128), BF16),
    ((NZ * NS, SLOT, 128), BF16),
    ((NB, 256, 128), F32),
    ((NB, 256, 128), F32),
    ((2, D - 256, NEG_DEV), BF16),
    ((2, 4, 256, 128), BF16),
    ((2, 4, 4, NEG_OWN, 128), BF16),
    ((D - 256, NEG_DEV), BF16),
    ((4, 2, 256, 128), BF16),
    ((4, 2, 4, NEG_OWN, 128), BF16),
    ((NEG_DEV, 256), BF16),
    ((2, 256, 128), BF16),
    ((2, 4, NEG_OWN, 128), BF16),
    ((NS, NEG_OWN, 256), BF16),
    ((8, NEG_OWN, 128), BF16),
    ((8, NEG_OWN, 128), BF16),
    ((REL, D), F32),
    ((REL // 2, D), F32),
    ((REL // 2, D), BF16),
    ((NS, 16, D), BF16),
    ((NZ, 16, D), F32),
    ((REL, D), BF16),
]


def per_device(
    head_rows, tail_rows, rel_ids, relations, edge_weights, neg_rows, send_slots, dest_rows
):
    vmem = pl.BlockSpec(memory_space=pltpu.VMEM)
    anywhere = pl.BlockSpec(memory_space=pl.ANY)
    results = pl.pallas_call(
        kernel,
        out_shape=(
            jax.ShapeDtypeStruct((NZ * NS, 48, 128), BF16),
            jax.ShapeDtypeStruct((NZ * NS, SLOT, 128), BF16),
            jax.ShapeDtypeStruct((NZ * NS, 48, 128), BF16),
            jax.ShapeDtypeStruct((NZ * NS, SLOT, 128), BF16),
            jax.ShapeDtypeStruct((8, NEG_OWN, 128), BF16),
            jax.ShapeDtypeStruct((8, NEG_OWN, 128), BF16),
            jax.ShapeDtypeStruct((NS, NEG_OWN, 256), BF16),
            jax.ShapeDtypeStruct((REL, D), BF16),
        ),
        in_specs=[vmem] * 8,
        out_specs=(anywhere,) * 8,
        scratch_shapes=[pltpu.VMEM(shape, dtype) for shape, dtype in SCRATCH]
        + [
            pltpu.SemaphoreType.DMA((32,)),
            pltpu.SemaphoreType.DMA((32,)),
            pltpu.SemaphoreType.REGULAR((4,)),
            pltpu.SemaphoreType.DMA((8,)),
            pltpu.SemaphoreType.DMA((NZ,)),
        ],
        compiler_params=pltpu.CompilerParams(
            collective_id=0, has_side_effects=True, vmem_limit_bytes=60 * 1024 * 1024
        ),
        cost_estimate=pl.CostEstimate(
            flops=2 * 3 * 1024 * 4096 * 400, bytes_accessed=8 * 1024 * 1024, transcendentals=1024 * 4096
        ),
        name="complex_backward",
    )(
        head_rows.T,
        tail_rows.T,
        rel_ids.reshape(1, E_DEV),
        relations.T,
        edge_weights.reshape(1, E_DEV),
        neg_rows.T,
        send_slots.T,
        dest_rows.T,
    )
    ent_t, neg_grad, rel_t = pl.pallas_call(
        finish,
        out_shape=(
            jax.ShapeDtypeStruct((D, ENT_DEV), F32),
            jax.ShapeDtypeStruct((NEG_OWN, D), F32),
            jax.ShapeDtypeStruct((D, REL), F32),
        ),
        in_specs=[anywhere] * 8,
        out_specs=(anywhere,) * 3,
        scratch_shapes=[
            pltpu.VMEM((NZ * NS, 48, 128), BF16),
            pltpu.VMEM((NZ * NS, SLOT, 128), BF16),
            pltpu.VMEM((NZ * NS, 48, 128), BF16),
            pltpu.VMEM((NZ * NS, SLOT, 128), BF16),
            pltpu.VMEM((8, NEG_OWN, 128), BF16),
            pltpu.VMEM((8, NEG_OWN, 128), BF16),
            pltpu.VMEM((NS, NEG_OWN, 256), BF16),
            pltpu.VMEM((REL, D), BF16),
            pltpu.VMEM((2, D, 512), F32),
            pltpu.VMEM((NEG_OWN, D), F32),
            pltpu.VMEM((D, REL), F32),
            pltpu.SemaphoreType.DMA((8,)),
            pltpu.SemaphoreType.DMA((4,)),
        ],
        compiler_params=pltpu.CompilerParams(vmem_limit_bytes=60 * 1024 * 1024),
        cost_estimate=pl.CostEstimate(
            flops=2 * 1024 * 2048 * 512, bytes_accessed=6 * 1024 * 1024, transcendentals=0
        ),
        name="make_outputs",
    )(*results)
    return ent_t.T, neg_grad, rel_t.T


def solution(mesh):
    return jax.shard_map(
        per_device,
        mesh=mesh,
        in_specs=(
            P(("bucket", "shard"), None),
            P(("bucket", "shard"), None),
            P(("bucket", "shard")),
            P(),
            P(("bucket", "shard")),
            P("bucket", None),
            P(("bucket", "shard"), None),
            P(("bucket", "shard"), None),
        ),
        out_specs=(P(("bucket", "shard"), None), P(("bucket", "shard"), None), P()),
        check_vma=False,
    )
```

```python
import functools

import jax
import jax.numpy as jnp
from jax import lax
from jax.experimental import pallas as pl
from jax.experimental.pallas import tpu as pltpu
from jax.sharding import PartitionSpec as P

D = 400
HALF = 200
DP = 512
E_DEV = 512
ENT_DEV = 1024
REL = 512
NEG_DEV = 1024
SLOT = 16
NB = 8
NS = 16
NZ = 4
EC = 256
NEG_OWN = 64

MESH = pl.DeviceIdType.MESH
F32 = jnp.float32
BF16 = jnp.bfloat16

(Q1_S, SQ1_S, Q2_S, SQ2_S, Q3_S, SQ3_S, ST1_S, O1_S, SC1_S, O2_S, ST2_S, O3_S, SC2_S,
 RC_S, R2_S, R3_S, R4_S, R5_S, ENT_S, Z1_S, X1_S, Y1_S, Z2_S, X2_S, Y2_S, GZ_S, GX_S, GY_S, O4_S,
 PX_S, PY_S) = range(31)


def nt(a, b):
    return lax.dot_general(a, b, (((1,), (1,)), ((), ())), preferred_element_type=F32)


def nn(a, b):
    return jnp.dot(a, b, preferred_element_type=F32)


def iota(shape, dim):
    return lax.broadcasted_iota(jnp.int32, shape, dim)


def hot_where(mask):
    return mask.astype(F32).astype(BF16)


def wait_bytes(ref, sem):
    pltpu.make_async_copy(ref, ref, sem).wait()


def kernel(
    head, tail, ids, rel, wts, neg, slots, drows,
    main_out, last_out, far_main_out, far_last_out, rx2_out, ry2_out, rz2_out, rel_sum_out,
    nbt, wide, nb, prob, qt, sq, hts, tts, rts, mb, st, st_in, sc, sc_in,
    ot, ot_pair, ot_own, o_sum, o_far, lt, qs, ends, rt_hi, rt_lo,
    packed, arrived, far_main, far_last, slot_col, dest_col,
    gz, gx, gy, rz1, rx1, ry1, az, ax, ay, rz2, rx2, ry2,
    rp, rp_in, r1b, r2in, r2all, rfin,
    send, recv, known, out_sem, ent_recv,
):
    bucket, shard = lax.axis_index("bucket"), lax.axis_index("shard")
    z, c = bucket // 2, bucket % 2
    x, y = shard // 4, shard % 4
    oc = 1 - c
    partner = (z * 2 + oc, shard)
    pair = ((z + 1 - 2 * (z % 2)) * 2 + c, shard)
    z_far = 3 - z
    far = (z_far * 2 + c, shard)

    def rcopy(src, dst, s_sem, r_sem, device):
        pltpu.make_async_remote_copy(
            src_ref=src, dst_ref=dst, send_sem=s_sem, recv_sem=r_sem,
            device_id=device, device_id_type=MESH,
        ).start()

    barrier = pltpu.get_barrier_semaphore()

    x_peers = [(bucket, lax.rem(x + i, 4) * 4 + y) for i in (1, 2, 3)]
    y_peers = [(bucket, x * 4 + lax.rem(y + i, 4)) for i in (1, 2, 3)]
    friends = [partner, pair, far] + x_peers + y_peers

    def tell(sem, devices):
        for device in devices:
            pl.semaphore_signal(sem, inc=1, device_id=device, device_id_type=MESH)

    tell(barrier, friends)

    for g in range(8):
        qt[g, D:DP, :] = jnp.zeros((DP - D, EC), BF16)
    wide[D:, :] = jnp.ones((16, NEG_DEV), BF16)

    for i in range(8):
        nbt[i] = neg[:, i * 128 : (i + 1) * 128]

    rel_1 = rel[...].astype(BF16)
    rest = rel[...] - rel_1.astype(F32)
    rel_2 = rest.astype(BF16)
    rel_3 = (rest - rel_2.astype(F32)).astype(BF16)
    for j in range(2):
        cols = slice(j * EC, (j + 1) * EC)
        h_t = head[:, cols].astype(F32)
        t_t = tail[:, cols].astype(F32)
        hot = hot_where(iota((REL, EC), 0) == ids[0:1, cols])
        r_t = (nn(rel_1, hot) + nn(rel_2, hot)) + nn(rel_3, hot)
        hre, him = h_t[:HALF], h_t[HALF:]
        rre, rim = r_t[:HALF], r_t[HALF:]
        q = jnp.concatenate([hre * rre - him * rim, hre * rim + him * rre], axis=0).astype(BF16)
        qt[2 * c + j, 0:D, :] = q
        sq[2 * c + j, 0:1, :] = jnp.sum(q.astype(F32) * t_t, axis=0, keepdims=True)
        sq[2 * c + j, 1:2, :] = wts[0:1, cols]
        sq[2 * c + j, 2:8, :] = jnp.zeros((6, EC), F32)
        hts[j] = h_t
        tts[j] = t_t
        rts[j] = r_t

    pl.semaphore_wait(barrier, len(friends))
    tell(known.at[0], y_peers)

    for i in (x, 4 + y):
        rcopy(nbt.at[i], nbt.at[8 + i], send.at[GZ_S], recv.at[GZ_S], far)
    mine, theirs, real = pl.ds(2 * c, 2), pl.ds(4 + 2 * c, 2), pl.ds(0, D)
    rcopy(qt.at[mine, real], qt.at[mine, real], send.at[Q1_S], recv.at[Q1_S], partner)
    rcopy(sq.at[mine], sq.at[mine], send.at[SQ1_S], recv.at[SQ1_S], partner)
    rcopy(qt.at[mine, real], qt.at[theirs, real], send.at[Q2_S], recv.at[Q2_S], pair)
    rcopy(sq.at[mine], sq.at[theirs], send.at[SQ2_S], recv.at[SQ2_S], pair)

    ones = jnp.ones((SLOT, 128), BF16)
    tables = []
    for ref in (slots, drows):
        value = ref[...].astype(F32)
        high = jnp.floor(value * (1.0 / 32.0))
        tables.append((high.astype(BF16), (value - 32.0 * high).astype(BF16)))

    def columns(b, carry):
        owner_hot = hot_where(iota((256, 128), 1) == iota((256, 128), 0) // SLOT + b * NS)
        keep = iota((256, SLOT), 1) == iota((256, SLOT), 0) % SLOT
        for (high, low), out in zip(tables, (slot_col, dest_col)):
            h = jnp.where(keep, nt(owner_hot, high), 0.0).astype(BF16)
            l = jnp.where(keep, nt(owner_hot, low), 0.0).astype(BF16)
            out[b] = 32.0 * nn(h, ones) + nn(l, ones)
        return carry

    lax.fori_loop(0, NB, columns, 0)
    nb[:, 384:DP] = jnp.zeros((NEG_DEV, 128), BF16)

    def flip(b):
        for i in range(8):
            part = nbt[b * 8 + i]
            wide[0:D, i * 128 : (i + 1) * 128] = part
            nb[i * 128 : (i + 1) * 128, 0:D] = part.astype(F32).T.astype(BF16)

    def block(b, two):

        chunks = (2 * two, 2 * two + 1)
        scores = [nn(nb[...], qt[g]) for g in chunks]
        for g, s in zip(chunks, scores):
            m = jnp.max(s, axis=0, keepdims=True)
            pb = jnp.exp(s - m).astype(BF16)
            prob[b, :, pl.ds(pl.multiple_of(g * EC, EC), EC)] = pb
            o = nn(wide[...], pb)
            l = o[D : D + 1]
            o = o[0:D]
            mb[b, g, 0:1, :] = m
            if b == 0:
                st[g, 0:1, :] = m
                st[g, 1:2, :] = l
                st[g, 2:8, :] = jnp.zeros((6, EC), F32)
                ot[g] = o
            else:
                m_old = st[g, 0:1, :]
                m_new = jnp.maximum(m_old, m)
                f_old = jnp.exp(m_old - m_new)
                f_new = jnp.exp(m - m_new)
                st[g, 0:1, :] = m_new
                st[g, 1:2, :] = st[g, 1:2, :] * f_old + l * f_new
                ot[g] = ot[g] * f_old + o * f_new

    flip(0)
    block(0, c)
    pl.semaphore_wait(known.at[0], 3)
    tell(known.at[1], (pair, far))
    wait_bytes(nbt.at[pl.ds(8, 2)], recv.at[GZ_S])
    for i in (1, 3, 2):
        xx, yy = lax.rem(x + i, 4), lax.rem(y + i, 4)
        rcopy(nbt.at[8 + x], nbt.at[8 + x], send.at[GX_S], recv.at[GX_S], (bucket, xx * 4 + y))
        rcopy(nbt.at[12 + y], nbt.at[12 + y], send.at[GY_S], recv.at[GY_S], (bucket, x * 4 + yy))
    wait_bytes(qt.at[mine, real], recv.at[Q1_S])
    wait_bytes(sq.at[mine], recv.at[SQ1_S])
    block(0, oc)
    pl.semaphore_wait(known.at[1], 2)
    tell(known.at[2], (pair, far))
    wait_bytes(qt.at[mine, real], recv.at[Q2_S])
    wait_bytes(sq.at[mine], recv.at[SQ2_S])
    rcopy(qt.at[theirs, real], qt.at[theirs, real], send.at[Q3_S], recv.at[Q3_S], partner)
    rcopy(sq.at[theirs], sq.at[theirs], send.at[SQ3_S], recv.at[SQ3_S], partner)
    block(0, 2 + c)
    wait_bytes(qt.at[mine, real], recv.at[Q3_S])
    wait_bytes(sq.at[mine], recv.at[SQ3_S])
    block(0, 2 + oc)
    wait_bytes(nbt.at[pl.ds(8, 3)], recv.at[GX_S])
    wait_bytes(nbt.at[pl.ds(8, 3)], recv.at[GY_S])
    flip(1)
    block(1, 2 + oc)
    pl.semaphore_wait(known.at[2], 2)
    tell(known.at[3], (partner,))
    rcopy(
        ot.at[pl.ds(4 + 2 * oc, 2)], ot_pair, send.at[O1_S], recv.at[O1_S], partner
    )
    block(1, 2 + c)
    own_half, pair_half = pl.ds(0, 4), pl.ds(4, 4)
    rcopy(st.at[pair_half], st_in.at[pair_half], send.at[ST1_S], recv.at[ST1_S], partner)

    def merge(g):
        m_a, m_b = st[g, 0:1, :], st_in[g, 0:1, :]
        m = jnp.maximum(m_a, m_b)
        f_a, f_b = jnp.exp(m_a - m), jnp.exp(m_b - m)
        sc[g, 0:1, :] = m
        sc[g, 1:2, :] = st[g, 1:2, :] * f_a + st_in[g, 1:2, :] * f_b
        sc[g, 2:8, :] = jnp.zeros((6, EC), F32)
        return f_a, f_b

    block(1, oc)
    pl.semaphore_wait(known.at[3], 1)
    rcopy(ot.at[pl.ds(2 * oc, 2)], ot_own, send.at[O3_S], recv.at[O3_S], partner)
    wait_bytes(st_in.at[pair_half], recv.at[ST1_S])
    wait_bytes(ot_pair, recv.at[O1_S])
    for g in range(4, 8):
        merge(g)
    for j in range(2):
        f_a, f_b = merge(4 + 2 * c + j)
        o_sum[j] = (ot[4 + 2 * c + j] * f_a + ot_pair[j] * f_b).astype(BF16)
    rcopy(o_sum.at[0], o_far.at[0], send.at[O4_S], recv.at[O4_S], pair)
    rcopy(sc.at[pair_half], sc_in.at[own_half], send.at[SC1_S], recv.at[SC1_S], pair)
    block(1, c)
    rcopy(st.at[own_half], st_in.at[own_half], send.at[ST2_S], recv.at[ST2_S], partner)
    wait_bytes(st_in.at[own_half], recv.at[ST2_S])
    for g in range(4):
        merge(g)
    rcopy(sc.at[own_half], sc_in.at[pair_half], send.at[SC2_S], recv.at[SC2_S], pair)
    rcopy(o_sum.at[1], o_far.at[1], send.at[O2_S], recv.at[O2_S], pair)
    wait_bytes(sc_in.at[own_half], recv.at[SC1_S])
    wait_bytes(sc_in.at[pair_half], recv.at[SC2_S])
    for g in range(8):
        pos = sq[g, 0:1, :]
        m0, m1 = sc[g, 0:1, :], sc_in[g, 0:1, :]
        top = jnp.maximum(pos, jnp.maximum(m0, m1))
        total = (
            jnp.exp(pos - top)
            + sc[g, 1:2, :] * jnp.exp(m0 - top)
            + sc_in[g, 1:2, :] * jnp.exp(m1 - top)
        )
        lt[g, 0:1, :] = top + jnp.log(total)

    def neg_block(b):
        for g in range(8):
            scale = sq[g, 1:2, :] * jnp.exp(mb[b, g, 0:1, :] - lt[g, 0:1, :])
            qs[:, g * EC : (g + 1) * EC] = (qt[g].astype(F32) * scale).astype(BF16)

        def rows_of(h, carry):
            rr = pl.ds(pl.multiple_of(h * 512, 512), 512)
            acc = nt(prob[b, rr, :], qs[...])
            for u in range(2):
                part = acc[u * 256 : (u + 1) * 256]
                gx[b, 2 * h + u] = part[:, 0:128].astype(BF16)
                for yy in range(4):
                    gy[b, yy, 2 * h + u] = part[yy * 64 : (yy + 1) * 64, 128:256].astype(BF16)
            gz[b, :, rr] = acc[:, 256:512].T[0 : D - 256].astype(BF16)
            return carry

        lax.fori_loop(0, 2, rows_of, 0)
        for i in (1, 3, 2):
            xx, yy = lax.rem(x + i, 4), lax.rem(y + i, 4)
            rcopy(gx.at[b, xx], rx1.at[x, b], send.at[X1_S], recv.at[X1_S], (bucket, xx * 4 + y))
            rcopy(gy.at[b, yy], ry1.at[y, b], send.at[Y1_S], recv.at[Y1_S], (bucket, x * 4 + yy))

    neg_block(1)
    rcopy(gz.at[1], rz1, send.at[Z1_S], recv.at[Z1_S], far)
    wait_bytes(ot_own, recv.at[O3_S])
    wait_bytes(o_far.at[0], recv.at[O4_S])
    wait_bytes(o_far.at[1], recv.at[O2_S])
    ends[D:DP, :] = jnp.zeros((DP - D, 2 * E_DEV), BF16)
    for j in range(2):
        cols = slice(j * EC, (j + 1) * EC)
        tail_cols = slice(E_DEV + j * EC, E_DEV + (j + 1) * EC)
        g = 2 * c + j
        pos, w, ltot = sq[g, 0:1, :], sq[g, 1:2, :], lt[g, 0:1, :]
        pos_coef = w * (jnp.exp(pos - ltot) - 1.0)
        own = w * jnp.exp(st[g, 0:1, :] - ltot)
        other = w * jnp.exp(st_in[g, 0:1, :] - ltot)
        away = w * jnp.exp(sc_in[g, 0:1, :] - ltot)
        grad = pos_coef * tts[j] + ot[g] * own + ot_own[j] * other + o_far[j].astype(F32) * away
        gre, gim = grad[:HALF], grad[HALF:]
        rre, rim = rts[j, :HALF, :], rts[j, HALF:, :]
        hre, him = hts[j, :HALF, :], hts[j, HALF:, :]
        head_grad = jnp.concatenate(
            [gre * rre + gim * rim, gim * rre - gre * rim], axis=0
        ).astype(BF16)
        tail_grad = (pos_coef * qt[g, 0:D, :].astype(F32)).astype(BF16)
        for part, where_to in ((head_grad, cols), (tail_grad, tail_cols)):
            ends[0:D, where_to] = part
            ends[416:432, where_to] = part[384:D]
        term = jnp.concatenate([gre * hre + gim * him, gim * hre - gre * him], axis=0)
        hi = term.astype(BF16)
        rt_hi[:, cols] = hi
        rt_lo[:, cols] = (term - hi.astype(F32)).astype(BF16)

    src_chip = z * NS + shard

    def pack(k, first):
        zz = lax.rem(z + k, NZ)
        chips = pl.ds(pl.multiple_of(zz * NS, NS), NS)
        sel = []
        for d in range(2):
            sc_b = slot_col[zz * 2 + d]
            sel.append(jnp.concatenate(
                [hot_where(sc_b == (iota((256, 128), 1) + 128 * t).astype(F32)) for t in range(8)],
                axis=1,
            ))
        rows = nt(jnp.concatenate(sel, axis=0), ends[...])
        lane = iota((256, 128), 1)
        last = []
        for d in range(2):
            part = rows[d * 256 : (d + 1) * 256]
            for t in range(3):
                first_row = (d * 3 + t) * SLOT
                tile = part[:, t * 128 : (t + 1) * 128].astype(BF16).reshape(NS, SLOT, 128)
                packed[chips, first_row : first_row + SLOT, :] = tile
            dc = dest_col[zz * 2 + d]
            high = jnp.floor(dc * (1.0 / 32.0))
            code = jnp.where(lane == 32 * d + 16, high, jnp.where(lane == 32 * d + 17, dc - 32.0 * high, 0.0))
            last.append(part[:, 384:512] + code)
        tile = jnp.where(lane < 32, last[0], last[1]).astype(BF16).reshape(NS, SLOT, 128)
        packed[chips, 96:112, :] = tile
        for j in range(NS):
            ss = lax.rem(shard + j, NS)
            src = packed.at[zz * NS + ss]
            if first and j == 0:
                pltpu.make_async_copy(src, arrived.at[src_chip], ent_recv.at[k]).start()
            else:
                rcopy(src, arrived.at[src_chip], send.at[ENT_S], ent_recv.at[k], (zz * 2 + c, ss))

    def rel_chunk(r, carry):
        hot = hot_where(iota((128, E_DEV), 0) + r * 128 == ids[...])
        rp[pl.ds(pl.multiple_of(r * 128, 128), 128), :] = nt(hot, rt_hi[...]) + nt(hot, rt_lo[...])
        return carry

    lax.fori_loop(0, 4, rel_chunk, 0)
    rcopy(
        rp.at[pl.ds(pl.multiple_of(oc * 256, 256), 256)], rp_in, send.at[RC_S], recv.at[RC_S], partner
    )

    def pack_other(k, carry):
        pack(k, False)
        return carry

    pack(0, True)
    lax.fori_loop(1, 2, pack_other, 0)

    wait_bytes(rp_in, recv.at[RC_S])
    r1b[...] = (rp[pl.ds(pl.multiple_of(c * 256, 256), 256), :] + rp_in[...]).astype(BF16)
    for j in range(1, NS):
        ss = lax.rem(shard + j, NS)
        rows = r1b.at[pl.ds(pl.multiple_of(ss * 16, 16), 16)]
        rcopy(rows, r2in.at[shard], send.at[R2_S], recv.at[R2_S], (bucket, ss))
    r2in[shard] = r1b[pl.ds(pl.multiple_of(shard * 16, 16), 16), :]
    neg_block(0)

    wait_bytes(r2in.at[pl.ds(0, NS - 1)], recv.at[R2_S])
    r2 = r2in[0].astype(F32)
    for i in range(1, NS):
        r2 = r2 + r2in[i].astype(F32)
    r2all[z] = r2
    for k in (1, 3, 2):
        zz = lax.rem(z + k, NZ)
        rcopy(r2all.at[z], r2all.at[z], send.at[R3_S], recv.at[R3_S], (zz * 2 + c, shard))

    lax.fori_loop(2, NZ, pack_other, 0)


    my_rows = pl.ds(pl.multiple_of(shard * NEG_OWN, NEG_OWN), NEG_OWN)
    wait_bytes(rx1.at[pl.ds(0, 3)], recv.at[X1_S])
    for b in range(2):
        total = gx[b, x].astype(F32)
        for i in range(1, 4):
            total = total + rx1[lax.rem(x + i, 4), b].astype(F32)
        ax[b] = total.astype(BF16)
    for i in range(4):
        yy = lax.rem(y + i, 4)
        rows = pl.ds(pl.multiple_of(yy * NEG_OWN, NEG_OWN), NEG_OWN)
        if i:
            rcopy(ax.at[0, rows], rx2.at[y], send.at[X2_S], recv.at[X2_S], (bucket, x * 4 + yy))
        else:
            rx2[y] = ax[0, rows, :]
        rcopy(
            ax.at[1, rows], rx2.at[4 + y], send.at[X2_S], recv.at[X2_S], (z_far * 2 + c, x * 4 + yy)
        )
    wait_bytes(ry1.at[pl.ds(0, 3)], recv.at[Y1_S])
    for b in range(2):
        total = gy[b, y].astype(F32)
        for i in range(1, 4):
            total = total + ry1[lax.rem(y + i, 4), b].astype(F32)
        ay[b] = total.astype(BF16)
    for i in range(4):
        xx = lax.rem(x + i, 4)
        if i:
            rcopy(ay.at[0, xx], ry2.at[x], send.at[Y2_S], recv.at[Y2_S], (bucket, xx * 4 + y))
        else:
            ry2[x] = ay[0, x]
        rcopy(
            ay.at[1, xx], ry2.at[4 + x], send.at[Y2_S], recv.at[Y2_S], (z_far * 2 + c, xx * 4 + y)
        )
    wait_bytes(rz1, recv.at[Z1_S])

    def sum_z(r, carry):
        rr = pl.ds(pl.multiple_of(r * 256, 256), 256)
        total = gz[0, :, rr].astype(F32) + rz1[:, rr].astype(F32)
        wide_sum = jnp.concatenate([total, jnp.zeros((256 - (D - 256), 256), F32)], axis=0)
        az[rr, :] = wide_sum.T.astype(BF16)
        return carry

    lax.fori_loop(0, 4, sum_z, 0)
    for j in range(1, NS):
        ss = lax.rem(shard + j, NS)
        rows = az.at[pl.ds(pl.multiple_of(ss * NEG_OWN, NEG_OWN), NEG_OWN)]
        rcopy(rows, rz2.at[shard], send.at[Z2_S], recv.at[Z2_S], (bucket, ss))
    rz2[shard] = az[my_rows, :]

    wait_bytes(r2all.at[pl.ds(0, 3)], recv.at[R3_S])
    rel_row = pl.ds(pl.multiple_of(c * 256 + shard * 16, 16), 16)
    rfin[rel_row, :] = (((r2all[0] + r2all[1]) + r2all[2]) + r2all[3]).astype(BF16)
    for j in range(1, NS):
        ss = lax.rem(shard + j, NS)
        rcopy(rfin.at[rel_row], rfin.at[rel_row], send.at[R4_S], recv.at[R4_S], (bucket, ss))

    def give(src, dst, sem):
        pltpu.make_async_copy(src, dst, sem).start()

    other_rows, last_rows = pl.ds(pl.multiple_of(oc * 48, 16), 48), pl.ds(96, SLOT)
    for k in range(NZ):
        chips = pl.ds(pl.multiple_of(lax.rem(z + NZ - k, NZ) * NS, NS), NS)
        wait_bytes(arrived.at[chips], ent_recv.at[k])
        rcopy(arrived.at[chips, other_rows], far_main.at[chips], send.at[PX_S], recv.at[PX_S], partner)
        rcopy(arrived.at[chips, last_rows], far_last.at[chips], send.at[PY_S], recv.at[PY_S], partner)
    give(arrived.at[:, pl.ds(pl.multiple_of(c * 48, 16), 48)], main_out, out_sem.at[0])
    give(arrived.at[:, last_rows], last_out, out_sem.at[5])
    wait_bytes(rfin.at[pl.ds(0, 240)], recv.at[R4_S])
    half_rel = rfin.at[pl.ds(pl.multiple_of(c * 256, 256), 256)]
    rcopy(half_rel, half_rel, send.at[R5_S], recv.at[R5_S], partner)
    wait_bytes(rx2.at[pl.ds(0, 7)], recv.at[X2_S])
    give(rx2, rx2_out, out_sem.at[1])
    wait_bytes(ry2.at[pl.ds(0, 7)], recv.at[Y2_S])
    give(ry2, ry2_out, out_sem.at[2])
    wait_bytes(rz2.at[pl.ds(0, NS - 1)], recv.at[Z2_S])
    give(rz2, rz2_out, out_sem.at[3])
    wait_bytes(half_rel, recv.at[R5_S])
    give(rfin, rel_sum_out, out_sem.at[4])
    wait_bytes(far_main, recv.at[PX_S])
    give(far_main, far_main_out, out_sem.at[6])
    wait_bytes(far_last, recv.at[PY_S])
    give(far_last, far_last_out, out_sem.at[7])

    wait_bytes(nbt.at[pl.ds(0, 2)], send.at[GZ_S])
    wait_bytes(nbt.at[pl.ds(0, 3)], send.at[GX_S])
    wait_bytes(nbt.at[pl.ds(0, 3)], send.at[GY_S])
    for number in (Q1_S, Q2_S, Q3_S):
        wait_bytes(qt.at[mine, real], send.at[number])
    for number in (SQ1_S, SQ2_S, SQ3_S):
        wait_bytes(sq.at[mine], send.at[number])
    for number in (ST1_S, ST2_S, SC1_S, SC2_S):
        wait_bytes(st.at[own_half], send.at[number])
    wait_bytes(ot_pair, send.at[O1_S])
    wait_bytes(o_far.at[0], send.at[O4_S])
    wait_bytes(o_far.at[1], send.at[O2_S])
    wait_bytes(ot_own, send.at[O3_S])
    wait_bytes(arrived.at[pl.ds(0, 63)], send.at[ENT_S])
    wait_bytes(far_main, send.at[PX_S])
    wait_bytes(far_last, send.at[PY_S])
    wait_bytes(rp_in, send.at[RC_S])
    wait_bytes(r2in.at[pl.ds(0, NS - 1)], send.at[R2_S])
    wait_bytes(r2all.at[pl.ds(0, 3)], send.at[R3_S])
    wait_bytes(rfin.at[pl.ds(0, 240)], send.at[R4_S])
    wait_bytes(half_rel, send.at[R5_S])
    wait_bytes(rz1, send.at[Z1_S])
    wait_bytes(rx1.at[pl.ds(0, 3)], send.at[X1_S])
    wait_bytes(ry1.at[pl.ds(0, 3)], send.at[Y1_S])
    wait_bytes(rx2.at[pl.ds(0, 7)], send.at[X2_S])
    wait_bytes(ry2.at[pl.ds(0, 7)], send.at[Y2_S])
    wait_bytes(rz2.at[pl.ds(0, NS - 1)], send.at[Z2_S])
    for number in (0, 6):
        wait_bytes(far_main, out_sem.at[number])
    for number in (5, 7):
        wait_bytes(far_last, out_sem.at[number])
    wait_bytes(rx2, out_sem.at[1])
    wait_bytes(ry2, out_sem.at[2])
    wait_bytes(rz2, out_sem.at[3])
    wait_bytes(rfin, out_sem.at[4])


def finish(
    main_in, last_in, far_main_in, far_last_in, rx2_in, ry2_in, rz2_in, rel_in,
    ent_out, neg_out, rel_out,
    main, last, far_main, far_last, rx2, ry2, rz2, rel_sum, ent, neg_sum, rel_t, in_sem, out_sem,
):
    loads = [
        pltpu.make_async_copy(src, dst, in_sem.at[i])
        for i, (src, dst) in enumerate((
            (rel_in, rel_sum), (last_in, last), (far_last_in, far_last), (main_in, main),
            (far_main_in, far_main), (rx2_in, rx2), (ry2_in, ry2), (rz2_in, rz2),
        ))
    ]
    for load in loads:
        load.start()
    loads[0].wait()
    for r in range(4):
        rows = rel_sum[r * 128 : (r + 1) * 128, :].astype(F32)
        wide = jnp.concatenate([rows, jnp.zeros((128, DP - D), F32)], axis=1)
        rel_t[:, r * 128 : (r + 1) * 128] = wide.T[0:D]
    stores = [pltpu.make_async_copy(rel_t, rel_out, out_sem.at[0])]
    stores[0].start()

    c = lax.axis_index("bucket") % 2
    lane = iota((8, 128), 1) - 32 * c
    unit = jnp.where(lane == 16, 32.0, jnp.where(lane == 17, 1.0, 0.0)).astype(BF16)
    for load in loads[1:5]:
        load.wait()
    slots, row_ids = [], []
    for tiles, tail in ((main, last), (far_main, far_last)):
        tail_rows = tail[...].reshape(1024, 128)
        columns = [tiles[:, t * SLOT : (t + 1) * SLOT, :].reshape(1024, 128) for t in range(3)]
        slots.append(jnp.concatenate(columns + [tail_rows], axis=1))
        row_ids.append(nt(unit, tail_rows)[0:1, :])
    for r in range(2):
        numbers = (iota((512, 1024), 0) + r * 512).astype(F32)
        got = nn(hot_where(numbers == row_ids[0]), slots[0]) + nn(hot_where(numbers == row_ids[1]), slots[1])
        turned = got.T
        ent[r, 0:384] = turned[0:384]
        ent[r, 384:D] = jnp.where(c == 0, turned[384:400], turned[416:432])
        store = pltpu.make_async_copy(ent.at[r], ent_out.at[:, pl.ds(r * 512, 512)], out_sem.at[1 + r])
        store.start()
        stores.append(store)

    def sum_all(ref):
        total = ref[0].astype(F32)
        for i in range(1, ref.shape[0]):
            total = total + ref[i].astype(F32)
        return total

    for load in loads[5:]:
        load.wait()
    neg_sum[:, 0:128] = sum_all(rx2)
    neg_sum[:, 128:256] = sum_all(ry2)
    neg_sum[:, 256:D] = sum_all(rz2)[:, 0 : D - 256]
    stores.append(pltpu.make_async_copy(neg_sum, neg_out, out_sem.at[3]))
    stores[-1].start()
    for store in stores:
        store.wait()


SCRATCH = [
    ((16, D, 128), BF16),
    ((D + 16, NEG_DEV), BF16),
    ((NEG_DEV, DP), BF16),
    ((2, NEG_DEV, 8 * EC), BF16),
    ((8, DP, EC), BF16),
    ((8, 8, EC), F32),
    ((2, D, EC), F32),
    ((2, D, EC), F32),
    ((2, D, EC), F32),
    ((2, 8, 8, EC), F32),
    ((8, 8, EC), F32),
    ((8, 8, EC), F32),
    ((8, 8, EC), F32),
    ((8, 8, EC), F32),
    ((8, D, EC), F32),
    ((2, D, EC), F32),
    ((2, D, EC), F32),
    ((2, D, EC), BF16),
    ((2, D, EC), BF16),
    ((8, 8, EC), F32),
    ((DP, 8 * EC), BF16),
    ((DP, 2 * E_DEV), BF16),
    ((D, E_DEV), BF16),
    ((D, E_DEV), BF16),
    ((NZ * NS, 112, 128), BF16),
    ((NZ * NS, 112, 128), BF16),
    ((NZ * NS, 48, 128), BF16),
    ((NZ * NS, SLOT, 128), BF16),
    ((NB, 256, 128), F32),
    ((NB, 256, 128), F32),
    ((2, D - 256, NEG_DEV), BF16),
    ((2, 4, 256, 128), BF16),
    ((2, 4, 4, NEG_OWN, 128), BF16),
    ((D - 256, NEG_DEV), BF16),
    ((4, 2, 256, 128), BF16),
    ((4, 2, 4, NEG_OWN, 128), BF16),
    ((NEG_DEV, 256), BF16),
    ((2, 256, 128), BF16),
    ((2, 4, NEG_OWN, 128), BF16),
    ((NS, NEG_OWN, 256), BF16),
    ((8, NEG_OWN, 128), BF16),
    ((8, NEG_OWN, 128), BF16),
    ((REL, D), F32),
    ((REL // 2, D), F32),
    ((REL // 2, D), BF16),
    ((NS, 16, D), BF16),
    ((NZ, 16, D), F32),
    ((REL, D), BF16),
]


def per_device(
    head_rows, tail_rows, rel_ids, relations, edge_weights, neg_rows, send_slots, dest_rows
):
    vmem = pl.BlockSpec(memory_space=pltpu.VMEM)
    anywhere = pl.BlockSpec(memory_space=pl.ANY)
    results = pl.pallas_call(
        kernel,
        out_shape=(
            jax.ShapeDtypeStruct((NZ * NS, 48, 128), BF16),
            jax.ShapeDtypeStruct((NZ * NS, SLOT, 128), BF16),
            jax.ShapeDtypeStruct((NZ * NS, 48, 128), BF16),
            jax.ShapeDtypeStruct((NZ * NS, SLOT, 128), BF16),
            jax.ShapeDtypeStruct((8, NEG_OWN, 128), BF16),
            jax.ShapeDtypeStruct((8, NEG_OWN, 128), BF16),
            jax.ShapeDtypeStruct((NS, NEG_OWN, 256), BF16),
            jax.ShapeDtypeStruct((REL, D), BF16),
        ),
        in_specs=[vmem] * 8,
        out_specs=(anywhere,) * 8,
        scratch_shapes=[pltpu.VMEM(shape, dtype) for shape, dtype in SCRATCH]
        + [
            pltpu.SemaphoreType.DMA((31,)),
            pltpu.SemaphoreType.DMA((31,)),
            pltpu.SemaphoreType.REGULAR((4,)),
            pltpu.SemaphoreType.DMA((8,)),
            pltpu.SemaphoreType.DMA((NZ,)),
        ],
        compiler_params=pltpu.CompilerParams(
            collective_id=0, has_side_effects=True, vmem_limit_bytes=60 * 1024 * 1024
        ),
        cost_estimate=pl.CostEstimate(
            flops=2 * 3 * 1024 * 4096 * 400, bytes_accessed=8 * 1024 * 1024, transcendentals=1024 * 4096
        ),
        name="complex_backward",
    )(
        head_rows.T,
        tail_rows.T,
        rel_ids.reshape(1, E_DEV),
        relations.T,
        edge_weights.reshape(1, E_DEV),
        neg_rows.T,
        send_slots.T,
        dest_rows.T,
    )
    ent_t, neg_grad, rel_t = pl.pallas_call(
        finish,
        out_shape=(
            jax.ShapeDtypeStruct((D, ENT_DEV), F32),
            jax.ShapeDtypeStruct((NEG_OWN, D), F32),
            jax.ShapeDtypeStruct((D, REL), F32),
        ),
        in_specs=[anywhere] * 8,
        out_specs=(anywhere,) * 3,
        scratch_shapes=[
            pltpu.VMEM((NZ * NS, 48, 128), BF16),
            pltpu.VMEM((NZ * NS, SLOT, 128), BF16),
            pltpu.VMEM((NZ * NS, 48, 128), BF16),
            pltpu.VMEM((NZ * NS, SLOT, 128), BF16),
            pltpu.VMEM((8, NEG_OWN, 128), BF16),
            pltpu.VMEM((8, NEG_OWN, 128), BF16),
            pltpu.VMEM((NS, NEG_OWN, 256), BF16),
            pltpu.VMEM((REL, D), BF16),
            pltpu.VMEM((2, D, 512), F32),
            pltpu.VMEM((NEG_OWN, D), F32),
            pltpu.VMEM((D, REL), F32),
            pltpu.SemaphoreType.DMA((8,)),
            pltpu.SemaphoreType.DMA((4,)),
        ],
        compiler_params=pltpu.CompilerParams(vmem_limit_bytes=60 * 1024 * 1024),
        cost_estimate=pl.CostEstimate(
            flops=2 * 1024 * 2048 * 512, bytes_accessed=6 * 1024 * 1024, transcendentals=0
        ),
        name="make_outputs",
    )(*results)
    return ent_t.T, neg_grad, rel_t.T


def solution(mesh):
    return jax.shard_map(
        per_device,
        mesh=mesh,
        in_specs=(
            P(("bucket", "shard"), None),
            P(("bucket", "shard"), None),
            P(("bucket", "shard")),
            P(),
            P(("bucket", "shard")),
            P("bucket", None),
            P(("bucket", "shard"), None),
            P(("bucket", "shard"), None),
        ),
        out_specs=(P(("bucket", "shard"), None), P(("bucket", "shard"), None), P()),
        check_vma=False,
    )
```

```python
import functools

import jax
import jax.numpy as jnp
from jax import lax
from jax.experimental import pallas as pl
from jax.experimental.pallas import tpu as pltpu
from jax.sharding import PartitionSpec as P

D = 400
HALF = 200
DP = 512
E_DEV = 512
ENT_DEV = 1024
REL = 512
NEG_DEV = 1024
SLOT = 16
NB = 8
NS = 16
NZ = 4
EC = 256
NEG_OWN = 64

MESH = pl.DeviceIdType.MESH
F32 = jnp.float32
BF16 = jnp.bfloat16

(Q1_S, SQ1_S, Q2_S, SQ2_S, Q3_S, SQ3_S, ST1_S, O1_S, SC1_S, O2_S, ST2_S, O3_S, SC2_S,
 RC_S, R2_S, R3_S, R4_S, R5_S, ENT_S, Z1_S, X1_S, Y1_S, Z2_S, X2_S, Y2_S, GZ_S, GX_S, GY_S, O4_S,
 PX_S, PY_S, ZX_S) = range(32)


def nt(a, b):
    return lax.dot_general(a, b, (((1,), (1,)), ((), ())), preferred_element_type=F32)


def nn(a, b):
    return jnp.dot(a, b, preferred_element_type=F32)


def iota(shape, dim):
    return lax.broadcasted_iota(jnp.int32, shape, dim)


def hot_where(mask):
    return mask.astype(F32).astype(BF16)


def wait_bytes(ref, sem):
    pltpu.make_async_copy(ref, ref, sem).wait()


def kernel(
    head, tail, ids, rel, wts, neg, slots, drows,
    main_out, last_out, far_main_out, far_last_out, rx2_out, ry2_out, rz2_out, rel_sum_out,
    nbt, wide, nb, prob, qt, sq, hts, tts, rts, mb, st, st_in, sc, sc_in,
    ot, ot_pair, ot_own, o_sum, o_far, lt, qs, ends, rt_hi, rt_lo,
    packed, arrived, far_main, far_last, slot_col, dest_col,
    gz, gx, gy, rz1, rx1, ry1, azx, rzx, az, ax, ay, rz2, rx2, ry2,
    rp, rp_in, r1b, r2in, r2all, rfin,
    send, recv, known, out_sem, ent_recv,
):
    bucket, shard = lax.axis_index("bucket"), lax.axis_index("shard")
    z, c = bucket // 2, bucket % 2
    x, y = shard // 4, shard % 4
    oc = 1 - c
    partner = (z * 2 + oc, shard)
    pair = ((z + 1 - 2 * (z % 2)) * 2 + c, shard)
    z_far = 3 - z
    far = (z_far * 2 + c, shard)

    def rcopy(src, dst, s_sem, r_sem, device):
        pltpu.make_async_remote_copy(
            src_ref=src, dst_ref=dst, send_sem=s_sem, recv_sem=r_sem,
            device_id=device, device_id_type=MESH,
        ).start()

    barrier = pltpu.get_barrier_semaphore()

    x_peers = [(bucket, lax.rem(x + i, 4) * 4 + y) for i in (1, 2, 3)]
    y_peers = [(bucket, x * 4 + lax.rem(y + i, 4)) for i in (1, 2, 3)]
    friends = [partner, pair, far] + x_peers + y_peers

    def tell(sem, devices):
        for device in devices:
            pl.semaphore_signal(sem, inc=1, device_id=device, device_id_type=MESH)

    tell(barrier, friends)

    for g in range(8):
        qt[g, D:DP, :] = jnp.zeros((DP - D, EC), BF16)
    wide[D:, :] = jnp.ones((16, NEG_DEV), BF16)

    for i in range(8):
        nbt[i] = neg[:, i * 128 : (i + 1) * 128]

    rel_1 = rel[...].astype(BF16)
    rest = rel[...] - rel_1.astype(F32)
    rel_2 = rest.astype(BF16)
    rel_3 = (rest - rel_2.astype(F32)).astype(BF16)
    for j in range(2):
        cols = slice(j * EC, (j + 1) * EC)
        h_t = head[:, cols].astype(F32)
        t_t = tail[:, cols].astype(F32)
        hot = hot_where(iota((REL, EC), 0) == ids[0:1, cols])
        r_t = (nn(rel_1, hot) + nn(rel_2, hot)) + nn(rel_3, hot)
        hre, him = h_t[:HALF], h_t[HALF:]
        rre, rim = r_t[:HALF], r_t[HALF:]
        q = jnp.concatenate([hre * rre - him * rim, hre * rim + him * rre], axis=0).astype(BF16)
        qt[2 * c + j, 0:D, :] = q
        sq[2 * c + j, 0:1, :] = jnp.sum(q.astype(F32) * t_t, axis=0, keepdims=True)
        sq[2 * c + j, 1:2, :] = wts[0:1, cols]
        sq[2 * c + j, 2:8, :] = jnp.zeros((6, EC), F32)
        hts[j] = h_t
        tts[j] = t_t
        rts[j] = r_t

    pl.semaphore_wait(barrier, len(friends))
    tell(known.at[0], y_peers)

    for i in (x, 4 + y):
        rcopy(nbt.at[i], nbt.at[8 + i], send.at[GZ_S], recv.at[GZ_S], far)
    mine, theirs, real = pl.ds(2 * c, 2), pl.ds(4 + 2 * c, 2), pl.ds(0, D)
    rcopy(qt.at[mine, real], qt.at[mine, real], send.at[Q1_S], recv.at[Q1_S], partner)
    rcopy(sq.at[mine], sq.at[mine], send.at[SQ1_S], recv.at[SQ1_S], partner)
    rcopy(qt.at[mine, real], qt.at[theirs, real], send.at[Q2_S], recv.at[Q2_S], pair)
    rcopy(sq.at[mine], sq.at[theirs], send.at[SQ2_S], recv.at[SQ2_S], pair)

    ones = jnp.ones((SLOT, 128), BF16)
    tables = []
    for ref in (slots, drows):
        value = ref[...].astype(F32)
        high = jnp.floor(value * (1.0 / 32.0))
        tables.append((high.astype(BF16), (value - 32.0 * high).astype(BF16)))

    def columns(b, carry):
        owner_hot = hot_where(iota((256, 128), 1) == iota((256, 128), 0) // SLOT + b * NS)
        keep = iota((256, SLOT), 1) == iota((256, SLOT), 0) % SLOT
        for (high, low), out in zip(tables, (slot_col, dest_col)):
            h = jnp.where(keep, nt(owner_hot, high), 0.0).astype(BF16)
            l = jnp.where(keep, nt(owner_hot, low), 0.0).astype(BF16)
            out[b] = 32.0 * nn(h, ones) + nn(l, ones)
        return carry

    lax.fori_loop(0, NB, columns, 0)
    nb[:, 384:DP] = jnp.zeros((NEG_DEV, 128), BF16)

    def flip(b):
        for i in range(8):
            part = nbt[b * 8 + i]
            wide[0:D, i * 128 : (i + 1) * 128] = part
            nb[i * 128 : (i + 1) * 128, 0:D] = part.astype(F32).T.astype(BF16)

    def block(b, two):

        chunks = (2 * two, 2 * two + 1)
        scores = nn(nb[...], jnp.concatenate([qt[g] for g in chunks], axis=1))
        for u, g in enumerate(chunks):
            s = scores[:, u * EC : (u + 1) * EC]
            m = jnp.max(s, axis=0, keepdims=True)
            pb = jnp.exp(s - m).astype(BF16)
            prob[b, :, pl.ds(pl.multiple_of(g * EC, EC), EC)] = pb
            o = nn(wide[...], pb)
            l = o[D : D + 1]
            o = o[0:D]
            mb[b, g, 0:1, :] = m
            if b == 0:
                st[g, 0:1, :] = m
                st[g, 1:2, :] = l
                st[g, 2:8, :] = jnp.zeros((6, EC), F32)
                ot[g] = o
            else:
                m_old = st[g, 0:1, :]
                m_new = jnp.maximum(m_old, m)
                f_old = jnp.exp(m_old - m_new)
                f_new = jnp.exp(m - m_new)
                st[g, 0:1, :] = m_new
                st[g, 1:2, :] = st[g, 1:2, :] * f_old + l * f_new
                ot[g] = ot[g] * f_old + o * f_new

    flip(0)
    block(0, c)
    pl.semaphore_wait(known.at[0], 3)
    tell(known.at[1], (pair, far))
    wait_bytes(nbt.at[pl.ds(8, 2)], recv.at[GZ_S])
    for i in (1, 3, 2):
        xx, yy = lax.rem(x + i, 4), lax.rem(y + i, 4)
        rcopy(nbt.at[8 + x], nbt.at[8 + x], send.at[GX_S], recv.at[GX_S], (bucket, xx * 4 + y))
        rcopy(nbt.at[12 + y], nbt.at[12 + y], send.at[GY_S], recv.at[GY_S], (bucket, x * 4 + yy))
    wait_bytes(qt.at[mine, real], recv.at[Q1_S])
    wait_bytes(sq.at[mine], recv.at[SQ1_S])
    block(0, oc)
    pl.semaphore_wait(known.at[1], 2)
    tell(known.at[2], (pair, far))
    wait_bytes(qt.at[mine, real], recv.at[Q2_S])
    wait_bytes(sq.at[mine], recv.at[SQ2_S])
    rcopy(qt.at[theirs, real], qt.at[theirs, real], send.at[Q3_S], recv.at[Q3_S], partner)
    rcopy(sq.at[theirs], sq.at[theirs], send.at[SQ3_S], recv.at[SQ3_S], partner)
    block(0, 2 + c)
    wait_bytes(qt.at[mine, real], recv.at[Q3_S])
    wait_bytes(sq.at[mine], recv.at[SQ3_S])
    block(0, 2 + oc)
    wait_bytes(nbt.at[pl.ds(8, 3)], recv.at[GX_S])
    wait_bytes(nbt.at[pl.ds(8, 3)], recv.at[GY_S])
    flip(1)
    block(1, 2 + oc)
    pl.semaphore_wait(known.at[2], 2)
    tell(known.at[3], (partner,))
    rcopy(
        ot.at[pl.ds(4 + 2 * oc, 2)], ot_pair, send.at[O1_S], recv.at[O1_S], partner
    )
    block(1, 2 + c)
    own_half, pair_half = pl.ds(0, 4), pl.ds(4, 4)
    rcopy(st.at[pair_half], st_in.at[pair_half], send.at[ST1_S], recv.at[ST1_S], partner)

    def merge(g):
        m_a, m_b = st[g, 0:1, :], st_in[g, 0:1, :]
        m = jnp.maximum(m_a, m_b)
        f_a, f_b = jnp.exp(m_a - m), jnp.exp(m_b - m)
        sc[g, 0:1, :] = m
        sc[g, 1:2, :] = st[g, 1:2, :] * f_a + st_in[g, 1:2, :] * f_b
        sc[g, 2:8, :] = jnp.zeros((6, EC), F32)
        return f_a, f_b

    block(1, oc)
    pl.semaphore_wait(known.at[3], 1)
    rcopy(ot.at[pl.ds(2 * oc, 2)], ot_own, send.at[O3_S], recv.at[O3_S], partner)
    wait_bytes(st_in.at[pair_half], recv.at[ST1_S])
    wait_bytes(ot_pair, recv.at[O1_S])
    for g in range(4, 8):
        merge(g)
    for j in range(2):
        f_a, f_b = merge(4 + 2 * c + j)
        o_sum[j] = (ot[4 + 2 * c + j] * f_a + ot_pair[j] * f_b).astype(BF16)
    rcopy(o_sum.at[0], o_far.at[0], send.at[O4_S], recv.at[O4_S], pair)
    rcopy(sc.at[pair_half], sc_in.at[own_half], send.at[SC1_S], recv.at[SC1_S], pair)
    block(1, c)
    rcopy(st.at[own_half], st_in.at[own_half], send.at[ST2_S], recv.at[ST2_S], partner)
    wait_bytes(st_in.at[own_half], recv.at[ST2_S])
    for g in range(4):
        merge(g)
    rcopy(sc.at[own_half], sc_in.at[pair_half], send.at[SC2_S], recv.at[SC2_S], pair)
    rcopy(o_sum.at[1], o_far.at[1], send.at[O2_S], recv.at[O2_S], pair)
    wait_bytes(sc_in.at[own_half], recv.at[SC1_S])
    wait_bytes(sc_in.at[pair_half], recv.at[SC2_S])
    for g in range(8):
        pos = sq[g, 0:1, :]
        m0, m1 = sc[g, 0:1, :], sc_in[g, 0:1, :]
        top = jnp.maximum(pos, jnp.maximum(m0, m1))
        total = (
            jnp.exp(pos - top)
            + sc[g, 1:2, :] * jnp.exp(m0 - top)
            + sc_in[g, 1:2, :] * jnp.exp(m1 - top)
        )
        lt[g, 0:1, :] = top + jnp.log(total)

    def neg_block(b):
        for g in range(8):
            scale = sq[g, 1:2, :] * jnp.exp(mb[b, g, 0:1, :] - lt[g, 0:1, :])
            qs[:, g * EC : (g + 1) * EC] = (qt[g].astype(F32) * scale).astype(BF16)

        def rows_of(h, carry):
            rr = pl.ds(pl.multiple_of(h * 512, 512), 512)
            acc = nt(prob[b, rr, :], qs[...])
            for u in range(2):
                part = acc[u * 256 : (u + 1) * 256]
                gx[b, 2 * h + u] = part[:, 0:128].astype(BF16)
                for yy in range(4):
                    gy[b, yy, 2 * h + u] = part[yy * 64 : (yy + 1) * 64, 128:256].astype(BF16)
            gz[b, :, rr] = acc[:, 256:512].T[0 : D - 256].astype(BF16)
            return carry

        lax.fori_loop(0, 2, rows_of, 0)
        for i in (1, 3, 2):
            xx, yy = lax.rem(x + i, 4), lax.rem(y + i, 4)
            rcopy(gx.at[b, xx], rx1.at[x, b], send.at[X1_S], recv.at[X1_S], (bucket, xx * 4 + y))
            rcopy(gy.at[b, yy], ry1.at[y, b], send.at[Y1_S], recv.at[Y1_S], (bucket, x * 4 + yy))

    neg_block(1)
    rcopy(gz.at[1], rz1, send.at[Z1_S], recv.at[Z1_S], far)
    wait_bytes(ot_own, recv.at[O3_S])
    wait_bytes(o_far.at[0], recv.at[O4_S])
    wait_bytes(o_far.at[1], recv.at[O2_S])
    ends[D:DP, :] = jnp.zeros((DP - D, 2 * E_DEV), BF16)
    for j in range(2):
        cols = slice(j * EC, (j + 1) * EC)
        tail_cols = slice(E_DEV + j * EC, E_DEV + (j + 1) * EC)
        g = 2 * c + j
        pos, w, ltot = sq[g, 0:1, :], sq[g, 1:2, :], lt[g, 0:1, :]
        pos_coef = w * (jnp.exp(pos - ltot) - 1.0)
        own = w * jnp.exp(st[g, 0:1, :] - ltot)
        other = w * jnp.exp(st_in[g, 0:1, :] - ltot)
        away = w * jnp.exp(sc_in[g, 0:1, :] - ltot)
        grad = pos_coef * tts[j] + ot[g] * own + ot_own[j] * other + o_far[j].astype(F32) * away
        gre, gim = grad[:HALF], grad[HALF:]
        rre, rim = rts[j, :HALF, :], rts[j, HALF:, :]
        hre, him = hts[j, :HALF, :], hts[j, HALF:, :]
        head_grad = jnp.concatenate(
            [gre * rre + gim * rim, gim * rre - gre * rim], axis=0
        ).astype(BF16)
        tail_grad = (pos_coef * qt[g, 0:D, :].astype(F32)).astype(BF16)
        for part, where_to in ((head_grad, cols), (tail_grad, tail_cols)):
            ends[0:D, where_to] = part
            ends[416:432, where_to] = part[384:D]
        term = jnp.concatenate([gre * hre + gim * him, gim * hre - gre * him], axis=0)
        hi = term.astype(BF16)
        rt_hi[:, cols] = hi
        rt_lo[:, cols] = (term - hi.astype(F32)).astype(BF16)

    src_chip = z * NS + shard

    def pack(k, first):
        zz = lax.rem(z + k, NZ)
        chips = pl.ds(pl.multiple_of(zz * NS, NS), NS)
        sel = []
        for d in range(2):
            sc_b = slot_col[zz * 2 + d]
            sel.append(jnp.concatenate(
                [hot_where(sc_b == (iota((256, 128), 1) + 128 * t).astype(F32)) for t in range(8)],
                axis=1,
            ))
        rows = nt(jnp.concatenate(sel, axis=0), ends[...])
        lane = iota((256, 128), 1)
        last = []
        for d in range(2):
            part = rows[d * 256 : (d + 1) * 256]
            for t in range(3):
                first_row = (d * 3 + t) * SLOT
                tile = part[:, t * 128 : (t + 1) * 128].astype(BF16).reshape(NS, SLOT, 128)
                packed[chips, first_row : first_row + SLOT, :] = tile
            dc = dest_col[zz * 2 + d]
            high = jnp.floor(dc * (1.0 / 32.0))
            code = jnp.where(lane == 32 * d + 16, high, jnp.where(lane == 32 * d + 17, dc - 32.0 * high, 0.0))
            last.append(part[:, 384:512] + code)
        tile = jnp.where(lane < 32, last[0], last[1]).astype(BF16).reshape(NS, SLOT, 128)
        packed[chips, 96:112, :] = tile
        for j in range(NS):
            ss = lax.rem(shard + j, NS)
            src = packed.at[zz * NS + ss]
            if first and j == 0:
                pltpu.make_async_copy(src, arrived.at[src_chip], ent_recv.at[k]).start()
            else:
                rcopy(src, arrived.at[src_chip], send.at[ENT_S], ent_recv.at[k], (zz * 2 + c, ss))

    def rel_chunk(r, carry):
        hot = hot_where(iota((128, E_DEV), 0) + r * 128 == ids[...])
        rp[pl.ds(pl.multiple_of(r * 128, 128), 128), :] = nt(hot, rt_hi[...]) + nt(hot, rt_lo[...])
        return carry

    lax.fori_loop(0, 4, rel_chunk, 0)
    rcopy(
        rp.at[pl.ds(pl.multiple_of(oc * 256, 256), 256)], rp_in, send.at[RC_S], recv.at[RC_S], partner
    )

    def pack_other(k, carry):
        pack(k, False)
        return carry

    pack(0, True)
    lax.fori_loop(1, 2, pack_other, 0)

    wait_bytes(rp_in, recv.at[RC_S])
    r1b[...] = (rp[pl.ds(pl.multiple_of(c * 256, 256), 256), :] + rp_in[...]).astype(BF16)
    for j in range(1, NS):
        ss = lax.rem(shard + j, NS)
        rows = r1b.at[pl.ds(pl.multiple_of(ss * 16, 16), 16)]
        rcopy(rows, r2in.at[shard], send.at[R2_S], recv.at[R2_S], (bucket, ss))
    r2in[shard] = r1b[pl.ds(pl.multiple_of(shard * 16, 16), 16), :]
    neg_block(0)

    wait_bytes(rz1, recv.at[Z1_S])
    for r in range(4):
        rr = slice(r * 256, (r + 1) * 256)
        azx[r] = (gz[0, :, rr].astype(F32) + rz1[:, rr].astype(F32)).astype(BF16)
    for i in (1, 3, 2):
        xx = lax.rem(x + i, 4)
        rcopy(azx.at[xx], rzx.at[x], send.at[ZX_S], recv.at[ZX_S], (bucket, xx * 4 + y))

    wait_bytes(r2in.at[pl.ds(0, NS - 1)], recv.at[R2_S])
    r2 = r2in[0].astype(F32)
    for i in range(1, NS):
        r2 = r2 + r2in[i].astype(F32)
    r2all[z] = r2
    for k in (1, 3, 2):
        zz = lax.rem(z + k, NZ)
        rcopy(r2all.at[z], r2all.at[z], send.at[R3_S], recv.at[R3_S], (zz * 2 + c, shard))

    lax.fori_loop(2, NZ, pack_other, 0)


    wait_bytes(rx1.at[pl.ds(0, 3)], recv.at[X1_S])
    for b in range(2):
        total = gx[b, x].astype(F32)
        for i in range(1, 4):
            total = total + rx1[lax.rem(x + i, 4), b].astype(F32)
        ax[b] = total.astype(BF16)
    for i in range(4):
        yy = lax.rem(y + i, 4)
        rows = pl.ds(pl.multiple_of(yy * NEG_OWN, NEG_OWN), NEG_OWN)
        if i:
            rcopy(ax.at[0, rows], rx2.at[y], send.at[X2_S], recv.at[X2_S], (bucket, x * 4 + yy))
        else:
            rx2[y] = ax[0, rows, :]
        rcopy(
            ax.at[1, rows], rx2.at[4 + y], send.at[X2_S], recv.at[X2_S], (z_far * 2 + c, x * 4 + yy)
        )
    wait_bytes(ry1.at[pl.ds(0, 3)], recv.at[Y1_S])
    for b in range(2):
        total = gy[b, y].astype(F32)
        for i in range(1, 4):
            total = total + ry1[lax.rem(y + i, 4), b].astype(F32)
        ay[b] = total.astype(BF16)
    for i in range(4):
        xx = lax.rem(x + i, 4)
        if i:
            rcopy(ay.at[0, xx], ry2.at[x], send.at[Y2_S], recv.at[Y2_S], (bucket, xx * 4 + y))
        else:
            ry2[x] = ay[0, x]
        rcopy(
            ay.at[1, xx], ry2.at[4 + x], send.at[Y2_S], recv.at[Y2_S], (z_far * 2 + c, xx * 4 + y)
        )
    wait_bytes(rzx.at[pl.ds(0, 3)], recv.at[ZX_S])
    total = azx[x].astype(F32)
    for i in range(1, 4):
        total = total + rzx[lax.rem(x + i, 4)].astype(F32)
    wide_sum = jnp.concatenate([total, jnp.zeros((256 - (D - 256), 256), F32)], axis=0)
    az[...] = wide_sum.T.astype(BF16)
    for i in range(4):
        yy = lax.rem(y + i, 4)
        rows = pl.ds(pl.multiple_of(yy * NEG_OWN, NEG_OWN), NEG_OWN)
        if i:
            rcopy(az.at[rows], rz2.at[y], send.at[Z2_S], recv.at[Z2_S], (bucket, x * 4 + yy))
        else:
            rz2[y] = az[rows, :]

    wait_bytes(r2all.at[pl.ds(0, 3)], recv.at[R3_S])
    rel_row = pl.ds(pl.multiple_of(c * 256 + shard * 16, 16), 16)
    rfin[rel_row, :] = (((r2all[0] + r2all[1]) + r2all[2]) + r2all[3]).astype(BF16)
    for j in range(1, NS):
        ss = lax.rem(shard + j, NS)
        rcopy(rfin.at[rel_row], rfin.at[rel_row], send.at[R4_S], recv.at[R4_S], (bucket, ss))

    def give(src, dst, sem):
        pltpu.make_async_copy(src, dst, sem).start()

    other_rows, last_rows = pl.ds(pl.multiple_of(oc * 48, 16), 48), pl.ds(96, SLOT)
    for k in range(NZ):
        chips = pl.ds(pl.multiple_of(lax.rem(z + NZ - k, NZ) * NS, NS), NS)
        wait_bytes(arrived.at[chips], ent_recv.at[k])
        rcopy(arrived.at[chips, other_rows], far_main.at[chips], send.at[PX_S], recv.at[PX_S], partner)
        rcopy(arrived.at[chips, last_rows], far_last.at[chips], send.at[PY_S], recv.at[PY_S], partner)
    give(arrived.at[:, pl.ds(pl.multiple_of(c * 48, 16), 48)], main_out, out_sem.at[0])
    give(arrived.at[:, last_rows], last_out, out_sem.at[5])
    wait_bytes(rfin.at[pl.ds(0, 240)], recv.at[R4_S])
    half_rel = rfin.at[pl.ds(pl.multiple_of(c * 256, 256), 256)]
    rcopy(half_rel, half_rel, send.at[R5_S], recv.at[R5_S], partner)
    wait_bytes(rx2.at[pl.ds(0, 7)], recv.at[X2_S])
    give(rx2, rx2_out, out_sem.at[1])
    wait_bytes(ry2.at[pl.ds(0, 7)], recv.at[Y2_S])
    give(ry2, ry2_out, out_sem.at[2])
    wait_bytes(rz2.at[pl.ds(0, 3)], recv.at[Z2_S])
    give(rz2, rz2_out, out_sem.at[3])
    wait_bytes(half_rel, recv.at[R5_S])
    give(rfin, rel_sum_out, out_sem.at[4])
    wait_bytes(far_main, recv.at[PX_S])
    give(far_main, far_main_out, out_sem.at[6])
    wait_bytes(far_last, recv.at[PY_S])
    give(far_last, far_last_out, out_sem.at[7])

    wait_bytes(nbt.at[pl.ds(0, 2)], send.at[GZ_S])
    wait_bytes(nbt.at[pl.ds(0, 3)], send.at[GX_S])
    wait_bytes(nbt.at[pl.ds(0, 3)], send.at[GY_S])
    for number in (Q1_S, Q2_S, Q3_S):
        wait_bytes(qt.at[mine, real], send.at[number])
    for number in (SQ1_S, SQ2_S, SQ3_S):
        wait_bytes(sq.at[mine], send.at[number])
    for number in (ST1_S, ST2_S, SC1_S, SC2_S):
        wait_bytes(st.at[own_half], send.at[number])
    wait_bytes(ot_pair, send.at[O1_S])
    wait_bytes(o_far.at[0], send.at[O4_S])
    wait_bytes(o_far.at[1], send.at[O2_S])
    wait_bytes(ot_own, send.at[O3_S])
    wait_bytes(arrived.at[pl.ds(0, 63)], send.at[ENT_S])
    wait_bytes(far_main, send.at[PX_S])
    wait_bytes(far_last, send.at[PY_S])
    wait_bytes(rp_in, send.at[RC_S])
    wait_bytes(r2in.at[pl.ds(0, NS - 1)], send.at[R2_S])
    wait_bytes(r2all.at[pl.ds(0, 3)], send.at[R3_S])
    wait_bytes(rfin.at[pl.ds(0, 240)], send.at[R4_S])
    wait_bytes(half_rel, send.at[R5_S])
    wait_bytes(rz1, send.at[Z1_S])
    wait_bytes(rx1.at[pl.ds(0, 3)], send.at[X1_S])
    wait_bytes(ry1.at[pl.ds(0, 3)], send.at[Y1_S])
    wait_bytes(rx2.at[pl.ds(0, 7)], send.at[X2_S])
    wait_bytes(ry2.at[pl.ds(0, 7)], send.at[Y2_S])
    wait_bytes(rz2.at[pl.ds(0, 3)], send.at[Z2_S])
    wait_bytes(rzx.at[pl.ds(0, 3)], send.at[ZX_S])
    for number in (0, 6):
        wait_bytes(far_main, out_sem.at[number])
    for number in (5, 7):
        wait_bytes(far_last, out_sem.at[number])
    wait_bytes(rx2, out_sem.at[1])
    wait_bytes(ry2, out_sem.at[2])
    wait_bytes(rz2, out_sem.at[3])
    wait_bytes(rfin, out_sem.at[4])


def finish(
    main_in, last_in, far_main_in, far_last_in, rx2_in, ry2_in, rz2_in, rel_in,
    ent_out, neg_out, rel_out,
    main, last, far_main, far_last, rx2, ry2, rz2, rel_sum, ent, neg_sum, rel_t, in_sem, out_sem,
):
    loads = [
        pltpu.make_async_copy(src, dst, in_sem.at[i])
        for i, (src, dst) in enumerate((
            (rel_in, rel_sum), (last_in, last), (far_last_in, far_last), (main_in, main),
            (far_main_in, far_main), (rx2_in, rx2), (ry2_in, ry2), (rz2_in, rz2),
        ))
    ]
    for load in loads:
        load.start()
    loads[0].wait()
    for r in range(4):
        rows = rel_sum[r * 128 : (r + 1) * 128, :].astype(F32)
        wide = jnp.concatenate([rows, jnp.zeros((128, DP - D), F32)], axis=1)
        rel_t[:, r * 128 : (r + 1) * 128] = wide.T[0:D]
    stores = [pltpu.make_async_copy(rel_t, rel_out, out_sem.at[0])]
    stores[0].start()

    c = lax.axis_index("bucket") % 2
    lane = iota((8, 128), 1) - 32 * c
    unit = jnp.where(lane == 16, 32.0, jnp.where(lane == 17, 1.0, 0.0)).astype(BF16)
    for load in loads[1:5]:
        load.wait()
    slots, row_ids = [], []
    for tiles, tail in ((main, last), (far_main, far_last)):
        tail_rows = tail[...].reshape(1024, 128)
        columns = [tiles[:, t * SLOT : (t + 1) * SLOT, :].reshape(1024, 128) for t in range(3)]
        slots.append(jnp.concatenate(columns + [tail_rows], axis=1))
        row_ids.append(nt(unit, tail_rows)[0:1, :])
    for r in range(2):
        numbers = (iota((512, 1024), 0) + r * 512).astype(F32)
        got = nn(hot_where(numbers == row_ids[0]), slots[0]) + nn(hot_where(numbers == row_ids[1]), slots[1])
        turned = got.T
        ent[r, 0:384] = turned[0:384]
        ent[r, 384:D] = jnp.where(c == 0, turned[384:400], turned[416:432])
        store = pltpu.make_async_copy(ent.at[r], ent_out.at[:, pl.ds(r * 512, 512)], out_sem.at[1 + r])
        store.start()
        stores.append(store)

    def sum_all(ref):
        total = ref[0].astype(F32)
        for i in range(1, ref.shape[0]):
            total = total + ref[i].astype(F32)
        return total

    for load in loads[5:]:
        load.wait()
    neg_sum[:, 0:128] = sum_all(rx2)
    neg_sum[:, 128:256] = sum_all(ry2)
    neg_sum[:, 256:D] = sum_all(rz2)[:, 0 : D - 256]
    stores.append(pltpu.make_async_copy(neg_sum, neg_out, out_sem.at[3]))
    stores[-1].start()
    for store in stores:
        store.wait()


SCRATCH = [
    ((16, D, 128), BF16),
    ((D + 16, NEG_DEV), BF16),
    ((NEG_DEV, DP), BF16),
    ((2, NEG_DEV, 8 * EC), BF16),
    ((8, DP, EC), BF16),
    ((8, 8, EC), F32),
    ((2, D, EC), F32),
    ((2, D, EC), F32),
    ((2, D, EC), F32),
    ((2, 8, 8, EC), F32),
    ((8, 8, EC), F32),
    ((8, 8, EC), F32),
    ((8, 8, EC), F32),
    ((8, 8, EC), F32),
    ((8, D, EC), F32),
    ((2, D, EC), F32),
    ((2, D, EC), F32),
    ((2, D, EC), BF16),
    ((2, D, EC), BF16),
    ((8, 8, EC), F32),
    ((DP, 8 * EC), BF16),
    ((DP, 2 * E_DEV), BF16),
    ((D, E_DEV), BF16),
    ((D, E_DEV), BF16),
    ((NZ * NS, 112, 128), BF16),
    ((NZ * NS, 112, 128), BF16),
    ((NZ * NS, 48, 128), BF16),
    ((NZ * NS, SLOT, 128), BF16),
    ((NB, 256, 128), F32),
    ((NB, 256, 128), F32),
    ((2, D - 256, NEG_DEV), BF16),
    ((2, 4, 256, 128), BF16),
    ((2, 4, 4, NEG_OWN, 128), BF16),
    ((D - 256, NEG_DEV), BF16),
    ((4, 2, 256, 128), BF16),
    ((4, 2, 4, NEG_OWN, 128), BF16),
    ((4, D - 256, 256), BF16),
    ((4, D - 256, 256), BF16),
    ((256, 256), BF16),
    ((2, 256, 128), BF16),
    ((2, 4, NEG_OWN, 128), BF16),
    ((4, NEG_OWN, 256), BF16),
    ((8, NEG_OWN, 128), BF16),
    ((8, NEG_OWN, 128), BF16),
    ((REL, D), F32),
    ((REL // 2, D), F32),
    ((REL // 2, D), BF16),
    ((NS, 16, D), BF16),
    ((NZ, 16, D), F32),
    ((REL, D), BF16),
]


def per_device(
    head_rows, tail_rows, rel_ids, relations, edge_weights, neg_rows, send_slots, dest_rows
):
    vmem = pl.BlockSpec(memory_space=pltpu.VMEM)
    anywhere = pl.BlockSpec(memory_space=pl.ANY)
    results = pl.pallas_call(
        kernel,
        out_shape=(
            jax.ShapeDtypeStruct((NZ * NS, 48, 128), BF16),
            jax.ShapeDtypeStruct((NZ * NS, SLOT, 128), BF16),
            jax.ShapeDtypeStruct((NZ * NS, 48, 128), BF16),
            jax.ShapeDtypeStruct((NZ * NS, SLOT, 128), BF16),
            jax.ShapeDtypeStruct((8, NEG_OWN, 128), BF16),
            jax.ShapeDtypeStruct((8, NEG_OWN, 128), BF16),
            jax.ShapeDtypeStruct((4, NEG_OWN, 256), BF16),
            jax.ShapeDtypeStruct((REL, D), BF16),
        ),
        in_specs=[vmem] * 8,
        out_specs=(anywhere,) * 8,
        scratch_shapes=[pltpu.VMEM(shape, dtype) for shape, dtype in SCRATCH]
        + [
            pltpu.SemaphoreType.DMA((32,)),
            pltpu.SemaphoreType.DMA((32,)),
            pltpu.SemaphoreType.REGULAR((4,)),
            pltpu.SemaphoreType.DMA((8,)),
            pltpu.SemaphoreType.DMA((NZ,)),
        ],
        compiler_params=pltpu.CompilerParams(
            collective_id=0, has_side_effects=True, vmem_limit_bytes=60 * 1024 * 1024
        ),
        cost_estimate=pl.CostEstimate(
            flops=2 * 3 * 1024 * 4096 * 400, bytes_accessed=8 * 1024 * 1024, transcendentals=1024 * 4096
        ),
        name="complex_backward",
    )(
        head_rows.T,
        tail_rows.T,
        rel_ids.reshape(1, E_DEV),
        relations.T,
        edge_weights.reshape(1, E_DEV),
        neg_rows.T,
        send_slots.T,
        dest_rows.T,
    )
    ent_t, neg_grad, rel_t = pl.pallas_call(
        finish,
        out_shape=(
            jax.ShapeDtypeStruct((D, ENT_DEV), F32),
            jax.ShapeDtypeStruct((NEG_OWN, D), F32),
            jax.ShapeDtypeStruct((D, REL), F32),
        ),
        in_specs=[anywhere] * 8,
        out_specs=(anywhere,) * 3,
        scratch_shapes=[
            pltpu.VMEM((NZ * NS, 48, 128), BF16),
            pltpu.VMEM((NZ * NS, SLOT, 128), BF16),
            pltpu.VMEM((NZ * NS, 48, 128), BF16),
            pltpu.VMEM((NZ * NS, SLOT, 128), BF16),
            pltpu.VMEM((8, NEG_OWN, 128), BF16),
            pltpu.VMEM((8, NEG_OWN, 128), BF16),
            pltpu.VMEM((4, NEG_OWN, 256), BF16),
            pltpu.VMEM((REL, D), BF16),
            pltpu.VMEM((2, D, 512), F32),
            pltpu.VMEM((NEG_OWN, D), F32),
            pltpu.VMEM((D, REL), F32),
            pltpu.SemaphoreType.DMA((8,)),
            pltpu.SemaphoreType.DMA((4,)),
        ],
        compiler_params=pltpu.CompilerParams(vmem_limit_bytes=60 * 1024 * 1024),
        cost_estimate=pl.CostEstimate(
            flops=2 * 1024 * 2048 * 512, bytes_accessed=6 * 1024 * 1024, transcendentals=0
        ),
        name="make_outputs",
    )(*results)
    return ent_t.T, neg_grad, rel_t.T


def solution(mesh):
    return jax.shard_map(
        per_device,
        mesh=mesh,
        in_specs=(
            P(("bucket", "shard"), None),
            P(("bucket", "shard"), None),
            P(("bucket", "shard")),
            P(),
            P(("bucket", "shard")),
            P("bucket", None),
            P(("bucket", "shard"), None),
            P(("bucket", "shard"), None),
        ),
        out_specs=(P(("bucket", "shard"), None), P(("bucket", "shard"), None), P()),
        check_vma=False,
    )
```

```python
import functools

import jax
import jax.numpy as jnp
from jax import lax
from jax.experimental import pallas as pl
from jax.experimental.pallas import tpu as pltpu
from jax.sharding import PartitionSpec as P

D = 400
HALF = 200
DP = 512
E_DEV = 512
ENT_DEV = 1024
REL = 512
NEG_DEV = 1024
SLOT = 16
NB = 8
NS = 16
NZ = 4
EC = 256
NEG_OWN = 64

MESH = pl.DeviceIdType.MESH
F32 = jnp.float32
BF16 = jnp.bfloat16

(Q1_S, SQ1_S, Q2_S, SQ2_S, Q3_S, SQ3_S, ST1_S, O1_S, SC1_S, O2_S, ST2_S, O3_S, SC2_S,
 RC_S, R2_S, R3_S, R4_S, R5_S, ENT_S, Z1_S, X1_S, Y1_S, Z2_S, X2_S, Y2_S, GZ_S, GX_S, GY_S, O4_S,
 PX_S, PY_S, ZX_S) = range(32)


def nt(a, b):
    return lax.dot_general(a, b, (((1,), (1,)), ((), ())), preferred_element_type=F32)


def nn(a, b):
    return jnp.dot(a, b, preferred_element_type=F32)


def iota(shape, dim):
    return lax.broadcasted_iota(jnp.int32, shape, dim)


def hot_where(mask):
    return mask.astype(F32).astype(BF16)


def wait_bytes(ref, sem):
    pltpu.make_async_copy(ref, ref, sem).wait()


def kernel(
    head_in, tail_in, ids, rel_in, wts, neg_in, slots, drows,
    main_out, last_out, far_main_out, far_last_out, rx2_out, ry2_out, rz2_out, rel_sum_out,
    head, tail, rel, neg, nbt, wide, nb, prob, qt, sq, hts, tts, rts, mb, st, st_in, sc, sc_in,
    ot, ot_pair, ot_own, o_sum, o_far, lt, qs, ends, rt_hi, rt_lo,
    packed, arrived, far_main, far_last, slot_col, dest_col,
    gz, gx, gy, rz1, rx1, ry1, azx, rzx, az, ax, ay, rz2, rx2, ry2,
    rp, rp_in, r1b, r2in, r2all, rfin,
    send, recv, known, out_sem, ent_recv, in_sem,
):
    bucket, shard = lax.axis_index("bucket"), lax.axis_index("shard")
    z, c = bucket // 2, bucket % 2
    x, y = shard // 4, shard % 4
    oc = 1 - c
    partner = (z * 2 + oc, shard)
    pair = ((z + 1 - 2 * (z % 2)) * 2 + c, shard)
    z_far = 3 - z
    far = (z_far * 2 + c, shard)

    def rcopy(src, dst, s_sem, r_sem, device):
        pltpu.make_async_remote_copy(
            src_ref=src, dst_ref=dst, send_sem=s_sem, recv_sem=r_sem,
            device_id=device, device_id_type=MESH,
        ).start()

    barrier = pltpu.get_barrier_semaphore()

    x_peers = [(bucket, lax.rem(x + i, 4) * 4 + y) for i in (1, 2, 3)]
    y_peers = [(bucket, x * 4 + lax.rem(y + i, 4)) for i in (1, 2, 3)]
    friends = [partner, pair, far] + x_peers + y_peers

    def tell(sem, devices):
        for device in devices:
            pl.semaphore_signal(sem, inc=1, device_id=device, device_id_type=MESH)

    loads = [
        pltpu.make_async_copy(src, dst, in_sem.at[i])
        for i, (src, dst) in enumerate(((rel_in, rel), (head_in, head), (tail_in, tail), (neg_in, neg)))
    ]
    for load in loads:
        load.start()
    tell(barrier, friends)

    for g in range(8):
        qt[g, D:DP, :] = jnp.zeros((DP - D, EC), BF16)
    wide[D:, :] = jnp.ones((16, NEG_DEV), BF16)

    for load in loads[0:3]:
        load.wait()
    rel_1 = rel[...].astype(BF16)
    rest = rel[...] - rel_1.astype(F32)
    rel_2 = rest.astype(BF16)
    rel_3 = (rest - rel_2.astype(F32)).astype(BF16)
    for j in range(2):
        cols = slice(j * EC, (j + 1) * EC)
        h_t = head[:, cols].astype(F32)
        t_t = tail[:, cols].astype(F32)
        hot = hot_where(iota((REL, EC), 0) == ids[0:1, cols])
        r_t = (nn(rel_1, hot) + nn(rel_2, hot)) + nn(rel_3, hot)
        hre, him = h_t[:HALF], h_t[HALF:]
        rre, rim = r_t[:HALF], r_t[HALF:]
        q = jnp.concatenate([hre * rre - him * rim, hre * rim + him * rre], axis=0).astype(BF16)
        qt[2 * c + j, 0:D, :] = q
        sq[2 * c + j, 0:1, :] = jnp.sum(q.astype(F32) * t_t, axis=0, keepdims=True)
        sq[2 * c + j, 1:2, :] = wts[0:1, cols]
        sq[2 * c + j, 2:8, :] = jnp.zeros((6, EC), F32)
        hts[j] = h_t
        tts[j] = t_t
        rts[j] = r_t

    loads[3].wait()
    for i in range(8):
        nbt[i] = neg[:, i * 128 : (i + 1) * 128]

    pl.semaphore_wait(barrier, len(friends))
    tell(known.at[0], y_peers)

    for i in (x, 4 + y):
        rcopy(nbt.at[i], nbt.at[8 + i], send.at[GZ_S], recv.at[GZ_S], far)
    mine, theirs, real = pl.ds(2 * c, 2), pl.ds(4 + 2 * c, 2), pl.ds(0, D)
    rcopy(qt.at[mine, real], qt.at[mine, real], send.at[Q1_S], recv.at[Q1_S], partner)
    rcopy(sq.at[mine], sq.at[mine], send.at[SQ1_S], recv.at[SQ1_S], partner)
    rcopy(qt.at[mine, real], qt.at[theirs, real], send.at[Q2_S], recv.at[Q2_S], pair)
    rcopy(sq.at[mine], sq.at[theirs], send.at[SQ2_S], recv.at[SQ2_S], pair)

    ones = jnp.ones((SLOT, 128), BF16)
    tables = []
    for ref in (slots, drows):
        value = ref[...].astype(F32)
        high = jnp.floor(value * (1.0 / 32.0))
        tables.append((high.astype(BF16), (value - 32.0 * high).astype(BF16)))

    def columns(b, carry):
        owner_hot = hot_where(iota((256, 128), 1) == iota((256, 128), 0) // SLOT + b * NS)
        keep = iota((256, SLOT), 1) == iota((256, SLOT), 0) % SLOT
        for (high, low), out in zip(tables, (slot_col, dest_col)):
            h = jnp.where(keep, nt(owner_hot, high), 0.0).astype(BF16)
            l = jnp.where(keep, nt(owner_hot, low), 0.0).astype(BF16)
            out[b] = 32.0 * nn(h, ones) + nn(l, ones)
        return carry

    lax.fori_loop(0, NB, columns, 0)
    nb[:, 384:DP] = jnp.zeros((NEG_DEV, 128), BF16)

    def flip(b):
        for i in range(8):
            part = nbt[b * 8 + i]
            wide[0:D, i * 128 : (i + 1) * 128] = part
            nb[i * 128 : (i + 1) * 128, 0:D] = part.astype(F32).T.astype(BF16)

    def block(b, two):

        chunks = (2 * two, 2 * two + 1)
        scores = nn(nb[...], jnp.concatenate([qt[g] for g in chunks], axis=1))
        for u, g in enumerate(chunks):
            s = scores[:, u * EC : (u + 1) * EC]
            m = jnp.max(s, axis=0, keepdims=True)
            pb = jnp.exp(s - m).astype(BF16)
            prob[b, :, pl.ds(pl.multiple_of(g * EC, EC), EC)] = pb
            o = nn(wide[...], pb)
            l = o[D : D + 1]
            o = o[0:D]
            mb[b, g, 0:1, :] = m
            if b == 0:
                st[g, 0:1, :] = m
                st[g, 1:2, :] = l
                st[g, 2:8, :] = jnp.zeros((6, EC), F32)
                ot[g] = o
            else:
                m_old = st[g, 0:1, :]
                m_new = jnp.maximum(m_old, m)
                f_old = jnp.exp(m_old - m_new)
                f_new = jnp.exp(m - m_new)
                st[g, 0:1, :] = m_new
                st[g, 1:2, :] = st[g, 1:2, :] * f_old + l * f_new
                ot[g] = ot[g] * f_old + o * f_new

    def score_far(two):
        chunks = (2 * two, 2 * two + 1)
        scores = nn(nb[...], jnp.concatenate([qt[g] for g in chunks], axis=1))
        for u, g in enumerate(chunks):
            s = scores[:, u * EC : (u + 1) * EC]
            m = jnp.max(s, axis=0, keepdims=True)
            p = jnp.exp(s - m)
            prob[1, :, pl.ds(pl.multiple_of(g * EC, EC), EC)] = p.astype(BF16)
            l = jnp.sum(p, axis=0, keepdims=True)
            mb[1, g, 0:1, :] = m
            m_old = mb[0, g, 0:1, :]
            m_new = jnp.maximum(m_old, m)
            st[g, 0:1, :] = m_new
            st[g, 1:2, :] = st[g, 1:2, :] * jnp.exp(m_old - m_new) + l * jnp.exp(m - m_new)

    def sum_far(two):
        for g in (2 * two, 2 * two + 1):
            o = nn(wide[0:D, :], prob[1, :, pl.ds(pl.multiple_of(g * EC, EC), EC)])
            m_old, m = mb[0, g, 0:1, :], mb[1, g, 0:1, :]
            m_new = jnp.maximum(m_old, m)
            ot[g] = ot[g] * jnp.exp(m_old - m_new) + o * jnp.exp(m - m_new)

    flip(0)
    block(0, c)
    pl.semaphore_wait(known.at[0], 3)
    tell(known.at[1], (pair, far))
    wait_bytes(nbt.at[pl.ds(8, 2)], recv.at[GZ_S])
    for i in (1, 3, 2):
        xx, yy = lax.rem(x + i, 4), lax.rem(y + i, 4)
        rcopy(nbt.at[8 + x], nbt.at[8 + x], send.at[GX_S], recv.at[GX_S], (bucket, xx * 4 + y))
        rcopy(nbt.at[12 + y], nbt.at[12 + y], send.at[GY_S], recv.at[GY_S], (bucket, x * 4 + yy))
    wait_bytes(qt.at[mine, real], recv.at[Q1_S])
    wait_bytes(sq.at[mine], recv.at[SQ1_S])
    block(0, oc)
    pl.semaphore_wait(known.at[1], 2)
    tell(known.at[2], (pair, far))
    wait_bytes(qt.at[mine, real], recv.at[Q2_S])
    wait_bytes(sq.at[mine], recv.at[SQ2_S])
    rcopy(qt.at[theirs, real], qt.at[theirs, real], send.at[Q3_S], recv.at[Q3_S], partner)
    rcopy(sq.at[theirs], sq.at[theirs], send.at[SQ3_S], recv.at[SQ3_S], partner)
    block(0, 2 + c)
    wait_bytes(qt.at[mine, real], recv.at[Q3_S])
    wait_bytes(sq.at[mine], recv.at[SQ3_S])
    block(0, 2 + oc)
    wait_bytes(nbt.at[pl.ds(8, 3)], recv.at[GX_S])
    wait_bytes(nbt.at[pl.ds(8, 3)], recv.at[GY_S])
    flip(1)
    block(1, 2 + oc)
    pl.semaphore_wait(known.at[2], 2)
    tell(known.at[3], (partner,))
    rcopy(
        ot.at[pl.ds(4 + 2 * oc, 2)], ot_pair, send.at[O1_S], recv.at[O1_S], partner
    )
    block(1, 2 + c)
    own_half, pair_half = pl.ds(0, 4), pl.ds(4, 4)
    rcopy(st.at[pair_half], st_in.at[pair_half], send.at[ST1_S], recv.at[ST1_S], partner)

    def merge(g):
        m_a, m_b = st[g, 0:1, :], st_in[g, 0:1, :]
        m = jnp.maximum(m_a, m_b)
        f_a, f_b = jnp.exp(m_a - m), jnp.exp(m_b - m)
        sc[g, 0:1, :] = m
        sc[g, 1:2, :] = st[g, 1:2, :] * f_a + st_in[g, 1:2, :] * f_b
        sc[g, 2:8, :] = jnp.zeros((6, EC), F32)
        return f_a, f_b

    score_far(oc)
    score_far(c)
    rcopy(st.at[own_half], st_in.at[own_half], send.at[ST2_S], recv.at[ST2_S], partner)
    sum_far(oc)
    pl.semaphore_wait(known.at[3], 1)
    rcopy(ot.at[pl.ds(2 * oc, 2)], ot_own, send.at[O3_S], recv.at[O3_S], partner)
    wait_bytes(st_in.at[pair_half], recv.at[ST1_S])
    wait_bytes(ot_pair, recv.at[O1_S])
    for g in range(4, 8):
        merge(g)
    for j in range(2):
        f_a, f_b = merge(4 + 2 * c + j)
        o_sum[j] = (ot[4 + 2 * c + j] * f_a + ot_pair[j] * f_b).astype(BF16)
    rcopy(o_sum.at[0], o_far.at[0], send.at[O4_S], recv.at[O4_S], pair)
    rcopy(sc.at[pair_half], sc_in.at[own_half], send.at[SC1_S], recv.at[SC1_S], pair)
    wait_bytes(st_in.at[own_half], recv.at[ST2_S])
    for g in range(4):
        merge(g)
    rcopy(sc.at[own_half], sc_in.at[pair_half], send.at[SC2_S], recv.at[SC2_S], pair)
    rcopy(o_sum.at[1], o_far.at[1], send.at[O2_S], recv.at[O2_S], pair)
    sum_far(c)
    wait_bytes(sc_in.at[own_half], recv.at[SC1_S])
    wait_bytes(sc_in.at[pair_half], recv.at[SC2_S])
    for g in range(8):
        pos = sq[g, 0:1, :]
        m0, m1 = sc[g, 0:1, :], sc_in[g, 0:1, :]
        top = jnp.maximum(pos, jnp.maximum(m0, m1))
        total = (
            jnp.exp(pos - top)
            + sc[g, 1:2, :] * jnp.exp(m0 - top)
            + sc_in[g, 1:2, :] * jnp.exp(m1 - top)
        )
        lt[g, 0:1, :] = top + jnp.log(total)

    def neg_block(b):
        for g in range(8):
            scale = sq[g, 1:2, :] * jnp.exp(mb[b, g, 0:1, :] - lt[g, 0:1, :])
            qs[:, g * EC : (g + 1) * EC] = (qt[g].astype(F32) * scale).astype(BF16)

        def rows_of(h, carry):
            rr = pl.ds(pl.multiple_of(h * 512, 512), 512)
            acc = nt(prob[b, rr, :], qs[...])
            for u in range(2):
                part = acc[u * 256 : (u + 1) * 256]
                gx[b, 2 * h + u] = part[:, 0:128].astype(BF16)
                for yy in range(4):
                    gy[b, yy, 2 * h + u] = part[yy * 64 : (yy + 1) * 64, 128:256].astype(BF16)
            gz[b, :, rr] = acc[:, 256:512].T[0 : D - 256].astype(BF16)
            return carry

        lax.fori_loop(0, 2, rows_of, 0)
        for i in (1, 3, 2):
            xx, yy = lax.rem(x + i, 4), lax.rem(y + i, 4)
            rcopy(gx.at[b, xx], rx1.at[x, b], send.at[X1_S], recv.at[X1_S], (bucket, xx * 4 + y))
            rcopy(gy.at[b, yy], ry1.at[y, b], send.at[Y1_S], recv.at[Y1_S], (bucket, x * 4 + yy))

    neg_block(1)
    rcopy(gz.at[1], rz1, send.at[Z1_S], recv.at[Z1_S], far)
    wait_bytes(ot_own, recv.at[O3_S])
    wait_bytes(o_far.at[0], recv.at[O4_S])
    wait_bytes(o_far.at[1], recv.at[O2_S])
    ends[D:DP, :] = jnp.zeros((DP - D, 2 * E_DEV), BF16)
    for j in range(2):
        cols = slice(j * EC, (j + 1) * EC)
        tail_cols = slice(E_DEV + j * EC, E_DEV + (j + 1) * EC)
        g = 2 * c + j
        pos, w, ltot = sq[g, 0:1, :], sq[g, 1:2, :], lt[g, 0:1, :]
        pos_coef = w * (jnp.exp(pos - ltot) - 1.0)
        own = w * jnp.exp(st[g, 0:1, :] - ltot)
        other = w * jnp.exp(st_in[g, 0:1, :] - ltot)
        away = w * jnp.exp(sc_in[g, 0:1, :] - ltot)
        grad = pos_coef * tts[j] + ot[g] * own + ot_own[j] * other + o_far[j].astype(F32) * away
        gre, gim = grad[:HALF], grad[HALF:]
        rre, rim = rts[j, :HALF, :], rts[j, HALF:, :]
        hre, him = hts[j, :HALF, :], hts[j, HALF:, :]
        head_grad = jnp.concatenate(
            [gre * rre + gim * rim, gim * rre - gre * rim], axis=0
        ).astype(BF16)
        tail_grad = (pos_coef * qt[g, 0:D, :].astype(F32)).astype(BF16)
        for part, where_to in ((head_grad, cols), (tail_grad, tail_cols)):
            ends[0:D, where_to] = part
            ends[416:432, where_to] = part[384:D]
        term = jnp.concatenate([gre * hre + gim * him, gim * hre - gre * him], axis=0)
        hi = term.astype(BF16)
        rt_hi[:, cols] = hi
        rt_lo[:, cols] = (term - hi.astype(F32)).astype(BF16)

    src_chip = z * NS + shard

    def pack(k, first):
        zz = lax.rem(z + k, NZ)
        chips = pl.ds(pl.multiple_of(zz * NS, NS), NS)
        sel = []
        for d in range(2):
            sc_b = slot_col[zz * 2 + d]
            sel.append(jnp.concatenate(
                [hot_where(sc_b == (iota((256, 128), 1) + 128 * t).astype(F32)) for t in range(8)],
                axis=1,
            ))
        rows = nt(jnp.concatenate(sel, axis=0), ends[...])
        lane = iota((256, 128), 1)
        last = []
        for d in range(2):
            part = rows[d * 256 : (d + 1) * 256]
            for t in range(3):
                first_row = (d * 3 + t) * SLOT
                tile = part[:, t * 128 : (t + 1) * 128].astype(BF16).reshape(NS, SLOT, 128)
                packed[chips, first_row : first_row + SLOT, :] = tile
            dc = dest_col[zz * 2 + d]
            high = jnp.floor(dc * (1.0 / 32.0))
            code = jnp.where(lane == 32 * d + 16, high, jnp.where(lane == 32 * d + 17, dc - 32.0 * high, 0.0))
            last.append(part[:, 384:512] + code)
        tile = jnp.where(lane < 32, last[0], last[1]).astype(BF16).reshape(NS, SLOT, 128)
        packed[chips, 96:112, :] = tile
        for j in range(NS):
            ss = lax.rem(shard + j, NS)
            src = packed.at[zz * NS + ss]
            if first and j == 0:
                pltpu.make_async_copy(src, arrived.at[src_chip], ent_recv.at[k]).start()
            else:
                rcopy(src, arrived.at[src_chip], send.at[ENT_S], ent_recv.at[k], (zz * 2 + c, ss))

    def rel_chunk(r, carry):
        hot = hot_where(iota((128, E_DEV), 0) + r * 128 == ids[...])
        rp[pl.ds(pl.multiple_of(r * 128, 128), 128), :] = nt(hot, rt_hi[...]) + nt(hot, rt_lo[...])
        return carry

    lax.fori_loop(0, 4, rel_chunk, 0)
    rcopy(
        rp.at[pl.ds(pl.multiple_of(oc * 256, 256), 256)], rp_in, send.at[RC_S], recv.at[RC_S], partner
    )

    def pack_other(k, carry):
        pack(k, False)
        return carry

    pack(0, True)
    lax.fori_loop(1, 2, pack_other, 0)

    wait_bytes(rp_in, recv.at[RC_S])
    r1b[...] = (rp[pl.ds(pl.multiple_of(c * 256, 256), 256), :] + rp_in[...]).astype(BF16)
    for j in range(1, NS):
        ss = lax.rem(shard + j, NS)
        rows = r1b.at[pl.ds(pl.multiple_of(ss * 16, 16), 16)]
        rcopy(rows, r2in.at[shard], send.at[R2_S], recv.at[R2_S], (bucket, ss))
    r2in[shard] = r1b[pl.ds(pl.multiple_of(shard * 16, 16), 16), :]
    neg_block(0)

    wait_bytes(rz1, recv.at[Z1_S])
    for r in range(4):
        rr = slice(r * 256, (r + 1) * 256)
        azx[r] = (gz[0, :, rr].astype(F32) + rz1[:, rr].astype(F32)).astype(BF16)
    for i in (1, 3, 2):
        xx = lax.rem(x + i, 4)
        rcopy(azx.at[xx], rzx.at[x], send.at[ZX_S], recv.at[ZX_S], (bucket, xx * 4 + y))

    wait_bytes(r2in.at[pl.ds(0, NS - 1)], recv.at[R2_S])
    r2 = r2in[0].astype(F32)
    for i in range(1, NS):
        r2 = r2 + r2in[i].astype(F32)
    r2all[z] = r2
    for k in (1, 3, 2):
        zz = lax.rem(z + k, NZ)
        rcopy(r2all.at[z], r2all.at[z], send.at[R3_S], recv.at[R3_S], (zz * 2 + c, shard))

    lax.fori_loop(2, NZ, pack_other, 0)


    wait_bytes(r2all.at[pl.ds(0, 3)], recv.at[R3_S])
    rel_row = pl.ds(pl.multiple_of(c * 256 + shard * 16, 16), 16)
    rfin[rel_row, :] = (((r2all[0] + r2all[1]) + r2all[2]) + r2all[3]).astype(BF16)
    for j in range(1, NS):
        ss = lax.rem(shard + j, NS)
        rcopy(rfin.at[rel_row], rfin.at[rel_row], send.at[R4_S], recv.at[R4_S], (bucket, ss))

    wait_bytes(rx1.at[pl.ds(0, 3)], recv.at[X1_S])
    for b in range(2):
        total = gx[b, x].astype(F32)
        for i in range(1, 4):
            total = total + rx1[lax.rem(x + i, 4), b].astype(F32)
        ax[b] = total.astype(BF16)
    for i in range(4):
        yy = lax.rem(y + i, 4)
        rows = pl.ds(pl.multiple_of(yy * NEG_OWN, NEG_OWN), NEG_OWN)
        if i:
            rcopy(ax.at[0, rows], rx2.at[y], send.at[X2_S], recv.at[X2_S], (bucket, x * 4 + yy))
        else:
            rx2[y] = ax[0, rows, :]
        rcopy(
            ax.at[1, rows], rx2.at[4 + y], send.at[X2_S], recv.at[X2_S], (z_far * 2 + c, x * 4 + yy)
        )
    wait_bytes(ry1.at[pl.ds(0, 3)], recv.at[Y1_S])
    for b in range(2):
        total = gy[b, y].astype(F32)
        for i in range(1, 4):
            total = total + ry1[lax.rem(y + i, 4), b].astype(F32)
        ay[b] = total.astype(BF16)
    for i in range(4):
        xx = lax.rem(x + i, 4)
        if i:
            rcopy(ay.at[0, xx], ry2.at[x], send.at[Y2_S], recv.at[Y2_S], (bucket, xx * 4 + y))
        else:
            ry2[x] = ay[0, x]
        rcopy(
            ay.at[1, xx], ry2.at[4 + x], send.at[Y2_S], recv.at[Y2_S], (z_far * 2 + c, xx * 4 + y)
        )
    wait_bytes(rzx.at[pl.ds(0, 3)], recv.at[ZX_S])
    total = azx[x].astype(F32)
    for i in range(1, 4):
        total = total + rzx[lax.rem(x + i, 4)].astype(F32)
    wide_sum = jnp.concatenate([total, jnp.zeros((256 - (D - 256), 256), F32)], axis=0)
    az[...] = wide_sum.T.astype(BF16)
    for i in range(4):
        yy = lax.rem(y + i, 4)
        rows = pl.ds(pl.multiple_of(yy * NEG_OWN, NEG_OWN), NEG_OWN)
        if i:
            rcopy(az.at[rows], rz2.at[y], send.at[Z2_S], recv.at[Z2_S], (bucket, x * 4 + yy))
        else:
            rz2[y] = az[rows, :]

    def give(src, dst, sem):
        pltpu.make_async_copy(src, dst, sem).start()

    other_rows, last_rows = pl.ds(pl.multiple_of(oc * 48, 16), 48), pl.ds(96, SLOT)
    for k in range(NZ):
        chips = pl.ds(pl.multiple_of(lax.rem(z + NZ - k, NZ) * NS, NS), NS)
        wait_bytes(arrived.at[chips], ent_recv.at[k])
        rcopy(arrived.at[chips, other_rows], far_main.at[chips], send.at[PX_S], recv.at[PX_S], partner)
        rcopy(arrived.at[chips, last_rows], far_last.at[chips], send.at[PY_S], recv.at[PY_S], partner)
    give(arrived.at[:, pl.ds(pl.multiple_of(c * 48, 16), 48)], main_out, out_sem.at[0])
    give(arrived.at[:, last_rows], last_out, out_sem.at[5])
    wait_bytes(rfin.at[pl.ds(0, 240)], recv.at[R4_S])
    half_rel = rfin.at[pl.ds(pl.multiple_of(c * 256, 256), 256)]
    rcopy(half_rel, half_rel, send.at[R5_S], recv.at[R5_S], partner)
    wait_bytes(rx2.at[pl.ds(0, 7)], recv.at[X2_S])
    give(rx2, rx2_out, out_sem.at[1])
    wait_bytes(ry2.at[pl.ds(0, 7)], recv.at[Y2_S])
    give(ry2, ry2_out, out_sem.at[2])
    wait_bytes(rz2.at[pl.ds(0, 3)], recv.at[Z2_S])
    give(rz2, rz2_out, out_sem.at[3])
    wait_bytes(half_rel, recv.at[R5_S])
    give(rfin, rel_sum_out, out_sem.at[4])
    wait_bytes(far_main, recv.at[PX_S])
    give(far_main, far_main_out, out_sem.at[6])
    wait_bytes(far_last, recv.at[PY_S])
    give(far_last, far_last_out, out_sem.at[7])

    wait_bytes(nbt.at[pl.ds(0, 2)], send.at[GZ_S])
    wait_bytes(nbt.at[pl.ds(0, 3)], send.at[GX_S])
    wait_bytes(nbt.at[pl.ds(0, 3)], send.at[GY_S])
    for number in (Q1_S, Q2_S, Q3_S):
        wait_bytes(qt.at[mine, real], send.at[number])
    for number in (SQ1_S, SQ2_S, SQ3_S):
        wait_bytes(sq.at[mine], send.at[number])
    for number in (ST1_S, ST2_S, SC1_S, SC2_S):
        wait_bytes(st.at[own_half], send.at[number])
    wait_bytes(ot_pair, send.at[O1_S])
    wait_bytes(o_far.at[0], send.at[O4_S])
    wait_bytes(o_far.at[1], send.at[O2_S])
    wait_bytes(ot_own, send.at[O3_S])
    wait_bytes(arrived.at[pl.ds(0, 63)], send.at[ENT_S])
    wait_bytes(far_main, send.at[PX_S])
    wait_bytes(far_last, send.at[PY_S])
    wait_bytes(rp_in, send.at[RC_S])
    wait_bytes(r2in.at[pl.ds(0, NS - 1)], send.at[R2_S])
    wait_bytes(r2all.at[pl.ds(0, 3)], send.at[R3_S])
    wait_bytes(rfin.at[pl.ds(0, 240)], send.at[R4_S])
    wait_bytes(half_rel, send.at[R5_S])
    wait_bytes(rz1, send.at[Z1_S])
    wait_bytes(rx1.at[pl.ds(0, 3)], send.at[X1_S])
    wait_bytes(ry1.at[pl.ds(0, 3)], send.at[Y1_S])
    wait_bytes(rx2.at[pl.ds(0, 7)], send.at[X2_S])
    wait_bytes(ry2.at[pl.ds(0, 7)], send.at[Y2_S])
    wait_bytes(rz2.at[pl.ds(0, 3)], send.at[Z2_S])
    wait_bytes(rzx.at[pl.ds(0, 3)], send.at[ZX_S])
    for number in (0, 6):
        wait_bytes(far_main, out_sem.at[number])
    for number in (5, 7):
        wait_bytes(far_last, out_sem.at[number])
    wait_bytes(rx2, out_sem.at[1])
    wait_bytes(ry2, out_sem.at[2])
    wait_bytes(rz2, out_sem.at[3])
    wait_bytes(rfin, out_sem.at[4])


def finish(
    main_in, last_in, far_main_in, far_last_in, rx2_in, ry2_in, rz2_in, rel_in,
    ent_out, neg_out, rel_out,
    main, last, far_main, far_last, rx2, ry2, rz2, rel_sum, ent, neg_sum, rel_t, in_sem, out_sem,
):
    loads = [
        pltpu.make_async_copy(src, dst, in_sem.at[i])
        for i, (src, dst) in enumerate((
            (rel_in, rel_sum), (last_in, last), (far_last_in, far_last), (main_in, main),
            (far_main_in, far_main), (rx2_in, rx2), (ry2_in, ry2), (rz2_in, rz2),
        ))
    ]
    for load in loads:
        load.start()
    loads[0].wait()
    for r in range(4):
        rows = rel_sum[r * 128 : (r + 1) * 128, :].astype(F32)
        wide = jnp.concatenate([rows, jnp.zeros((128, DP - D), F32)], axis=1)
        rel_t[:, r * 128 : (r + 1) * 128] = wide.T[0:D]
    stores = [pltpu.make_async_copy(rel_t, rel_out, out_sem.at[0])]
    stores[0].start()

    c = lax.axis_index("bucket") % 2
    lane = iota((8, 128), 1) - 32 * c
    unit = jnp.where(lane == 16, 32.0, jnp.where(lane == 17, 1.0, 0.0)).astype(BF16)
    for load in loads[1:5]:
        load.wait()
    slots, row_ids = [], []
    for tiles, tail in ((main, last), (far_main, far_last)):
        tail_rows = tail[...].reshape(1024, 128)
        columns = [tiles[:, t * SLOT : (t + 1) * SLOT, :].reshape(1024, 128) for t in range(3)]
        slots.append(jnp.concatenate(columns + [tail_rows], axis=1))
        row_ids.append(nt(unit, tail_rows)[0:1, :])
    for r in range(2):
        numbers = (iota((512, 1024), 0) + r * 512).astype(F32)
        got = nn(hot_where(numbers == row_ids[0]), slots[0]) + nn(hot_where(numbers == row_ids[1]), slots[1])
        turned = got.T
        ent[r, 0:384] = turned[0:384]
        ent[r, 384:D] = jnp.where(c == 0, turned[384:400], turned[416:432])
        store = pltpu.make_async_copy(ent.at[r], ent_out.at[:, pl.ds(r * 512, 512)], out_sem.at[1 + r])
        store.start()
        stores.append(store)

    def sum_all(ref):
        total = ref[0].astype(F32)
        for i in range(1, ref.shape[0]):
            total = total + ref[i].astype(F32)
        return total

    for load in loads[5:]:
        load.wait()
    neg_sum[:, 0:128] = sum_all(rx2)
    neg_sum[:, 128:256] = sum_all(ry2)
    neg_sum[:, 256:D] = sum_all(rz2)[:, 0 : D - 256]
    stores.append(pltpu.make_async_copy(neg_sum, neg_out, out_sem.at[3]))
    stores[-1].start()
    for store in stores:
        store.wait()


SCRATCH = [
    ((D, E_DEV), BF16),
    ((D, E_DEV), BF16),
    ((D, REL), F32),
    ((D, NEG_DEV), BF16),
    ((16, D, 128), BF16),
    ((D + 16, NEG_DEV), BF16),
    ((NEG_DEV, DP), BF16),
    ((2, NEG_DEV, 8 * EC), BF16),
    ((8, DP, EC), BF16),
    ((8, 8, EC), F32),
    ((2, D, EC), F32),
    ((2, D, EC), F32),
    ((2, D, EC), F32),
    ((2, 8, 8, EC), F32),
    ((8, 8, EC), F32),
    ((8, 8, EC), F32),
    ((8, 8, EC), F32),
    ((8, 8, EC), F32),
    ((8, D, EC), F32),
    ((2, D, EC), F32),
    ((2, D, EC), F32),
    ((2, D, EC), BF16),
    ((2, D, EC), BF16),
    ((8, 8, EC), F32),
    ((DP, 8 * EC), BF16),
    ((DP, 2 * E_DEV), BF16),
    ((D, E_DEV), BF16),
    ((D, E_DEV), BF16),
    ((NZ * NS, 112, 128), BF16),
    ((NZ * NS, 112, 128), BF16),
    ((NZ * NS, 48, 128), BF16),
    ((NZ * NS, SLOT, 128), BF16),
    ((NB, 256, 128), F32),
    ((NB, 256, 128), F32),
    ((2, D - 256, NEG_DEV), BF16),
    ((2, 4, 256, 128), BF16),
    ((2, 4, 4, NEG_OWN, 128), BF16),
    ((D - 256, NEG_DEV), BF16),
    ((4, 2, 256, 128), BF16),
    ((4, 2, 4, NEG_OWN, 128), BF16),
    ((4, D - 256, 256), BF16),
    ((4, D - 256, 256), BF16),
    ((256, 256), BF16),
    ((2, 256, 128), BF16),
    ((2, 4, NEG_OWN, 128), BF16),
    ((4, NEG_OWN, 256), BF16),
    ((8, NEG_OWN, 128), BF16),
    ((8, NEG_OWN, 128), BF16),
    ((REL, D), F32),
    ((REL // 2, D), F32),
    ((REL // 2, D), BF16),
    ((NS, 16, D), BF16),
    ((NZ, 16, D), F32),
    ((REL, D), BF16),
]


def per_device(
    head_rows, tail_rows, rel_ids, relations, edge_weights, neg_rows, send_slots, dest_rows
):
    vmem = pl.BlockSpec(memory_space=pltpu.VMEM)
    anywhere = pl.BlockSpec(memory_space=pl.ANY)
    results = pl.pallas_call(
        kernel,
        out_shape=(
            jax.ShapeDtypeStruct((NZ * NS, 48, 128), BF16),
            jax.ShapeDtypeStruct((NZ * NS, SLOT, 128), BF16),
            jax.ShapeDtypeStruct((NZ * NS, 48, 128), BF16),
            jax.ShapeDtypeStruct((NZ * NS, SLOT, 128), BF16),
            jax.ShapeDtypeStruct((8, NEG_OWN, 128), BF16),
            jax.ShapeDtypeStruct((8, NEG_OWN, 128), BF16),
            jax.ShapeDtypeStruct((4, NEG_OWN, 256), BF16),
            jax.ShapeDtypeStruct((REL, D), BF16),
        ),
        in_specs=[anywhere, anywhere, vmem, anywhere, vmem, anywhere, vmem, vmem],
        out_specs=(anywhere,) * 8,
        scratch_shapes=[pltpu.VMEM(shape, dtype) for shape, dtype in SCRATCH]
        + [
            pltpu.SemaphoreType.DMA((32,)),
            pltpu.SemaphoreType.DMA((32,)),
            pltpu.SemaphoreType.REGULAR((4,)),
            pltpu.SemaphoreType.DMA((8,)),
            pltpu.SemaphoreType.DMA((NZ,)),
            pltpu.SemaphoreType.DMA((4,)),
        ],
        compiler_params=pltpu.CompilerParams(
            collective_id=0, has_side_effects=True, vmem_limit_bytes=60 * 1024 * 1024
        ),
        cost_estimate=pl.CostEstimate(
            flops=2 * 3 * 1024 * 4096 * 400, bytes_accessed=8 * 1024 * 1024, transcendentals=1024 * 4096
        ),
        name="complex_backward",
    )(
        head_rows.T,
        tail_rows.T,
        rel_ids.reshape(1, E_DEV),
        relations.T,
        edge_weights.reshape(1, E_DEV),
        neg_rows.T,
        send_slots.T,
        dest_rows.T,
    )
    ent_t, neg_grad, rel_t = pl.pallas_call(
        finish,
        out_shape=(
            jax.ShapeDtypeStruct((D, ENT_DEV), F32),
            jax.ShapeDtypeStruct((NEG_OWN, D), F32),
            jax.ShapeDtypeStruct((D, REL), F32),
        ),
        in_specs=[anywhere] * 8,
        out_specs=(anywhere,) * 3,
        scratch_shapes=[
            pltpu.VMEM((NZ * NS, 48, 128), BF16),
            pltpu.VMEM((NZ * NS, SLOT, 128), BF16),
            pltpu.VMEM((NZ * NS, 48, 128), BF16),
            pltpu.VMEM((NZ * NS, SLOT, 128), BF16),
            pltpu.VMEM((8, NEG_OWN, 128), BF16),
            pltpu.VMEM((8, NEG_OWN, 128), BF16),
            pltpu.VMEM((4, NEG_OWN, 256), BF16),
            pltpu.VMEM((REL, D), BF16),
            pltpu.VMEM((2, D, 512), F32),
            pltpu.VMEM((NEG_OWN, D), F32),
            pltpu.VMEM((D, REL), F32),
            pltpu.SemaphoreType.DMA((8,)),
            pltpu.SemaphoreType.DMA((4,)),
        ],
        compiler_params=pltpu.CompilerParams(vmem_limit_bytes=60 * 1024 * 1024),
        cost_estimate=pl.CostEstimate(
            flops=2 * 1024 * 2048 * 512, bytes_accessed=6 * 1024 * 1024, transcendentals=0
        ),
        name="make_outputs",
    )(*results)
    return ent_t.T, neg_grad, rel_t.T


def solution(mesh):
    return jax.shard_map(
        per_device,
        mesh=mesh,
        in_specs=(
            P(("bucket", "shard"), None),
            P(("bucket", "shard"), None),
            P(("bucket", "shard")),
            P(),
            P(("bucket", "shard")),
            P("bucket", None),
            P(("bucket", "shard"), None),
            P(("bucket", "shard"), None),
        ),
        out_specs=(P(("bucket", "shard"), None), P(("bucket", "shard"), None), P()),
        check_vma=False,
    )
```

```python
import functools

import jax
import jax.numpy as jnp
from jax import lax
from jax.experimental import pallas as pl
from jax.experimental.pallas import tpu as pltpu
from jax.sharding import PartitionSpec as P

D = 400
HALF = 200
DP = 512
E_DEV = 512
ENT_DEV = 1024
REL = 512
NEG_DEV = 1024
SLOT = 16
NB = 8
NS = 16
NZ = 4
EC = 256
NEG_OWN = 64

MESH = pl.DeviceIdType.MESH
F32 = jnp.float32
BF16 = jnp.bfloat16

(Q1_S, SQ1_S, Q2_S, SQ2_S, Q3_S, SQ3_S, ST1_S, O1_S, SC1_S, O2_S, ST2_S, O3_S, SC2_S,
 RC_S, R2_S, R3_S, R4_S, R5_S, ENT_S, Z1_S, X1_S, Y1_S, Z2_S, X2_S, Y2_S, GZ_S, GX_S, GY_S, O4_S,
 PX_S, PY_S, ZX_S) = range(32)


def nt(a, b):
    return lax.dot_general(a, b, (((1,), (1,)), ((), ())), preferred_element_type=F32)


def nn(a, b):
    return jnp.dot(a, b, preferred_element_type=F32)


def iota(shape, dim):
    return lax.broadcasted_iota(jnp.int32, shape, dim)


def hot_where(mask):
    return mask.astype(F32).astype(BF16)


def wait_bytes(ref, sem):
    pltpu.make_async_copy(ref, ref, sem).wait()


def kernel(
    head_in, tail_in, ids, rel_in, wts, neg_in, slots, drows,
    main_out, last_out, far_main_out, far_last_out, rx2_out, ry2_out, rz2_out, rel_sum_out,
    head, tail, rel, neg, nbt, wide, nb, prob, qt, sq, hts, tts, rts, mb, st, st_in, sc, sc_in,
    ot, ot_pair, ot_own, o_sum, o_far, lt, qs, ends, rt_hi, rt_lo,
    packed, arrived, far_main, far_last, slot_col, dest_col,
    gz, gx, gy, rz1, rx1, ry1, azx, rzx, az, ax, ay, rz2, rx2, ry2,
    rp, rp_in, r1b, r2in, r2all, rfin,
    send, recv, known, out_sem, ent_recv, in_sem,
):
    bucket, shard = lax.axis_index("bucket"), lax.axis_index("shard")
    z, c = bucket // 2, bucket % 2
    x, y = shard // 4, shard % 4
    oc = 1 - c
    partner = (z * 2 + oc, shard)
    pair = ((z + 1 - 2 * (z % 2)) * 2 + c, shard)
    z_far = 3 - z
    far = (z_far * 2 + c, shard)

    def rcopy(src, dst, s_sem, r_sem, device):
        pltpu.make_async_remote_copy(
            src_ref=src, dst_ref=dst, send_sem=s_sem, recv_sem=r_sem,
            device_id=device, device_id_type=MESH,
        ).start()

    barrier = pltpu.get_barrier_semaphore()

    x_peers = [(bucket, lax.rem(x + i, 4) * 4 + y) for i in (1, 2, 3)]
    y_peers = [(bucket, x * 4 + lax.rem(y + i, 4)) for i in (1, 2, 3)]
    friends = [partner, pair, far] + x_peers + y_peers

    def tell(sem, devices):
        for device in devices:
            pl.semaphore_signal(sem, inc=1, device_id=device, device_id_type=MESH)

    loads = [
        pltpu.make_async_copy(src, dst, in_sem.at[i])
        for i, (src, dst) in enumerate(((rel_in, rel), (head_in, head), (tail_in, tail), (neg_in, neg)))
    ]
    for load in loads:
        load.start()
    tell(barrier, friends)

    for g in range(8):
        qt[g, D:DP, :] = jnp.zeros((DP - D, EC), BF16)
    wide[D:, :] = jnp.ones((16, NEG_DEV), BF16)

    for load in loads[0:3]:
        load.wait()
    rel_1 = rel[...].astype(BF16)
    rest = rel[...] - rel_1.astype(F32)
    rel_2 = rest.astype(BF16)
    rel_3 = (rest - rel_2.astype(F32)).astype(BF16)
    for j in range(2):
        cols = slice(j * EC, (j + 1) * EC)
        h_t = head[:, cols].astype(F32)
        t_t = tail[:, cols].astype(F32)
        hot = hot_where(iota((REL, EC), 0) == ids[0:1, cols])
        r_t = (nn(rel_1, hot) + nn(rel_2, hot)) + nn(rel_3, hot)
        hre, him = h_t[:HALF], h_t[HALF:]
        rre, rim = r_t[:HALF], r_t[HALF:]
        q = jnp.concatenate([hre * rre - him * rim, hre * rim + him * rre], axis=0).astype(BF16)
        qt[2 * c + j, 0:D, :] = q
        sq[2 * c + j, 0:1, :] = jnp.sum(q.astype(F32) * t_t, axis=0, keepdims=True)
        sq[2 * c + j, 1:2, :] = wts[0:1, cols]
        sq[2 * c + j, 2:8, :] = jnp.zeros((6, EC), F32)
        hts[j] = h_t
        tts[j] = t_t
        rts[j] = r_t

    loads[3].wait()
    for i in range(8):
        nbt[i] = neg[:, i * 128 : (i + 1) * 128]

    pl.semaphore_wait(barrier, len(friends))
    tell(known.at[0], y_peers)

    for i in (x, 4 + y):
        rcopy(nbt.at[i], nbt.at[8 + i], send.at[GZ_S], recv.at[GZ_S], far)
    mine, theirs, real = pl.ds(2 * c, 2), pl.ds(4 + 2 * c, 2), pl.ds(0, D)
    rcopy(qt.at[mine, real], qt.at[mine, real], send.at[Q1_S], recv.at[Q1_S], partner)
    rcopy(sq.at[mine], sq.at[mine], send.at[SQ1_S], recv.at[SQ1_S], partner)
    rcopy(qt.at[mine, real], qt.at[theirs, real], send.at[Q2_S], recv.at[Q2_S], pair)
    rcopy(sq.at[mine], sq.at[theirs], send.at[SQ2_S], recv.at[SQ2_S], pair)

    ones = jnp.ones((SLOT, 128), BF16)
    tables = []
    for ref in (slots, drows):
        value = ref[...].astype(F32)
        high = jnp.floor(value * (1.0 / 32.0))
        tables.append((high.astype(BF16), (value - 32.0 * high).astype(BF16)))

    def columns(b, carry):
        owner_hot = hot_where(iota((256, 128), 1) == iota((256, 128), 0) // SLOT + b * NS)
        keep = iota((256, SLOT), 1) == iota((256, SLOT), 0) % SLOT
        for (high, low), out in zip(tables, (slot_col, dest_col)):
            h = jnp.where(keep, nt(owner_hot, high), 0.0).astype(BF16)
            l = jnp.where(keep, nt(owner_hot, low), 0.0).astype(BF16)
            out[b] = 32.0 * nn(h, ones) + nn(l, ones)
        return carry

    lax.fori_loop(0, NB, columns, 0)
    nb[:, 384:DP] = jnp.zeros((NEG_DEV, 128), BF16)

    def flip(b):
        for i in range(8):
            part = nbt[b * 8 + i]
            wide[0:D, i * 128 : (i + 1) * 128] = part
            nb[i * 128 : (i + 1) * 128, 0:D] = part.astype(F32).T.astype(BF16)

    def block(b, two):

        chunks = (2 * two, 2 * two + 1)
        scores = nn(nb[...], jnp.concatenate([qt[g] for g in chunks], axis=1))
        for u, g in enumerate(chunks):
            s = scores[:, u * EC : (u + 1) * EC]
            m = jnp.max(s, axis=0, keepdims=True)
            pb = jnp.exp(s - m).astype(BF16)
            prob[b, :, pl.ds(pl.multiple_of(g * EC, EC), EC)] = pb
            o = nn(wide[...], pb)
            l = o[D : D + 1]
            o = o[0:D]
            mb[b, g, 0:1, :] = m
            if b == 0:
                st[g, 0:1, :] = m
                st[g, 1:2, :] = l
                st[g, 2:8, :] = jnp.zeros((6, EC), F32)
                ot[g] = o
            else:
                m_old = st[g, 0:1, :]
                m_new = jnp.maximum(m_old, m)
                f_old = jnp.exp(m_old - m_new)
                f_new = jnp.exp(m - m_new)
                st[g, 0:1, :] = m_new
                st[g, 1:2, :] = st[g, 1:2, :] * f_old + l * f_new
                ot[g] = ot[g] * f_old + o * f_new

    def score_far(two):
        chunks = (2 * two, 2 * two + 1)
        scores = nn(nb[...], jnp.concatenate([qt[g] for g in chunks], axis=1))
        for u, g in enumerate(chunks):
            s = scores[:, u * EC : (u + 1) * EC]
            m = jnp.max(s, axis=0, keepdims=True)
            p = jnp.exp(s - m)
            prob[1, :, pl.ds(pl.multiple_of(g * EC, EC), EC)] = p.astype(BF16)
            l = jnp.sum(p, axis=0, keepdims=True)
            mb[1, g, 0:1, :] = m
            m_old = mb[0, g, 0:1, :]
            m_new = jnp.maximum(m_old, m)
            st[g, 0:1, :] = m_new
            st[g, 1:2, :] = st[g, 1:2, :] * jnp.exp(m_old - m_new) + l * jnp.exp(m - m_new)

    def sum_far(two):
        for g in (2 * two, 2 * two + 1):
            o = nn(wide[0:D, :], prob[1, :, pl.ds(pl.multiple_of(g * EC, EC), EC)])
            m_old, m = mb[0, g, 0:1, :], mb[1, g, 0:1, :]
            m_new = jnp.maximum(m_old, m)
            ot[g] = ot[g] * jnp.exp(m_old - m_new) + o * jnp.exp(m - m_new)

    flip(0)
    block(0, c)
    pl.semaphore_wait(known.at[0], 3)
    tell(known.at[1], (pair, far))
    wait_bytes(nbt.at[pl.ds(8, 2)], recv.at[GZ_S])
    for i in (1, 3, 2):
        xx, yy = lax.rem(x + i, 4), lax.rem(y + i, 4)
        rcopy(nbt.at[8 + x], nbt.at[8 + x], send.at[GX_S], recv.at[GX_S], (bucket, xx * 4 + y))
        rcopy(nbt.at[12 + y], nbt.at[12 + y], send.at[GY_S], recv.at[GY_S], (bucket, x * 4 + yy))
    wait_bytes(qt.at[mine, real], recv.at[Q1_S])
    wait_bytes(sq.at[mine], recv.at[SQ1_S])
    block(0, oc)
    pl.semaphore_wait(known.at[1], 2)
    tell(known.at[2], (pair, far))
    wait_bytes(qt.at[mine, real], recv.at[Q2_S])
    wait_bytes(sq.at[mine], recv.at[SQ2_S])
    rcopy(qt.at[theirs, real], qt.at[theirs, real], send.at[Q3_S], recv.at[Q3_S], partner)
    rcopy(sq.at[theirs], sq.at[theirs], send.at[SQ3_S], recv.at[SQ3_S], partner)
    block(0, 2 + c)
    wait_bytes(qt.at[mine, real], recv.at[Q3_S])
    wait_bytes(sq.at[mine], recv.at[SQ3_S])
    block(0, 2 + oc)
    wait_bytes(nbt.at[pl.ds(8, 3)], recv.at[GX_S])
    wait_bytes(nbt.at[pl.ds(8, 3)], recv.at[GY_S])
    flip(1)
    block(1, 2 + oc)
    pl.semaphore_wait(known.at[2], 2)
    tell(known.at[3], (partner,))
    rcopy(
        ot.at[pl.ds(4 + 2 * oc, 2)], ot_pair, send.at[O1_S], recv.at[O1_S], partner
    )
    block(1, 2 + c)
    own_half, pair_half = pl.ds(0, 4), pl.ds(4, 4)
    rcopy(st.at[pair_half], st_in.at[pair_half], send.at[ST1_S], recv.at[ST1_S], partner)

    def merge(g):
        m_a, m_b = st[g, 0:1, :], st_in[g, 0:1, :]
        m = jnp.maximum(m_a, m_b)
        f_a, f_b = jnp.exp(m_a - m), jnp.exp(m_b - m)
        sc[g, 0:1, :] = m
        sc[g, 1:2, :] = st[g, 1:2, :] * f_a + st_in[g, 1:2, :] * f_b
        sc[g, 2:8, :] = jnp.zeros((6, EC), F32)
        return f_a, f_b

    score_far(oc)
    score_far(c)
    rcopy(st.at[own_half], st_in.at[own_half], send.at[ST2_S], recv.at[ST2_S], partner)
    sum_far(oc)
    pl.semaphore_wait(known.at[3], 1)
    rcopy(ot.at[pl.ds(2 * oc, 2)], ot_own, send.at[O3_S], recv.at[O3_S], partner)
    wait_bytes(st_in.at[pair_half], recv.at[ST1_S])
    wait_bytes(ot_pair, recv.at[O1_S])
    for g in range(4, 8):
        merge(g)
    for j in range(2):
        f_a, f_b = merge(4 + 2 * c + j)
        o_sum[j] = (ot[4 + 2 * c + j] * f_a + ot_pair[j] * f_b).astype(BF16)
    rcopy(o_sum.at[0], o_far.at[0], send.at[O4_S], recv.at[O4_S], pair)
    rcopy(sc.at[pair_half], sc_in.at[own_half], send.at[SC1_S], recv.at[SC1_S], pair)
    wait_bytes(st_in.at[own_half], recv.at[ST2_S])
    for g in range(4):
        merge(g)
    rcopy(sc.at[own_half], sc_in.at[pair_half], send.at[SC2_S], recv.at[SC2_S], pair)
    rcopy(o_sum.at[1], o_far.at[1], send.at[O2_S], recv.at[O2_S], pair)
    sum_far(c)
    wait_bytes(sc_in.at[own_half], recv.at[SC1_S])
    wait_bytes(sc_in.at[pair_half], recv.at[SC2_S])
    for g in range(8):
        pos = sq[g, 0:1, :]
        m0, m1 = sc[g, 0:1, :], sc_in[g, 0:1, :]
        top = jnp.maximum(pos, jnp.maximum(m0, m1))
        total = (
            jnp.exp(pos - top)
            + sc[g, 1:2, :] * jnp.exp(m0 - top)
            + sc_in[g, 1:2, :] * jnp.exp(m1 - top)
        )
        lt[g, 0:1, :] = top + jnp.log(total)

    def neg_block(b):
        for g in range(8):
            scale = sq[g, 1:2, :] * jnp.exp(mb[b, g, 0:1, :] - lt[g, 0:1, :])
            qs[:, g * EC : (g + 1) * EC] = (qt[g].astype(F32) * scale).astype(BF16)

        def rows_of(h, carry):
            rr = pl.ds(pl.multiple_of(h * 512, 512), 512)
            acc = nt(prob[b, rr, :], qs[...])
            for u in range(2):
                part = acc[u * 256 : (u + 1) * 256]
                gx[b, 2 * h + u] = part[:, 0:128].astype(BF16)
                for yy in range(4):
                    gy[b, yy, 2 * h + u] = part[yy * 64 : (yy + 1) * 64, 128:256].astype(BF16)
            gz[b, :, rr] = acc[:, 256:512].T[0 : D - 256].astype(BF16)
            return carry

        lax.fori_loop(0, 2, rows_of, 0)
        for i in (1, 3, 2):
            xx, yy = lax.rem(x + i, 4), lax.rem(y + i, 4)
            rcopy(gx.at[b, xx], rx1.at[x, b], send.at[X1_S], recv.at[X1_S], (bucket, xx * 4 + y))
            rcopy(gy.at[b, yy], ry1.at[y, b], send.at[Y1_S], recv.at[Y1_S], (bucket, x * 4 + yy))

    neg_block(1)
    rcopy(gz.at[1], rz1, send.at[Z1_S], recv.at[Z1_S], far)
    wait_bytes(ot_own, recv.at[O3_S])
    wait_bytes(o_far.at[0], recv.at[O4_S])
    wait_bytes(o_far.at[1], recv.at[O2_S])
    ends[D:DP, :] = jnp.zeros((DP - D, 2 * E_DEV), BF16)
    for j in range(2):
        cols = slice(j * EC, (j + 1) * EC)
        tail_cols = slice(E_DEV + j * EC, E_DEV + (j + 1) * EC)
        g = 2 * c + j
        pos, w, ltot = sq[g, 0:1, :], sq[g, 1:2, :], lt[g, 0:1, :]
        pos_coef = w * (jnp.exp(pos - ltot) - 1.0)
        own = w * jnp.exp(st[g, 0:1, :] - ltot)
        other = w * jnp.exp(st_in[g, 0:1, :] - ltot)
        away = w * jnp.exp(sc_in[g, 0:1, :] - ltot)
        grad = pos_coef * tts[j] + ot[g] * own + ot_own[j] * other + o_far[j].astype(F32) * away
        gre, gim = grad[:HALF], grad[HALF:]
        rre, rim = rts[j, :HALF, :], rts[j, HALF:, :]
        hre, him = hts[j, :HALF, :], hts[j, HALF:, :]
        head_grad = jnp.concatenate(
            [gre * rre + gim * rim, gim * rre - gre * rim], axis=0
        ).astype(BF16)
        tail_grad = (pos_coef * qt[g, 0:D, :].astype(F32)).astype(BF16)
        for part, where_to in ((head_grad, cols), (tail_grad, tail_cols)):
            ends[0:D, where_to] = part
            ends[416:432, where_to] = part[384:D]
        term = jnp.concatenate([gre * hre + gim * him, gim * hre - gre * him], axis=0)
        hi = term.astype(BF16)
        rt_hi[:, cols] = hi
        rt_lo[:, cols] = (term - hi.astype(F32)).astype(BF16)

    src_chip = z * NS + shard

    def pack(k, first):
        zz = lax.rem(z + k, NZ)
        chips = pl.ds(pl.multiple_of(zz * NS, NS), NS)
        sel = []
        for d in range(2):
            sc_b = slot_col[zz * 2 + d]
            sel.append(jnp.concatenate(
                [hot_where(sc_b == (iota((256, 128), 1) + 128 * t).astype(F32)) for t in range(8)],
                axis=1,
            ))
        rows = nt(jnp.concatenate(sel, axis=0), ends[...])
        lane = iota((256, 128), 1)
        last = []
        for d in range(2):
            part = rows[d * 256 : (d + 1) * 256]
            for t in range(3):
                first_row = (d * 3 + t) * SLOT
                tile = part[:, t * 128 : (t + 1) * 128].astype(BF16).reshape(NS, SLOT, 128)
                packed[chips, first_row : first_row + SLOT, :] = tile
            dc = dest_col[zz * 2 + d]
            high = jnp.floor(dc * (1.0 / 32.0))
            code = jnp.where(lane == 32 * d + 16, high, jnp.where(lane == 32 * d + 17, dc - 32.0 * high, 0.0))
            last.append(part[:, 384:512] + code)
        tile = jnp.where(lane < 32, last[0], last[1]).astype(BF16).reshape(NS, SLOT, 128)
        packed[chips, 96:112, :] = tile
        for j in range(NS):
            ss = lax.rem(shard + j, NS)
            src = packed.at[zz * NS + ss]
            if first and j == 0:
                pltpu.make_async_copy(src, arrived.at[src_chip], ent_recv.at[k]).start()
            else:
                rcopy(src, arrived.at[src_chip], send.at[ENT_S], ent_recv.at[k], (zz * 2 + c, ss))

    def rel_chunk(r, carry):
        hot = hot_where(iota((128, E_DEV), 0) + r * 128 == ids[...])
        rp[pl.ds(pl.multiple_of(r * 128, 128), 128), :] = nt(hot, rt_hi[...]) + nt(hot, rt_lo[...])
        return carry

    lax.fori_loop(0, 4, rel_chunk, 0)
    rcopy(
        rp.at[pl.ds(pl.multiple_of(oc * 256, 256), 256)], rp_in, send.at[RC_S], recv.at[RC_S], partner
    )

    def pack_other(k, carry):
        pack(k, False)
        return carry

    pack(0, True)
    lax.fori_loop(1, 2, pack_other, 0)

    wait_bytes(rp_in, recv.at[RC_S])
    r1b[...] = (rp[pl.ds(pl.multiple_of(c * 256, 256), 256), :] + rp_in[...]).astype(BF16)
    for j in range(1, NS):
        ss = lax.rem(shard + j, NS)
        rows = r1b.at[pl.ds(pl.multiple_of(ss * 16, 16), 16)]
        rcopy(rows, r2in.at[shard], send.at[R2_S], recv.at[R2_S], (bucket, ss))
    r2in[shard] = r1b[pl.ds(pl.multiple_of(shard * 16, 16), 16), :]
    neg_block(0)

    wait_bytes(rz1, recv.at[Z1_S])
    for r in range(4):
        rr = slice(r * 256, (r + 1) * 256)
        azx[r] = (gz[0, :, rr].astype(F32) + rz1[:, rr].astype(F32)).astype(BF16)
    for i in (1, 3, 2):
        xx = lax.rem(x + i, 4)
        rcopy(azx.at[xx], rzx.at[x], send.at[ZX_S], recv.at[ZX_S], (bucket, xx * 4 + y))

    wait_bytes(r2in.at[pl.ds(0, NS - 1)], recv.at[R2_S])
    r2 = r2in[0].astype(F32)
    for i in range(1, NS):
        r2 = r2 + r2in[i].astype(F32)
    r2all[z] = r2
    for k in (1, 3, 2):
        zz = lax.rem(z + k, NZ)
        rcopy(r2all.at[z], r2all.at[z], send.at[R3_S], recv.at[R3_S], (zz * 2 + c, shard))

    lax.fori_loop(2, NZ, pack_other, 0)


    wait_bytes(rx1.at[pl.ds(0, 3)], recv.at[X1_S])
    for b in range(2):
        total = gx[b, x].astype(F32)
        for i in range(1, 4):
            total = total + rx1[lax.rem(x + i, 4), b].astype(F32)
        ax[b] = total.astype(BF16)
    for i in range(4):
        yy = lax.rem(y + i, 4)
        rows = pl.ds(pl.multiple_of(yy * NEG_OWN, NEG_OWN), NEG_OWN)
        if i:
            rcopy(ax.at[0, rows], rx2.at[y], send.at[X2_S], recv.at[X2_S], (bucket, x * 4 + yy))
        else:
            rx2[y] = ax[0, rows, :]
        rcopy(
            ax.at[1, rows], rx2.at[4 + y], send.at[X2_S], recv.at[X2_S], (z_far * 2 + c, x * 4 + yy)
        )
    wait_bytes(ry1.at[pl.ds(0, 3)], recv.at[Y1_S])
    for b in range(2):
        total = gy[b, y].astype(F32)
        for i in range(1, 4):
            total = total + ry1[lax.rem(y + i, 4), b].astype(F32)
        ay[b] = total.astype(BF16)
    for i in range(4):
        xx = lax.rem(x + i, 4)
        if i:
            rcopy(ay.at[0, xx], ry2.at[x], send.at[Y2_S], recv.at[Y2_S], (bucket, xx * 4 + y))
        else:
            ry2[x] = ay[0, x]
        rcopy(
            ay.at[1, xx], ry2.at[4 + x], send.at[Y2_S], recv.at[Y2_S], (z_far * 2 + c, xx * 4 + y)
        )
    wait_bytes(rzx.at[pl.ds(0, 3)], recv.at[ZX_S])
    total = azx[x].astype(F32)
    for i in range(1, 4):
        total = total + rzx[lax.rem(x + i, 4)].astype(F32)
    wide_sum = jnp.concatenate([total, jnp.zeros((256 - (D - 256), 256), F32)], axis=0)
    az[...] = wide_sum.T.astype(BF16)
    for i in range(4):
        yy = lax.rem(y + i, 4)
        rows = pl.ds(pl.multiple_of(yy * NEG_OWN, NEG_OWN), NEG_OWN)
        if i:
            rcopy(az.at[rows], rz2.at[y], send.at[Z2_S], recv.at[Z2_S], (bucket, x * 4 + yy))
        else:
            rz2[y] = az[rows, :]

    wait_bytes(r2all.at[pl.ds(0, 3)], recv.at[R3_S])
    rel_row = pl.ds(pl.multiple_of(c * 256 + shard * 16, 16), 16)
    rfin[rel_row, :] = (((r2all[0] + r2all[1]) + r2all[2]) + r2all[3]).astype(BF16)
    for j in range(1, NS):
        ss = lax.rem(shard + j, NS)
        rcopy(rfin.at[rel_row], rfin.at[rel_row], send.at[R4_S], recv.at[R4_S], (bucket, ss))

    def give(src, dst, sem):
        pltpu.make_async_copy(src, dst, sem).start()

    other_rows, last_rows = pl.ds(pl.multiple_of(oc * 48, 16), 48), pl.ds(96, SLOT)
    for k in range(NZ):
        chips = pl.ds(pl.multiple_of(lax.rem(z + NZ - k, NZ) * NS, NS), NS)
        wait_bytes(arrived.at[chips], ent_recv.at[k])
        rcopy(arrived.at[chips, other_rows], far_main.at[chips], send.at[PX_S], recv.at[PX_S], partner)
        rcopy(arrived.at[chips, last_rows], far_last.at[chips], send.at[PY_S], recv.at[PY_S], partner)
    give(arrived.at[:, pl.ds(pl.multiple_of(c * 48, 16), 48)], main_out, out_sem.at[0])
    give(arrived.at[:, last_rows], last_out, out_sem.at[5])
    wait_bytes(rfin.at[pl.ds(0, 240)], recv.at[R4_S])
    half_rel = rfin.at[pl.ds(pl.multiple_of(c * 256, 256), 256)]
    rcopy(half_rel, half_rel, send.at[R5_S], recv.at[R5_S], partner)
    wait_bytes(rx2.at[pl.ds(0, 7)], recv.at[X2_S])
    give(rx2, rx2_out, out_sem.at[1])
    wait_bytes(ry2.at[pl.ds(0, 7)], recv.at[Y2_S])
    give(ry2, ry2_out, out_sem.at[2])
    wait_bytes(rz2.at[pl.ds(0, 3)], recv.at[Z2_S])
    give(rz2, rz2_out, out_sem.at[3])
    wait_bytes(half_rel, recv.at[R5_S])
    give(rfin, rel_sum_out, out_sem.at[4])
    wait_bytes(far_main, recv.at[PX_S])
    give(far_main, far_main_out, out_sem.at[6])
    wait_bytes(far_last, recv.at[PY_S])
    give(far_last, far_last_out, out_sem.at[7])

    wait_bytes(nbt.at[pl.ds(0, 2)], send.at[GZ_S])
    wait_bytes(nbt.at[pl.ds(0, 3)], send.at[GX_S])
    wait_bytes(nbt.at[pl.ds(0, 3)], send.at[GY_S])
    for number in (Q1_S, Q2_S, Q3_S):
        wait_bytes(qt.at[mine, real], send.at[number])
    for number in (SQ1_S, SQ2_S, SQ3_S):
        wait_bytes(sq.at[mine], send.at[number])
    for number in (ST1_S, ST2_S, SC1_S, SC2_S):
        wait_bytes(st.at[own_half], send.at[number])
    wait_bytes(ot_pair, send.at[O1_S])
    wait_bytes(o_far.at[0], send.at[O4_S])
    wait_bytes(o_far.at[1], send.at[O2_S])
    wait_bytes(ot_own, send.at[O3_S])
    wait_bytes(arrived.at[pl.ds(0, 63)], send.at[ENT_S])
    wait_bytes(far_main, send.at[PX_S])
    wait_bytes(far_last, send.at[PY_S])
    wait_bytes(rp_in, send.at[RC_S])
    wait_bytes(r2in.at[pl.ds(0, NS - 1)], send.at[R2_S])
    wait_bytes(r2all.at[pl.ds(0, 3)], send.at[R3_S])
    wait_bytes(rfin.at[pl.ds(0, 240)], send.at[R4_S])
    wait_bytes(half_rel, send.at[R5_S])
    wait_bytes(rz1, send.at[Z1_S])
    wait_bytes(rx1.at[pl.ds(0, 3)], send.at[X1_S])
    wait_bytes(ry1.at[pl.ds(0, 3)], send.at[Y1_S])
    wait_bytes(rx2.at[pl.ds(0, 7)], send.at[X2_S])
    wait_bytes(ry2.at[pl.ds(0, 7)], send.at[Y2_S])
    wait_bytes(rz2.at[pl.ds(0, 3)], send.at[Z2_S])
    wait_bytes(rzx.at[pl.ds(0, 3)], send.at[ZX_S])
    for number in (0, 6):
        wait_bytes(far_main, out_sem.at[number])
    for number in (5, 7):
        wait_bytes(far_last, out_sem.at[number])
    wait_bytes(rx2, out_sem.at[1])
    wait_bytes(ry2, out_sem.at[2])
    wait_bytes(rz2, out_sem.at[3])
    wait_bytes(rfin, out_sem.at[4])


def finish(
    main_in, last_in, far_main_in, far_last_in, rx2_in, ry2_in, rz2_in, rel_in,
    ent_out, neg_out, rel_out,
    main, last, far_main, far_last, rx2, ry2, rz2, rel_sum, ent, neg_sum, rel_t, in_sem, out_sem,
):
    loads = [
        pltpu.make_async_copy(src, dst, in_sem.at[i])
        for i, (src, dst) in enumerate((
            (rel_in, rel_sum), (last_in, last), (far_last_in, far_last), (main_in, main),
            (far_main_in, far_main), (rx2_in, rx2), (ry2_in, ry2), (rz2_in, rz2),
        ))
    ]
    for load in loads:
        load.start()
    loads[0].wait()
    for r in range(4):
        rows = rel_sum[r * 128 : (r + 1) * 128, :].astype(F32)
        wide = jnp.concatenate([rows, jnp.zeros((128, DP - D), F32)], axis=1)
        rel_t[:, r * 128 : (r + 1) * 128] = wide.T[0:D]
    stores = [pltpu.make_async_copy(rel_t, rel_out, out_sem.at[0])]
    stores[0].start()

    c = lax.axis_index("bucket") % 2
    lane = iota((8, 128), 1) - 32 * c
    unit = jnp.where(lane == 16, 32.0, jnp.where(lane == 17, 1.0, 0.0)).astype(BF16)
    for load in loads[1:5]:
        load.wait()
    slots, row_ids = [], []
    for tiles, tail in ((main, last), (far_main, far_last)):
        tail_rows = tail[...].reshape(1024, 128)
        columns = [tiles[:, t * SLOT : (t + 1) * SLOT, :].reshape(1024, 128) for t in range(3)]
        slots.append(jnp.concatenate(columns + [tail_rows], axis=1))
        row_ids.append(nt(unit, tail_rows)[0:1, :])
    for r in range(2):
        numbers = (iota((512, 1024), 0) + r * 512).astype(F32)
        got = nn(hot_where(numbers == row_ids[0]), slots[0]) + nn(hot_where(numbers == row_ids[1]), slots[1])
        turned = got.T
        ent[r, 0:384] = turned[0:384]
        ent[r, 384:D] = jnp.where(c == 0, turned[384:400], turned[416:432])
        store = pltpu.make_async_copy(ent.at[r], ent_out.at[:, pl.ds(r * 512, 512)], out_sem.at[1 + r])
        store.start()
        stores.append(store)

    def sum_all(ref):
        total = ref[0].astype(F32)
        for i in range(1, ref.shape[0]):
            total = total + ref[i].astype(F32)
        return total

    for load in loads[5:]:
        load.wait()
    neg_sum[:, 0:128] = sum_all(rx2)
    neg_sum[:, 128:256] = sum_all(ry2)
    neg_sum[:, 256:D] = sum_all(rz2)[:, 0 : D - 256]
    stores.append(pltpu.make_async_copy(neg_sum, neg_out, out_sem.at[3]))
    stores[-1].start()
    for store in stores:
        store.wait()


SCRATCH = [
    ((D, E_DEV), BF16),
    ((D, E_DEV), BF16),
    ((D, REL), F32),
    ((D, NEG_DEV), BF16),
    ((16, D, 128), BF16),
    ((D + 16, NEG_DEV), BF16),
    ((NEG_DEV, DP), BF16),
    ((2, NEG_DEV, 8 * EC), BF16),
    ((8, DP, EC), BF16),
    ((8, 8, EC), F32),
    ((2, D, EC), F32),
    ((2, D, EC), F32),
    ((2, D, EC), F32),
    ((2, 8, 8, EC), F32),
    ((8, 8, EC), F32),
    ((8, 8, EC), F32),
    ((8, 8, EC), F32),
    ((8, 8, EC), F32),
    ((8, D, EC), F32),
    ((2, D, EC), F32),
    ((2, D, EC), F32),
    ((2, D, EC), BF16),
    ((2, D, EC), BF16),
    ((8, 8, EC), F32),
    ((DP, 8 * EC), BF16),
    ((DP, 2 * E_DEV), BF16),
    ((D, E_DEV), BF16),
    ((D, E_DEV), BF16),
    ((NZ * NS, 112, 128), BF16),
    ((NZ * NS, 112, 128), BF16),
    ((NZ * NS, 48, 128), BF16),
    ((NZ * NS, SLOT, 128), BF16),
    ((NB, 256, 128), F32),
    ((NB, 256, 128), F32),
    ((2, D - 256, NEG_DEV), BF16),
    ((2, 4, 256, 128), BF16),
    ((2, 4, 4, NEG_OWN, 128), BF16),
    ((D - 256, NEG_DEV), BF16),
    ((4, 2, 256, 128), BF16),
    ((4, 2, 4, NEG_OWN, 128), BF16),
    ((4, D - 256, 256), BF16),
    ((4, D - 256, 256), BF16),
    ((256, 256), BF16),
    ((2, 256, 128), BF16),
    ((2, 4, NEG_OWN, 128), BF16),
    ((4, NEG_OWN, 256), BF16),
    ((8, NEG_OWN, 128), BF16),
    ((8, NEG_OWN, 128), BF16),
    ((REL, D), F32),
    ((REL // 2, D), F32),
    ((REL // 2, D), BF16),
    ((NS, 16, D), BF16),
    ((NZ, 16, D), F32),
    ((REL, D), BF16),
]


def per_device(
    head_rows, tail_rows, rel_ids, relations, edge_weights, neg_rows, send_slots, dest_rows
):
    vmem = pl.BlockSpec(memory_space=pltpu.VMEM)
    anywhere = pl.BlockSpec(memory_space=pl.ANY)
    results = pl.pallas_call(
        kernel,
        out_shape=(
            jax.ShapeDtypeStruct((NZ * NS, 48, 128), BF16),
            jax.ShapeDtypeStruct((NZ * NS, SLOT, 128), BF16),
            jax.ShapeDtypeStruct((NZ * NS, 48, 128), BF16),
            jax.ShapeDtypeStruct((NZ * NS, SLOT, 128), BF16),
            jax.ShapeDtypeStruct((8, NEG_OWN, 128), BF16),
            jax.ShapeDtypeStruct((8, NEG_OWN, 128), BF16),
            jax.ShapeDtypeStruct((4, NEG_OWN, 256), BF16),
            jax.ShapeDtypeStruct((REL, D), BF16),
        ),
        in_specs=[anywhere, anywhere, vmem, anywhere, vmem, anywhere, vmem, vmem],
        out_specs=(anywhere,) * 8,
        scratch_shapes=[pltpu.VMEM(shape, dtype) for shape, dtype in SCRATCH]
        + [
            pltpu.SemaphoreType.DMA((32,)),
            pltpu.SemaphoreType.DMA((32,)),
            pltpu.SemaphoreType.REGULAR((4,)),
            pltpu.SemaphoreType.DMA((8,)),
            pltpu.SemaphoreType.DMA((NZ,)),
            pltpu.SemaphoreType.DMA((4,)),
        ],
        compiler_params=pltpu.CompilerParams(
            collective_id=0, has_side_effects=True, vmem_limit_bytes=60 * 1024 * 1024
        ),
        cost_estimate=pl.CostEstimate(
            flops=2 * 3 * 1024 * 4096 * 400, bytes_accessed=8 * 1024 * 1024, transcendentals=1024 * 4096
        ),
        name="complex_backward",
    )(
        head_rows.T,
        tail_rows.T,
        rel_ids.reshape(1, E_DEV),
        relations.T,
        edge_weights.reshape(1, E_DEV),
        neg_rows.T,
        send_slots.T,
        dest_rows.T,
    )
    ent_t, neg_grad, rel_t = pl.pallas_call(
        finish,
        out_shape=(
            jax.ShapeDtypeStruct((D, ENT_DEV), F32),
            jax.ShapeDtypeStruct((NEG_OWN, D), F32),
            jax.ShapeDtypeStruct((D, REL), F32),
        ),
        in_specs=[anywhere] * 8,
        out_specs=(anywhere,) * 3,
        scratch_shapes=[
            pltpu.VMEM((NZ * NS, 48, 128), BF16),
            pltpu.VMEM((NZ * NS, SLOT, 128), BF16),
            pltpu.VMEM((NZ * NS, 48, 128), BF16),
            pltpu.VMEM((NZ * NS, SLOT, 128), BF16),
            pltpu.VMEM((8, NEG_OWN, 128), BF16),
            pltpu.VMEM((8, NEG_OWN, 128), BF16),
            pltpu.VMEM((4, NEG_OWN, 256), BF16),
            pltpu.VMEM((REL, D), BF16),
            pltpu.VMEM((2, D, 512), F32),
            pltpu.VMEM((NEG_OWN, D), F32),
            pltpu.VMEM((D, REL), F32),
            pltpu.SemaphoreType.DMA((8,)),
            pltpu.SemaphoreType.DMA((4,)),
        ],
        compiler_params=pltpu.CompilerParams(vmem_limit_bytes=60 * 1024 * 1024),
        cost_estimate=pl.CostEstimate(
            flops=2 * 1024 * 2048 * 512, bytes_accessed=6 * 1024 * 1024, transcendentals=0
        ),
        name="make_outputs",
    )(*results)
    return ent_t.T, neg_grad, rel_t.T


def solution(mesh):
    return jax.shard_map(
        per_device,
        mesh=mesh,
        in_specs=(
            P(("bucket", "shard"), None),
            P(("bucket", "shard"), None),
            P(("bucket", "shard")),
            P(),
            P(("bucket", "shard")),
            P("bucket", None),
            P(("bucket", "shard"), None),
            P(("bucket", "shard"), None),
        ),
        out_specs=(P(("bucket", "shard"), None), P(("bucket", "shard"), None), P()),
        check_vma=False,
    )
```

```python
import functools

import jax
import jax.numpy as jnp
from jax import lax
from jax.experimental import pallas as pl
from jax.experimental.pallas import tpu as pltpu
from jax.sharding import PartitionSpec as P

D = 400
HALF = 200
DP = 512
E_DEV = 512
ENT_DEV = 1024
REL = 512
NEG_DEV = 1024
SLOT = 16
NB = 8
NS = 16
NZ = 4
EC = 256
NEG_OWN = 64

MESH = pl.DeviceIdType.MESH
F32 = jnp.float32
BF16 = jnp.bfloat16

(Q1_S, SQ1_S, Q2_S, SQ2_S, Q3_S, SQ3_S, ST1_S, O1_S, SC1_S, O2_S, ST2_S, O3_S, SC2_S,
 RC_S, R2_S, R3_S, R4_S, R5_S, ENT_S, Z1_S, X1_S, Y1_S, Z2_S, X2_S, Y2_S, GZ_S, GX_S, GY_S, O4_S,
 PX_S, PY_S, ZX_S) = range(32)


def nt(a, b):
    return lax.dot_general(a, b, (((1,), (1,)), ((), ())), preferred_element_type=F32)


def nn(a, b):
    return jnp.dot(a, b, preferred_element_type=F32)


def iota(shape, dim):
    return lax.broadcasted_iota(jnp.int32, shape, dim)


def hot_where(mask):
    return mask.astype(F32).astype(BF16)


def wait_bytes(ref, sem):
    pltpu.make_async_copy(ref, ref, sem).wait()


def kernel(
    head, tail, ids, rel, wts, neg, slots, drows,
    main_out, last_out, far_main_out, far_last_out, rx2_out, ry2_out, rz2_out, rel_sum_out,
    nbt, wide, nb, prob, qt, sq, hts, tts, rts, mb, st, st_in, sc, sc_in,
    ot, ot_pair, ot_own, o_sum, o_far, lt, qs, ends, rt_hi, rt_lo,
    packed, arrived, far_main, far_last, slot_col, dest_col,
    gz, gx, gy, rz1, rx1, ry1, azx, rzx, az, ax, ay, rz2, rx2, ry2,
    rp, rp_in, r1b, r2in, r2all, rfin,
    send, recv, known, out_sem, ent_recv,
):
    bucket, shard = lax.axis_index("bucket"), lax.axis_index("shard")
    z, c = bucket // 2, bucket % 2
    x, y = shard // 4, shard % 4
    oc = 1 - c
    partner = (z * 2 + oc, shard)
    pair = ((z + 1 - 2 * (z % 2)) * 2 + c, shard)
    z_far = 3 - z
    far = (z_far * 2 + c, shard)

    def rcopy(src, dst, s_sem, r_sem, device):
        pltpu.make_async_remote_copy(
            src_ref=src, dst_ref=dst, send_sem=s_sem, recv_sem=r_sem,
            device_id=device, device_id_type=MESH,
        ).start()

    barrier = pltpu.get_barrier_semaphore()

    x_peers = [(bucket, lax.rem(x + i, 4) * 4 + y) for i in (1, 2, 3)]
    y_peers = [(bucket, x * 4 + lax.rem(y + i, 4)) for i in (1, 2, 3)]
    friends = [partner, pair, far] + x_peers + y_peers

    def tell(sem, devices):
        for device in devices:
            pl.semaphore_signal(sem, inc=1, device_id=device, device_id_type=MESH)

    tell(barrier, friends)

    for g in range(8):
        qt[g, D:DP, :] = jnp.zeros((DP - D, EC), BF16)
    wide[D:, :] = jnp.ones((16, NEG_DEV), BF16)

    for i in range(8):
        nbt[i] = neg[:, i * 128 : (i + 1) * 128]

    rel_1 = rel[...].astype(BF16)
    rest = rel[...] - rel_1.astype(F32)
    rel_2 = rest.astype(BF16)
    rel_3 = (rest - rel_2.astype(F32)).astype(BF16)
    for j in range(2):
        cols = slice(j * EC, (j + 1) * EC)
        h_t = head[:, cols].astype(F32)
        t_t = tail[:, cols].astype(F32)
        hot = hot_where(iota((REL, EC), 0) == ids[0:1, cols])
        r_t = (nn(rel_1, hot) + nn(rel_2, hot)) + nn(rel_3, hot)
        hre, him = h_t[:HALF], h_t[HALF:]
        rre, rim = r_t[:HALF], r_t[HALF:]
        q = jnp.concatenate([hre * rre - him * rim, hre * rim + him * rre], axis=0).astype(BF16)
        qt[2 * c + j, 0:D, :] = q
        sq[2 * c + j, 0:1, :] = jnp.sum(q.astype(F32) * t_t, axis=0, keepdims=True)
        sq[2 * c + j, 1:2, :] = wts[0:1, cols]
        sq[2 * c + j, 2:8, :] = jnp.zeros((6, EC), F32)
        hts[j] = h_t
        tts[j] = t_t
        rts[j] = r_t

    pl.semaphore_wait(barrier, len(friends))
    tell(known.at[0], y_peers)

    for i in (x, 4 + y):
        rcopy(nbt.at[i], nbt.at[8 + i], send.at[GZ_S], recv.at[GZ_S], far)
    mine, theirs, real = pl.ds(2 * c, 2), pl.ds(4 + 2 * c, 2), pl.ds(0, D)
    rcopy(qt.at[mine, real], qt.at[mine, real], send.at[Q1_S], recv.at[Q1_S], partner)
    rcopy(sq.at[mine], sq.at[mine], send.at[SQ1_S], recv.at[SQ1_S], partner)
    rcopy(qt.at[mine, real], qt.at[theirs, real], send.at[Q2_S], recv.at[Q2_S], pair)
    rcopy(sq.at[mine], sq.at[theirs], send.at[SQ2_S], recv.at[SQ2_S], pair)

    ones = jnp.ones((SLOT, 128), BF16)
    tables = []
    for ref in (slots, drows):
        value = ref[...].astype(F32)
        high = jnp.floor(value * (1.0 / 32.0))
        tables.append((high.astype(BF16), (value - 32.0 * high).astype(BF16)))

    def columns(b, carry):
        owner_hot = hot_where(iota((256, 128), 1) == iota((256, 128), 0) // SLOT + b * NS)
        keep = iota((256, SLOT), 1) == iota((256, SLOT), 0) % SLOT
        for (high, low), out in zip(tables, (slot_col, dest_col)):
            h = jnp.where(keep, nt(owner_hot, high), 0.0).astype(BF16)
            l = jnp.where(keep, nt(owner_hot, low), 0.0).astype(BF16)
            out[b] = 32.0 * nn(h, ones) + nn(l, ones)
        return carry

    lax.fori_loop(0, NB, columns, 0)
    nb[:, 384:DP] = jnp.zeros((NEG_DEV, 128), BF16)

    def flip(b):
        for i in range(8):
            part = nbt[b * 8 + i]
            wide[0:D, i * 128 : (i + 1) * 128] = part
            nb[i * 128 : (i + 1) * 128, 0:D] = part.astype(F32).T.astype(BF16)

    def block(b, two):

        chunks = (2 * two, 2 * two + 1)
        scores = nn(nb[...], jnp.concatenate([qt[g] for g in chunks], axis=1))
        for u, g in enumerate(chunks):
            s = scores[:, u * EC : (u + 1) * EC]
            m = jnp.max(s, axis=0, keepdims=True)
            pb = jnp.exp(s - m).astype(BF16)
            prob[b, :, pl.ds(pl.multiple_of(g * EC, EC), EC)] = pb
            o = nn(wide[...], pb)
            l = o[D : D + 1]
            o = o[0:D]
            mb[b, g, 0:1, :] = m
            if b == 0:
                st[g, 0:1, :] = m
                st[g, 1:2, :] = l
                st[g, 2:8, :] = jnp.zeros((6, EC), F32)
                ot[g] = o
            else:
                m_old = st[g, 0:1, :]
                m_new = jnp.maximum(m_old, m)
                f_old = jnp.exp(m_old - m_new)
                f_new = jnp.exp(m - m_new)
                st[g, 0:1, :] = m_new
                st[g, 1:2, :] = st[g, 1:2, :] * f_old + l * f_new
                ot[g] = ot[g] * f_old + o * f_new

    flip(0)
    block(0, c)
    pl.semaphore_wait(known.at[0], 3)
    tell(known.at[1], (pair, far))
    wait_bytes(nbt.at[pl.ds(8, 2)], recv.at[GZ_S])
    for i in (1, 3, 2):
        xx, yy = lax.rem(x + i, 4), lax.rem(y + i, 4)
        rcopy(nbt.at[8 + x], nbt.at[8 + x], send.at[GX_S], recv.at[GX_S], (bucket, xx * 4 + y))
        rcopy(nbt.at[12 + y], nbt.at[12 + y], send.at[GY_S], recv.at[GY_S], (bucket, x * 4 + yy))
    wait_bytes(qt.at[mine, real], recv.at[Q1_S])
    wait_bytes(sq.at[mine], recv.at[SQ1_S])
    block(0, oc)
    pl.semaphore_wait(known.at[1], 2)
    tell(known.at[2], (pair, far))
    wait_bytes(qt.at[mine, real], recv.at[Q2_S])
    wait_bytes(sq.at[mine], recv.at[SQ2_S])
    rcopy(qt.at[theirs, real], qt.at[theirs, real], send.at[Q3_S], recv.at[Q3_S], partner)
    rcopy(sq.at[theirs], sq.at[theirs], send.at[SQ3_S], recv.at[SQ3_S], partner)
    block(0, 2 + c)
    wait_bytes(qt.at[mine, real], recv.at[Q3_S])
    wait_bytes(sq.at[mine], recv.at[SQ3_S])
    block(0, 2 + oc)
    wait_bytes(nbt.at[pl.ds(8, 3)], recv.at[GX_S])
    wait_bytes(nbt.at[pl.ds(8, 3)], recv.at[GY_S])
    flip(1)
    block(1, 2 + oc)
    pl.semaphore_wait(known.at[2], 2)
    tell(known.at[3], (partner,))
    rcopy(
        ot.at[pl.ds(4 + 2 * oc, 2)], ot_pair, send.at[O1_S], recv.at[O1_S], partner
    )
    block(1, 2 + c)
    own_half, pair_half = pl.ds(0, 4), pl.ds(4, 4)
    rcopy(st.at[pair_half], st_in.at[pair_half], send.at[ST1_S], recv.at[ST1_S], partner)

    def merge(g):
        m_a, m_b = st[g, 0:1, :], st_in[g, 0:1, :]
        m = jnp.maximum(m_a, m_b)
        f_a, f_b = jnp.exp(m_a - m), jnp.exp(m_b - m)
        sc[g, 0:1, :] = m
        sc[g, 1:2, :] = st[g, 1:2, :] * f_a + st_in[g, 1:2, :] * f_b
        sc[g, 2:8, :] = jnp.zeros((6, EC), F32)
        return f_a, f_b

    block(1, oc)
    pl.semaphore_wait(known.at[3], 1)
    rcopy(ot.at[pl.ds(2 * oc, 2)], ot_own, send.at[O3_S], recv.at[O3_S], partner)
    wait_bytes(st_in.at[pair_half], recv.at[ST1_S])
    wait_bytes(ot_pair, recv.at[O1_S])
    for g in range(4, 8):
        merge(g)
    for j in range(2):
        f_a, f_b = merge(4 + 2 * c + j)
        o_sum[j] = (ot[4 + 2 * c + j] * f_a + ot_pair[j] * f_b).astype(BF16)
    rcopy(o_sum.at[0], o_far.at[0], send.at[O4_S], recv.at[O4_S], pair)
    rcopy(sc.at[pair_half], sc_in.at[own_half], send.at[SC1_S], recv.at[SC1_S], pair)
    block(1, c)
    rcopy(st.at[own_half], st_in.at[own_half], send.at[ST2_S], recv.at[ST2_S], partner)
    wait_bytes(st_in.at[own_half], recv.at[ST2_S])
    for g in range(4):
        merge(g)
    rcopy(sc.at[own_half], sc_in.at[pair_half], send.at[SC2_S], recv.at[SC2_S], pair)
    rcopy(o_sum.at[1], o_far.at[1], send.at[O2_S], recv.at[O2_S], pair)
    wait_bytes(sc_in.at[own_half], recv.at[SC1_S])
    wait_bytes(sc_in.at[pair_half], recv.at[SC2_S])
    for g in range(8):
        pos = sq[g, 0:1, :]
        m0, m1 = sc[g, 0:1, :], sc_in[g, 0:1, :]
        top = jnp.maximum(pos, jnp.maximum(m0, m1))
        total = (
            jnp.exp(pos - top)
            + sc[g, 1:2, :] * jnp.exp(m0 - top)
            + sc_in[g, 1:2, :] * jnp.exp(m1 - top)
        )
        lt[g, 0:1, :] = top + jnp.log(total)

    def neg_block(b):
        for g in range(8):
            scale = sq[g, 1:2, :] * jnp.exp(mb[b, g, 0:1, :] - lt[g, 0:1, :])
            qs[:, g * EC : (g + 1) * EC] = (qt[g].astype(F32) * scale).astype(BF16)

        def rows_of(h, carry):
            rr = pl.ds(pl.multiple_of(h * 512, 512), 512)
            acc = nt(prob[b, rr, :], qs[...])
            for u in range(2):
                part = acc[u * 256 : (u + 1) * 256]
                gx[b, 2 * h + u] = part[:, 0:128].astype(BF16)
                for yy in range(4):
                    gy[b, yy, 2 * h + u] = part[yy * 64 : (yy + 1) * 64, 128:256].astype(BF16)
            gz[b, :, rr] = acc[:, 256:512].T[0 : D - 256].astype(BF16)
            return carry

        lax.fori_loop(0, 2, rows_of, 0)
        for i in (1, 3, 2):
            xx, yy = lax.rem(x + i, 4), lax.rem(y + i, 4)
            rcopy(gx.at[b, xx], rx1.at[x, b], send.at[X1_S], recv.at[X1_S], (bucket, xx * 4 + y))
            rcopy(gy.at[b, yy], ry1.at[y, b], send.at[Y1_S], recv.at[Y1_S], (bucket, x * 4 + yy))

    neg_block(1)
    rcopy(gz.at[1], rz1, send.at[Z1_S], recv.at[Z1_S], far)
    wait_bytes(ot_own, recv.at[O3_S])
    wait_bytes(o_far.at[0], recv.at[O4_S])
    wait_bytes(o_far.at[1], recv.at[O2_S])
    ends[D:DP, :] = jnp.zeros((DP - D, 2 * E_DEV), BF16)
    for j in range(2):
        cols = slice(j * EC, (j + 1) * EC)
        tail_cols = slice(E_DEV + j * EC, E_DEV + (j + 1) * EC)
        g = 2 * c + j
        pos, w, ltot = sq[g, 0:1, :], sq[g, 1:2, :], lt[g, 0:1, :]
        pos_coef = w * (jnp.exp(pos - ltot) - 1.0)
        own = w * jnp.exp(st[g, 0:1, :] - ltot)
        other = w * jnp.exp(st_in[g, 0:1, :] - ltot)
        away = w * jnp.exp(sc_in[g, 0:1, :] - ltot)
        grad = pos_coef * tts[j] + ot[g] * own + ot_own[j] * other + o_far[j].astype(F32) * away
        gre, gim = grad[:HALF], grad[HALF:]
        rre, rim = rts[j, :HALF, :], rts[j, HALF:, :]
        hre, him = hts[j, :HALF, :], hts[j, HALF:, :]
        head_grad = jnp.concatenate(
            [gre * rre + gim * rim, gim * rre - gre * rim], axis=0
        ).astype(BF16)
        tail_grad = (pos_coef * qt[g, 0:D, :].astype(F32)).astype(BF16)
        for part, where_to in ((head_grad, cols), (tail_grad, tail_cols)):
            ends[0:D, where_to] = part
            ends[416:432, where_to] = part[384:D]
        term = jnp.concatenate([gre * hre + gim * him, gim * hre - gre * him], axis=0)
        hi = term.astype(BF16)
        rt_hi[:, cols] = hi
        rt_lo[:, cols] = (term - hi.astype(F32)).astype(BF16)

    src_chip = z * NS + shard

    def pack(k, first):
        zz = lax.rem(z + k, NZ)
        chips = pl.ds(pl.multiple_of(zz * NS, NS), NS)
        sel = []
        for d in range(2):
            sc_b = slot_col[zz * 2 + d]
            sel.append(jnp.concatenate(
                [hot_where(sc_b == (iota((256, 128), 1) + 128 * t).astype(F32)) for t in range(8)],
                axis=1,
            ))
        rows = nt(jnp.concatenate(sel, axis=0), ends[...])
        lane = iota((256, 128), 1)
        last = []
        for d in range(2):
            part = rows[d * 256 : (d + 1) * 256]
            for t in range(3):
                first_row = (d * 3 + t) * SLOT
                tile = part[:, t * 128 : (t + 1) * 128].astype(BF16).reshape(NS, SLOT, 128)
                packed[chips, first_row : first_row + SLOT, :] = tile
            dc = dest_col[zz * 2 + d]
            high = jnp.floor(dc * (1.0 / 32.0))
            code = jnp.where(lane == 32 * d + 16, high, jnp.where(lane == 32 * d + 17, dc - 32.0 * high, 0.0))
            last.append(part[:, 384:512] + code)
        tile = jnp.where(lane < 32, last[0], last[1]).astype(BF16).reshape(NS, SLOT, 128)
        packed[chips, 96:112, :] = tile
        for j in range(NS):
            ss = lax.rem(shard + j, NS)
            src = packed.at[zz * NS + ss]
            if first and j == 0:
                pltpu.make_async_copy(src, arrived.at[src_chip], ent_recv.at[k]).start()
            else:
                rcopy(src, arrived.at[src_chip], send.at[ENT_S], ent_recv.at[k], (zz * 2 + c, ss))

    def rel_chunk(r, carry):
        hot = hot_where(iota((128, E_DEV), 0) + r * 128 == ids[...])
        rp[pl.ds(pl.multiple_of(r * 128, 128), 128), :] = nt(hot, rt_hi[...]) + nt(hot, rt_lo[...])
        return carry

    lax.fori_loop(0, 4, rel_chunk, 0)
    rcopy(
        rp.at[pl.ds(pl.multiple_of(oc * 256, 256), 256)], rp_in, send.at[RC_S], recv.at[RC_S], partner
    )

    def pack_other(k, carry):
        pack(k, False)
        return carry

    pack(0, True)

    wait_bytes(rp_in, recv.at[RC_S])
    r1b[...] = (rp[pl.ds(pl.multiple_of(c * 256, 256), 256), :] + rp_in[...]).astype(BF16)
    for j in range(1, NS):
        ss = lax.rem(shard + j, NS)
        rows = r1b.at[pl.ds(pl.multiple_of(ss * 16, 16), 16)]
        rcopy(rows, r2in.at[shard], send.at[R2_S], recv.at[R2_S], (bucket, ss))
    r2in[shard] = r1b[pl.ds(pl.multiple_of(shard * 16, 16), 16), :]
    lax.fori_loop(1, 2, pack_other, 0)
    neg_block(0)

    wait_bytes(rz1, recv.at[Z1_S])
    for r in range(4):
        rr = slice(r * 256, (r + 1) * 256)
        azx[r] = (gz[0, :, rr].astype(F32) + rz1[:, rr].astype(F32)).astype(BF16)
    for i in (1, 3, 2):
        xx = lax.rem(x + i, 4)
        rcopy(azx.at[xx], rzx.at[x], send.at[ZX_S], recv.at[ZX_S], (bucket, xx * 4 + y))

    wait_bytes(r2in.at[pl.ds(0, NS - 1)], recv.at[R2_S])
    r2 = r2in[0].astype(F32)
    for i in range(1, NS):
        r2 = r2 + r2in[i].astype(F32)
    r2all[z] = r2
    for k in (1, 3, 2):
        zz = lax.rem(z + k, NZ)
        rcopy(r2all.at[z], r2all.at[z], send.at[R3_S], recv.at[R3_S], (zz * 2 + c, shard))

    lax.fori_loop(2, NZ, pack_other, 0)


    wait_bytes(rx1.at[pl.ds(0, 3)], recv.at[X1_S])
    for b in range(2):
        total = gx[b, x].astype(F32)
        for i in range(1, 4):
            total = total + rx1[lax.rem(x + i, 4), b].astype(F32)
        ax[b] = total.astype(BF16)
    for i in range(4):
        yy = lax.rem(y + i, 4)
        rows = pl.ds(pl.multiple_of(yy * NEG_OWN, NEG_OWN), NEG_OWN)
        if i:
            rcopy(ax.at[0, rows], rx2.at[y], send.at[X2_S], recv.at[X2_S], (bucket, x * 4 + yy))
        else:
            rx2[y] = ax[0, rows, :]
        rcopy(
            ax.at[1, rows], rx2.at[4 + y], send.at[X2_S], recv.at[X2_S], (z_far * 2 + c, x * 4 + yy)
        )
    wait_bytes(ry1.at[pl.ds(0, 3)], recv.at[Y1_S])
    for b in range(2):
        total = gy[b, y].astype(F32)
        for i in range(1, 4):
            total = total + ry1[lax.rem(y + i, 4), b].astype(F32)
        ay[b] = total.astype(BF16)
    for i in range(4):
        xx = lax.rem(x + i, 4)
        if i:
            rcopy(ay.at[0, xx], ry2.at[x], send.at[Y2_S], recv.at[Y2_S], (bucket, xx * 4 + y))
        else:
            ry2[x] = ay[0, x]
        rcopy(
            ay.at[1, xx], ry2.at[4 + x], send.at[Y2_S], recv.at[Y2_S], (z_far * 2 + c, xx * 4 + y)
        )
    wait_bytes(rzx.at[pl.ds(0, 3)], recv.at[ZX_S])
    total = azx[x].astype(F32)
    for i in range(1, 4):
        total = total + rzx[lax.rem(x + i, 4)].astype(F32)
    wide_sum = jnp.concatenate([total, jnp.zeros((256 - (D - 256), 256), F32)], axis=0)
    az[...] = wide_sum.T.astype(BF16)
    for i in range(4):
        yy = lax.rem(y + i, 4)
        rows = pl.ds(pl.multiple_of(yy * NEG_OWN, NEG_OWN), NEG_OWN)
        if i:
            rcopy(az.at[rows], rz2.at[y], send.at[Z2_S], recv.at[Z2_S], (bucket, x * 4 + yy))
        else:
            rz2[y] = az[rows, :]

    wait_bytes(r2all.at[pl.ds(0, 3)], recv.at[R3_S])
    rel_row = pl.ds(pl.multiple_of(c * 256 + shard * 16, 16), 16)
    rfin[rel_row, :] = (((r2all[0] + r2all[1]) + r2all[2]) + r2all[3]).astype(BF16)
    for j in range(1, NS):
        ss = lax.rem(shard + j, NS)
        rcopy(rfin.at[rel_row], rfin.at[rel_row], send.at[R4_S], recv.at[R4_S], (bucket, ss))

    def give(src, dst, sem):
        pltpu.make_async_copy(src, dst, sem).start()

    other_rows, last_rows = pl.ds(pl.multiple_of(oc * 48, 16), 48), pl.ds(96, SLOT)
    for k in range(NZ):
        chips = pl.ds(pl.multiple_of(lax.rem(z + NZ - k, NZ) * NS, NS), NS)
        wait_bytes(arrived.at[chips], ent_recv.at[k])
        rcopy(arrived.at[chips, other_rows], far_main.at[chips], send.at[PX_S], recv.at[PX_S], partner)
        rcopy(arrived.at[chips, last_rows], far_last.at[chips], send.at[PY_S], recv.at[PY_S], partner)
    give(arrived.at[:, pl.ds(pl.multiple_of(c * 48, 16), 48)], main_out, out_sem.at[0])
    give(arrived.at[:, last_rows], last_out, out_sem.at[5])
    wait_bytes(rfin.at[pl.ds(0, 240)], recv.at[R4_S])
    half_rel = rfin.at[pl.ds(pl.multiple_of(c * 256, 256), 256)]
    rcopy(half_rel, half_rel, send.at[R5_S], recv.at[R5_S], partner)
    wait_bytes(rx2.at[pl.ds(0, 7)], recv.at[X2_S])
    give(rx2, rx2_out, out_sem.at[1])
    wait_bytes(ry2.at[pl.ds(0, 7)], recv.at[Y2_S])
    give(ry2, ry2_out, out_sem.at[2])
    wait_bytes(rz2.at[pl.ds(0, 3)], recv.at[Z2_S])
    give(rz2, rz2_out, out_sem.at[3])
    wait_bytes(half_rel, recv.at[R5_S])
    give(rfin, rel_sum_out, out_sem.at[4])
    wait_bytes(far_main, recv.at[PX_S])
    give(far_main, far_main_out, out_sem.at[6])
    wait_bytes(far_last, recv.at[PY_S])
    give(far_last, far_last_out, out_sem.at[7])

    wait_bytes(nbt.at[pl.ds(0, 2)], send.at[GZ_S])
    wait_bytes(nbt.at[pl.ds(0, 3)], send.at[GX_S])
    wait_bytes(nbt.at[pl.ds(0, 3)], send.at[GY_S])
    for number in (Q1_S, Q2_S, Q3_S):
        wait_bytes(qt.at[mine, real], send.at[number])
    for number in (SQ1_S, SQ2_S, SQ3_S):
        wait_bytes(sq.at[mine], send.at[number])
    for number in (ST1_S, ST2_S, SC1_S, SC2_S):
        wait_bytes(st.at[own_half], send.at[number])
    wait_bytes(ot_pair, send.at[O1_S])
    wait_bytes(o_far.at[0], send.at[O4_S])
    wait_bytes(o_far.at[1], send.at[O2_S])
    wait_bytes(ot_own, send.at[O3_S])
    wait_bytes(arrived.at[pl.ds(0, 63)], send.at[ENT_S])
    wait_bytes(far_main, send.at[PX_S])
    wait_bytes(far_last, send.at[PY_S])
    wait_bytes(rp_in, send.at[RC_S])
    wait_bytes(r2in.at[pl.ds(0, NS - 1)], send.at[R2_S])
    wait_bytes(r2all.at[pl.ds(0, 3)], send.at[R3_S])
    wait_bytes(rfin.at[pl.ds(0, 240)], send.at[R4_S])
    wait_bytes(half_rel, send.at[R5_S])
    wait_bytes(rz1, send.at[Z1_S])
    wait_bytes(rx1.at[pl.ds(0, 3)], send.at[X1_S])
    wait_bytes(ry1.at[pl.ds(0, 3)], send.at[Y1_S])
    wait_bytes(rx2.at[pl.ds(0, 7)], send.at[X2_S])
    wait_bytes(ry2.at[pl.ds(0, 7)], send.at[Y2_S])
    wait_bytes(rz2.at[pl.ds(0, 3)], send.at[Z2_S])
    wait_bytes(rzx.at[pl.ds(0, 3)], send.at[ZX_S])
    for number in (0, 6):
        wait_bytes(far_main, out_sem.at[number])
    for number in (5, 7):
        wait_bytes(far_last, out_sem.at[number])
    wait_bytes(rx2, out_sem.at[1])
    wait_bytes(ry2, out_sem.at[2])
    wait_bytes(rz2, out_sem.at[3])
    wait_bytes(rfin, out_sem.at[4])


def finish(
    main_in, last_in, far_main_in, far_last_in, rx2_in, ry2_in, rz2_in, rel_in,
    ent_out, neg_out, rel_out,
    main, last, far_main, far_last, rx2, ry2, rz2, rel_sum, ent, neg_sum, rel_t, in_sem, out_sem,
):
    loads = [
        pltpu.make_async_copy(src, dst, in_sem.at[i])
        for i, (src, dst) in enumerate((
            (rel_in, rel_sum), (last_in, last), (far_last_in, far_last), (main_in, main),
            (far_main_in, far_main), (rx2_in, rx2), (ry2_in, ry2), (rz2_in, rz2),
        ))
    ]
    for load in loads:
        load.start()
    loads[0].wait()
    for r in range(4):
        rows = rel_sum[r * 128 : (r + 1) * 128, :].astype(F32)
        wide = jnp.concatenate([rows, jnp.zeros((128, DP - D), F32)], axis=1)
        rel_t[:, r * 128 : (r + 1) * 128] = wide.T[0:D]
    stores = [pltpu.make_async_copy(rel_t, rel_out, out_sem.at[0])]
    stores[0].start()

    c = lax.axis_index("bucket") % 2
    lane = iota((8, 128), 1) - 32 * c
    unit = jnp.where(lane == 16, 32.0, jnp.where(lane == 17, 1.0, 0.0)).astype(BF16)
    for load in loads[1:5]:
        load.wait()
    slots, row_ids = [], []
    for tiles, tail in ((main, last), (far_main, far_last)):
        tail_rows = tail[...].reshape(1024, 128)
        columns = [tiles[:, t * SLOT : (t + 1) * SLOT, :].reshape(1024, 128) for t in range(3)]
        slots.append(jnp.concatenate(columns + [tail_rows], axis=1))
        row_ids.append(nt(unit, tail_rows)[0:1, :])
    for r in range(2):
        numbers = (iota((512, 1024), 0) + r * 512).astype(F32)
        got = nn(hot_where(numbers == row_ids[0]), slots[0]) + nn(hot_where(numbers == row_ids[1]), slots[1])
        turned = got.T
        ent[r, 0:384] = turned[0:384]
        ent[r, 384:D] = jnp.where(c == 0, turned[384:400], turned[416:432])
        store = pltpu.make_async_copy(ent.at[r], ent_out.at[:, pl.ds(r * 512, 512)], out_sem.at[1 + r])
        store.start()
        stores.append(store)

    def sum_all(ref):
        total = ref[0].astype(F32)
        for i in range(1, ref.shape[0]):
            total = total + ref[i].astype(F32)
        return total

    for load in loads[5:]:
        load.wait()
    neg_sum[:, 0:128] = sum_all(rx2)
    neg_sum[:, 128:256] = sum_all(ry2)
    neg_sum[:, 256:D] = sum_all(rz2)[:, 0 : D - 256]
    stores.append(pltpu.make_async_copy(neg_sum, neg_out, out_sem.at[3]))
    stores[-1].start()
    for store in stores:
        store.wait()


SCRATCH = [
    ((16, D, 128), BF16),
    ((D + 16, NEG_DEV), BF16),
    ((NEG_DEV, DP), BF16),
    ((2, NEG_DEV, 8 * EC), BF16),
    ((8, DP, EC), BF16),
    ((8, 8, EC), F32),
    ((2, D, EC), F32),
    ((2, D, EC), F32),
    ((2, D, EC), F32),
    ((2, 8, 8, EC), F32),
    ((8, 8, EC), F32),
    ((8, 8, EC), F32),
    ((8, 8, EC), F32),
    ((8, 8, EC), F32),
    ((8, D, EC), F32),
    ((2, D, EC), F32),
    ((2, D, EC), F32),
    ((2, D, EC), BF16),
    ((2, D, EC), BF16),
    ((8, 8, EC), F32),
    ((DP, 8 * EC), BF16),
    ((DP, 2 * E_DEV), BF16),
    ((D, E_DEV), BF16),
    ((D, E_DEV), BF16),
    ((NZ * NS, 112, 128), BF16),
    ((NZ * NS, 112, 128), BF16),
    ((NZ * NS, 48, 128), BF16),
    ((NZ * NS, SLOT, 128), BF16),
    ((NB, 256, 128), F32),
    ((NB, 256, 128), F32),
    ((2, D - 256, NEG_DEV), BF16),
    ((2, 4, 256, 128), BF16),
    ((2, 4, 4, NEG_OWN, 128), BF16),
    ((D - 256, NEG_DEV), BF16),
    ((4, 2, 256, 128), BF16),
    ((4, 2, 4, NEG_OWN, 128), BF16),
    ((4, D - 256, 256), BF16),
    ((4, D - 256, 256), BF16),
    ((256, 256), BF16),
    ((2, 256, 128), BF16),
    ((2, 4, NEG_OWN, 128), BF16),
    ((4, NEG_OWN, 256), BF16),
    ((8, NEG_OWN, 128), BF16),
    ((8, NEG_OWN, 128), BF16),
    ((REL, D), F32),
    ((REL // 2, D), F32),
    ((REL // 2, D), BF16),
    ((NS, 16, D), BF16),
    ((NZ, 16, D), F32),
    ((REL, D), BF16),
]


def per_device(
    head_rows, tail_rows, rel_ids, relations, edge_weights, neg_rows, send_slots, dest_rows
):
    vmem = pl.BlockSpec(memory_space=pltpu.VMEM)
    anywhere = pl.BlockSpec(memory_space=pl.ANY)
    results = pl.pallas_call(
        kernel,
        out_shape=(
            jax.ShapeDtypeStruct((NZ * NS, 48, 128), BF16),
            jax.ShapeDtypeStruct((NZ * NS, SLOT, 128), BF16),
            jax.ShapeDtypeStruct((NZ * NS, 48, 128), BF16),
            jax.ShapeDtypeStruct((NZ * NS, SLOT, 128), BF16),
            jax.ShapeDtypeStruct((8, NEG_OWN, 128), BF16),
            jax.ShapeDtypeStruct((8, NEG_OWN, 128), BF16),
            jax.ShapeDtypeStruct((4, NEG_OWN, 256), BF16),
            jax.ShapeDtypeStruct((REL, D), BF16),
        ),
        in_specs=[vmem] * 8,
        out_specs=(anywhere,) * 8,
        scratch_shapes=[pltpu.VMEM(shape, dtype) for shape, dtype in SCRATCH]
        + [
            pltpu.SemaphoreType.DMA((32,)),
            pltpu.SemaphoreType.DMA((32,)),
            pltpu.SemaphoreType.REGULAR((4,)),
            pltpu.SemaphoreType.DMA((8,)),
            pltpu.SemaphoreType.DMA((NZ,)),
        ],
        compiler_params=pltpu.CompilerParams(
            collective_id=0, has_side_effects=True, vmem_limit_bytes=60 * 1024 * 1024
        ),
        cost_estimate=pl.CostEstimate(
            flops=2 * 3 * 1024 * 4096 * 400, bytes_accessed=8 * 1024 * 1024, transcendentals=1024 * 4096
        ),
        name="complex_backward",
    )(
        head_rows.T,
        tail_rows.T,
        rel_ids.reshape(1, E_DEV),
        relations.T,
        edge_weights.reshape(1, E_DEV),
        neg_rows.T,
        send_slots.T,
        dest_rows.T,
    )
    ent_t, neg_grad, rel_t = pl.pallas_call(
        finish,
        out_shape=(
            jax.ShapeDtypeStruct((D, ENT_DEV), F32),
            jax.ShapeDtypeStruct((NEG_OWN, D), F32),
            jax.ShapeDtypeStruct((D, REL), F32),
        ),
        in_specs=[anywhere] * 8,
        out_specs=(anywhere,) * 3,
        scratch_shapes=[
            pltpu.VMEM((NZ * NS, 48, 128), BF16),
            pltpu.VMEM((NZ * NS, SLOT, 128), BF16),
            pltpu.VMEM((NZ * NS, 48, 128), BF16),
            pltpu.VMEM((NZ * NS, SLOT, 128), BF16),
            pltpu.VMEM((8, NEG_OWN, 128), BF16),
            pltpu.VMEM((8, NEG_OWN, 128), BF16),
            pltpu.VMEM((4, NEG_OWN, 256), BF16),
            pltpu.VMEM((REL, D), BF16),
            pltpu.VMEM((2, D, 512), F32),
            pltpu.VMEM((NEG_OWN, D), F32),
            pltpu.VMEM((D, REL), F32),
            pltpu.SemaphoreType.DMA((8,)),
            pltpu.SemaphoreType.DMA((4,)),
        ],
        compiler_params=pltpu.CompilerParams(vmem_limit_bytes=60 * 1024 * 1024),
        cost_estimate=pl.CostEstimate(
            flops=2 * 1024 * 2048 * 512, bytes_accessed=6 * 1024 * 1024, transcendentals=0
        ),
        name="make_outputs",
    )(*results)
    return ent_t.T, neg_grad, rel_t.T


def solution(mesh):
    return jax.shard_map(
        per_device,
        mesh=mesh,
        in_specs=(
            P(("bucket", "shard"), None),
            P(("bucket", "shard"), None),
            P(("bucket", "shard")),
            P(),
            P(("bucket", "shard")),
            P("bucket", None),
            P(("bucket", "shard"), None),
            P(("bucket", "shard"), None),
        ),
        out_specs=(P(("bucket", "shard"), None), P(("bucket", "shard"), None), P()),
        check_vma=False,
    )
```

```python
import functools

import jax
import jax.numpy as jnp
from jax import lax
from jax.experimental import pallas as pl
from jax.experimental.pallas import tpu as pltpu
from jax.sharding import PartitionSpec as P

D = 400
HALF = 200
DP = 512
E_DEV = 512
ENT_DEV = 1024
REL = 512
NEG_DEV = 1024
SLOT = 16
NB = 8
NS = 16
NZ = 4
EC = 256
NEG_OWN = 64

MESH = pl.DeviceIdType.MESH
F32 = jnp.float32
BF16 = jnp.bfloat16

(Q1_S, SQ1_S, Q2_S, SQ2_S, Q3_S, SQ3_S, ST1_S, O1_S, SC1_S, O2_S, ST2_S, O3_S, SC2_S,
 RC_S, R2_S, R3_S, R4_S, R5_S, ENT_S, Z1_S, X1_S, Y1_S, Z2_S, X2_S, Y2_S, GZ_S, GX_S, GY_S, O4_S,
 PX_S, PY_S, ZX_S) = range(32)


def nt(a, b):
    return lax.dot_general(a, b, (((1,), (1,)), ((), ())), preferred_element_type=F32)


def nn(a, b):
    return jnp.dot(a, b, preferred_element_type=F32)


def iota(shape, dim):
    return lax.broadcasted_iota(jnp.int32, shape, dim)


def hot_where(mask):
    return mask.astype(F32).astype(BF16)


def wait_bytes(ref, sem):
    pltpu.make_async_copy(ref, ref, sem).wait()


def kernel(
    head, tail, ids, rel, wts, neg, slots, drows,
    main_out, last_out, far_main_out, far_last_out, rx2_out, ry2_out, rz2_out, rel_sum_out,
    nbt, wide, nb, prob, qt, sq, hts, tts, rts, mb, st, st_in, sc, sc_in,
    ot, ot_pair, ot_own, o_sum, o_far, lt, qs, ends, rt_hi, rt_lo,
    packed, arrived, far_main, far_last, slot_col, dest_col,
    gz, gx, gy, rz1, rx1, ry1, azx, rzx, az, ax, ay, rz2, rx2, ry2,
    rp, rp_in, r1b, r2in, r2all, rfin,
    send, recv, known, out_sem, ent_recv,
):
    bucket, shard = lax.axis_index("bucket"), lax.axis_index("shard")
    z, c = bucket // 2, bucket % 2
    x, y = shard // 4, shard % 4
    oc = 1 - c
    partner = (z * 2 + oc, shard)
    pair = ((z + 1 - 2 * (z % 2)) * 2 + c, shard)
    z_far = 3 - z
    far = (z_far * 2 + c, shard)

    def rcopy(src, dst, s_sem, r_sem, device):
        pltpu.make_async_remote_copy(
            src_ref=src, dst_ref=dst, send_sem=s_sem, recv_sem=r_sem,
            device_id=device, device_id_type=MESH,
        ).start()

    barrier = pltpu.get_barrier_semaphore()

    x_peers = [(bucket, lax.rem(x + i, 4) * 4 + y) for i in (1, 2, 3)]
    y_peers = [(bucket, x * 4 + lax.rem(y + i, 4)) for i in (1, 2, 3)]
    friends = [partner, pair, far] + x_peers + y_peers

    def tell(sem, devices):
        for device in devices:
            pl.semaphore_signal(sem, inc=1, device_id=device, device_id_type=MESH)

    tell(barrier, friends)

    for g in range(8):
        qt[g, D:DP, :] = jnp.zeros((DP - D, EC), BF16)
    wide[D:, :] = jnp.ones((16, NEG_DEV), BF16)

    for i in range(8):
        nbt[i] = neg[:, i * 128 : (i + 1) * 128]

    rel_1 = rel[...].astype(BF16)
    rest = rel[...] - rel_1.astype(F32)
    rel_2 = rest.astype(BF16)
    rel_3 = (rest - rel_2.astype(F32)).astype(BF16)
    for j in range(2):
        cols = slice(j * EC, (j + 1) * EC)
        h_t = head[:, cols].astype(F32)
        t_t = tail[:, cols].astype(F32)
        hot = hot_where(iota((REL, EC), 0) == ids[0:1, cols])
        r_t = (nn(rel_1, hot) + nn(rel_2, hot)) + nn(rel_3, hot)
        hre, him = h_t[:HALF], h_t[HALF:]
        rre, rim = r_t[:HALF], r_t[HALF:]
        q = jnp.concatenate([hre * rre - him * rim, hre * rim + him * rre], axis=0).astype(BF16)
        qt[2 * c + j, 0:D, :] = q
        sq[2 * c + j, 0:1, :] = jnp.sum(q.astype(F32) * t_t, axis=0, keepdims=True)
        sq[2 * c + j, 1:2, :] = wts[0:1, cols]
        sq[2 * c + j, 2:8, :] = jnp.zeros((6, EC), F32)
        hts[j] = h_t
        tts[j] = t_t
        rts[j] = r_t

    pl.semaphore_wait(barrier, len(friends))
    tell(known.at[0], y_peers)

    for i in (x, 4 + y):
        rcopy(nbt.at[i], nbt.at[8 + i], send.at[GZ_S], recv.at[GZ_S], far)
    mine, theirs, real = pl.ds(2 * c, 2), pl.ds(4 + 2 * c, 2), pl.ds(0, D)
    rcopy(qt.at[mine, real], qt.at[mine, real], send.at[Q1_S], recv.at[Q1_S], partner)
    rcopy(sq.at[mine], sq.at[mine], send.at[SQ1_S], recv.at[SQ1_S], partner)
    rcopy(qt.at[mine, real], qt.at[theirs, real], send.at[Q2_S], recv.at[Q2_S], pair)
    rcopy(sq.at[mine], sq.at[theirs], send.at[SQ2_S], recv.at[SQ2_S], pair)

    ones = jnp.ones((SLOT, 128), BF16)
    tables = []
    for ref in (slots, drows):
        value = ref[...].astype(F32)
        high = jnp.floor(value * (1.0 / 32.0))
        tables.append((high.astype(BF16), (value - 32.0 * high).astype(BF16)))

    def columns(b, carry):
        owner_hot = hot_where(iota((256, 128), 1) == iota((256, 128), 0) // SLOT + b * NS)
        keep = iota((256, SLOT), 1) == iota((256, SLOT), 0) % SLOT
        for (high, low), out in zip(tables, (slot_col, dest_col)):
            h = jnp.where(keep, nt(owner_hot, high), 0.0).astype(BF16)
            l = jnp.where(keep, nt(owner_hot, low), 0.0).astype(BF16)
            out[b] = 32.0 * nn(h, ones) + nn(l, ones)
        return carry

    lax.fori_loop(0, NB, columns, 0)
    nb[:, 384:DP] = jnp.zeros((NEG_DEV, 128), BF16)

    def flip(b):
        for i in range(8):
            part = nbt[b * 8 + i]
            wide[0:D, i * 128 : (i + 1) * 128] = part
            nb[i * 128 : (i + 1) * 128, 0:D] = part.astype(F32).T.astype(BF16)

    def block(b, two):

        chunks = (2 * two, 2 * two + 1)
        scores = nn(nb[...], jnp.concatenate([qt[g] for g in chunks], axis=1))
        for u, g in enumerate(chunks):
            s = scores[:, u * EC : (u + 1) * EC]
            m = jnp.max(s, axis=0, keepdims=True)
            pb = jnp.exp(s - m).astype(BF16)
            prob[b, :, pl.ds(pl.multiple_of(g * EC, EC), EC)] = pb
            o = nn(wide[...], pb)
            l = o[D : D + 1]
            o = o[0:D]
            mb[b, g, 0:1, :] = m
            if b == 0:
                st[g, 0:1, :] = m
                st[g, 1:2, :] = l
                st[g, 2:8, :] = jnp.zeros((6, EC), F32)
                ot[g] = o
            else:
                m_old = st[g, 0:1, :]
                m_new = jnp.maximum(m_old, m)
                f_old = jnp.exp(m_old - m_new)
                f_new = jnp.exp(m - m_new)
                st[g, 0:1, :] = m_new
                st[g, 1:2, :] = st[g, 1:2, :] * f_old + l * f_new
                ot[g] = ot[g] * f_old + o * f_new

    flip(0)
    block(0, c)
    pl.semaphore_wait(known.at[0], 3)
    tell(known.at[1], (pair, far))
    wait_bytes(nbt.at[pl.ds(8, 2)], recv.at[GZ_S])
    for i in (1, 3, 2):
        xx, yy = lax.rem(x + i, 4), lax.rem(y + i, 4)
        rcopy(nbt.at[8 + x], nbt.at[8 + x], send.at[GX_S], recv.at[GX_S], (bucket, xx * 4 + y))
        rcopy(nbt.at[12 + y], nbt.at[12 + y], send.at[GY_S], recv.at[GY_S], (bucket, x * 4 + yy))
    wait_bytes(qt.at[mine, real], recv.at[Q1_S])
    wait_bytes(sq.at[mine], recv.at[SQ1_S])
    block(0, oc)
    pl.semaphore_wait(known.at[1], 2)
    tell(known.at[2], (pair, far))
    wait_bytes(qt.at[mine, real], recv.at[Q2_S])
    wait_bytes(sq.at[mine], recv.at[SQ2_S])
    rcopy(qt.at[theirs, real], qt.at[theirs, real], send.at[Q3_S], recv.at[Q3_S], partner)
    rcopy(sq.at[theirs], sq.at[theirs], send.at[SQ3_S], recv.at[SQ3_S], partner)
    block(0, 2 + c)
    wait_bytes(qt.at[mine, real], recv.at[Q3_S])
    wait_bytes(sq.at[mine], recv.at[SQ3_S])
    block(0, 2 + oc)
    wait_bytes(nbt.at[pl.ds(8, 3)], recv.at[GX_S])
    wait_bytes(nbt.at[pl.ds(8, 3)], recv.at[GY_S])
    flip(1)
    block(1, 2 + oc)
    pl.semaphore_wait(known.at[2], 2)
    tell(known.at[3], (partner,))
    rcopy(
        ot.at[pl.ds(4 + 2 * oc, 2)], ot_pair, send.at[O1_S], recv.at[O1_S], partner
    )
    block(1, 2 + c)
    own_half, pair_half = pl.ds(0, 4), pl.ds(4, 4)
    rcopy(st.at[pair_half], st_in.at[pair_half], send.at[ST1_S], recv.at[ST1_S], partner)

    def merge(g):
        m_a, m_b = st[g, 0:1, :], st_in[g, 0:1, :]
        m = jnp.maximum(m_a, m_b)
        f_a, f_b = jnp.exp(m_a - m), jnp.exp(m_b - m)
        sc[g, 0:1, :] = m
        sc[g, 1:2, :] = st[g, 1:2, :] * f_a + st_in[g, 1:2, :] * f_b
        sc[g, 2:8, :] = jnp.zeros((6, EC), F32)
        return f_a, f_b

    block(1, oc)
    pl.semaphore_wait(known.at[3], 1)
    rcopy(ot.at[pl.ds(2 * oc, 2)], ot_own, send.at[O3_S], recv.at[O3_S], partner)
    wait_bytes(st_in.at[pair_half], recv.at[ST1_S])
    wait_bytes(ot_pair, recv.at[O1_S])
    for g in range(4, 8):
        merge(g)
    for j in range(2):
        f_a, f_b = merge(4 + 2 * c + j)
        o_sum[j] = (ot[4 + 2 * c + j] * f_a + ot_pair[j] * f_b).astype(BF16)
    rcopy(o_sum.at[0], o_far.at[0], send.at[O4_S], recv.at[O4_S], pair)
    rcopy(sc.at[pair_half], sc_in.at[own_half], send.at[SC1_S], recv.at[SC1_S], pair)
    block(1, c)
    rcopy(st.at[own_half], st_in.at[own_half], send.at[ST2_S], recv.at[ST2_S], partner)
    wait_bytes(st_in.at[own_half], recv.at[ST2_S])
    for g in range(4):
        merge(g)
    rcopy(sc.at[own_half], sc_in.at[pair_half], send.at[SC2_S], recv.at[SC2_S], pair)
    rcopy(o_sum.at[1], o_far.at[1], send.at[O2_S], recv.at[O2_S], pair)
    wait_bytes(sc_in.at[own_half], recv.at[SC1_S])
    wait_bytes(sc_in.at[pair_half], recv.at[SC2_S])
    for g in range(8):
        pos = sq[g, 0:1, :]
        m0, m1 = sc[g, 0:1, :], sc_in[g, 0:1, :]
        top = jnp.maximum(pos, jnp.maximum(m0, m1))
        total = (
            jnp.exp(pos - top)
            + sc[g, 1:2, :] * jnp.exp(m0 - top)
            + sc_in[g, 1:2, :] * jnp.exp(m1 - top)
        )
        lt[g, 0:1, :] = top + jnp.log(total)

    def neg_block(b):
        for g in range(8):
            scale = sq[g, 1:2, :] * jnp.exp(mb[b, g, 0:1, :] - lt[g, 0:1, :])
            qs[:, g * EC : (g + 1) * EC] = (qt[g].astype(F32) * scale).astype(BF16)

        def rows_of(h, carry):
            rr = pl.ds(pl.multiple_of(h * 512, 512), 512)
            acc = nt(prob[b, rr, :], qs[...])
            for u in range(2):
                part = acc[u * 256 : (u + 1) * 256]
                gx[b, 2 * h + u] = part[:, 0:128].astype(BF16)
                for yy in range(4):
                    gy[b, yy, 2 * h + u] = part[yy * 64 : (yy + 1) * 64, 128:256].astype(BF16)
            gz[b, :, rr] = acc[:, 256:512].T[0 : D - 256].astype(BF16)
            return carry

        lax.fori_loop(0, 2, rows_of, 0)
        for i in (1, 3, 2):
            xx, yy = lax.rem(x + i, 4), lax.rem(y + i, 4)
            rcopy(gx.at[b, xx], rx1.at[x, b], send.at[X1_S], recv.at[X1_S], (bucket, xx * 4 + y))
            rcopy(gy.at[b, yy], ry1.at[y, b], send.at[Y1_S], recv.at[Y1_S], (bucket, x * 4 + yy))

    neg_block(1)
    rcopy(gz.at[1], rz1, send.at[Z1_S], recv.at[Z1_S], far)
    wait_bytes(ot_own, recv.at[O3_S])
    wait_bytes(o_far.at[0], recv.at[O4_S])
    wait_bytes(o_far.at[1], recv.at[O2_S])
    ends[D:DP, :] = jnp.zeros((DP - D, 2 * E_DEV), BF16)
    for j in range(2):
        cols = slice(j * EC, (j + 1) * EC)
        tail_cols = slice(E_DEV + j * EC, E_DEV + (j + 1) * EC)
        g = 2 * c + j
        pos, w, ltot = sq[g, 0:1, :], sq[g, 1:2, :], lt[g, 0:1, :]
        pos_coef = w * (jnp.exp(pos - ltot) - 1.0)
        own = w * jnp.exp(st[g, 0:1, :] - ltot)
        other = w * jnp.exp(st_in[g, 0:1, :] - ltot)
        away = w * jnp.exp(sc_in[g, 0:1, :] - ltot)
        grad = pos_coef * tts[j] + ot[g] * own + ot_own[j] * other + o_far[j].astype(F32) * away
        gre, gim = grad[:HALF], grad[HALF:]
        rre, rim = rts[j, :HALF, :], rts[j, HALF:, :]
        hre, him = hts[j, :HALF, :], hts[j, HALF:, :]
        head_grad = jnp.concatenate(
            [gre * rre + gim * rim, gim * rre - gre * rim], axis=0
        ).astype(BF16)
        tail_grad = (pos_coef * qt[g, 0:D, :].astype(F32)).astype(BF16)
        for part, where_to in ((head_grad, cols), (tail_grad, tail_cols)):
            ends[0:D, where_to] = part
            ends[416:432, where_to] = part[384:D]
        term = jnp.concatenate([gre * hre + gim * him, gim * hre - gre * him], axis=0)
        hi = term.astype(BF16)
        rt_hi[:, cols] = hi
        rt_lo[:, cols] = (term - hi.astype(F32)).astype(BF16)

    src_chip = z * NS + shard

    def pack(k, first):
        zz = lax.rem(z + k, NZ)
        chips = pl.ds(pl.multiple_of(zz * NS, NS), NS)
        sel = []
        for d in range(2):
            sc_b = slot_col[zz * 2 + d]
            sel.append(jnp.concatenate(
                [hot_where(sc_b == (iota((256, 128), 1) + 128 * t).astype(F32)) for t in range(8)],
                axis=1,
            ))
        rows = nt(jnp.concatenate(sel, axis=0), ends[...])
        lane = iota((256, 128), 1)
        last = []
        for d in range(2):
            part = rows[d * 256 : (d + 1) * 256]
            for t in range(3):
                first_row = (d * 3 + t) * SLOT
                tile = part[:, t * 128 : (t + 1) * 128].astype(BF16).reshape(NS, SLOT, 128)
                packed[chips, first_row : first_row + SLOT, :] = tile
            dc = dest_col[zz * 2 + d]
            high = jnp.floor(dc * (1.0 / 32.0))
            code = jnp.where(lane == 32 * d + 16, high, jnp.where(lane == 32 * d + 17, dc - 32.0 * high, 0.0))
            last.append(part[:, 384:512] + code)
        tile = jnp.where(lane < 32, last[0], last[1]).astype(BF16).reshape(NS, SLOT, 128)
        packed[chips, 96:112, :] = tile
        for j in range(NS):
            ss = lax.rem(shard + j, NS)
            src = packed.at[zz * NS + ss]
            if first and j == 0:
                pltpu.make_async_copy(src, arrived.at[src_chip], ent_recv.at[k]).start()
            else:
                rcopy(src, arrived.at[src_chip], send.at[ENT_S], ent_recv.at[k], (zz * 2 + c, ss))

    def rel_chunk(r, carry):
        hot = hot_where(iota((128, E_DEV), 0) + r * 128 == ids[...])
        rp[pl.ds(pl.multiple_of(r * 128, 128), 128), :] = nt(hot, rt_hi[...]) + nt(hot, rt_lo[...])
        return carry

    lax.fori_loop(0, 4, rel_chunk, 0)
    rcopy(
        rp.at[pl.ds(pl.multiple_of(oc * 256, 256), 256)], rp_in, send.at[RC_S], recv.at[RC_S], partner
    )

    def pack_other(k, carry):
        pack(k, False)
        return carry

    wait_bytes(rp_in, recv.at[RC_S])
    r1b[...] = (rp[pl.ds(pl.multiple_of(c * 256, 256), 256), :] + rp_in[...]).astype(BF16)
    for j in range(1, NS):
        ss = lax.rem(shard + j, NS)
        rows = r1b.at[pl.ds(pl.multiple_of(ss * 16, 16), 16)]
        rcopy(rows, r2in.at[shard], send.at[R2_S], recv.at[R2_S], (bucket, ss))
    r2in[shard] = r1b[pl.ds(pl.multiple_of(shard * 16, 16), 16), :]

    pack(0, True)
    lax.fori_loop(1, 2, pack_other, 0)
    neg_block(0)

    wait_bytes(rz1, recv.at[Z1_S])
    for r in range(4):
        rr = slice(r * 256, (r + 1) * 256)
        azx[r] = (gz[0, :, rr].astype(F32) + rz1[:, rr].astype(F32)).astype(BF16)
    for i in (1, 3, 2):
        xx = lax.rem(x + i, 4)
        rcopy(azx.at[xx], rzx.at[x], send.at[ZX_S], recv.at[ZX_S], (bucket, xx * 4 + y))

    wait_bytes(r2in.at[pl.ds(0, NS - 1)], recv.at[R2_S])
    r2 = r2in[0].astype(F32)
    for i in range(1, NS):
        r2 = r2 + r2in[i].astype(F32)
    r2all[z] = r2
    for k in (1, 3, 2):
        zz = lax.rem(z + k, NZ)
        rcopy(r2all.at[z], r2all.at[z], send.at[R3_S], recv.at[R3_S], (zz * 2 + c, shard))

    lax.fori_loop(2, NZ, pack_other, 0)


    wait_bytes(rx1.at[pl.ds(0, 3)], recv.at[X1_S])
    for b in range(2):
        total = gx[b, x].astype(F32)
        for i in range(1, 4):
            total = total + rx1[lax.rem(x + i, 4), b].astype(F32)
        ax[b] = total.astype(BF16)
    for i in range(4):
        yy = lax.rem(y + i, 4)
        rows = pl.ds(pl.multiple_of(yy * NEG_OWN, NEG_OWN), NEG_OWN)
        if i:
            rcopy(ax.at[0, rows], rx2.at[y], send.at[X2_S], recv.at[X2_S], (bucket, x * 4 + yy))
        else:
            rx2[y] = ax[0, rows, :]
        rcopy(
            ax.at[1, rows], rx2.at[4 + y], send.at[X2_S], recv.at[X2_S], (z_far * 2 + c, x * 4 + yy)
        )
    wait_bytes(ry1.at[pl.ds(0, 3)], recv.at[Y1_S])
    for b in range(2):
        total = gy[b, y].astype(F32)
        for i in range(1, 4):
            total = total + ry1[lax.rem(y + i, 4), b].astype(F32)
        ay[b] = total.astype(BF16)
    for i in range(4):
        xx = lax.rem(x + i, 4)
        if i:
            rcopy(ay.at[0, xx], ry2.at[x], send.at[Y2_S], recv.at[Y2_S], (bucket, xx * 4 + y))
        else:
            ry2[x] = ay[0, x]
        rcopy(
            ay.at[1, xx], ry2.at[4 + x], send.at[Y2_S], recv.at[Y2_S], (z_far * 2 + c, xx * 4 + y)
        )
    wait_bytes(rzx.at[pl.ds(0, 3)], recv.at[ZX_S])
    total = azx[x].astype(F32)
    for i in range(1, 4):
        total = total + rzx[lax.rem(x + i, 4)].astype(F32)
    wide_sum = jnp.concatenate([total, jnp.zeros((256 - (D - 256), 256), F32)], axis=0)
    az[...] = wide_sum.T.astype(BF16)
    for i in range(4):
        yy = lax.rem(y + i, 4)
        rows = pl.ds(pl.multiple_of(yy * NEG_OWN, NEG_OWN), NEG_OWN)
        if i:
            rcopy(az.at[rows], rz2.at[y], send.at[Z2_S], recv.at[Z2_S], (bucket, x * 4 + yy))
        else:
            rz2[y] = az[rows, :]

    wait_bytes(r2all.at[pl.ds(0, 3)], recv.at[R3_S])
    rel_row = pl.ds(pl.multiple_of(c * 256 + shard * 16, 16), 16)
    rfin[rel_row, :] = (((r2all[0] + r2all[1]) + r2all[2]) + r2all[3]).astype(BF16)
    for j in range(1, NS):
        ss = lax.rem(shard + j, NS)
        rcopy(rfin.at[rel_row], rfin.at[rel_row], send.at[R4_S], recv.at[R4_S], (bucket, ss))

    def give(src, dst, sem):
        pltpu.make_async_copy(src, dst, sem).start()

    other_rows, last_rows = pl.ds(pl.multiple_of(oc * 48, 16), 48), pl.ds(96, SLOT)
    for k in range(NZ):
        chips = pl.ds(pl.multiple_of(lax.rem(z + NZ - k, NZ) * NS, NS), NS)
        wait_bytes(arrived.at[chips], ent_recv.at[k])
        rcopy(arrived.at[chips, other_rows], far_main.at[chips], send.at[PX_S], recv.at[PX_S], partner)
        rcopy(arrived.at[chips, last_rows], far_last.at[chips], send.at[PY_S], recv.at[PY_S], partner)
    give(arrived.at[:, pl.ds(pl.multiple_of(c * 48, 16), 48)], main_out, out_sem.at[0])
    give(arrived.at[:, last_rows], last_out, out_sem.at[5])
    wait_bytes(rfin.at[pl.ds(0, 240)], recv.at[R4_S])
    half_rel = rfin.at[pl.ds(pl.multiple_of(c * 256, 256), 256)]
    rcopy(half_rel, half_rel, send.at[R5_S], recv.at[R5_S], partner)
    wait_bytes(rx2.at[pl.ds(0, 7)], recv.at[X2_S])
    give(rx2, rx2_out, out_sem.at[1])
    wait_bytes(ry2.at[pl.ds(0, 7)], recv.at[Y2_S])
    give(ry2, ry2_out, out_sem.at[2])
    wait_bytes(rz2.at[pl.ds(0, 3)], recv.at[Z2_S])
    give(rz2, rz2_out, out_sem.at[3])
    wait_bytes(half_rel, recv.at[R5_S])
    give(rfin, rel_sum_out, out_sem.at[4])
    wait_bytes(far_main, recv.at[PX_S])
    give(far_main, far_main_out, out_sem.at[6])
    wait_bytes(far_last, recv.at[PY_S])
    give(far_last, far_last_out, out_sem.at[7])

    wait_bytes(nbt.at[pl.ds(0, 2)], send.at[GZ_S])
    wait_bytes(nbt.at[pl.ds(0, 3)], send.at[GX_S])
    wait_bytes(nbt.at[pl.ds(0, 3)], send.at[GY_S])
    for number in (Q1_S, Q2_S, Q3_S):
        wait_bytes(qt.at[mine, real], send.at[number])
    for number in (SQ1_S, SQ2_S, SQ3_S):
        wait_bytes(sq.at[mine], send.at[number])
    for number in (ST1_S, ST2_S, SC1_S, SC2_S):
        wait_bytes(st.at[own_half], send.at[number])
    wait_bytes(ot_pair, send.at[O1_S])
    wait_bytes(o_far.at[0], send.at[O4_S])
    wait_bytes(o_far.at[1], send.at[O2_S])
    wait_bytes(ot_own, send.at[O3_S])
    wait_bytes(arrived.at[pl.ds(0, 63)], send.at[ENT_S])
    wait_bytes(far_main, send.at[PX_S])
    wait_bytes(far_last, send.at[PY_S])
    wait_bytes(rp_in, send.at[RC_S])
    wait_bytes(r2in.at[pl.ds(0, NS - 1)], send.at[R2_S])
    wait_bytes(r2all.at[pl.ds(0, 3)], send.at[R3_S])
    wait_bytes(rfin.at[pl.ds(0, 240)], send.at[R4_S])
    wait_bytes(half_rel, send.at[R5_S])
    wait_bytes(rz1, send.at[Z1_S])
    wait_bytes(rx1.at[pl.ds(0, 3)], send.at[X1_S])
    wait_bytes(ry1.at[pl.ds(0, 3)], send.at[Y1_S])
    wait_bytes(rx2.at[pl.ds(0, 7)], send.at[X2_S])
    wait_bytes(ry2.at[pl.ds(0, 7)], send.at[Y2_S])
    wait_bytes(rz2.at[pl.ds(0, 3)], send.at[Z2_S])
    wait_bytes(rzx.at[pl.ds(0, 3)], send.at[ZX_S])
    for number in (0, 6):
        wait_bytes(far_main, out_sem.at[number])
    for number in (5, 7):
        wait_bytes(far_last, out_sem.at[number])
    wait_bytes(rx2, out_sem.at[1])
    wait_bytes(ry2, out_sem.at[2])
    wait_bytes(rz2, out_sem.at[3])
    wait_bytes(rfin, out_sem.at[4])


def finish(
    main_in, last_in, far_main_in, far_last_in, rx2_in, ry2_in, rz2_in, rel_in,
    ent_out, neg_out, rel_out,
    main, last, far_main, far_last, rx2, ry2, rz2, rel_sum, ent, neg_sum, rel_t, in_sem, out_sem,
):
    loads = [
        pltpu.make_async_copy(src, dst, in_sem.at[i])
        for i, (src, dst) in enumerate((
            (rel_in, rel_sum), (last_in, last), (far_last_in, far_last), (main_in, main),
            (far_main_in, far_main), (rx2_in, rx2), (ry2_in, ry2), (rz2_in, rz2),
        ))
    ]
    for load in loads:
        load.start()
    loads[0].wait()
    for r in range(4):
        rows = rel_sum[r * 128 : (r + 1) * 128, :].astype(F32)
        wide = jnp.concatenate([rows, jnp.zeros((128, DP - D), F32)], axis=1)
        rel_t[:, r * 128 : (r + 1) * 128] = wide.T[0:D]
    stores = [pltpu.make_async_copy(rel_t, rel_out, out_sem.at[0])]
    stores[0].start()

    c = lax.axis_index("bucket") % 2
    lane = iota((8, 128), 1) - 32 * c
    unit = jnp.where(lane == 16, 32.0, jnp.where(lane == 17, 1.0, 0.0)).astype(BF16)
    for load in loads[1:5]:
        load.wait()
    slots, row_ids = [], []
    for tiles, tail in ((main, last), (far_main, far_last)):
        tail_rows = tail[...].reshape(1024, 128)
        columns = [tiles[:, t * SLOT : (t + 1) * SLOT, :].reshape(1024, 128) for t in range(3)]
        slots.append(jnp.concatenate(columns + [tail_rows], axis=1))
        row_ids.append(nt(unit, tail_rows)[0:1, :])
    for r in range(2):
        numbers = (iota((512, 1024), 0) + r * 512).astype(F32)
        got = nn(hot_where(numbers == row_ids[0]), slots[0]) + nn(hot_where(numbers == row_ids[1]), slots[1])
        turned = got.T
        ent[r, 0:384] = turned[0:384]
        ent[r, 384:D] = jnp.where(c == 0, turned[384:400], turned[416:432])
        store = pltpu.make_async_copy(ent.at[r], ent_out.at[:, pl.ds(r * 512, 512)], out_sem.at[1 + r])
        store.start()
        stores.append(store)

    def sum_all(ref):
        total = ref[0].astype(F32)
        for i in range(1, ref.shape[0]):
            total = total + ref[i].astype(F32)
        return total

    for load in loads[5:]:
        load.wait()
    neg_sum[:, 0:128] = sum_all(rx2)
    neg_sum[:, 128:256] = sum_all(ry2)
    neg_sum[:, 256:D] = sum_all(rz2)[:, 0 : D - 256]
    stores.append(pltpu.make_async_copy(neg_sum, neg_out, out_sem.at[3]))
    stores[-1].start()
    for store in stores:
        store.wait()


SCRATCH = [
    ((16, D, 128), BF16),
    ((D + 16, NEG_DEV), BF16),
    ((NEG_DEV, DP), BF16),
    ((2, NEG_DEV, 8 * EC), BF16),
    ((8, DP, EC), BF16),
    ((8, 8, EC), F32),
    ((2, D, EC), F32),
    ((2, D, EC), F32),
    ((2, D, EC), F32),
    ((2, 8, 8, EC), F32),
    ((8, 8, EC), F32),
    ((8, 8, EC), F32),
    ((8, 8, EC), F32),
    ((8, 8, EC), F32),
    ((8, D, EC), F32),
    ((2, D, EC), F32),
    ((2, D, EC), F32),
    ((2, D, EC), BF16),
    ((2, D, EC), BF16),
    ((8, 8, EC), F32),
    ((DP, 8 * EC), BF16),
    ((DP, 2 * E_DEV), BF16),
    ((D, E_DEV), BF16),
    ((D, E_DEV), BF16),
    ((NZ * NS, 112, 128), BF16),
    ((NZ * NS, 112, 128), BF16),
    ((NZ * NS, 48, 128), BF16),
    ((NZ * NS, SLOT, 128), BF16),
    ((NB, 256, 128), F32),
    ((NB, 256, 128), F32),
    ((2, D - 256, NEG_DEV), BF16),
    ((2, 4, 256, 128), BF16),
    ((2, 4, 4, NEG_OWN, 128), BF16),
    ((D - 256, NEG_DEV), BF16),
    ((4, 2, 256, 128), BF16),
    ((4, 2, 4, NEG_OWN, 128), BF16),
    ((4, D - 256, 256), BF16),
    ((4, D - 256, 256), BF16),
    ((256, 256), BF16),
    ((2, 256, 128), BF16),
    ((2, 4, NEG_OWN, 128), BF16),
    ((4, NEG_OWN, 256), BF16),
    ((8, NEG_OWN, 128), BF16),
    ((8, NEG_OWN, 128), BF16),
    ((REL, D), F32),
    ((REL // 2, D), F32),
    ((REL // 2, D), BF16),
    ((NS, 16, D), BF16),
    ((NZ, 16, D), F32),
    ((REL, D), BF16),
]


def per_device(
    head_rows, tail_rows, rel_ids, relations, edge_weights, neg_rows, send_slots, dest_rows
):
    vmem = pl.BlockSpec(memory_space=pltpu.VMEM)
    anywhere = pl.BlockSpec(memory_space=pl.ANY)
    results = pl.pallas_call(
        kernel,
        out_shape=(
            jax.ShapeDtypeStruct((NZ * NS, 48, 128), BF16),
            jax.ShapeDtypeStruct((NZ * NS, SLOT, 128), BF16),
            jax.ShapeDtypeStruct((NZ * NS, 48, 128), BF16),
            jax.ShapeDtypeStruct((NZ * NS, SLOT, 128), BF16),
            jax.ShapeDtypeStruct((8, NEG_OWN, 128), BF16),
            jax.ShapeDtypeStruct((8, NEG_OWN, 128), BF16),
            jax.ShapeDtypeStruct((4, NEG_OWN, 256), BF16),
            jax.ShapeDtypeStruct((REL, D), BF16),
        ),
        in_specs=[vmem] * 8,
        out_specs=(anywhere,) * 8,
        scratch_shapes=[pltpu.VMEM(shape, dtype) for shape, dtype in SCRATCH]
        + [
            pltpu.SemaphoreType.DMA((32,)),
            pltpu.SemaphoreType.DMA((32,)),
            pltpu.SemaphoreType.REGULAR((4,)),
            pltpu.SemaphoreType.DMA((8,)),
            pltpu.SemaphoreType.DMA((NZ,)),
        ],
        compiler_params=pltpu.CompilerParams(
            collective_id=0, has_side_effects=True, vmem_limit_bytes=60 * 1024 * 1024
        ),
        cost_estimate=pl.CostEstimate(
            flops=2 * 3 * 1024 * 4096 * 400, bytes_accessed=8 * 1024 * 1024, transcendentals=1024 * 4096
        ),
        name="complex_backward",
    )(
        head_rows.T,
        tail_rows.T,
        rel_ids.reshape(1, E_DEV),
        relations.T,
        edge_weights.reshape(1, E_DEV),
        neg_rows.T,
        send_slots.T,
        dest_rows.T,
    )
    ent_t, neg_grad, rel_t = pl.pallas_call(
        finish,
        out_shape=(
            jax.ShapeDtypeStruct((D, ENT_DEV), F32),
            jax.ShapeDtypeStruct((NEG_OWN, D), F32),
            jax.ShapeDtypeStruct((D, REL), F32),
        ),
        in_specs=[anywhere] * 8,
        out_specs=(anywhere,) * 3,
        scratch_shapes=[
            pltpu.VMEM((NZ * NS, 48, 128), BF16),
            pltpu.VMEM((NZ * NS, SLOT, 128), BF16),
            pltpu.VMEM((NZ * NS, 48, 128), BF16),
            pltpu.VMEM((NZ * NS, SLOT, 128), BF16),
            pltpu.VMEM((8, NEG_OWN, 128), BF16),
            pltpu.VMEM((8, NEG_OWN, 128), BF16),
            pltpu.VMEM((4, NEG_OWN, 256), BF16),
            pltpu.VMEM((REL, D), BF16),
            pltpu.VMEM((2, D, 512), F32),
            pltpu.VMEM((NEG_OWN, D), F32),
            pltpu.VMEM((D, REL), F32),
            pltpu.SemaphoreType.DMA((8,)),
            pltpu.SemaphoreType.DMA((4,)),
        ],
        compiler_params=pltpu.CompilerParams(vmem_limit_bytes=60 * 1024 * 1024),
        cost_estimate=pl.CostEstimate(
            flops=2 * 1024 * 2048 * 512, bytes_accessed=6 * 1024 * 1024, transcendentals=0
        ),
        name="make_outputs",
    )(*results)
    return ent_t.T, neg_grad, rel_t.T


def solution(mesh):
    return jax.shard_map(
        per_device,
        mesh=mesh,
        in_specs=(
            P(("bucket", "shard"), None),
            P(("bucket", "shard"), None),
            P(("bucket", "shard")),
            P(),
            P(("bucket", "shard")),
            P("bucket", None),
            P(("bucket", "shard"), None),
            P(("bucket", "shard"), None),
        ),
        out_specs=(P(("bucket", "shard"), None), P(("bucket", "shard"), None), P()),
        check_vma=False,
    )
```
